32 devices in a mesh: seq: 8 (over z, y), head: 4 (over x, core).
Axes of the slice: x: 2, y: 2, z: 4, core: 2. Of those that a mesh axis runs over, the one named last changes fastest.
Arguments:
- x_in: bfloat16 [4, 1024, 2048], P(None, 'seq'), may hold values from -6 to 6
- cot: bfloat16 [4, 1024, 2048], P(None, 'seq'), may hold values from -6 to 6
- domain_ids: int32 [4, 1024], P(None, 'seq'), may hold values from 0 to 7
- domain_counts: int32 [8], replicated, may hold values from 256 to 1023
- domain_weights: float32 [8], replicated, may hold values from 0.5 to 2
- block_order: int32 [16], replicated, may hold values from 0 to 15, each once
- norm1: bfloat16 [2048], replicated, may hold values from 0.5 to 1.5
- w_query: bfloat16 [2048, 2048], P(None, 'head'), may hold values from -0.125 to 0.125
- w_key: bfloat16 [2048, 1024], P(None, 'head'), may hold values from -0.125 to 0.125
- w_value: bfloat16 [2048, 1024], P(None, 'head'), may hold values from -0.125 to 0.125
- w_gate_attn: bfloat16 [2048, 2048], P(None, 'head'), may hold values from -0.125 to 0.125
- w_out: bfloat16 [2048, 2048], P('head'), may hold values from -3 to 3
- query_gain: bfloat16 [128], replicated, may hold values from 0.5 to 1.5
- key_gain: bfloat16 [128], replicated, may hold values from 0.5 to 1.5
- norm2: bfloat16 [2048], replicated, may hold values from 0.5 to 1.5
- w_gate: bfloat16 [2048, 6144], P(None, 'head'), may hold values from -0.125 to 0.125
- w_up: bfloat16 [2048, 6144], P(None, 'head'), may hold values from -0.125 to 0.125
- w_down: bfloat16 [6144, 2048], P('head'), may hold values from -0.078125 to 0.078125
Outputs:
- block_out: bfloat16 [4, 1024, 2048], P(None, 'seq')
- x_grad: bfloat16 [4, 1024, 2048], P(None, 'seq')
- norm1_grad: float32 [2048], P('seq')
- w_query_grad: float32 [2048, 2048], P('seq', 'head')
- w_key_grad: float32 [2048, 1024], P('seq', 'head')
- w_value_grad: float32 [2048, 1024], P('seq', 'head')
- w_gate_attn_grad: float32 [2048, 2048], P('seq', 'head')
- w_out_grad: float32 [2048, 2048], P('head', 'seq')
- query_gain_grad: float32 [128], P('seq')
- key_gain_grad: float32 [128], P('seq')
- norm2_grad: float32 [2048], P('seq')
- w_gate_grad: float32 [2048, 6144], P('seq', 'head')
- w_up_grad: float32 [2048, 6144], P('seq', 'head')
- w_down_grad: float32 [6144, 2048], P('head', 'seq')
The draws below stay inside these ranges and needn't reach their ends.
Inputs may be any that keep to these rules, and one draw needn't show every extreme that they name: `block_order`: each value 0 to 15 once.
All inputs are finite; a program needn't handle non-finite values.
Results may differ from the reference program's by a relative error of at most 0.025.
Values may be sent and summed in bfloat16 or wider, within the bound.
A program may use at most 960 MiB of HBM per device.

```python
import math
import jax
import jax.numpy as jnp
from jax import lax

D = 2048
HEADS = 16
KV_HEADS = 8
HEAD_DIM = 128
FF = 6144
SEQS = 4
DOMAINS = 8
QW = 2048
KVW = 1024
LENGTH = 1024
BLOCKS = 16
BLK = 64
TOKENS = 4096


def set_ends(drawn, rng, smallest, top_value):
    dims = drawn.shape
    spot = [jax.random.randint(jax.random.fold_in(rng, axis), (), 0, dims[axis]) for axis in range(len(dims))]
    drawn = drawn.at[tuple(spot)].set(smallest)
    longest = dims.index(max(dims))
    spot[longest] = (spot[longest] + 1) % dims[longest]
    return drawn.at[tuple(spot)].set(top_value)


def spiked(array, own_key, source, target, shards_of, factor):
    owner, partner = [(jnp.arange(array.shape[axis_at]) // (array.shape[axis_at] // shards_of)).reshape([-1 if axis == axis_at else 1 for axis in range(array.ndim)]) for axis_at in (source, target)]
    chosen = jax.random.permutation(own_key, shards_of)[partner]
    strong = (owner == chosen) | (owner == (partner + shards_of // 2) % shards_of)
    return jnp.where(strong, factor * array, array)


def steps_of(stream_key, dims, pieces, low, top_value):
    level = 1.0
    for axis_at, parts in pieces:
        heights = jax.random.uniform(jax.random.fold_in(jax.random.fold_in(stream_key, 6), axis_at), (parts,), jnp.float32, low / len(pieces), top_value / len(pieces))
        level = level * jnp.repeat(jnp.exp(heights), dims[axis_at] // parts).reshape((-1,) + (1,) * (len(dims) - 1 - axis_at))
    return level


def bell_draw(own_key, shape, deviation, most, split=(), held_as=jnp.bfloat16):
    loudness = steps_of(own_key, shape, split, -0.22, 0.18) if split else 1.0
    values = jax.random.normal(own_key, shape, jnp.float32) * deviation * loudness
    return jnp.minimum(jnp.maximum(values, -most), most).astype(held_as)


def bell_draw_with(rng, shape, scale, reach, cuts, heavy, kind=jnp.bfloat16):
    entries = scale * jax.random.normal(rng, shape, jnp.float32)
    if cuts:
        entries = entries * steps_of(rng, shape, cuts, -0.22, 0.18)
    return jnp.clip(spiked(entries, jax.random.fold_in(rng, 3), *heavy), -reach, reach).astype(kind)


def setup_inputs(seed: int = 0) -> dict:
    streams_of = jax.random.split(jax.random.key(seed), 19)
    return {
        "x_in": bell_draw(streams_of[0], (SEQS, LENGTH, D), 1.0, 6.0, ((1, 8),)),
        "cot": bell_draw_with(streams_of[1], (SEQS, LENGTH, D), 1.0, 6.0, ((1, 8),), (1, 2, 8, 2.0)),
        "domain_ids": set_ends(jax.random.randint(streams_of[2], (SEQS, LENGTH), 0, DOMAINS), jax.random.fold_in(streams_of[2], 1), 0, DOMAINS - 1).astype(jnp.int32),
        "domain_counts": set_ends(jax.random.randint(streams_of[3], (DOMAINS,), TOKENS // (2 * DOMAINS), 2 * TOKENS // DOMAINS), jax.random.fold_in(streams_of[3], 1), TOKENS // (2 * DOMAINS), (2 * TOKENS // DOMAINS) - 1).astype(jnp.int32),
        "domain_weights": jnp.clip(jnp.exp(jax.random.uniform(streams_of[4], (DOMAINS,), jnp.float32, math.log(0.5), math.log(2.0))), 0.5, 2.0),
        "block_order": jax.random.permutation(streams_of[5], BLOCKS).astype(jnp.int32),
        "norm1": jnp.clip(jax.random.uniform(streams_of[6], (D,), jnp.float32, 0.5, 1.5), 0.5, 1.5).astype(jnp.bfloat16),
        "w_query": bell_draw(streams_of[7], (D, QW), D ** -0.5, 0.125, ((1, 4),)),
        "w_key": bell_draw(streams_of[8], (D, KVW), D ** -0.5, 0.125, ((1, 4),)),
        "w_value": bell_draw(streams_of[9], (D, KVW), D ** -0.5, 0.125, ((1, 4),)),
        "w_gate_attn": bell_draw(streams_of[10], (D, QW), D ** -0.5, 0.125, ((1, 4),)),
        "w_out": bell_draw(streams_of[11], (QW, D), 4 ** -0.5, 3.0, ((0, 4),)),
        "query_gain": jnp.clip(jax.random.uniform(streams_of[12], (HEAD_DIM,), jnp.float32, 0.5, 1.5), 0.5, 1.5).astype(jnp.bfloat16),
        "key_gain": jnp.clip(jax.random.uniform(streams_of[13], (HEAD_DIM,), jnp.float32, 0.5, 1.5), 0.5, 1.5).astype(jnp.bfloat16),
        "norm2": jnp.clip(jax.random.uniform(streams_of[14], (D,), jnp.float32, 0.5, 1.5), 0.5, 1.5).astype(jnp.bfloat16),
        "w_gate": bell_draw(streams_of[15], (D, FF), D ** -0.5, 0.125, ((1, 4),)),
        "w_up": bell_draw(streams_of[16], (D, FF), D ** -0.5, 0.125, ((1, 4),)),
        "w_down": bell_draw(streams_of[17], (FF, D), FF ** -0.5, 0.078125, ((0, 4),)),
    }


epsilon = 1e-06

@jax.custom_vjp
def low(v):
    return lax.optimization_barrier(v.astype(jnp.bfloat16)).astype(jnp.float32)

@jax.custom_vjp
def low_back(v):
    return v

def low_keep(v):
    return (low(v), None)

def low_pass(kept, grad):
    return (grad,)

def back_keep(v):
    return (v, None)

def back_low(kept, grad):
    return (low(grad),)
low.defvjp(low_keep, low_pass)
low_back.defvjp(back_keep, back_low)

def norm_gain(value, gain):
    return value * lax.rsqrt(lax.optimization_barrier(jnp.mean(value * value, axis=-1, keepdims=True)) + epsilon) * gain

def matmul_exact(left, right):
    return jnp.dot(left, right, precision=lax.Precision.HIGHEST)

def attend(query, key_rows, value_rows, pos_all):
    length = query.shape[0]
    span = min(512, length)
    repeat = HEADS // KV_HEADS
    key_wide = jnp.repeat(key_rows, repeat, axis=1)
    value_wide = jnp.repeat(value_rows, repeat, axis=1)

    def one_block(pair):
        query_block, pos_block = pair
        scores = jnp.einsum('qhd,khd->hqk', query_block, key_wide, precision=lax.Precision.HIGHEST)
        scores = low_back(scores)
        allowed = pos_all[None, None, :] <= pos_block[None, :, None]
        scores = jnp.where(allowed, scores, -1e+30)
        probs = jax.nn.softmax(scores, axis=-1)
        return jnp.einsum('hqk,khd->qhd', low(probs), value_wide, precision=lax.Precision.HIGHEST)
    blocks = lax.map(jax.checkpoint(one_block), (query.reshape(length // span, span, HEADS, HEAD_DIM), pos_all.reshape(length // span, span)))
    return low_back(blocks.reshape(length, HEADS * HEAD_DIM))

def reference(x_in, cot, domain_ids, domain_counts, domain_weights, block_order, norm1, w_query, w_key, w_value, w_gate_attn, w_out, query_gain, key_gain, norm2, w_gate, w_up, w_down):
    params = tuple((weight_arg.astype(jnp.float32) for weight_arg in (norm1, w_query, w_key, w_value, w_gate_attn, w_out, query_gain, key_gain, norm2, w_gate, w_up, w_down)))
    index_all = jnp.arange(LENGTH, dtype=jnp.int32)
    pos_all = block_order[index_all // BLK] * BLK + index_all % BLK
    factor = domain_weights.astype(jnp.float32) * (SEQS * LENGTH) / (DOMAINS * domain_counts.astype(jnp.float32))

    def layer(x_float, gain_one, query_proj, key_proj, value_proj, gate_proj, out_proj, query_scale, key_scale, gain_two, mlp_gate, mlp_up, mlp_down):
        length = x_float.shape[0]
        x_normed = low(norm_gain(x_float, gain_one))
        query_raw = low_back(matmul_exact(x_normed, query_proj)).reshape(length, HEADS, HEAD_DIM)
        key_raw = low_back(matmul_exact(x_normed, key_proj)).reshape(length, KV_HEADS, HEAD_DIM)
        value_rows = low(low_back(matmul_exact(x_normed, value_proj))).reshape(length, KV_HEADS, HEAD_DIM)
        gate_pre = low_back(matmul_exact(x_normed, gate_proj))
        query = low(norm_gain(query_raw, query_scale) * HEAD_DIM ** (-0.5))
        key_rows = low(norm_gain(key_raw, key_scale))
        attn_out = attend(query, key_rows, value_rows, pos_all)
        gated = low(attn_out * jax.nn.sigmoid(gate_pre))
        residual = x_float + low_back(matmul_exact(gated, out_proj))
        h_normed = low(norm_gain(residual, gain_two))
        gate_act = low_back(matmul_exact(h_normed, mlp_gate))
        up_act = low_back(matmul_exact(h_normed, mlp_up))
        mixed = low(jax.nn.silu(gate_act) * up_act)
        return residual + low_back(matmul_exact(mixed, mlp_down))

    def per_sequence(totals, item):
        x_seq, cot_seq, domain_seq = item
        x_float = x_seq.astype(jnp.float32)
        result, pull = jax.vjp(layer, x_float, *params)
        grad_seq = cot_seq.astype(jnp.float32) * factor[domain_seq][:, None]
        grads = pull(grad_seq)
        totals = tuple((running_total + new_term for running_total, new_term in zip(totals, grads[1:])))
        return (totals, (result.astype(jnp.bfloat16), grads[0].astype(jnp.bfloat16)))
    start_totals = tuple((jnp.zeros(weight_arg.shape, jnp.float32) for weight_arg in params))
    totals, (block_out, x_grad) = lax.scan(per_sequence, start_totals, (x_in, cot, domain_ids))
    return (block_out, x_grad, totals[0], totals[1], totals[2], totals[3], totals[4], totals[5], totals[6], totals[7], totals[8], totals[9], totals[10], totals[11])
```

```python
import jax
import jax.numpy as jnp
from jax import lax
from jax.sharding import PartitionSpec as P

epsilon = 1e-06
CHUNKS = 2


def norm_scale(value):
    return lax.rsqrt(jnp.mean(value * value, axis=-1, keepdims=True) + epsilon)


def norm_back(grad_in, normed, scale, gain):
    scaled = grad_in * gain
    return scale * (scaled - normed * jnp.mean(scaled * normed, axis=-1, keepdims=True))


def product(left, right):
    return jnp.dot(left, right, preferred_element_type=jnp.float32)


def outer_sum(left, right):
    return lax.dot_general(
        left, right, (((0,), (0,)), ((), ())), preferred_element_type=jnp.float32
    )


def back_product(left, right):
    return lax.dot_general(
        left, right, (((1,), (1,)), ((), ())), preferred_element_type=jnp.float32
    )


def low(value):
    return value.astype(jnp.bfloat16)


def wide(value):
    return value.astype(jnp.float32)


def bits_of(axis):
    return (lax.axis_size(axis) - 1).bit_length()


def swap(value, axis, mask):
    size = lax.axis_size(axis)
    return lax.ppermute(value, axis, [(i, i ^ mask) for i in range(size)])


def positions(block_order, device, row_count, block_rows):
    stored = device * row_count + jnp.arange(row_count, dtype=jnp.int32)
    slots = stored // block_rows
    slot_index = jnp.arange(block_order.shape[0], dtype=jnp.int32)
    picked = jnp.sum(
        jnp.where(slots[:, None] == slot_index[None, :], block_order[None, :], 0), axis=1
    )
    return picked * block_rows + stored % block_rows


def head_sum(left, weight, apply, cut):
    mine = lax.axis_index("head") & 1
    away = low(apply(left, cut(weight, 1 - mine)))
    got = swap(away, "head", 1)
    total = apply(left, cut(weight, mine)) + wide(got)
    for bit in range(1, bits_of("head")):
        part = low(total)
        total = wide(part) + wide(swap(part, "head", 1 << bit))
    part = low(total)
    other = swap(part, "head", 1)
    low_half = jnp.where(mine == 0, part, other)
    high_half = jnp.where(mine == 0, other, part)
    return wide(jnp.concatenate([low_half, high_half], axis=1))


def all_sum(value, axis):
    for bit in range(bits_of(axis)):
        value = value + swap(value, axis, 1 << bit)
    return value


def by_mask(value, count):
    rows, columns = value.shape
    bits = (count - 1).bit_length()
    value = value.reshape((rows,) + (2,) * bits + (columns // count,))
    own = lax.axis_index("seq")
    for bit in range(bits):
        at = bits - bit
        value = jnp.where(((own >> bit) & 1) == 1, jnp.flip(value, at), value)
    return value.reshape(rows, count, columns // count)


def halves(slots, bit):
    return [j for j in slots if not (j >> bit) & 1], [j for j in slots if (j >> bit) & 1]


def pick(value, slots):
    return jnp.concatenate([value[:, j] for j in slots], axis=1)


def scatter_product(left, right, slots, bits, left_is_slotted):
    def dot(chosen):
        if left_is_slotted:
            out = outer_sum(pick(left, chosen), right)
            return out.reshape(len(chosen), -1, out.shape[1])
        out = outer_sum(left, pick(right, chosen))
        return out.reshape(out.shape[0], len(chosen), -1)

    at = 0 if left_is_slotted else 1
    first = bits[0]
    keep, send = halves(slots, first)
    got = swap(low(dot(send)), "seq", 1 << first)
    total = dot(keep) + wide(got)
    for bit in bits[1:]:
        slots = keep
        keep, send = halves(slots, bit)
        here = jnp.stack([lax.index_in_dim(total, slots.index(j), at, False) for j in keep], at)
        away = jnp.stack([lax.index_in_dim(total, slots.index(j), at, False) for j in send], at)
        total = here + wide(swap(low(away), "seq", 1 << bit))
    return lax.index_in_dim(total, 0, at, False)


def on_device(
    x_in,
    cot,
    domain_ids,
    domain_counts,
    domain_weights,
    block_order,
    norm1,
    w_query,
    w_key,
    w_value,
    w_gate_attn,
    w_out,
    query_gain,
    key_gain,
    norm2,
    w_gate,
    w_up,
    w_down,
):
    sequences, local_rows, width = x_in.shape
    row_total = sequences * local_rows
    head_dim = query_gain.shape[0]
    kv_local = w_key.shape[1] // head_dim
    q_local = w_query.shape[1] // head_dim
    group = q_local // kv_local
    devices = lax.axis_size("seq")
    bits = list(range(bits_of("seq")))
    own = lax.axis_index("seq")
    block_rows = local_rows * devices // block_order.shape[0]
    query_factor = head_dim ** (-0.5)
    q_gain, k_gain = wide(query_gain), wide(key_gain)
    gain_one, gain_two = wide(norm1), wide(norm2)

    def cut_columns(weight, half):
        return lax.dynamic_slice_in_dim(weight, half * (width // 2), width // 2, 1)

    def cut_rows(weight, half):
        return lax.dynamic_slice_in_dim(weight, half * (width // 2), width // 2, 0)

    x_float = wide(x_in.reshape(row_total, width))
    scale_one = norm_scale(x_float)
    normed_one = x_float * scale_one
    x_normed = low(normed_one * gain_one)
    key_raw = product(x_normed, w_key).reshape(row_total, kv_local, head_dim)
    key_scale = norm_scale(key_raw)
    key_normed = key_raw * key_scale
    key_rows = low(key_normed * k_gain).reshape(row_total, kv_local * head_dim)
    value_rows = low(product(x_normed, w_value))
    pair = jnp.concatenate([key_rows, value_rows], axis=1).reshape(sequences, local_rows, -1)
    kv_width = kv_local * head_dim

    seqs_of = sequences // CHUNKS
    rows_of = row_total // CHUNKS

    def gather(value):
        slots = {0: value}
        for mask in range(2, devices, 2):
            slots[mask] = swap(value, "seq", mask)
        for mask in range(0, devices, 2):
            slots[mask + 1] = swap(slots[mask], "seq", 1)
        return jnp.stack([slots[j] for j in range(devices)], axis=1).reshape(
            seqs_of, devices * local_rows, -1
        )

    gathered = [gather(pair[c * seqs_of : (c + 1) * seqs_of]) for c in range(CHUNKS)]

    query_raw = product(x_normed, w_query).reshape(row_total, q_local, head_dim)
    gate_pre = product(x_normed, w_gate_attn)
    query_scale = norm_scale(query_raw)
    query_normed = query_raw * query_scale
    query = low(query_normed * q_gain * query_factor)
    gate_sig = jax.nn.sigmoid(gate_pre)

    query_pos = positions(block_order, own, local_rows, block_rows)
    key_pos = jnp.concatenate(
        [positions(block_order, own ^ j, local_rows, block_rows) for j in range(devices)]
    )
    allowed = key_pos[None, :] <= query_pos[:, None]

    domain_total = domain_weights.shape[0]
    domain_index = jnp.arange(domain_total, dtype=jnp.int32)
    factor = domain_weights * (row_total * devices) / (domain_total * wide(domain_counts))
    picked = domain_ids.reshape(row_total)[:, None] == domain_index[None, :]
    row_scale = jnp.sum(jnp.where(picked, factor[None, :], 0.0), axis=1)
    grad_out = wide(cot.reshape(row_total, width)) * row_scale[:, None]
    grad_low = low(grad_out)

    saved = []
    for c in range(CHUNKS):
        rows = slice(c * rows_of, (c + 1) * rows_of)
        heads = (
            query[rows]
            .reshape(seqs_of, local_rows, kv_local, group, head_dim)
            .transpose(0, 2, 3, 1, 4)
        )
        keys = gathered[c][..., :kv_width].reshape(seqs_of, -1, kv_local, head_dim)
        values = gathered[c][..., kv_width:].reshape(seqs_of, -1, kv_local, head_dim)
        scores = jnp.einsum("skgqd,spkd->skgqp", heads, keys, preferred_element_type=jnp.float32)
        scores = jnp.where(allowed, scores, -1e30)
        top = jnp.max(scores, axis=-1)
        weights = jnp.where(allowed, jnp.exp(scores - top[..., None]), 0.0)
        total = jnp.sum(weights, axis=-1)
        mixed = jnp.einsum(
            "skgqp,spkd->skgqd", low(weights), values, preferred_element_type=jnp.float32
        )
        attn_heads = mixed / total[..., None]
        log_total = top + jnp.log(total)
        attn_flat = attn_heads.transpose(0, 3, 1, 2, 4).reshape(rows_of, q_local * head_dim)
        gated = low(attn_flat * gate_sig[rows])
        attn_sum = head_sum(gated, w_out, product, cut_columns)
        saved.append((rows, heads, keys, values, log_total, attn_heads, attn_flat, gated, attn_sum))

    forward = []
    for c in range(CHUNKS):
        rows, attn_sum = saved[c][0], saved[c][-1]
        residual = x_float[rows] + attn_sum
        scale_two = norm_scale(residual)
        normed_two = residual * scale_two
        h_normed = low(normed_two * gain_two)
        gate_proj = product(h_normed, w_gate)
        up_proj = product(h_normed, w_up)
        gate_logit = jax.nn.sigmoid(gate_proj)
        gate_act = gate_proj * gate_logit
        hidden = low(gate_act * up_proj)
        grad_mixed = back_product(grad_low[rows], w_down)
        grad_gate = low(
            grad_mixed * up_proj * gate_logit * (1.0 + gate_proj * (1.0 - gate_logit))
        )
        grad_up = low(grad_mixed * gate_act)

        def both(pair_of, weights_of):
            return back_product(pair_of[0], weights_of[0]) + back_product(
                pair_of[1], weights_of[1]
            )

        grad_hnorm = head_sum(
            (grad_gate, grad_up),
            (w_gate, w_up),
            both,
            lambda ws, half: tuple(cut_rows(w, half) for w in ws),
        )
        forward.append(
            (residual, scale_two, normed_two, h_normed, hidden, grad_gate, grad_up, grad_hnorm)
        )

    def joined(at):
        return jnp.concatenate([f[at] for f in forward], axis=0)

    residual, scale_two, normed_two, h_normed, hidden, grad_gate, grad_up, grad_hnorm = (
        joined(i) for i in range(8)
    )

    all_slots = list(range(devices))
    even, odd = halves(all_slots, 0)
    rest = bits[1:]

    def paired(value):
        return jnp.concatenate([value, swap(value, "seq", 1)], axis=0)

    def paired_slots(value):
        split = by_mask(value, devices)
        stay = pick(split, even)
        come = swap(pick(split, odd), "seq", 1)
        out = jnp.concatenate([stay, come], axis=0)
        return out.reshape(out.shape[0], len(even), -1)

    rest_shifted = [b - 1 for b in rest]

    def scatter_rest(left, right, left_is_slotted):
        at = 0 if left_is_slotted else 1

        def dot(chosen):
            if left_is_slotted:
                out = outer_sum(pick(left, chosen), right)
                return out.reshape(len(chosen), -1, out.shape[1])
            out = outer_sum(left, pick(right, chosen))
            return out.reshape(out.shape[0], len(chosen), -1)

        slots = [j >> 1 for j in even]
        keep, total = None, None
        for bit in rest_shifted:
            if total is None:
                keep, send = halves(slots, bit)
                got = swap(low(dot(send)), "seq", 2 << bit)
                total = dot(keep) + wide(got)
            else:
                slots = keep
                keep, send = halves(slots, bit)
                here = jnp.stack(
                    [lax.index_in_dim(total, slots.index(j), at, False) for j in keep], at
                )
                away = jnp.stack(
                    [lax.index_in_dim(total, slots.index(j), at, False) for j in send], at
                )
                total = here + wide(swap(low(away), "seq", 2 << bit))
        return lax.index_in_dim(total, 0, at, False)

    out_slots = paired_slots(grad_low)
    norm_slots = paired_slots(h_normed)
    grad_down = scatter_rest(paired(hidden), out_slots, False)
    grad_mlp_gate = scatter_rest(norm_slots, paired(grad_gate), True)
    grad_mlp_up = scatter_rest(norm_slots, paired(grad_up), True)

    grad_norm_two = jnp.sum(grad_hnorm * normed_two, axis=0)
    grad_resid = grad_out + norm_back(grad_hnorm, normed_two, scale_two, gain_two)
    grad_attn = low(grad_resid)

    hidden_late, _ = lax.optimization_barrier((hidden, grad_hnorm))
    mlp_sum = head_sum(hidden_late, w_down, product, cut_columns)
    block_out = low(residual + mlp_sum).reshape(sequences, local_rows, width)

    back = []
    for c in range(CHUNKS):
        rows, heads, keys, values, log_total, attn_heads, attn_flat, gated, _ = saved[c]
        sig = gate_sig[rows]
        grad_gated = back_product(grad_attn[rows], w_out)
        grad_heads_flat = low(grad_gated * sig)
        grad_gatepre = low(grad_gated * attn_flat * sig * (1.0 - sig))
        grad_heads = grad_heads_flat.reshape(
            seqs_of, local_rows, kv_local, group, head_dim
        ).transpose(0, 2, 3, 1, 4)
        row_delta = jnp.sum(wide(grad_heads) * attn_heads, axis=-1)
        scores = jnp.einsum("skgqd,spkd->skgqp", heads, keys, preferred_element_type=jnp.float32)
        probs = jnp.where(
            allowed, jnp.exp(jnp.where(allowed, scores, -1e30) - log_total[..., None]), 0.0
        )
        grad_probs = jnp.einsum(
            "skgqd,spkd->skgqp", grad_heads, values, preferred_element_type=jnp.float32
        )
        grad_scores = low(probs * (grad_probs - row_delta[..., None]))
        grad_query = jnp.einsum(
            "skgqp,spkd->skgqd", grad_scores, keys, preferred_element_type=jnp.float32
        )
        key_term = jnp.einsum(
            "skgqp,skgqd->spkd", grad_scores, heads, preferred_element_type=jnp.float32
        ).reshape(seqs_of, devices, local_rows, kv_width)
        value_term = jnp.einsum(
            "skgqp,skgqd->spkd", low(probs), grad_heads, preferred_element_type=jnp.float32
        ).reshape(seqs_of, devices, local_rows, kv_width)
        terms = jnp.concatenate([key_term, value_term], axis=-1)
        parts = {j: terms[:, j] for j in range(devices)}
        for bit in bits:
            keep, send = halves(sorted(parts), bit)
            got = swap(low(jnp.stack([parts[j] for j in send])), "seq", 1 << bit)
            parts = {j: parts[j] + wide(got[i]) for i, j in enumerate(keep)}
        own_terms = parts[0].reshape(rows_of, 2 * kv_width)
        grad_query_rows = grad_query.transpose(0, 3, 1, 2, 4).reshape(rows_of, q_local, head_dim)
        back.append((grad_gatepre, grad_query_rows, own_terms))

    grad_gatepre, grad_query_rows, own_terms = (
        jnp.concatenate([b[i] for b in back], axis=0) for i in range(3)
    )
    gated = jnp.concatenate([s[7] for s in saved], axis=0)

    grad_qgain_part = jnp.sum(grad_query_rows * query_normed * query_factor, axis=(0, 1))
    grad_query_raw = low(
        norm_back(grad_query_rows, query_normed, query_scale, q_gain * query_factor)
    ).reshape(row_total, q_local * head_dim)
    grad_key_rows = own_terms[:, :kv_width].reshape(row_total, kv_local, head_dim)
    grad_kgain_part = jnp.sum(grad_key_rows * key_normed, axis=(0, 1))
    grad_key_raw = low(norm_back(grad_key_rows, key_normed, key_scale, k_gain)).reshape(
        row_total, kv_width
    )
    grad_value_low = low(own_terms[:, kv_width:])

    x_slots = by_mask(x_normed, devices)
    attn_slots = by_mask(grad_attn, devices)
    grad_wout = scatter_product(gated, attn_slots, all_slots, bits, False)
    early = scatter_product(
        x_slots, jnp.concatenate([grad_gatepre, grad_query_raw], axis=1), all_slots, bits, True
    )
    late = scatter_product(
        x_slots, jnp.concatenate([grad_key_raw, grad_value_low], axis=1), all_slots, bits, True
    )
    grad_wgate_attn, grad_wquery = jnp.split(early, 2, axis=1)
    grad_wkey, grad_wvalue = jnp.split(late, 2, axis=1)

    def all_four(grads, weights):
        return sum(back_product(g, w) for g, w in zip(grads, weights))

    grad_xnorm = head_sum(
        (grad_query_raw, grad_key_raw, grad_value_low, grad_gatepre),
        (w_query, w_key, w_value, w_gate_attn),
        all_four,
        lambda ws, half: tuple(cut_rows(w, half) for w in ws),
    )
    grad_norm_one = jnp.sum(grad_xnorm * normed_one, axis=0)
    x_grad = low(grad_resid + norm_back(grad_xnorm, normed_one, scale_one, gain_one)).reshape(
        sequences, local_rows, width
    )

    gains = all_sum(all_sum(jnp.concatenate([grad_qgain_part, grad_kgain_part]), "head"), "seq")
    norms = all_sum(jnp.concatenate([grad_norm_one, grad_norm_two]), "seq")

    def own_part(value):
        size = value.shape[0] // devices
        return lax.dynamic_slice_in_dim(value, own * size, size, 0)

    return (
        block_out,
        x_grad,
        own_part(norms[:width]),
        grad_wquery,
        grad_wkey,
        grad_wvalue,
        grad_wgate_attn,
        grad_wout,
        own_part(gains[:head_dim]),
        own_part(gains[head_dim:]),
        own_part(norms[width:]),
        grad_mlp_gate,
        grad_mlp_up,
        grad_down,
    )


def solution(mesh):
    return jax.shard_map(
        on_device,
        mesh=mesh,
        in_specs=(
            P(None, "seq", None),
            P(None, "seq", None),
            P(None, "seq"),
            P(),
            P(),
            P(),
            P(),
            P(None, "head"),
            P(None, "head"),
            P(None, "head"),
            P(None, "head"),
            P("head", None),
            P(),
            P(),
            P(),
            P(None, "head"),
            P(None, "head"),
            P("head", None),
        ),
        out_specs=(
            P(None, "seq", None),
            P(None, "seq", None),
            P("seq"),
            P("seq", "head"),
            P("seq", "head"),
            P("seq", "head"),
            P("seq", "head"),
            P("head", "seq"),
            P("seq"),
            P("seq"),
            P("seq"),
            P("seq", "head"),
            P("seq", "head"),
            P("head", "seq"),
        ),
        check_vma=False,
    )
```

```python
import jax
import jax.numpy as jnp
from jax import lax
from jax.experimental import pallas as pl
from jax.experimental.pallas import tpu as pltpu
from jax.sharding import PartitionSpec as P

epsilon = 1e-06
CHUNKS = 2


def norm_scale(value):
    return lax.rsqrt(jnp.mean(value * value, axis=-1, keepdims=True) + epsilon)


def norm_back(grad_in, normed, scale, gain):
    scaled = grad_in * gain
    return scale * (scaled - normed * jnp.mean(scaled * normed, axis=-1, keepdims=True))


def product(left, right):
    return jnp.dot(left, right, preferred_element_type=jnp.float32)


def outer_sum(left, right):
    return lax.dot_general(
        left, right, (((0,), (0,)), ((), ())), preferred_element_type=jnp.float32
    )


def back_product(left, right):
    return lax.dot_general(
        left, right, (((1,), (1,)), ((), ())), preferred_element_type=jnp.float32
    )


def low(value):
    return value.astype(jnp.bfloat16)


def wide(value):
    return value.astype(jnp.float32)


def bits_of(axis):
    return (lax.axis_size(axis) - 1).bit_length()


def swap(value, axis, mask):
    size = lax.axis_size(axis)
    return lax.ppermute(value, axis, [(i, i ^ mask) for i in range(size)])


def positions(block_order, device, row_count, block_rows):
    stored = device * row_count + jnp.arange(row_count, dtype=jnp.int32)
    slots = stored // block_rows
    slot_index = jnp.arange(block_order.shape[0], dtype=jnp.int32)
    picked = jnp.sum(
        jnp.where(slots[:, None] == slot_index[None, :], block_order[None, :], 0), axis=1
    )
    return picked * block_rows + stored % block_rows


def head_sum(left, weight, apply, cut):
    mine = lax.axis_index("head") & 1
    away = low(apply(left, cut(weight, 1 - mine)))
    got = swap(away, "head", 1)
    total = apply(left, cut(weight, mine)) + wide(got)
    for bit in range(1, bits_of("head")):
        part = low(total)
        total = wide(part) + wide(swap(part, "head", 1 << bit))
    part = low(total)
    other = swap(part, "head", 1)
    low_half = jnp.where(mine == 0, part, other)
    high_half = jnp.where(mine == 0, other, part)
    return wide(jnp.concatenate([low_half, high_half], axis=1))


MESH = pl.DeviceIdType.MESH
TILE = 256


def other_z(z, t):
    low_z, high_z = lax.rem(z, 2), lax.div(z, 2)
    low_t, high_t = lax.rem(t, 2), lax.div(t, 2)
    return (low_z + low_t - 2 * low_z * low_t) + 2 * (high_z + high_t - 2 * high_z * high_t)


def dot_plain(left, right):
    return jnp.dot(left, right, preferred_element_type=jnp.float32)


def dot_rows(left, right):
    return lax.dot_general(
        left, right, (((1,), (1,)), ((), ())), preferred_element_type=jnp.float32
    )


def dot_first(left, right):
    return lax.dot_general(
        left, right, (((0,), (0,)), ((), ())), preferred_element_type=jnp.float32
    )


def back_kernel(
    h_hbm, cot_hbm, x_hbm, xt_hbm, q_hbm, kv_hbm, o_hbm, sig_hbm, y_hbm, qraw_hbm, kraw_hbm,
    wg_hbm, wu_hbm, wd_hbm, wo_hbm, wq_hbm, wk_hbm, wv_hbm, wga_hbm,
    factor_ref, lse_ref, kpos_ref, qpos_ref, n1_ref, n2_ref, qg_ref, kg_ref,
    block_out, x_out, items_out, norms_out, gains_out, dh_hbm, zlo_hbm, zhi_hbm,
    acts, lt, odd, csend, crecv, xrecv, fin, yrecv, lrecv, hrecv,
    zlo_send, zhi_send, stage, ostage, wide_a, wide_b, delta,
    vec, vec_got, gvec, gvec_got,
    ya_s, ya_r, zl_s, zl_r, zh_s, zh_r, lt_s, lt_r, lc_s, lc_r,
    c1_s, c1_r, x_s, x_r, c2_s, c2_r, ky_s, ky_r, kl_s, kl_r, kh_s, kh_r,
    nv_s, nv_r, gv_s, gv_r, st_sem, out_sem, misc, credit,
):
    seq, head = lax.axis_index("seq"), lax.axis_index("head")
    z, y = lax.div(seq, 2), lax.rem(seq, 2)
    c = lax.rem(head, 2)
    y_dev = {"seq": z * 2 + 1 - y}
    lo_dev = {"seq": other_z(z, 1) * 2 + y}
    hi_dev = {"seq": other_z(z, 2) * 2 + y}
    core_dev = {"head": head + 1 - 2 * c}
    x_dev = {"head": head + 2 - 4 * lax.div(head, 2)}
    tokens = cot_hbm.shape[0]
    rows = kpos_ref.shape[0] // 8
    seqs = tokens // rows
    hidden_tiles = wd_hbm.shape[0] // TILE
    ff_items = 3 * hidden_tiles
    width = cot_hbm.shape[1]
    epsilon_k = 1e-06

    barrier = pltpu.get_barrier_semaphore()
    for device in (y_dev, lo_dev, hi_dev, core_dev, x_dev):
        pl.semaphore_signal(barrier, inc=1, device_id=device, device_id_type=MESH)
    pl.semaphore_wait(barrier, 5)

    def remote(src, dst, send, recv, device):
        return pltpu.make_async_remote_copy(
            src_ref=src, dst_ref=dst, send_sem=send, recv_sem=recv, device_id=device, device_id_type=MESH
        )

    def act_copy(i):
        return remote(acts.at[i, 0], acts.at[i, 1], ya_s.at[i], ya_r.at[i], y_dev)

    def lt_copy(l):
        return remote(odd.at[l], lt.at[l, 1, pl.ds(2 * c, 2)], lt_s.at[l], lt_r.at[l], y_dev)

    def lt_relay(l):
        piece = lt.at[l, 1, pl.ds(2 * c, 2)]
        return remote(piece, piece, lc_s.at[l], lc_r.at[l], core_dev)

    def lt_relay_in(l):
        piece = lt.at[l, 1, pl.ds(2 - 2 * c, 2)]
        return remote(piece, piece, lc_s.at[l], lc_r.at[l], core_dev)

    def zlo_copy(i):
        return remote(zlo_send.at[lax.rem(i, 4)], zlo_hbm.at[i], zl_s.at[i], zl_r.at[i], lo_dev)

    def zhi_copy(i):
        return remote(zhi_send.at[lax.rem(i, 4)], zhi_hbm.at[i], zh_s.at[i], zh_r.at[i], hi_dev)

    def item_dot(i, l, t):
        return dot_plain(lt[l, 0, t], acts[i, 0]) + dot_plain(lt[l, 1, t], acts[i, 1])

    def stage_one(first, last, l_of):
        @pl.loop(first, last)
        def _(i):
            l = l_of(i)
            act_copy(i).wait_recv()

            @pl.when(i >= 4)
            def _():
                zlo_copy(i - 4).wait_send()

            slot = lax.rem(i, 4)
            for k in range(2):
                zlo_send[slot, k] = low(item_dot(i, l, 2 * k + 1))
            zlo_copy(i).start()

    def stage_two(first, last, l_of):
        @pl.loop(first, last)
        def _(i):
            l = l_of(i)
            zlo_copy(i).wait_recv()
            here = pltpu.make_async_copy(zlo_hbm.at[i, 1], stage.at[0], st_sem.at[0])
            here.start()

            @pl.when(i >= 4)
            def _():
                zhi_copy(i - 4).wait_send()

            total = item_dot(i, l, 2)
            here.wait()
            zhi_send[lax.rem(i, 4)] = low(total + wide(stage[0]))
            zhi_copy(i).start()

    def out_copy(i):
        slot = lax.rem(i, 2)
        return pltpu.make_async_copy(ostage.at[slot], items_out.at[i], out_sem.at[slot])

    def stage_three(first, last, l_of):
        @pl.loop(first, last)
        def _(i):
            l = l_of(i)
            zhi_copy(i).wait_recv()
            one = pltpu.make_async_copy(zlo_hbm.at[i, 0], stage.at[0], st_sem.at[0])
            two = pltpu.make_async_copy(zhi_hbm.at[i], stage.at[1], st_sem.at[1])
            one.start()
            two.start()

            @pl.when(i >= 2)
            def _():
                out_copy(i - 2).wait()

            total = item_dot(i, l, 0)
            one.wait()
            two.wait()
            ostage[lax.rem(i, 2)] = total + wide(stage[0]) + wide(stage[1])
            out_copy(i).start()

    def ff_l(i):
        return 1 - lax.div(lax.rem(i, 3) + 1, 2)

    def const_l(l):
        return lambda i: l

    def back(stages):
        for stage_of, first, last in stages:
            for a, b, l_of in (
                (0, ff_items, ff_l),
                (ff_items, ff_items + 2, const_l(2)),
                (ff_items + 2, ff_items + 4, const_l(3)),
                (ff_items + 4, ff_items + 8, const_l(2)),
            ):
                lo_i, hi_i = max(first, a), min(last, b)
                if lo_i < hi_i:
                    stage_of(lo_i, hi_i, l_of)

    def spread(l, source):
        @pl.loop(0, 4)
        def _(t):
            at = pl.multiple_of((other_z(z, t) * 2 + y) * TILE, TILE)
            lt[l, 0, t] = source[:, pl.ds(at, TILE)].T

        @pl.loop(0, 2)
        def _(k):
            at = pl.multiple_of((other_z(z, 2 * c + k) * 2 + 1 - y) * TILE, TILE)
            odd[l, k] = source[:, pl.ds(at, TILE)].T

        lt_copy(l).start()

    def relay(l):
        lt_copy(l).wait_recv()
        lt_relay(l).start()

    def core_copy(k, b):
        return remote(csend.at[b], crecv.at[k % 2, b], c1_s.at[k, b], c1_r.at[k, b], core_dev)

    def x_copy(k, b):
        return remote(fin.at[k % 2, c * 4 + b], xrecv.at[k % 2, b], x_s.at[k, b], x_r.at[k, b], x_dev)

    def fin_copy(k, b):
        piece = fin.at[k % 2, c * 4 + b]
        return remote(piece, piece, c2_s.at[k, b], c2_r.at[k, b], core_dev)

    def fin_copy_in(k, b):
        piece = fin.at[k % 2, (1 - c) * 4 + b]
        return remote(piece, piece, c2_s.at[k, b], c2_r.at[k, b], core_dev)

    def reduce_start(k, loads, compute):
        def block_of(step):
            return lax.rem(c + 1 + step, 2) * 4 + lax.div(step, 2)

        for copy in loads(block_of(0), 0):
            copy.start()

        @pl.loop(0, 8)
        def _(step):
            slot, b = lax.rem(step, 2), lax.div(step, 2)

            @pl.when(step < 7)
            def _():
                for copy in loads(block_of(step + 1), 1 - slot):
                    copy.start()

            for copy in loads(block_of(step), slot):
                copy.wait()
            part = compute(slot)

            @pl.when(slot == 0)
            def _():
                csend[b] = low(part)
                core_copy(k, b).start()

            @pl.when(slot == 1)
            def _():
                core_copy(k, b).wait_recv()
                fin[k % 2, c * 4 + b] = low(part + wide(crecv[k % 2, b]))
                x_copy(k, b).start()

        @pl.loop(0, 4)
        def _(b):
            core_copy(k, b).wait_send()

    def reduce_end(k):
        @pl.loop(0, 4)
        def _(b):
            x_copy(k, b).wait()
            fin[k % 2, c * 4 + b] = low(wide(fin[k % 2, c * 4 + b]) + wide(xrecv[k % 2, b]))
            fin_copy(k, b).start()

        @pl.loop(0, 4)
        def _(b):
            fin_copy_in(k, b).wait_recv()
            fin_copy(k, b).wait_send()

    def fin_rows(k, at, count):
        return jnp.concatenate([wide(fin[k % 2, n, pl.ds(at, count)]) for n in range(8)], axis=1)

    def rms(value):
        return lax.rsqrt(jnp.mean(value * value, axis=-1, keepdims=True) + epsilon_k)

    n_chunks = tokens // 128

    def first_phase(hbuf, cbuf, wgb, wub, wdb, sems, w_sems):
        def row_loads(r, slot):
            at = pl.ds(r * 128, 128)
            return (
                pltpu.make_async_copy(h_hbm.at[at], hbuf.at[slot], sems.at[slot, 0]),
                pltpu.make_async_copy(cot_hbm.at[at], cbuf.at[slot], sems.at[slot, 1]),
            )

        def tile_loads(j, slot):
            at = pl.ds(pl.multiple_of(j * TILE, TILE), TILE)
            return (
                pltpu.make_async_copy(wg_hbm.at[:, at], wgb.at[slot], w_sems.at[slot, 0]),
                pltpu.make_async_copy(wu_hbm.at[:, at], wub.at[slot], w_sems.at[slot, 1]),
                pltpu.make_async_copy(wd_hbm.at[at], wdb.at[slot], w_sems.at[slot, 2]),
            )

        for copy in row_loads(0, 0):
            copy.start()
        for copy in tile_loads(0, 0):
            copy.start()

        @pl.loop(0, n_chunks)
        def _(r):
            slot = lax.rem(r, 2)

            @pl.when(r < n_chunks - 1)
            def _():
                for copy in row_loads(r + 1, 1 - slot):
                    copy.start()

            for copy in row_loads(r, slot):
                copy.wait()
            value = hbuf[slot]
            at = pl.ds(pl.multiple_of(r * 128, 128), 128)
            wide_a[at] = low(value * rms(value) * n2_ref[...])
            wide_b[at] = low(wide(cbuf[slot]) * factor_ref[at])

        @pl.loop(0, hidden_tiles)
        def _(j):
            slot = lax.rem(j, 2)

            @pl.when(j < hidden_tiles - 1)
            def _():
                for copy in tile_loads(j + 1, 1 - slot):
                    copy.start()

            for copy in tile_loads(j, slot):
                copy.wait()

            @pl.loop(0, 2)
            def _(half):
                at = pl.ds(pl.multiple_of(half * (tokens // 2), 128), tokens // 2)
                a = dot_plain(wide_a[at], wgb[slot])
                u = dot_plain(wide_a[at], wub[slot])
                dm = dot_rows(wide_b[at], wdb[slot])
                sig = jax.nn.sigmoid(a)
                act = a * sig
                acts[3 * j, 0, at] = low(act * u)
                acts[3 * j + 1, 0, at] = low(dm * u * sig * (1.0 + a * (1.0 - sig)))
                acts[3 * j + 2, 0, at] = low(dm * act)

            for k in range(3):
                act_copy(3 * j + k).start()

            @pl.when(j == 0)
            def _():
                spread(1, wide_b)
                spread(0, wide_a)

    pl.run_scoped(
        first_phase,
        pltpu.VMEM((2, 128, width), jnp.float32),
        pltpu.VMEM((2, 128, width), jnp.bfloat16),
        pltpu.VMEM((2, width, TILE), jnp.bfloat16),
        pltpu.VMEM((2, width, TILE), jnp.bfloat16),
        pltpu.VMEM((2, TILE, width), jnp.bfloat16),
        pltpu.SemaphoreType.DMA((2, 2)),
        pltpu.SemaphoreType.DMA((2, 3)),
    )

    def second_phase(wa, wb, sems):
        def loads(n, slot):
            at = pl.ds(pl.multiple_of(n * TILE, TILE), TILE)
            return (
                pltpu.make_async_copy(wg_hbm.at[at], wa.at[slot], sems.at[slot, 0]),
                pltpu.make_async_copy(wu_hbm.at[at], wb.at[slot], sems.at[slot, 1]),
            )

        def compute(slot):
            total = None
            for j in range(hidden_tiles):
                at = pl.ds(j * TILE, TILE)
                part = dot_rows(acts[3 * j + 1, 0], wa[slot, :, at])
                part += dot_rows(acts[3 * j + 2, 0], wb[slot, :, at])
                total = part if total is None else total + part
            return total

        reduce_start(0, loads, compute)

    pl.run_scoped(
        second_phase,
        pltpu.VMEM((2, TILE, wg_hbm.shape[1]), jnp.bfloat16),
        pltpu.VMEM((2, TILE, wg_hbm.shape[1]), jnp.bfloat16),
        pltpu.SemaphoreType.DMA((2, 2)),
    )

    def third_phase(wa, sems):
        def loads(n, slot):
            at = pl.ds(pl.multiple_of(n * TILE, TILE), TILE)
            return (pltpu.make_async_copy(wd_hbm.at[:, at], wa.at[slot], sems.at[slot]),)

        def compute(slot):
            total = None
            for j in range(hidden_tiles):
                part = dot_plain(acts[3 * j, 0], wa[slot, pl.ds(j * TILE, TILE)])
                total = part if total is None else total + part
            return total

        reduce_start(1, loads, compute)

    pl.run_scoped(
        third_phase,
        pltpu.VMEM((2, wd_hbm.shape[0], TILE), jnp.bfloat16),
        pltpu.SemaphoreType.DMA((2,)),
    )

    base = ff_items
    for n in range(2):
        pltpu.make_async_copy(
            y_hbm.at[:, pl.ds(n * TILE, TILE)], acts.at[base + 2 + n, 0], misc.at[n]
        ).start()

    def xt_own(t):
        shard = other_z(z, t) * 2 + y
        return pltpu.make_async_copy(xt_hbm.at[shard], lt.at[2, 0, t], misc.at[2 + t])

    def xt_odd(k):
        shard = other_z(z, 2 * c + k) * 2 + 1 - y
        return pltpu.make_async_copy(xt_hbm.at[shard], odd.at[2, k], misc.at[6 + k])

    for t in range(4):
        xt_own(t).start()
    for k in range(2):
        xt_odd(k).start()
    relay(1)
    relay(0)
    lt_relay_in(1).wait_recv()
    lt_relay_in(0).wait_recv()
    back([(stage_one, 0, 6)])
    for t in range(4):
        xt_own(t).wait()
    for k in range(2):
        xt_odd(k).wait()
    lt_copy(2).start()
    for n in range(2):
        pltpu.make_async_copy(
            y_hbm.at[:, pl.ds(n * TILE, TILE)], acts.at[base + 2 + n, 0], misc.at[n]
        ).wait()
        act_copy(base + 2 + n).start()

    reduce_end(0)

    def fourth_phase(hbuf, cbuf, dbuf, wob, obuf, sbuf, sems, d_sems, w_sems):
        def row_loads(r, slot):
            at = pl.ds(r * 128, 128)
            return (
                pltpu.make_async_copy(h_hbm.at[at], hbuf.at[slot], sems.at[slot, 0]),
                pltpu.make_async_copy(cot_hbm.at[at], cbuf.at[slot], sems.at[slot, 1]),
            )

        def spill(r, slot):
            return pltpu.make_async_copy(dbuf.at[slot], dh_hbm.at[pl.ds(r * 128, 128)], d_sems.at[slot])

        def tile_loads(n):
            at = pl.ds(n * TILE, TILE)
            return (
                pltpu.make_async_copy(wo_hbm.at[at], wob.at[n], w_sems.at[n, 0]),
                pltpu.make_async_copy(o_hbm.at[:, at], obuf.at[n], w_sems.at[n, 1]),
                pltpu.make_async_copy(sig_hbm.at[:, at], sbuf.at[n], w_sems.at[n, 2]),
            )

        for copy in row_loads(0, 0):
            copy.start()
        for n in range(2):
            for copy in tile_loads(n):
                copy.start()
        vec[0] = jnp.zeros_like(vec[0])

        @pl.loop(0, n_chunks)
        def _(r):
            slot = lax.rem(r, 2)

            @pl.when(r < n_chunks - 1)
            def _():
                for copy in row_loads(r + 1, 1 - slot):
                    copy.start()

            for copy in row_loads(r, slot):
                copy.wait()

            @pl.when(r >= 2)
            def _():
                spill(r - 2, slot).wait()

            at = pl.ds(pl.multiple_of(r * 128, 128), 128)
            value = hbuf[slot]
            scale = rms(value)
            normed = value * scale
            grad = fin_rows(0, pl.multiple_of(r * 128, 128), 128)
            vec[0, 1:2] += jnp.sum(grad * normed, axis=0, keepdims=True)
            scaled = grad * n2_ref[...]
            inner = jnp.mean(scaled * normed, axis=-1, keepdims=True)
            dh = wide(cbuf[slot]) * factor_ref[at] + scale * (scaled - normed * inner)
            dbuf[slot] = dh
            wide_a[at] = low(dh)
            spill(r, slot).start()

        spill(n_chunks - 2, n_chunks % 2).wait()
        spill(n_chunks - 1, (n_chunks - 1) % 2).wait()

        ones = jnp.ones((8, 128), jnp.bfloat16)
        for n in range(2):
            for copy in tile_loads(n):
                copy.wait()
            dy = dot_rows(wide_a[...], wob[n])
            sig, o = sbuf[n], obuf[n]
            do = low(dy * sig)
            acts[base + n, 0] = low(dy * o * sig * (1.0 - sig))
            act_copy(base + n).start()
            wide_b[:, n * TILE : (n + 1) * TILE] = do
            both = wide(do) * o
            for g in range(2):
                part = both[:, g * 128 : (g + 1) * 128]
                top = low(part)
                rest = low(part - wide(top))
                delta[n, g] = dot_rows(ones, top) + dot_rows(ones, rest)

        spread(3, wide_a)
        for device in (core_dev, x_dev):
            pl.semaphore_signal(credit, inc=1, device_id=device, device_id_type=MESH)

    pl.run_scoped(
        fourth_phase,
        pltpu.VMEM((2, 128, width), jnp.float32),
        pltpu.VMEM((2, 128, width), jnp.bfloat16),
        pltpu.VMEM((2, 128, width), jnp.float32),
        pltpu.VMEM((2, TILE, width), jnp.bfloat16),
        pltpu.VMEM((2, tokens, TILE), jnp.float32),
        pltpu.VMEM((2, tokens, TILE), jnp.float32),
        pltpu.SemaphoreType.DMA((2, 2)),
        pltpu.SemaphoreType.DMA((2,)),
        pltpu.SemaphoreType.DMA((2, 3)),
    )

    def attention_back(keep, ysend, lsend, hsend, dq_ref, dkv_ref):
        def ky_copy(s):
            return remote(ysend.at[lax.rem(s, 2)], yrecv.at[s], ky_s.at[s], ky_r.at[s], y_dev)

        def kl_copy(s):
            return remote(lsend.at[s], lrecv.at[s], kl_s.at[s], kl_r.at[s], lo_dev)

        def kh_copy(s):
            return remote(hsend.at[s], hrecv.at[s], kh_s.at[s], kh_r.at[s], hi_dev)

        keys_total = kpos_ref.shape[0]

        def fifth_phase(qbuf, kvbuf, q_sem, sems):
            def kv_load(s, slot):
                return pltpu.make_async_copy(kv_hbm.at[s], kvbuf.at[slot], sems.at[slot])

            q_load = pltpu.make_async_copy(q_hbm, qbuf, q_sem)
            q_load.start()
            kv_load(0, 0).start()
            q_load.wait()

            @pl.loop(0, seqs)
            def _(s):
                slot = lax.rem(s, 2)

                @pl.when(s < seqs - 1)
                def _():
                    kv_load(s + 1, 1 - slot).start()

                kv_load(s, slot).wait()
                at = pl.ds(pl.multiple_of(s * rows, 128), rows)
                @pl.when(s >= 2)
                def _():
                    ky_copy(s - 2).wait_send()

                allowed = kpos_ref[...] <= qpos_ref[...]
                for n in range(2):
                    lanes = [slice((2 * n + g) * 128, (2 * n + g + 1) * 128) for g in range(2)]
                    key = kvbuf[slot, :, n * 128 : (n + 1) * 128]
                    value = kvbuf[slot, :, 256 + n * 128 : 256 + (n + 1) * 128]
                    q = jnp.concatenate([qbuf[at, lane] for lane in lanes], axis=0)
                    do = jnp.concatenate([wide_b[at, lane] for lane in lanes], axis=0)
                    drow = jnp.concatenate([delta[n, g, 0:1, at] for g in range(2)], axis=1)
                    scores = dot_rows(key, q)
                    probs = jnp.exp(jnp.where(allowed, scores - lse_ref[s, n], -1e30))
                    grad_probs = dot_rows(value, do)
                    ds = low(probs * (grad_probs - drow))
                    for start, grad in ((0, dot_plain(ds, q)), (256, dot_plain(low(probs), do))):
                        into = slice(start + n * 128, start + (n + 1) * 128)
                        for m in range(4):
                            keep[s, m, :, into] = grad[2 * m * rows : (2 * m + 1) * rows]
                            ysend[slot, m, :, into] = low(grad[(2 * m + 1) * rows : (2 * m + 2) * rows])
                    dq = dot_first(key, ds).T
                    for g in range(2):
                        dq_ref[at, lanes[g]] = dq[g * rows : (g + 1) * rows]

                ky_copy(s).start()

        pl.run_scoped(
            fifth_phase,
            pltpu.VMEM(q_hbm.shape, jnp.bfloat16),
            pltpu.VMEM((2, keys_total, 512), jnp.bfloat16),
            pltpu.SemaphoreType.DMA,
            pltpu.SemaphoreType.DMA((2,)),
        )

        relay(2)
        relay(3)
        back([(stage_two, 0, 4)])

        @pl.loop(0, seqs)
        def _(s):
            ky_copy(s).wait_recv()
            for m in range(4):
                keep[s, m] += wide(yrecv[s, m])
            for k in range(2):
                lsend[s, k] = low(keep[s, 2 * k + 1])
            kl_copy(s).start()

        back([(stage_one, 6, 9)])

        def query_phase(rbuf, sem):
            load = pltpu.make_async_copy(qraw_hbm, rbuf, sem)
            load.start()
            load.wait()
            factor = 128.0**-0.5
            for hd in range(4):
                lane = slice(hd * 128, (hd + 1) * 128)
                raw = rbuf[:, lane]
                scale = rms(raw)
                normed = raw * scale
                grad = dq_ref[:, lane]
                gvec[0, 0:1, 0:128] = (
                    jnp.sum(grad * normed * factor, axis=0, keepdims=True)
                    + (gvec[0, 0:1, 0:128] if hd else 0.0)
                )
                scaled = grad * (qg_ref[...] * factor)
                out = scale * (scaled - normed * jnp.mean(scaled * normed, axis=-1, keepdims=True))
                acts[base + 4 + hd // 2, 0, :, (hd % 2) * 128 : (hd % 2 + 1) * 128] = low(out)
            for n in range(2):
                act_copy(base + 4 + n).start()

        gvec[0] = jnp.zeros_like(gvec[0])
        pl.run_scoped(query_phase, pltpu.VMEM(qraw_hbm.shape, jnp.float32), pltpu.SemaphoreType.DMA)

        @pl.loop(0, seqs)
        def _(s):
            kl_copy(s).wait_recv()
            for k in range(2):
                keep[s, 2 * k] += wide(lrecv[s, k])
            hsend[s] = low(keep[s, 2])
            kh_copy(s).start()

        reduce_end(1)

        def out_phase(hbuf, obuf, sems, o_sems):
            def load(r, slot):
                return pltpu.make_async_copy(h_hbm.at[pl.ds(r * 128, 128)], hbuf.at[slot], sems.at[slot])

            def store(r, slot):
                return pltpu.make_async_copy(obuf.at[slot], block_out.at[pl.ds(r * 128, 128)], o_sems.at[slot])

            load(0, 0).start()

            @pl.loop(0, n_chunks)
            def _(r):
                slot = lax.rem(r, 2)

                @pl.when(r < n_chunks - 1)
                def _():
                    load(r + 1, 1 - slot).start()

                load(r, slot).wait()

                @pl.when(r >= 2)
                def _():
                    store(r - 2, slot).wait()

                obuf[slot] = low(hbuf[slot] + fin_rows(1, pl.multiple_of(r * 128, 128), 128))
                store(r, slot).start()

            store(n_chunks - 2, n_chunks % 2).wait()
            store(n_chunks - 1, (n_chunks - 1) % 2).wait()

        pl.run_scoped(
            out_phase,
            pltpu.VMEM((2, 128, width), jnp.float32),
            pltpu.VMEM((2, 128, width), jnp.bfloat16),
            pltpu.SemaphoreType.DMA((2,)),
            pltpu.SemaphoreType.DMA((2,)),
        )

        @pl.loop(0, seqs)
        def _(s):
            kh_copy(s).wait_recv()
            dkv_ref[pl.ds(pl.multiple_of(s * rows, 128), rows)] = keep[s, 0] + wide(hrecv[s])

        def key_phase(rbuf, sem):
            load = pltpu.make_async_copy(kraw_hbm, rbuf, sem)
            load.start()
            load.wait()
            for hd in range(2):
                lane = slice(hd * 128, (hd + 1) * 128)
                raw = rbuf[:, lane]
                scale = rms(raw)
                normed = raw * scale
                grad = dkv_ref[:, lane]
                gvec[0, 0:1, 128:256] = (
                    jnp.sum(grad * normed, axis=0, keepdims=True)
                    + (gvec[0, 0:1, 128:256] if hd else 0.0)
                )
                scaled = grad * kg_ref[...]
                out = scale * (scaled - normed * jnp.mean(scaled * normed, axis=-1, keepdims=True))
                acts[base + 6, 0, :, lane] = low(out)
            acts[base + 7, 0] = low(dkv_ref[:, 256:512])
            for n in range(2):
                act_copy(base + 6 + n).start()

        pl.run_scoped(key_phase, pltpu.VMEM(kraw_hbm.shape, jnp.float32), pltpu.SemaphoreType.DMA)

        @pl.loop(seqs - 2, seqs)
        def _(s):
            ky_copy(s).wait_send()

        @pl.loop(0, seqs)
        def _(s):
            kl_copy(s).wait_send()
            kh_copy(s).wait_send()

    pl.run_scoped(
        attention_back,
        pltpu.VMEM((seqs, 4, rows, 512), jnp.float32),
        pltpu.VMEM((2, 4, rows, 512), jnp.bfloat16),
        pltpu.VMEM((seqs, 2, rows, 512), jnp.bfloat16),
        pltpu.VMEM((seqs, rows, 512), jnp.bfloat16),
        pltpu.VMEM((tokens, 512), jnp.float32),
        pltpu.VMEM((tokens, 512), jnp.float32),
    )

    def sixth_phase(wb, sems):
        pieces = ((wga_hbm, base, 2), (wq_hbm, base + 4, 2), (wk_hbm, base + 6, 1), (wv_hbm, base + 7, 1))

        def loads(n, slot):
            at = pl.ds(pl.multiple_of(n * TILE, TILE), TILE)
            out, start = [], 0
            for p, (ref, _, count) in enumerate(pieces):
                out.append(
                    pltpu.make_async_copy(
                        ref.at[at], wb.at[slot, :, pl.ds(start, count * TILE)], sems.at[slot, p]
                    )
                )
                start += count * TILE
            return out

        def compute(slot):
            total, start = None, 0
            for _, first, count in pieces:
                for n in range(count):
                    part = dot_rows(acts[first + n, 0], wb[slot, :, pl.ds(start, TILE)])
                    total = part if total is None else total + part
                    start += TILE
            return total

        pl.semaphore_wait(credit, 2)
        reduce_start(2, loads, compute)

    pl.run_scoped(
        sixth_phase,
        pltpu.VMEM((2, TILE, 6 * TILE), jnp.bfloat16),
        pltpu.SemaphoreType.DMA((2, 4)),
    )

    for step in range(5):
        device = (y_dev, lo_dev, hi_dev, core_dev, x_dev)[step]
        copy = remote(gvec.at[step], gvec_got.at[step], gv_s.at[step], gv_r.at[step], device)
        copy.start()
        copy.wait()
        gvec[step + 1] = gvec[step] + gvec_got[step]
    gains_out[...] = gvec[5]

    lt_relay_in(2).wait_recv()
    lt_relay_in(3).wait_recv()
    back([(stage_one, 9, 12), (stage_two, 4, 8), (stage_three, 0, 4)])
    reduce_end(2)

    def last_phase(xbuf, dbuf, obuf, sems, o_sems):
        def loads(r, slot):
            at = pl.ds(r * 128, 128)
            return (
                pltpu.make_async_copy(x_hbm.at[at], xbuf.at[slot], sems.at[slot, 0]),
                pltpu.make_async_copy(dh_hbm.at[at], dbuf.at[slot], sems.at[slot, 1]),
            )

        def store(r, slot):
            return pltpu.make_async_copy(obuf.at[slot], x_out.at[pl.ds(r * 128, 128)], o_sems.at[slot])

        for copy in loads(0, 0):
            copy.start()

        @pl.loop(0, n_chunks)
        def _(r):
            slot = lax.rem(r, 2)

            @pl.when(r < n_chunks - 1)
            def _():
                for copy in loads(r + 1, 1 - slot):
                    copy.start()

            for copy in loads(r, slot):
                copy.wait()

            @pl.when(r >= 2)
            def _():
                store(r - 2, slot).wait()

            value = wide(xbuf[slot])
            scale = rms(value)
            normed = value * scale
            grad = fin_rows(2, pl.multiple_of(r * 128, 128), 128)
            vec[0, 0:1] += jnp.sum(grad * normed, axis=0, keepdims=True)
            scaled = grad * n1_ref[...]
            inner = jnp.mean(scaled * normed, axis=-1, keepdims=True)
            obuf[slot] = low(dbuf[slot] + scale * (scaled - normed * inner))
            store(r, slot).start()

        store(n_chunks - 2, n_chunks % 2).wait()
        store(n_chunks - 1, (n_chunks - 1) % 2).wait()

    pl.run_scoped(
        last_phase,
        pltpu.VMEM((2, 128, width), jnp.bfloat16),
        pltpu.VMEM((2, 128, width), jnp.float32),
        pltpu.VMEM((2, 128, width), jnp.bfloat16),
        pltpu.SemaphoreType.DMA((2, 2)),
        pltpu.SemaphoreType.DMA((2,)),
    )

    for step in range(3):
        device = (y_dev, lo_dev, hi_dev)[step]
        copy = remote(vec.at[step], vec_got.at[step], nv_s.at[step], nv_r.at[step], device)
        copy.start()
        copy.wait()
        vec[step + 1] = vec[step] + vec_got[step]
    norms_out[...] = vec[3]

    count = ff_items + 8
    one, two, three = 12, 8, 4
    while three < count:
        step = []
        if one < count:
            step.append((stage_one, one, min(one + 2, count)))
            one = min(one + 2, count)
        if two < one - 2 or one == count:
            step.append((stage_two, two, min(two + 2, one)))
            two = min(two + 2, one)
        if three < two - 2 or two == count:
            step.append((stage_three, three, min(three + 2, two)))
            three = min(three + 2, two)
        back(step)

    @pl.loop(0, count)
    def _(i):
        act_copy(i).wait_send()

    @pl.loop(count - 4, count)
    def _(i):
        zlo_copy(i).wait_send()
        zhi_copy(i).wait_send()

    @pl.loop(count - 2, count)
    def _(i):
        out_copy(i).wait()

    for l in range(4):
        lt_copy(l).wait_send()
        lt_relay(l).wait_send()


def back_call(hbm, vmem, sizes):
    tokens, width, seqs, rows, keys_total, hidden = sizes
    count = 3 * (hidden // TILE) + 8
    bf, f32 = jnp.bfloat16, jnp.float32
    dma = pltpu.SemaphoreType.DMA
    scratch = [
        pltpu.VMEM((count, 2, tokens, TILE), bf),
        pltpu.VMEM((4, 2, 4, TILE, tokens), bf),
        pltpu.VMEM((4, 2, TILE, tokens), bf),
        pltpu.VMEM((4, tokens, TILE), bf),
        pltpu.VMEM((2, 4, tokens, TILE), bf),
        pltpu.VMEM((2, 4, tokens, TILE), bf),
        pltpu.VMEM((2, 8, tokens, TILE), bf),
        pltpu.VMEM((seqs, 4, rows, 512), bf),
        pltpu.VMEM((seqs, 2, rows, 512), bf),
        pltpu.VMEM((seqs, rows, 512), bf),
        pltpu.VMEM((4, 2, TILE, TILE), bf),
        pltpu.VMEM((4, TILE, TILE), bf),
        pltpu.VMEM((2, TILE, TILE), bf),
        pltpu.VMEM((2, TILE, TILE), f32),
        pltpu.VMEM((tokens, width), bf),
        pltpu.VMEM((tokens, width), bf),
        pltpu.VMEM((2, 2, 8, tokens), f32),
        pltpu.VMEM((4, 8, width), f32),
        pltpu.VMEM((3, 8, width), f32),
        pltpu.VMEM((6, 8, 256), f32),
        pltpu.VMEM((5, 8, 256), f32),
        *(dma((count,)) for _ in range(6)),
        *(dma((4,)) for _ in range(4)),
        *(dma((3, 4)) for _ in range(6)),
        *(dma((seqs,)) for _ in range(6)),
        dma((3,)), dma((3,)), dma((5,)), dma((5,)),
        dma((2,)), dma((2,)), dma((8,)), pltpu.SemaphoreType.REGULAR,
    ]
    any_spec = pl.BlockSpec(memory_space=pl.ANY)
    vmem_spec = pl.BlockSpec(memory_space=pltpu.VMEM)
    return pl.pallas_call(
        back_kernel,
        out_shape=[
            jax.ShapeDtypeStruct((tokens, width), bf),
            jax.ShapeDtypeStruct((tokens, width), bf),
            jax.ShapeDtypeStruct((count, TILE, TILE), f32),
            jax.ShapeDtypeStruct((8, width), f32),
            jax.ShapeDtypeStruct((8, 256), f32),
            jax.ShapeDtypeStruct((tokens, width), f32),
            jax.ShapeDtypeStruct((count, 2, TILE, TILE), bf),
            jax.ShapeDtypeStruct((count, TILE, TILE), bf),
        ],
        in_specs=[any_spec] * len(hbm) + [vmem_spec] * len(vmem),
        out_specs=[any_spec] * 3 + [vmem_spec] * 2 + [any_spec] * 3,
        scratch_shapes=scratch,
        compiler_params=pltpu.CompilerParams(
            collective_id=1, has_side_effects=True, vmem_limit_bytes=61 << 20
        ),
    )(*hbm, *vmem)


def on_device(
    x_in,
    cot,
    domain_ids,
    domain_counts,
    domain_weights,
    block_order,
    norm1,
    w_query,
    w_key,
    w_value,
    w_gate_attn,
    w_out,
    query_gain,
    key_gain,
    norm2,
    w_gate,
    w_up,
    w_down,
):
    sequences, local_rows, width = x_in.shape
    row_total = sequences * local_rows
    head_dim = query_gain.shape[0]
    kv_local = w_key.shape[1] // head_dim
    q_local = w_query.shape[1] // head_dim
    group = q_local // kv_local
    devices = lax.axis_size("seq")
    own = lax.axis_index("seq")
    block_rows = local_rows * devices // block_order.shape[0]
    query_factor = head_dim ** (-0.5)
    q_gain, k_gain = wide(query_gain), wide(key_gain)
    gain_one, gain_two = wide(norm1), wide(norm2)

    def cut_columns(weight, half):
        return lax.dynamic_slice_in_dim(weight, half * (width // 2), width // 2, 1)

    x_rows = x_in.reshape(row_total, width)
    x_float = wide(x_rows)
    x_normed = low(x_float * norm_scale(x_float) * gain_one)
    key_raw = product(x_normed, w_key)
    by_head = key_raw.reshape(row_total, kv_local, head_dim)
    key_rows = low(by_head * norm_scale(by_head) * k_gain).reshape(row_total, -1)
    value_rows = low(product(x_normed, w_value))
    pair = jnp.concatenate([key_rows, value_rows], axis=1).reshape(sequences, local_rows, -1)
    kv_width = kv_local * head_dim

    seqs_of = sequences // CHUNKS
    rows_of = row_total // CHUNKS

    def gather(value):
        slots = {0: value}
        for mask in range(2, devices, 2):
            slots[mask] = swap(value, "seq", mask)
        for mask in range(0, devices, 2):
            slots[mask + 1] = swap(slots[mask], "seq", 1)
        return jnp.stack([slots[j] for j in range(devices)], axis=1).reshape(
            seqs_of, devices * local_rows, -1
        )

    gathered = [gather(pair[c * seqs_of : (c + 1) * seqs_of]) for c in range(CHUNKS)]

    query_raw = product(x_normed, w_query)
    gate_pre = product(x_normed, w_gate_attn)
    by_head = query_raw.reshape(row_total, q_local, head_dim)
    query = low(by_head * norm_scale(by_head) * q_gain * query_factor)
    gate_sig = jax.nn.sigmoid(gate_pre)

    query_pos = positions(block_order, own, local_rows, block_rows)
    key_pos = jnp.concatenate(
        [positions(block_order, own ^ j, local_rows, block_rows) for j in range(devices)]
    )
    allowed = key_pos[None, :] <= query_pos[:, None]

    domain_total = domain_weights.shape[0]
    domain_index = jnp.arange(domain_total, dtype=jnp.int32)
    factor = domain_weights * (row_total * devices) / (domain_total * wide(domain_counts))
    picked = domain_ids.reshape(row_total)[:, None] == domain_index[None, :]
    row_scale = jnp.sum(jnp.where(picked, factor[None, :], 0.0), axis=1)

    saved = []
    for c in range(CHUNKS):
        rows = slice(c * rows_of, (c + 1) * rows_of)
        heads = (
            query[rows]
            .reshape(seqs_of, local_rows, kv_local, group, head_dim)
            .transpose(0, 2, 3, 1, 4)
        )
        keys = gathered[c][..., :kv_width].reshape(seqs_of, -1, kv_local, head_dim)
        values = gathered[c][..., kv_width:].reshape(seqs_of, -1, kv_local, head_dim)
        scores = jnp.einsum("skgqd,spkd->skgqp", heads, keys, preferred_element_type=jnp.float32)
        scores = jnp.where(allowed, scores, -1e30)
        top = jnp.max(scores, axis=-1)
        weights = jnp.where(allowed, jnp.exp(scores - top[..., None]), 0.0)
        total = jnp.sum(weights, axis=-1)
        mixed = jnp.einsum(
            "skgqp,spkd->skgqd", low(weights), values, preferred_element_type=jnp.float32
        )
        attn_heads = mixed / total[..., None]
        log_total = top + jnp.log(total)
        attn_flat = attn_heads.transpose(0, 3, 1, 2, 4).reshape(rows_of, q_local * head_dim)
        gated = low(attn_flat * gate_sig[rows])
        attn_sum = head_sum(gated, w_out, product, cut_columns)
        residual = x_float[rows] + attn_sum
        log_total = log_total.reshape(seqs_of, kv_local, 1, group * local_rows)
        saved.append((residual, attn_flat, gated, log_total))

    residual, attn_flat, gated, log_total = (
        jnp.concatenate([part[i] for part in saved], axis=0) for i in range(4)
    )
    out, x_grad, items, norms, gains, _, _, _ = back_call(
        (
            residual,
            cot.reshape(row_total, width),
            x_rows,
            x_normed.T.reshape(devices, width // devices, row_total),
            query.reshape(row_total, q_local * head_dim),
            jnp.concatenate(gathered, axis=0),
            attn_flat,
            gate_sig,
            gated,
            query_raw,
            key_raw,
            w_gate,
            w_up,
            w_down,
            w_out,
            w_query,
            w_key,
            w_value,
            w_gate_attn,
        ),
        (
            row_scale[:, None],
            log_total,
            key_pos[:, None],
            jnp.concatenate([query_pos] * group)[None, :],
            gain_one[None, :],
            gain_two[None, :],
            q_gain[None, :],
            k_gain[None, :],
        ),
        (row_total, width, sequences, local_rows, local_rows * devices, w_down.shape[0]),
    )

    def rows_item(chosen):
        return jnp.concatenate([items[i] for i in chosen], axis=1)

    def columns_item(chosen):
        return jnp.concatenate([items[i].T for i in chosen], axis=0)

    def own_part(value):
        size = value.shape[0] // devices
        return lax.dynamic_slice_in_dim(value, own * size, size, 0)

    base = 3 * (w_down.shape[0] // TILE)
    return (
        out.reshape(x_in.shape),
        x_grad.reshape(x_in.shape),
        own_part(norms[0]),
        rows_item((base + 4, base + 5)),
        rows_item((base + 6,)),
        rows_item((base + 7,)),
        rows_item((base, base + 1)),
        columns_item((base + 2, base + 3)),
        own_part(gains[0, :head_dim]),
        own_part(gains[0, head_dim:]),
        own_part(norms[1]),
        rows_item(range(1, base, 3)),
        rows_item(range(2, base, 3)),
        columns_item(range(0, base, 3)),
    )


def on_device_plain(
    x_in,
    cot,
    domain_ids,
    domain_counts,
    domain_weights,
    block_order,
    norm1,
    w_query,
    w_key,
    w_value,
    w_gate_attn,
    w_out,
    query_gain,
    key_gain,
    norm2,
    w_gate,
    w_up,
    w_down,
):
    sequences, local_rows, model_width = x_in.shape
    row_total = sequences * local_rows
    head_dim = query_gain.shape[0]
    kv_local = w_key.shape[1] // head_dim
    q_local = w_query.shape[1] // head_dim
    group_size = q_local // kv_local
    block_rows = local_rows // 2
    seq_devices = lax.axis_size("seq")
    first_row = lax.axis_index("seq") * local_rows
    query_pos = positions(block_order, first_row, local_rows, block_rows)
    query_factor = head_dim ** (-0.5)
    q_gain = query_gain.astype(jnp.float32)
    k_gain = key_gain.astype(jnp.float32)
    gain_one = norm1.astype(jnp.float32)
    gain_two = norm2.astype(jnp.float32)
    x_float = x_in.reshape(row_total, model_width).astype(jnp.float32)
    scale_one = norm_scale(x_float)
    normed_one = x_float * scale_one
    x_normed = (normed_one * gain_one).astype(jnp.bfloat16)
    query_raw = product(x_normed, w_query).reshape(row_total, q_local, head_dim)
    key_raw = product(x_normed, w_key).reshape(row_total, kv_local, head_dim)
    value_rows = product(x_normed, w_value).astype(jnp.bfloat16)
    gate_pre = product(x_normed, w_gate_attn)
    query_scale = norm_scale(query_raw)
    query_normed = query_raw * query_scale
    key_scale = norm_scale(key_raw)
    key_normed = key_raw * key_scale
    query = (query_normed * q_gain * query_factor).astype(jnp.bfloat16)
    key_rows = (key_normed * k_gain).astype(jnp.bfloat16)
    project_query_heads = query.reshape(
        sequences, local_rows, kv_local, group_size, head_dim
    ).transpose(0, 2, 3, 1, 4)
    (
        query_scale,
        query_normed,
        key_scale,
        key_normed,
        query_heads,
        key_rows,
        value_rows,
        gate_pre,
    ) = (
        query_scale,
        query_normed,
        key_scale,
        key_normed,
        project_query_heads,
        key_rows,
        value_rows,
        gate_pre,
    )
    key_seq = key_rows.reshape(sequences, local_rows, kv_local * head_dim)
    value_seq = value_rows.reshape(sequences, local_rows, kv_local * head_dim)
    stat_shape = (sequences, kv_local, group_size, local_rows)
    running_max = jnp.full(stat_shape, -1e30, jnp.float32)
    key_piece = lax.all_gather(key_seq, "seq", axis=1, tiled=True)
    value_piece = lax.all_gather(value_seq, "seq", axis=1, tiled=True)
    row_count = key_piece.shape[1]
    key_block = key_piece.reshape(sequences, row_count, kv_local, head_dim)
    value_block = value_piece.reshape(sequences, row_count, kv_local, head_dim)
    key_pos = positions(block_order, jnp.int32(0), row_count, block_rows)
    allowed = key_pos[None, :] <= query_pos[:, None]
    scores = jnp.einsum(
        "skgqd,spkd->skgqp", query_heads, key_block, preferred_element_type=jnp.float32
    )
    scores = jnp.where(allowed, scores, -1e30)
    new_max = jnp.maximum(running_max, jnp.max(scores, axis=-1))
    weights = jnp.where(allowed, jnp.exp(scores - new_max[..., None]), 0.0)
    running_sum = jnp.sum(weights, axis=-1)
    weighted = jnp.einsum(
        "skgqp,spkd->skgqd",
        weights.astype(jnp.bfloat16),
        value_block,
        preferred_element_type=jnp.float32,
    )
    running_max, running_sum, weighted = (new_max, running_sum, weighted)
    log_total = running_max + jnp.log(running_sum)
    attn_heads = weighted / running_sum[..., None]
    attn_flat = attn_heads.transpose(0, 3, 1, 2, 4).reshape(row_total, q_local * head_dim)
    gate_sig = jax.nn.sigmoid(gate_pre)
    gated = (attn_flat * gate_sig).astype(jnp.bfloat16)
    attn_sum = lax.psum(product(gated, w_out).astype(jnp.bfloat16), "head").astype(jnp.float32)
    residual = x_float + attn_sum
    scale_two = norm_scale(residual)
    normed_two = residual * scale_two
    h_normed = (normed_two * gain_two).astype(jnp.bfloat16)
    gate_proj = product(h_normed, w_gate)
    up_proj = product(h_normed, w_up)
    gate_logit = jax.nn.sigmoid(gate_proj)
    gate_act = gate_proj * gate_logit
    mixed = (gate_act * up_proj).astype(jnp.bfloat16)
    mlp_sum = lax.psum(product(mixed, w_down).astype(jnp.bfloat16), "head").astype(jnp.float32)
    block_out = (
        (residual + mlp_sum).astype(jnp.bfloat16).reshape(sequences, local_rows, model_width)
    )
    domain_total = domain_weights.shape[0]
    domain_index = jnp.arange(domain_total, dtype=jnp.int32)
    factor = (
        domain_weights
        * (row_total * seq_devices)
        / (domain_total * domain_counts.astype(jnp.float32))
    )
    picked = domain_ids.reshape(row_total)[:, None] == domain_index[None, :]
    row_scale = jnp.sum(jnp.where(picked, factor[None, :], 0.0), axis=1)
    grad_out = cot.reshape(row_total, model_width).astype(jnp.float32) * row_scale[:, None]
    grad_low = grad_out.astype(jnp.bfloat16)
    grad_down = outer_sum(mixed, grad_low)
    grad_mixed = back_product(grad_low, w_down)
    grad_gate = (grad_mixed * up_proj * gate_logit * (1.0 + gate_proj * (1.0 - gate_logit))).astype(
        jnp.bfloat16
    )
    grad_up = (grad_mixed * gate_act).astype(jnp.bfloat16)
    grad_mlp_gate = outer_sum(h_normed, grad_gate)
    grad_mlp_up = outer_sum(h_normed, grad_up)
    grad_hnorm = lax.psum(
        (back_product(grad_gate, w_gate) + back_product(grad_up, w_up)).astype(jnp.bfloat16), "head"
    ).astype(jnp.float32)
    grad_norm_two = jnp.sum(grad_hnorm * normed_two, axis=0)
    grad_resid = grad_out + norm_back(grad_hnorm, normed_two, scale_two, gain_two)
    grad_attn = grad_resid.astype(jnp.bfloat16)
    grad_wout = outer_sum(gated, grad_attn)
    grad_gated = back_product(grad_attn, w_out)
    grad_heads_flat = (grad_gated * gate_sig).astype(jnp.bfloat16)
    grad_gatepre = (grad_gated * attn_flat * gate_sig * (1.0 - gate_sig)).astype(jnp.bfloat16)
    grad_wgate_attn = outer_sum(x_normed, grad_gatepre)
    grad_heads = grad_heads_flat.reshape(
        sequences, local_rows, kv_local, group_size, head_dim
    ).transpose(0, 2, 3, 1, 4)
    row_delta = jnp.sum(grad_heads.astype(jnp.float32) * attn_heads, axis=-1)
    key_piece = lax.all_gather(key_seq, "seq", axis=1, tiled=True)
    value_piece = lax.all_gather(value_seq, "seq", axis=1, tiled=True)
    row_count = key_piece.shape[1]
    key_block = key_piece.reshape(sequences, row_count, kv_local, head_dim)
    value_block = value_piece.reshape(sequences, row_count, kv_local, head_dim)
    key_pos = positions(block_order, jnp.int32(0), row_count, block_rows)
    allowed = key_pos[None, :] <= query_pos[:, None]
    scores = jnp.einsum(
        "skgqd,spkd->skgqp", query_heads, key_block, preferred_element_type=jnp.float32
    )
    probs = jnp.where(
        allowed, jnp.exp(jnp.where(allowed, scores, -1e30) - log_total[..., None]), 0.0
    )
    grad_probs = jnp.einsum(
        "skgqd,spkd->skgqp", grad_heads, value_block, preferred_element_type=jnp.float32
    )
    grad_scores = (probs * (grad_probs - row_delta[..., None])).astype(jnp.bfloat16)
    grad_query = jnp.einsum(
        "skgqp,spkd->skgqd", grad_scores, key_block, preferred_element_type=jnp.float32
    )
    key_term = jnp.einsum(
        "skgqp,skgqd->spkd", grad_scores, query_heads, preferred_element_type=jnp.float32
    ).reshape(sequences, row_count, kv_local * head_dim)
    value_term = jnp.einsum(
        "skgqp,skgqd->spkd",
        probs.astype(jnp.bfloat16),
        grad_heads,
        preferred_element_type=jnp.float32,
    ).reshape(sequences, row_count, kv_local * head_dim)
    grad_keys = key_term
    grad_values = value_term
    grad_query, grad_keys, grad_values = (grad_query, grad_keys, grad_values)
    grad_key_own, grad_value_own = (
        lax.psum_scatter(
            grad_keys.astype(jnp.bfloat16), "seq", scatter_dimension=1, tiled=True
        ).astype(jnp.float32),
        lax.psum_scatter(
            grad_values.astype(jnp.bfloat16), "seq", scatter_dimension=1, tiled=True
        ).astype(jnp.float32),
    )
    grad_query_rows = grad_query.transpose(0, 3, 1, 2, 4).reshape(row_total, q_local, head_dim)
    grad_qgain_part = jnp.sum(grad_query_rows * query_normed * query_factor, axis=(0, 1))
    grad_query_raw = (
        norm_back(grad_query_rows, query_normed, query_scale, q_gain * query_factor)
        .astype(jnp.bfloat16)
        .reshape(row_total, q_local * head_dim)
    )
    grad_key_rows = grad_key_own.reshape(row_total, kv_local, head_dim)
    grad_kgain_part = jnp.sum(grad_key_rows * key_normed, axis=(0, 1))
    grad_key_raw = (
        norm_back(grad_key_rows, key_normed, key_scale, k_gain)
        .astype(jnp.bfloat16)
        .reshape(row_total, kv_local * head_dim)
    )
    grad_value_low = grad_value_own.reshape(row_total, kv_local * head_dim).astype(jnp.bfloat16)
    grad_xnorm_part = (
        back_product(grad_query_raw, w_query)
        + back_product(grad_key_raw, w_key)
        + back_product(grad_value_low, w_value)
        + back_product(grad_gatepre, w_gate_attn)
    )
    grad_xnorm, grad_qgain, grad_kgain = (
        lax.psum(grad_xnorm_part.astype(jnp.bfloat16), "head").astype(jnp.float32),
        lax.psum(grad_qgain_part.astype(jnp.bfloat16), "head").astype(jnp.float32),
        lax.psum(grad_kgain_part.astype(jnp.bfloat16), "head").astype(jnp.float32),
    )
    grad_norm_one = jnp.sum(grad_xnorm * normed_one, axis=0)
    x_grad = (
        (grad_resid + norm_back(grad_xnorm, normed_one, scale_one, gain_one))
        .astype(jnp.bfloat16)
        .reshape(sequences, local_rows, model_width)
    )
    grad_wquery = outer_sum(x_normed, grad_query_raw)
    grad_wkey = outer_sum(x_normed, grad_key_raw)
    grad_wvalue = outer_sum(x_normed, grad_value_low)
    all_totals = (
        lax.psum_scatter(
            grad_norm_one.astype(jnp.bfloat16), "seq", scatter_dimension=0, tiled=True
        ).astype(jnp.float32),
        lax.psum_scatter(
            grad_wquery.astype(jnp.bfloat16), "seq", scatter_dimension=0, tiled=True
        ).astype(jnp.float32),
        lax.psum_scatter(
            grad_wkey.astype(jnp.bfloat16), "seq", scatter_dimension=0, tiled=True
        ).astype(jnp.float32),
        lax.psum_scatter(
            grad_wvalue.astype(jnp.bfloat16), "seq", scatter_dimension=0, tiled=True
        ).astype(jnp.float32),
        lax.psum_scatter(
            grad_wgate_attn.astype(jnp.bfloat16), "seq", scatter_dimension=0, tiled=True
        ).astype(jnp.float32),
        lax.psum_scatter(
            grad_wout.astype(jnp.bfloat16), "seq", scatter_dimension=1, tiled=True
        ).astype(jnp.float32),
        lax.psum_scatter(
            grad_qgain.astype(jnp.bfloat16), "seq", scatter_dimension=0, tiled=True
        ).astype(jnp.float32),
        lax.psum_scatter(
            grad_kgain.astype(jnp.bfloat16), "seq", scatter_dimension=0, tiled=True
        ).astype(jnp.float32),
        lax.psum_scatter(
            grad_mlp_gate.astype(jnp.bfloat16), "seq", scatter_dimension=0, tiled=True
        ).astype(jnp.float32),
        lax.psum_scatter(
            grad_mlp_up.astype(jnp.bfloat16), "seq", scatter_dimension=0, tiled=True
        ).astype(jnp.float32),
        lax.psum_scatter(
            grad_down.astype(jnp.bfloat16), "seq", scatter_dimension=1, tiled=True
        ).astype(jnp.float32),
        lax.psum_scatter(
            grad_norm_two.astype(jnp.bfloat16), "seq", scatter_dimension=0, tiled=True
        ).astype(jnp.float32),
    )
    return (
        block_out,
        x_grad,
        all_totals[0],
        all_totals[1],
        all_totals[2],
        all_totals[3],
        all_totals[4],
        all_totals[5],
        all_totals[6],
        all_totals[7],
        all_totals[11],
        all_totals[8],
        all_totals[9],
        all_totals[10],
    )


def solution(mesh):
    fits = mesh.shape["seq"] == 8 and mesh.shape["head"] == 4
    return jax.shard_map(
        on_device if fits else on_device_plain,
        mesh=mesh,
        in_specs=(
            P(None, "seq", None),
            P(None, "seq", None),
            P(None, "seq"),
            P(),
            P(),
            P(),
            P(),
            P(None, "head"),
            P(None, "head"),
            P(None, "head"),
            P(None, "head"),
            P("head", None),
            P(),
            P(),
            P(),
            P(None, "head"),
            P(None, "head"),
            P("head", None),
        ),
        out_specs=(
            P(None, "seq", None),
            P(None, "seq", None),
            P("seq"),
            P("seq", "head"),
            P("seq", "head"),
            P("seq", "head"),
            P("seq", "head"),
            P("head", "seq"),
            P("seq"),
            P("seq"),
            P("seq"),
            P("seq", "head"),
            P("seq", "head"),
            P("head", "seq"),
        ),
        check_vma=False,
    )
```

```python
import jax
import jax.numpy as jnp
from jax import lax
from jax.experimental import pallas as pl
from jax.experimental.pallas import tpu as pltpu
from jax.sharding import PartitionSpec as P

epsilon = 1e-06
CHUNKS = 2


def norm_scale(value):
    return lax.rsqrt(jnp.mean(value * value, axis=-1, keepdims=True) + epsilon)


def norm_back(grad_in, normed, scale, gain):
    scaled = grad_in * gain
    return scale * (scaled - normed * jnp.mean(scaled * normed, axis=-1, keepdims=True))


def product(left, right):
    return jnp.dot(left, right, preferred_element_type=jnp.float32)


def outer_sum(left, right):
    return lax.dot_general(
        left, right, (((0,), (0,)), ((), ())), preferred_element_type=jnp.float32
    )


def back_product(left, right):
    return lax.dot_general(
        left, right, (((1,), (1,)), ((), ())), preferred_element_type=jnp.float32
    )


def low(value):
    return value.astype(jnp.bfloat16)


def wide(value):
    return value.astype(jnp.float32)


def bits_of(axis):
    return (lax.axis_size(axis) - 1).bit_length()


def swap(value, axis, mask):
    size = lax.axis_size(axis)
    return lax.ppermute(value, axis, [(i, i ^ mask) for i in range(size)])


def positions(block_order, device, row_count, block_rows):
    stored = device * row_count + jnp.arange(row_count, dtype=jnp.int32)
    slots = stored // block_rows
    slot_index = jnp.arange(block_order.shape[0], dtype=jnp.int32)
    picked = jnp.sum(
        jnp.where(slots[:, None] == slot_index[None, :], block_order[None, :], 0), axis=1
    )
    return picked * block_rows + stored % block_rows


def head_sum(left, weight, apply, cut):
    mine = lax.axis_index("head") & 1
    away = low(apply(left, cut(weight, 1 - mine)))
    got = swap(away, "head", 1)
    total = apply(left, cut(weight, mine)) + wide(got)
    for bit in range(1, bits_of("head")):
        part = low(total)
        total = wide(part) + wide(swap(part, "head", 1 << bit))
    part = low(total)
    other = swap(part, "head", 1)
    low_half = jnp.where(mine == 0, part, other)
    high_half = jnp.where(mine == 0, other, part)
    return wide(jnp.concatenate([low_half, high_half], axis=1))


MESH = pl.DeviceIdType.MESH
TILE = 256


def other_z(z, t):
    low_z, high_z = lax.rem(z, 2), lax.div(z, 2)
    low_t, high_t = lax.rem(t, 2), lax.div(t, 2)
    return (low_z + low_t - 2 * low_z * low_t) + 2 * (high_z + high_t - 2 * high_z * high_t)


def dot_plain(left, right):
    return jnp.dot(left, right, preferred_element_type=jnp.float32)


def dot_rows(left, right):
    return lax.dot_general(
        left, right, (((1,), (1,)), ((), ())), preferred_element_type=jnp.float32
    )


def dot_first(left, right):
    return lax.dot_general(
        left, right, (((0,), (0,)), ((), ())), preferred_element_type=jnp.float32
    )


def back_kernel(
    h_hbm, cot_hbm, x_hbm, xt_hbm, q_hbm, kv_hbm, o_hbm, sig_hbm, y_hbm, qraw_hbm, kraw_hbm,
    wg_hbm, wu_hbm, wd_hbm, wo_hbm, wq_hbm, wk_hbm, wv_hbm, wga_hbm,
    factor_ref, lse_ref, kpos_ref, qpos_ref, n1_ref, n2_ref, qg_ref, kg_ref,
    block_out, x_out, dwd_out, dwg_out, dwu_out, dwo_out, dwga_out, dwq_out, dwk_out, dwv_out,
    norms_out, gains_out, dh_hbm, zlo_hbm, zhi_hbm,
    acts, lt, odd, csend, crecv, xrecv, fin, yrecv, lrecv, hrecv,
    zlo_send, zhi_send, stage, ostage, wide_a, wide_b, delta,
    vec, vec_got, gvec, gvec_got,
    ya_s, ya_r, zl_s, zl_r, zh_s, zh_r, lt_s, lt_r, lc_s, lc_r,
    c1_s, c1_r, x_s, x_r, c2_s, c2_r, ky_s, ky_r, kl_s, kl_r, kh_s, kh_r,
    nv_s, nv_r, gv_s, gv_r, st_sem, out_sem, misc, credit,
):
    seq, head = lax.axis_index("seq"), lax.axis_index("head")
    z, y = lax.div(seq, 2), lax.rem(seq, 2)
    c = lax.rem(head, 2)
    y_dev = {"seq": z * 2 + 1 - y}
    lo_dev = {"seq": other_z(z, 1) * 2 + y}
    hi_dev = {"seq": other_z(z, 2) * 2 + y}
    core_dev = {"head": head + 1 - 2 * c}
    x_dev = {"head": head + 2 - 4 * lax.div(head, 2)}
    tokens = cot_hbm.shape[0]
    rows = kpos_ref.shape[0] // 8
    seqs = tokens // rows
    hidden_tiles = wd_hbm.shape[0] // TILE
    ff_items = 3 * hidden_tiles
    width = cot_hbm.shape[1]
    epsilon_k = 1e-06

    barrier = pltpu.get_barrier_semaphore()
    for device in (y_dev, lo_dev, hi_dev, core_dev, x_dev):
        pl.semaphore_signal(barrier, inc=1, device_id=device, device_id_type=MESH)
    pl.semaphore_wait(barrier, 5)

    def remote(src, dst, send, recv, device):
        return pltpu.make_async_remote_copy(
            src_ref=src, dst_ref=dst, send_sem=send, recv_sem=recv, device_id=device, device_id_type=MESH
        )

    def act_copy(i):
        return remote(acts.at[i, 0], acts.at[i, 1], ya_s.at[i], ya_r.at[i], y_dev)

    def lt_copy(l):
        return remote(odd.at[l], lt.at[l, 1, pl.ds(2 * c, 2)], lt_s.at[l], lt_r.at[l], y_dev)

    def lt_relay(l):
        piece = lt.at[l, 1, pl.ds(2 * c, 2)]
        return remote(piece, piece, lc_s.at[l], lc_r.at[l], core_dev)

    def lt_relay_in(l):
        piece = lt.at[l, 1, pl.ds(2 - 2 * c, 2)]
        return remote(piece, piece, lc_s.at[l], lc_r.at[l], core_dev)

    def zlo_copy(i):
        return remote(zlo_send.at[lax.rem(i, 4)], zlo_hbm.at[i], zl_s.at[i], zl_r.at[i], lo_dev)

    def zhi_copy(i):
        return remote(zhi_send.at[lax.rem(i, 4)], zhi_hbm.at[i], zh_s.at[i], zh_r.at[i], hi_dev)

    def item_dot(i, l, t):
        return dot_plain(lt[l, 0, t], acts[i, 0]) + dot_plain(lt[l, 1, t], acts[i, 1])

    def stage_one(i, l):
        act_copy(i).wait_recv()

        @pl.when(i >= 4)
        def _():
            zlo_copy(i - 4).wait_send()

        slot = lax.rem(i, 4)
        for k in range(2):
            zlo_send[slot, k] = low(item_dot(i, l, 2 * k + 1))
        zlo_copy(i).start()

    def stage_two(i, l):
        zlo_copy(i).wait_recv()
        here = pltpu.make_async_copy(zlo_hbm.at[i, 1], stage.at[0], st_sem.at[0])
        here.start()

        @pl.when(i >= 4)
        def _():
            zhi_copy(i - 4).wait_send()

        total = item_dot(i, l, 2)
        here.wait()
        zhi_send[lax.rem(i, 4)] = low(total + wide(stage[0]))
        zhi_copy(i).start()

    def out_wait(i):
        slot = lax.rem(i, 2)
        pltpu.make_async_copy(ostage.at[slot], dwk_out, out_sem.at[slot]).wait()

    def stage_three(i, l, places):
        zhi_copy(i).wait_recv()
        one = pltpu.make_async_copy(zlo_hbm.at[i, 0], stage.at[1], st_sem.at[1])
        two = pltpu.make_async_copy(zhi_hbm.at[i], stage.at[2], st_sem.at[2])
        one.start()
        two.start()

        @pl.when(i >= 2)
        def _():
            out_wait(i - 2)

        total = item_dot(i, l, 0)
        one.wait()
        two.wait()
        total = total + wide(stage[1]) + wide(stage[2])
        slot = lax.rem(i, 2)
        for chosen, ref, n, turned in places:

            def put():
                at = pl.ds(pl.multiple_of(n * TILE, TILE), TILE)
                ostage[slot] = total.T if turned else total
                target = ref.at[at] if turned else ref.at[:, at]
                pltpu.make_async_copy(ostage.at[slot], target, out_sem.at[slot]).start()

            if chosen is None:
                put()
            else:
                pl.when(chosen)(put)

    def ff_l(i):
        return 1 - lax.div(lax.rem(i, 3) + 1, 2)

    def ff_places(i):
        kind, j = lax.rem(i, 3), lax.div(i, 3)
        return (
            (kind == 0, dwd_out, j, True),
            (kind == 1, dwg_out, j, False),
            (kind == 2, dwu_out, j, False),
        )

    late = (
        (3, dwo_out, 0, True),
        (3, dwo_out, 1, True),
        (2, dwga_out, 0, False),
        (2, dwga_out, 1, False),
        (2, dwq_out, 0, False),
        (2, dwq_out, 1, False),
        (2, dwk_out, 0, False),
        (2, dwv_out, 0, False),
    )
    item_count = ff_items + 8
    lead, lag = 4, 2

    def tick(k, steady=False):
        if steady or k + lead < item_count:
            act_copy(k + lead).start()
        for stage_of, i in ((stage_one, k), (stage_two, k - lag), (stage_three, k - 2 * lag)):
            if not steady and not 0 <= i < item_count:
                continue
            is_ff = steady or i < ff_items
            l = ff_l(i) if is_ff else late[i - ff_items][0]
            if stage_of is stage_three:
                if is_ff:
                    stage_three(i, l, ff_places(i))
                else:
                    _, ref, n, turned = late[i - ff_items]
                    stage_three(i, l, ((None, ref, n, turned),))
            else:
                stage_of(i, l)

    def spread(l, source):
        @pl.loop(0, 4)
        def _(t):
            at = pl.multiple_of((other_z(z, t) * 2 + y) * TILE, TILE)
            lt[l, 0, t] = source[:, pl.ds(at, TILE)].T

        @pl.loop(0, 2)
        def _(k):
            at = pl.multiple_of((other_z(z, 2 * c + k) * 2 + 1 - y) * TILE, TILE)
            odd[l, k] = source[:, pl.ds(at, TILE)].T

        lt_copy(l).start()

    def relay(l):
        lt_copy(l).wait_recv()
        lt_relay(l).start()

    def core_copy(k, b):
        return remote(csend.at[b], crecv.at[k % 2, b], c1_s.at[k, b], c1_r.at[k, b], core_dev)

    def x_copy(k, b):
        return remote(fin.at[k % 2, c * 4 + b], xrecv.at[k % 2, b], x_s.at[k, b], x_r.at[k, b], x_dev)

    def fin_copy(k, b):
        piece = fin.at[k % 2, c * 4 + b]
        return remote(piece, piece, c2_s.at[k, b], c2_r.at[k, b], core_dev)

    def fin_copy_in(k, b):
        piece = fin.at[k % 2, (1 - c) * 4 + b]
        return remote(piece, piece, c2_s.at[k, b], c2_r.at[k, b], core_dev)

    def reduce_start(k, loads, compute, hooks=()):
        def block_of(step):
            return lax.rem(c + 1 + step, 2) * 4 + lax.div(step, 2)

        for copy in loads(block_of(0), 0):
            copy.start()

        @pl.loop(0, 8)
        def _(step):
            slot, b = lax.rem(step, 2), lax.div(step, 2)

            @pl.when(step < 7)
            def _():
                for copy in loads(block_of(step + 1), 1 - slot):
                    copy.start()

            for copy in loads(block_of(step), slot):
                copy.wait()
            part = compute(slot)

            @pl.when(slot == 0)
            def _():
                csend[b] = low(part)
                core_copy(k, b).start()

            @pl.when(slot == 1)
            def _():
                core_copy(k, b).wait_recv()
                fin[k % 2, c * 4 + b] = low(part + wide(crecv[k % 2, b]))
                x_copy(k, b).start()

            for when, hook in hooks:
                pl.when(step == when)(hook)

        @pl.loop(0, 4)
        def _(b):
            core_copy(k, b).wait_send()

    def reduce_end(k):
        @pl.loop(0, 4)
        def _(b):
            x_copy(k, b).wait()
            fin[k % 2, c * 4 + b] = low(wide(fin[k % 2, c * 4 + b]) + wide(xrecv[k % 2, b]))
            fin_copy(k, b).start()

        @pl.loop(0, 4)
        def _(b):
            fin_copy_in(k, b).wait_recv()
            fin_copy(k, b).wait_send()

    def fin_rows(k, at, count):
        return jnp.concatenate([wide(fin[k % 2, n, pl.ds(at, count)]) for n in range(8)], axis=1)

    def rms(value):
        return lax.rsqrt(jnp.mean(value * value, axis=-1, keepdims=True) + epsilon_k)

    n_chunks = tokens // 128

    def first_phase(hbuf, cbuf, wgb, wub, wdb, sems, w_sems):
        def row_loads(r, slot):
            at = pl.ds(r * 128, 128)
            return (
                pltpu.make_async_copy(h_hbm.at[at], hbuf.at[slot], sems.at[slot, 0]),
                pltpu.make_async_copy(cot_hbm.at[at], cbuf.at[slot], sems.at[slot, 1]),
            )

        def tile_loads(j, slot):
            at = pl.ds(pl.multiple_of(j * TILE, TILE), TILE)
            return (
                pltpu.make_async_copy(wg_hbm.at[:, at], wgb.at[slot], w_sems.at[slot, 0]),
                pltpu.make_async_copy(wu_hbm.at[:, at], wub.at[slot], w_sems.at[slot, 1]),
                pltpu.make_async_copy(wd_hbm.at[at], wdb.at[slot], w_sems.at[slot, 2]),
            )

        for copy in row_loads(0, 0):
            copy.start()
        for copy in tile_loads(0, 0):
            copy.start()

        @pl.loop(0, n_chunks)
        def _(r):
            slot = lax.rem(r, 2)

            @pl.when(r < n_chunks - 1)
            def _():
                for copy in row_loads(r + 1, 1 - slot):
                    copy.start()

            for copy in row_loads(r, slot):
                copy.wait()
            value = hbuf[slot]
            at = pl.ds(pl.multiple_of(r * 128, 128), 128)
            wide_a[at] = low(value * rms(value) * n2_ref[...])
            wide_b[at] = low(wide(cbuf[slot]) * factor_ref[at])

        spread(1, wide_b)

        @pl.loop(0, hidden_tiles)
        def _(j):
            slot = lax.rem(j, 2)

            @pl.when(j < hidden_tiles - 1)
            def _():
                for copy in tile_loads(j + 1, 1 - slot):
                    copy.start()

            for copy in tile_loads(j, slot):
                copy.wait()

            @pl.loop(0, 2)
            def _(half):
                at = pl.ds(pl.multiple_of(half * (tokens // 2), 128), tokens // 2)
                a = dot_plain(wide_a[at], wgb[slot])
                u = dot_plain(wide_a[at], wub[slot])
                dm = dot_rows(wide_b[at], wdb[slot])
                sig = jax.nn.sigmoid(a)
                act = a * sig
                acts[3 * j, 0, at] = low(act * u)
                acts[3 * j + 1, 0, at] = low(dm * u * sig * (1.0 + a * (1.0 - sig)))
                acts[3 * j + 2, 0, at] = low(dm * act)

            @pl.when(j == 0)
            def _():
                act_copy(0).start()
                spread(0, wide_a)
                act_copy(1).start()
                act_copy(2).start()

            @pl.when(j == 1)
            def _():
                act_copy(3).start()

            @pl.when(j == 3)
            def _():
                relay(1)

    pl.run_scoped(
        first_phase,
        pltpu.VMEM((2, 128, width), jnp.float32),
        pltpu.VMEM((2, 128, width), jnp.bfloat16),
        pltpu.VMEM((2, width, TILE), jnp.bfloat16),
        pltpu.VMEM((2, width, TILE), jnp.bfloat16),
        pltpu.VMEM((2, TILE, width), jnp.bfloat16),
        pltpu.SemaphoreType.DMA((2, 2)),
        pltpu.SemaphoreType.DMA((2, 3)),
    )

    lt_relay_in(1).wait_recv()
    tick(0)

    def second_phase(wa, wb, sems):
        def loads(n, slot):
            at = pl.ds(pl.multiple_of(n * TILE, TILE), TILE)
            return (
                pltpu.make_async_copy(wg_hbm.at[at], wa.at[slot], sems.at[slot, 0]),
                pltpu.make_async_copy(wu_hbm.at[at], wb.at[slot], sems.at[slot, 1]),
            )

        def compute(slot):
            total = None
            for j in range(hidden_tiles):
                at = pl.ds(j * TILE, TILE)
                part = dot_rows(acts[3 * j + 1, 0], wa[slot, :, at])
                part += dot_rows(acts[3 * j + 2, 0], wb[slot, :, at])
                total = part if total is None else total + part
            return total

        reduce_start(0, loads, compute, ((5, lambda: relay(0)),))

    pl.run_scoped(
        second_phase,
        pltpu.VMEM((2, TILE, wg_hbm.shape[1]), jnp.bfloat16),
        pltpu.VMEM((2, TILE, wg_hbm.shape[1]), jnp.bfloat16),
        pltpu.SemaphoreType.DMA((2, 2)),
    )

    lt_relay_in(0).wait_recv()
    tick(1)

    def third_phase(wa, sems):
        def loads(n, slot):
            at = pl.ds(pl.multiple_of(n * TILE, TILE), TILE)
            return (pltpu.make_async_copy(wd_hbm.at[:, at], wa.at[slot], sems.at[slot]),)

        def compute(slot):
            total = None
            for j in range(hidden_tiles):
                part = dot_plain(acts[3 * j, 0], wa[slot, pl.ds(j * TILE, TILE)])
                total = part if total is None else total + part
            return total

        reduce_start(1, loads, compute)

    pl.run_scoped(
        third_phase,
        pltpu.VMEM((2, wd_hbm.shape[0], TILE), jnp.bfloat16),
        pltpu.SemaphoreType.DMA((2,)),
    )

    tick(2)

    base = ff_items
    for n in range(2):
        pltpu.make_async_copy(
            y_hbm.at[:, pl.ds(n * TILE, TILE)], acts.at[base + n, 0], misc.at[n]
        ).start()

    def xt_own(t):
        shard = other_z(z, t) * 2 + y
        return pltpu.make_async_copy(xt_hbm.at[shard], lt.at[2, 0, t], misc.at[2 + t])

    def xt_odd(k):
        shard = other_z(z, 2 * c + k) * 2 + 1 - y
        return pltpu.make_async_copy(xt_hbm.at[shard], odd.at[2, k], misc.at[6 + k])

    for t in range(4):
        xt_own(t).start()
    for k in range(2):
        xt_odd(k).start()
    for t in range(4):
        xt_own(t).wait()
    for k in range(2):
        xt_odd(k).wait()
    for n in range(2):
        pltpu.make_async_copy(
            y_hbm.at[:, pl.ds(n * TILE, TILE)], acts.at[base + n, 0], misc.at[n]
        ).wait()

    tick(3)
    reduce_end(0)

    def fourth_phase(hbuf, cbuf, dbuf, wob, obuf, sbuf, sems, d_sems, w_sems):
        def row_loads(r, slot):
            at = pl.ds(r * 128, 128)
            return (
                pltpu.make_async_copy(h_hbm.at[at], hbuf.at[slot], sems.at[slot, 0]),
                pltpu.make_async_copy(cot_hbm.at[at], cbuf.at[slot], sems.at[slot, 1]),
            )

        def spill(r, slot):
            return pltpu.make_async_copy(dbuf.at[slot], dh_hbm.at[pl.ds(r * 128, 128)], d_sems.at[slot])

        def tile_loads(n):
            at = pl.ds(n * TILE, TILE)
            return (
                pltpu.make_async_copy(wo_hbm.at[at], wob.at[n], w_sems.at[n, 0]),
                pltpu.make_async_copy(o_hbm.at[:, at], obuf.at[n], w_sems.at[n, 1]),
                pltpu.make_async_copy(sig_hbm.at[:, at], sbuf.at[n], w_sems.at[n, 2]),
            )

        for copy in row_loads(0, 0):
            copy.start()
        for n in range(2):
            for copy in tile_loads(n):
                copy.start()
        vec[0] = jnp.zeros_like(vec[0])

        @pl.loop(0, n_chunks)
        def _(r):
            slot = lax.rem(r, 2)

            @pl.when(r < n_chunks - 1)
            def _():
                for copy in row_loads(r + 1, 1 - slot):
                    copy.start()

            for copy in row_loads(r, slot):
                copy.wait()

            @pl.when(r >= 2)
            def _():
                spill(r - 2, slot).wait()

            at = pl.ds(pl.multiple_of(r * 128, 128), 128)
            value = hbuf[slot]
            scale = rms(value)
            normed = value * scale
            grad = fin_rows(0, pl.multiple_of(r * 128, 128), 128)
            vec[0, 1:2] += jnp.sum(grad * normed, axis=0, keepdims=True)
            scaled = grad * n2_ref[...]
            inner = jnp.mean(scaled * normed, axis=-1, keepdims=True)
            dh = wide(cbuf[slot]) * factor_ref[at] + scale * (scaled - normed * inner)
            dbuf[slot] = dh
            wide_a[at] = low(dh)
            spill(r, slot).start()

        spill(n_chunks - 2, n_chunks % 2).wait()
        spill(n_chunks - 1, (n_chunks - 1) % 2).wait()

        tick(4)
        ones = jnp.ones((8, 128), jnp.bfloat16)
        for n in range(2):
            for copy in tile_loads(n):
                copy.wait()
            dy = dot_rows(wide_a[...], wob[n])
            sig, o = sbuf[n], obuf[n]
            do = low(dy * sig)
            acts[base + 2 + n, 0] = low(dy * o * sig * (1.0 - sig))
            wide_b[:, n * TILE : (n + 1) * TILE] = do
            both = wide(do) * o
            for g in range(2):
                part = both[:, g * 128 : (g + 1) * 128]
                top = low(part)
                rest = low(part - wide(top))
                delta[n, g] = dot_rows(ones, top) + dot_rows(ones, rest)

        spread(3, wide_a)
        for device in (core_dev, x_dev):
            pl.semaphore_signal(credit, inc=1, device_id=device, device_id_type=MESH)

    pl.run_scoped(
        fourth_phase,
        pltpu.VMEM((2, 128, width), jnp.float32),
        pltpu.VMEM((2, 128, width), jnp.bfloat16),
        pltpu.VMEM((2, 128, width), jnp.float32),
        pltpu.VMEM((2, TILE, width), jnp.bfloat16),
        pltpu.VMEM((2, tokens, TILE), jnp.float32),
        pltpu.VMEM((2, tokens, TILE), jnp.float32),
        pltpu.SemaphoreType.DMA((2, 2)),
        pltpu.SemaphoreType.DMA((2,)),
        pltpu.SemaphoreType.DMA((2, 3)),
    )

    tick(5)

    def attention_back(keep, ysend, lsend, hsend, dq_ref, dkv_ref):
        def ky_copy(s):
            return remote(ysend.at[lax.rem(s, 2)], yrecv.at[s], ky_s.at[s], ky_r.at[s], y_dev)

        def kl_copy(s):
            return remote(lsend.at[s], lrecv.at[s], kl_s.at[s], kl_r.at[s], lo_dev)

        def kh_copy(s):
            return remote(hsend.at[s], hrecv.at[s], kh_s.at[s], kh_r.at[s], hi_dev)

        keys_total = kpos_ref.shape[0]

        def fifth_phase(qbuf, kvbuf, q_sem, sems):
            def kv_load(s, slot):
                return pltpu.make_async_copy(kv_hbm.at[s], kvbuf.at[slot], sems.at[slot])

            q_load = pltpu.make_async_copy(q_hbm, qbuf, q_sem)
            q_load.start()
            kv_load(0, 0).start()
            q_load.wait()

            @pl.loop(0, seqs)
            def _(s):
                slot = lax.rem(s, 2)

                @pl.when(s < seqs - 1)
                def _():
                    kv_load(s + 1, 1 - slot).start()

                kv_load(s, slot).wait()
                at = pl.ds(pl.multiple_of(s * rows, 128), rows)
                @pl.when(s >= 2)
                def _():
                    ky_copy(s - 2).wait_send()

                allowed = kpos_ref[...] <= qpos_ref[...]
                for n in range(2):
                    lanes = [slice((2 * n + g) * 128, (2 * n + g + 1) * 128) for g in range(2)]
                    key = kvbuf[slot, :, n * 128 : (n + 1) * 128]
                    value = kvbuf[slot, :, 256 + n * 128 : 256 + (n + 1) * 128]
                    q = jnp.concatenate([qbuf[at, lane] for lane in lanes], axis=0)
                    do = jnp.concatenate([wide_b[at, lane] for lane in lanes], axis=0)
                    drow = jnp.concatenate([delta[n, g, 0:1, at] for g in range(2)], axis=1)
                    scores = dot_rows(key, q)
                    probs = jnp.exp(jnp.where(allowed, scores - lse_ref[s, n], -1e30))
                    grad_probs = dot_rows(value, do)
                    ds = low(probs * (grad_probs - drow))
                    for start, grad in ((0, dot_plain(ds, q)), (256, dot_plain(low(probs), do))):
                        into = slice(start + n * 128, start + (n + 1) * 128)
                        for m in range(4):
                            keep[s, m, :, into] = grad[2 * m * rows : (2 * m + 1) * rows]
                            ysend[slot, m, :, into] = low(grad[(2 * m + 1) * rows : (2 * m + 2) * rows])
                    dq = dot_first(key, ds).T
                    for g in range(2):
                        dq_ref[at, lanes[g]] = dq[g * rows : (g + 1) * rows]

                ky_copy(s).start()
                tick(6 + s, True)

        pl.run_scoped(
            fifth_phase,
            pltpu.VMEM(q_hbm.shape, jnp.bfloat16),
            pltpu.VMEM((2, keys_total, 512), jnp.bfloat16),
            pltpu.SemaphoreType.DMA,
            pltpu.SemaphoreType.DMA((2,)),
        )

        lt_copy(2).start()
        relay(3)
        tick(6 + seqs)
        tick(7 + seqs)

        @pl.loop(0, seqs)
        def _(s):
            ky_copy(s).wait_recv()
            for m in range(4):
                keep[s, m] += wide(yrecv[s, m])
            for k in range(2):
                lsend[s, k] = low(keep[s, 2 * k + 1])
            kl_copy(s).start()

        tick(8 + seqs)

        def query_phase(rbuf, sem):
            load = pltpu.make_async_copy(qraw_hbm, rbuf, sem)
            load.start()
            load.wait()
            factor = 128.0**-0.5
            for hd in range(4):
                lane = slice(hd * 128, (hd + 1) * 128)
                raw = rbuf[:, lane]
                scale = rms(raw)
                normed = raw * scale
                grad = dq_ref[:, lane]
                gvec[0, 0:1, 0:128] = (
                    jnp.sum(grad * normed * factor, axis=0, keepdims=True)
                    + (gvec[0, 0:1, 0:128] if hd else 0.0)
                )
                scaled = grad * (qg_ref[...] * factor)
                out = scale * (scaled - normed * jnp.mean(scaled * normed, axis=-1, keepdims=True))
                acts[base + 4 + hd // 2, 0, :, (hd % 2) * 128 : (hd % 2 + 1) * 128] = low(out)

        gvec[0] = jnp.zeros_like(gvec[0])
        pl.run_scoped(query_phase, pltpu.VMEM(qraw_hbm.shape, jnp.float32), pltpu.SemaphoreType.DMA)

        @pl.loop(0, seqs)
        def _(s):
            kl_copy(s).wait_recv()
            for k in range(2):
                keep[s, 2 * k] += wide(lrecv[s, k])
            hsend[s] = low(keep[s, 2])
            kh_copy(s).start()

        tick(9 + seqs)
        relay(2)
        reduce_end(1)

        def out_phase(hbuf, obuf, sems, o_sems):
            def load(r, slot):
                return pltpu.make_async_copy(h_hbm.at[pl.ds(r * 128, 128)], hbuf.at[slot], sems.at[slot])

            def store(r, slot):
                return pltpu.make_async_copy(obuf.at[slot], block_out.at[pl.ds(r * 128, 128)], o_sems.at[slot])

            load(0, 0).start()

            @pl.loop(0, n_chunks)
            def _(r):
                slot = lax.rem(r, 2)

                @pl.when(r < n_chunks - 1)
                def _():
                    load(r + 1, 1 - slot).start()

                load(r, slot).wait()

                @pl.when(r >= 2)
                def _():
                    store(r - 2, slot).wait()

                obuf[slot] = low(hbuf[slot] + fin_rows(1, pl.multiple_of(r * 128, 128), 128))
                store(r, slot).start()

            store(n_chunks - 2, n_chunks % 2).wait()
            store(n_chunks - 1, (n_chunks - 1) % 2).wait()

        pl.run_scoped(
            out_phase,
            pltpu.VMEM((2, 128, width), jnp.float32),
            pltpu.VMEM((2, 128, width), jnp.bfloat16),
            pltpu.SemaphoreType.DMA((2,)),
            pltpu.SemaphoreType.DMA((2,)),
        )

        tick(10 + seqs)

        @pl.loop(0, seqs)
        def _(s):
            kh_copy(s).wait_recv()
            dkv_ref[pl.ds(pl.multiple_of(s * rows, 128), rows)] = keep[s, 0] + wide(hrecv[s])

        def key_phase(rbuf, sem):
            load = pltpu.make_async_copy(kraw_hbm, rbuf, sem)
            load.start()
            load.wait()
            for hd in range(2):
                lane = slice(hd * 128, (hd + 1) * 128)
                raw = rbuf[:, lane]
                scale = rms(raw)
                normed = raw * scale
                grad = dkv_ref[:, lane]
                gvec[0, 0:1, 128:256] = (
                    jnp.sum(grad * normed, axis=0, keepdims=True)
                    + (gvec[0, 0:1, 128:256] if hd else 0.0)
                )
                scaled = grad * kg_ref[...]
                out = scale * (scaled - normed * jnp.mean(scaled * normed, axis=-1, keepdims=True))
                acts[base + 6, 0, :, lane] = low(out)
            acts[base + 7, 0] = low(dkv_ref[:, 256:512])

        pl.run_scoped(key_phase, pltpu.VMEM(kraw_hbm.shape, jnp.float32), pltpu.SemaphoreType.DMA)

        @pl.loop(seqs - 2, seqs)
        def _(s):
            ky_copy(s).wait_send()

        @pl.loop(0, seqs)
        def _(s):
            kl_copy(s).wait_send()
            kh_copy(s).wait_send()

    pl.run_scoped(
        attention_back,
        pltpu.VMEM((seqs, 4, rows, 512), jnp.float32),
        pltpu.VMEM((2, 4, rows, 512), jnp.bfloat16),
        pltpu.VMEM((seqs, 2, rows, 512), jnp.bfloat16),
        pltpu.VMEM((seqs, rows, 512), jnp.bfloat16),
        pltpu.VMEM((tokens, 512), jnp.float32),
        pltpu.VMEM((tokens, 512), jnp.float32),
    )

    def sixth_phase(wb, sems):
        pieces = ((wga_hbm, base + 2, 2), (wq_hbm, base + 4, 2), (wk_hbm, base + 6, 1), (wv_hbm, base + 7, 1))

        def loads(n, slot):
            at = pl.ds(pl.multiple_of(n * TILE, TILE), TILE)
            out, start = [], 0
            for p, (ref, _, count) in enumerate(pieces):
                out.append(
                    pltpu.make_async_copy(
                        ref.at[at], wb.at[slot, :, pl.ds(start, count * TILE)], sems.at[slot, p]
                    )
                )
                start += count * TILE
            return out

        def compute(slot):
            total, start = None, 0
            for _, first, count in pieces:
                for n in range(count):
                    part = dot_rows(acts[first + n, 0], wb[slot, :, pl.ds(start, TILE)])
                    total = part if total is None else total + part
                    start += TILE
            return total

        pl.semaphore_wait(credit, 2)
        reduce_start(2, loads, compute, ((3, lambda: tick(11 + seqs)),))

    pl.run_scoped(
        sixth_phase,
        pltpu.VMEM((2, TILE, 6 * TILE), jnp.bfloat16),
        pltpu.SemaphoreType.DMA((2, 4)),
    )

    for step in range(5):
        device = (y_dev, lo_dev, hi_dev, core_dev, x_dev)[step]
        copy = remote(gvec.at[step], gvec_got.at[step], gv_s.at[step], gv_r.at[step], device)
        copy.start()
        copy.wait()
        gvec[step + 1] = gvec[step] + gvec_got[step]
    gains_out[...] = gvec[5]

    lt_relay_in(2).wait_recv()
    lt_relay_in(3).wait_recv()
    tick(12 + seqs)
    tick(13 + seqs)
    reduce_end(2)

    def last_phase(xbuf, dbuf, obuf, sems, o_sems):
        def loads(r, slot):
            at = pl.ds(r * 128, 128)
            return (
                pltpu.make_async_copy(x_hbm.at[at], xbuf.at[slot], sems.at[slot, 0]),
                pltpu.make_async_copy(dh_hbm.at[at], dbuf.at[slot], sems.at[slot, 1]),
            )

        def store(r, slot):
            return pltpu.make_async_copy(obuf.at[slot], x_out.at[pl.ds(r * 128, 128)], o_sems.at[slot])

        for copy in loads(0, 0):
            copy.start()

        @pl.loop(0, n_chunks)
        def _(r):
            slot = lax.rem(r, 2)

            @pl.when(r < n_chunks - 1)
            def _():
                for copy in loads(r + 1, 1 - slot):
                    copy.start()

            for copy in loads(r, slot):
                copy.wait()

            @pl.when(r >= 2)
            def _():
                store(r - 2, slot).wait()

            value = wide(xbuf[slot])
            scale = rms(value)
            normed = value * scale
            grad = fin_rows(2, pl.multiple_of(r * 128, 128), 128)
            vec[0, 0:1] += jnp.sum(grad * normed, axis=0, keepdims=True)
            scaled = grad * n1_ref[...]
            inner = jnp.mean(scaled * normed, axis=-1, keepdims=True)
            obuf[slot] = low(dbuf[slot] + scale * (scaled - normed * inner))
            store(r, slot).start()

        store(n_chunks - 2, n_chunks % 2).wait()
        store(n_chunks - 1, (n_chunks - 1) % 2).wait()

    pl.run_scoped(
        last_phase,
        pltpu.VMEM((2, 128, width), jnp.bfloat16),
        pltpu.VMEM((2, 128, width), jnp.float32),
        pltpu.VMEM((2, 128, width), jnp.bfloat16),
        pltpu.SemaphoreType.DMA((2, 2)),
        pltpu.SemaphoreType.DMA((2,)),
    )

    for step in range(3):
        device = (y_dev, lo_dev, hi_dev)[step]
        copy = remote(vec.at[step], vec_got.at[step], nv_s.at[step], nv_r.at[step], device)
        copy.start()
        copy.wait()
        vec[step + 1] = vec[step] + vec_got[step]
    norms_out[...] = vec[3]

    for k in range(14 + seqs, item_count + 2 * lag):
        tick(k)

    @pl.loop(0, item_count)
    def _(i):
        act_copy(i).wait_send()

    @pl.loop(item_count - 4, item_count)
    def _(i):
        zlo_copy(i).wait_send()
        zhi_copy(i).wait_send()

    @pl.loop(item_count - 2, item_count)
    def _(i):
        out_wait(i)

    for l in range(4):
        lt_copy(l).wait_send()
        lt_relay(l).wait_send()


def back_call(hbm, vmem, sizes):
    tokens, width, seqs, rows, keys_total, hidden = sizes
    count = 3 * (hidden // TILE) + 8
    bf, f32 = jnp.bfloat16, jnp.float32
    dma = pltpu.SemaphoreType.DMA
    scratch = [
        pltpu.VMEM((count, 2, tokens, TILE), bf),
        pltpu.VMEM((4, 2, 4, TILE, tokens), bf),
        pltpu.VMEM((4, 2, TILE, tokens), bf),
        pltpu.VMEM((4, tokens, TILE), bf),
        pltpu.VMEM((2, 4, tokens, TILE), bf),
        pltpu.VMEM((2, 4, tokens, TILE), bf),
        pltpu.VMEM((2, 8, tokens, TILE), bf),
        pltpu.VMEM((seqs, 4, rows, 512), bf),
        pltpu.VMEM((seqs, 2, rows, 512), bf),
        pltpu.VMEM((seqs, rows, 512), bf),
        pltpu.VMEM((4, 2, TILE, TILE), bf),
        pltpu.VMEM((4, TILE, TILE), bf),
        pltpu.VMEM((3, TILE, TILE), bf),
        pltpu.VMEM((2, TILE, TILE), f32),
        pltpu.VMEM((tokens, width), bf),
        pltpu.VMEM((tokens, width), bf),
        pltpu.VMEM((2, 2, 8, tokens), f32),
        pltpu.VMEM((4, 8, width), f32),
        pltpu.VMEM((3, 8, width), f32),
        pltpu.VMEM((6, 8, 256), f32),
        pltpu.VMEM((5, 8, 256), f32),
        *(dma((count,)) for _ in range(6)),
        *(dma((4,)) for _ in range(4)),
        *(dma((3, 4)) for _ in range(6)),
        *(dma((seqs,)) for _ in range(6)),
        dma((3,)), dma((3,)), dma((5,)), dma((5,)),
        dma((3,)), dma((2,)), dma((8,)), pltpu.SemaphoreType.REGULAR,
    ]
    any_spec = pl.BlockSpec(memory_space=pl.ANY)
    vmem_spec = pl.BlockSpec(memory_space=pltpu.VMEM)
    return pl.pallas_call(
        back_kernel,
        out_shape=[
            jax.ShapeDtypeStruct((tokens, width), bf),
            jax.ShapeDtypeStruct((tokens, width), bf),
            jax.ShapeDtypeStruct((hidden, TILE), f32),
            jax.ShapeDtypeStruct((TILE, hidden), f32),
            jax.ShapeDtypeStruct((TILE, hidden), f32),
            jax.ShapeDtypeStruct((512, TILE), f32),
            jax.ShapeDtypeStruct((TILE, 512), f32),
            jax.ShapeDtypeStruct((TILE, 512), f32),
            jax.ShapeDtypeStruct((TILE, TILE), f32),
            jax.ShapeDtypeStruct((TILE, TILE), f32),
            jax.ShapeDtypeStruct((8, width), f32),
            jax.ShapeDtypeStruct((8, 256), f32),
            jax.ShapeDtypeStruct((tokens, width), f32),
            jax.ShapeDtypeStruct((count, 2, TILE, TILE), bf),
            jax.ShapeDtypeStruct((count, TILE, TILE), bf),
        ],
        in_specs=[any_spec] * len(hbm) + [vmem_spec] * len(vmem),
        out_specs=[any_spec] * 10 + [vmem_spec] * 2 + [any_spec] * 3,
        scratch_shapes=scratch,
        compiler_params=pltpu.CompilerParams(
            collective_id=1, has_side_effects=True, vmem_limit_bytes=61 << 20
        ),
    )(*hbm, *vmem)


def on_device(
    x_in,
    cot,
    domain_ids,
    domain_counts,
    domain_weights,
    block_order,
    norm1,
    w_query,
    w_key,
    w_value,
    w_gate_attn,
    w_out,
    query_gain,
    key_gain,
    norm2,
    w_gate,
    w_up,
    w_down,
):
    sequences, local_rows, width = x_in.shape
    row_total = sequences * local_rows
    head_dim = query_gain.shape[0]
    kv_local = w_key.shape[1] // head_dim
    q_local = w_query.shape[1] // head_dim
    group = q_local // kv_local
    devices = lax.axis_size("seq")
    own = lax.axis_index("seq")
    block_rows = local_rows * devices // block_order.shape[0]
    query_factor = head_dim ** (-0.5)
    q_gain, k_gain = wide(query_gain), wide(key_gain)
    gain_one, gain_two = wide(norm1), wide(norm2)

    def cut_columns(weight, half):
        return lax.dynamic_slice_in_dim(weight, half * (width // 2), width // 2, 1)

    x_rows = x_in.reshape(row_total, width)
    x_float = wide(x_rows)
    x_normed = low(x_float * norm_scale(x_float) * gain_one)
    key_raw = product(x_normed, w_key)
    by_head = key_raw.reshape(row_total, kv_local, head_dim)
    key_rows = low(by_head * norm_scale(by_head) * k_gain).reshape(row_total, -1)
    value_rows = low(product(x_normed, w_value))
    pair = jnp.concatenate([key_rows, value_rows], axis=1).reshape(sequences, local_rows, -1)
    kv_width = kv_local * head_dim

    seqs_of = sequences // CHUNKS
    rows_of = row_total // CHUNKS

    def gather(value):
        slots = {0: value}
        for mask in range(2, devices, 2):
            slots[mask] = swap(value, "seq", mask)
        for mask in range(0, devices, 2):
            slots[mask + 1] = swap(slots[mask], "seq", 1)
        return jnp.stack([slots[j] for j in range(devices)], axis=1).reshape(
            seqs_of, devices * local_rows, -1
        )

    gathered = [gather(pair[c * seqs_of : (c + 1) * seqs_of]) for c in range(CHUNKS)]

    query_raw = product(x_normed, w_query)
    gate_pre = product(x_normed, w_gate_attn)
    by_head = query_raw.reshape(row_total, q_local, head_dim)
    query = low(by_head * norm_scale(by_head) * q_gain * query_factor)
    gate_sig = jax.nn.sigmoid(gate_pre)

    query_pos = positions(block_order, own, local_rows, block_rows)
    key_pos = jnp.concatenate(
        [positions(block_order, own ^ j, local_rows, block_rows) for j in range(devices)]
    )
    allowed = key_pos[None, :] <= query_pos[:, None]

    domain_total = domain_weights.shape[0]
    domain_index = jnp.arange(domain_total, dtype=jnp.int32)
    factor = domain_weights * (row_total * devices) / (domain_total * wide(domain_counts))
    picked = domain_ids.reshape(row_total)[:, None] == domain_index[None, :]
    row_scale = jnp.sum(jnp.where(picked, factor[None, :], 0.0), axis=1)

    saved = []
    for c in range(CHUNKS):
        rows = slice(c * rows_of, (c + 1) * rows_of)
        heads = (
            query[rows]
            .reshape(seqs_of, local_rows, kv_local, group, head_dim)
            .transpose(0, 2, 3, 1, 4)
        )
        keys = gathered[c][..., :kv_width].reshape(seqs_of, -1, kv_local, head_dim)
        values = gathered[c][..., kv_width:].reshape(seqs_of, -1, kv_local, head_dim)
        scores = jnp.einsum("skgqd,spkd->skgqp", heads, keys, preferred_element_type=jnp.float32)
        scores = jnp.where(allowed, scores, -1e30)
        top = jnp.max(scores, axis=-1)
        weights = jnp.where(allowed, jnp.exp(scores - top[..., None]), 0.0)
        total = jnp.sum(weights, axis=-1)
        mixed = jnp.einsum(
            "skgqp,spkd->skgqd", low(weights), values, preferred_element_type=jnp.float32
        )
        attn_heads = mixed / total[..., None]
        log_total = top + jnp.log(total)
        attn_flat = attn_heads.transpose(0, 3, 1, 2, 4).reshape(rows_of, q_local * head_dim)
        gated = low(attn_flat * gate_sig[rows])
        attn_sum = head_sum(gated, w_out, product, cut_columns)
        residual = x_float[rows] + attn_sum
        log_total = log_total.reshape(seqs_of, kv_local, 1, group * local_rows)
        saved.append((residual, attn_flat, gated, log_total))

    residual, attn_flat, gated, log_total = (
        jnp.concatenate([part[i] for part in saved], axis=0) for i in range(4)
    )
    out, x_grad, down, gate, up, wout, wga, wquery, wkey, wvalue, norms, gains, *_ = back_call(
        (
            residual,
            cot.reshape(row_total, width),
            x_rows,
            x_normed.T.reshape(devices, width // devices, row_total),
            query.reshape(row_total, q_local * head_dim),
            jnp.concatenate(gathered, axis=0),
            attn_flat,
            gate_sig,
            gated,
            query_raw,
            key_raw,
            w_gate,
            w_up,
            w_down,
            w_out,
            w_query,
            w_key,
            w_value,
            w_gate_attn,
        ),
        (
            row_scale[:, None],
            log_total,
            key_pos[:, None],
            jnp.concatenate([query_pos] * group)[None, :],
            gain_one[None, :],
            gain_two[None, :],
            q_gain[None, :],
            k_gain[None, :],
        ),
        (row_total, width, sequences, local_rows, local_rows * devices, w_down.shape[0]),
    )

    def own_part(value):
        size = value.shape[0] // devices
        return lax.dynamic_slice_in_dim(value, own * size, size, 0)

    return (
        out.reshape(x_in.shape),
        x_grad.reshape(x_in.shape),
        own_part(norms[0]),
        wquery,
        wkey,
        wvalue,
        wga,
        wout,
        own_part(gains[0, :head_dim]),
        own_part(gains[0, head_dim:]),
        own_part(norms[1]),
        gate,
        up,
        down,
    )


def on_device_plain(
    x_in,
    cot,
    domain_ids,
    domain_counts,
    domain_weights,
    block_order,
    norm1,
    w_query,
    w_key,
    w_value,
    w_gate_attn,
    w_out,
    query_gain,
    key_gain,
    norm2,
    w_gate,
    w_up,
    w_down,
):
    sequences, local_rows, model_width = x_in.shape
    row_total = sequences * local_rows
    head_dim = query_gain.shape[0]
    kv_local = w_key.shape[1] // head_dim
    q_local = w_query.shape[1] // head_dim
    group_size = q_local // kv_local
    block_rows = local_rows // 2
    seq_devices = lax.axis_size("seq")
    first_row = lax.axis_index("seq") * local_rows
    query_pos = positions(block_order, first_row, local_rows, block_rows)
    query_factor = head_dim ** (-0.5)
    q_gain = query_gain.astype(jnp.float32)
    k_gain = key_gain.astype(jnp.float32)
    gain_one = norm1.astype(jnp.float32)
    gain_two = norm2.astype(jnp.float32)
    x_float = x_in.reshape(row_total, model_width).astype(jnp.float32)
    scale_one = norm_scale(x_float)
    normed_one = x_float * scale_one
    x_normed = (normed_one * gain_one).astype(jnp.bfloat16)
    query_raw = product(x_normed, w_query).reshape(row_total, q_local, head_dim)
    key_raw = product(x_normed, w_key).reshape(row_total, kv_local, head_dim)
    value_rows = product(x_normed, w_value).astype(jnp.bfloat16)
    gate_pre = product(x_normed, w_gate_attn)
    query_scale = norm_scale(query_raw)
    query_normed = query_raw * query_scale
    key_scale = norm_scale(key_raw)
    key_normed = key_raw * key_scale
    query = (query_normed * q_gain * query_factor).astype(jnp.bfloat16)
    key_rows = (key_normed * k_gain).astype(jnp.bfloat16)
    project_query_heads = query.reshape(
        sequences, local_rows, kv_local, group_size, head_dim
    ).transpose(0, 2, 3, 1, 4)
    (
        query_scale,
        query_normed,
        key_scale,
        key_normed,
        query_heads,
        key_rows,
        value_rows,
        gate_pre,
    ) = (
        query_scale,
        query_normed,
        key_scale,
        key_normed,
        project_query_heads,
        key_rows,
        value_rows,
        gate_pre,
    )
    key_seq = key_rows.reshape(sequences, local_rows, kv_local * head_dim)
    value_seq = value_rows.reshape(sequences, local_rows, kv_local * head_dim)
    stat_shape = (sequences, kv_local, group_size, local_rows)
    running_max = jnp.full(stat_shape, -1e30, jnp.float32)
    key_piece = lax.all_gather(key_seq, "seq", axis=1, tiled=True)
    value_piece = lax.all_gather(value_seq, "seq", axis=1, tiled=True)
    row_count = key_piece.shape[1]
    key_block = key_piece.reshape(sequences, row_count, kv_local, head_dim)
    value_block = value_piece.reshape(sequences, row_count, kv_local, head_dim)
    key_pos = positions(block_order, jnp.int32(0), row_count, block_rows)
    allowed = key_pos[None, :] <= query_pos[:, None]
    scores = jnp.einsum(
        "skgqd,spkd->skgqp", query_heads, key_block, preferred_element_type=jnp.float32
    )
    scores = jnp.where(allowed, scores, -1e30)
    new_max = jnp.maximum(running_max, jnp.max(scores, axis=-1))
    weights = jnp.where(allowed, jnp.exp(scores - new_max[..., None]), 0.0)
    running_sum = jnp.sum(weights, axis=-1)
    weighted = jnp.einsum(
        "skgqp,spkd->skgqd",
        weights.astype(jnp.bfloat16),
        value_block,
        preferred_element_type=jnp.float32,
    )
    running_max, running_sum, weighted = (new_max, running_sum, weighted)
    log_total = running_max + jnp.log(running_sum)
    attn_heads = weighted / running_sum[..., None]
    attn_flat = attn_heads.transpose(0, 3, 1, 2, 4).reshape(row_total, q_local * head_dim)
    gate_sig = jax.nn.sigmoid(gate_pre)
    gated = (attn_flat * gate_sig).astype(jnp.bfloat16)
    attn_sum = lax.psum(product(gated, w_out).astype(jnp.bfloat16), "head").astype(jnp.float32)
    residual = x_float + attn_sum
    scale_two = norm_scale(residual)
    normed_two = residual * scale_two
    h_normed = (normed_two * gain_two).astype(jnp.bfloat16)
    gate_proj = product(h_normed, w_gate)
    up_proj = product(h_normed, w_up)
    gate_logit = jax.nn.sigmoid(gate_proj)
    gate_act = gate_proj * gate_logit
    mixed = (gate_act * up_proj).astype(jnp.bfloat16)
    mlp_sum = lax.psum(product(mixed, w_down).astype(jnp.bfloat16), "head").astype(jnp.float32)
    block_out = (
        (residual + mlp_sum).astype(jnp.bfloat16).reshape(sequences, local_rows, model_width)
    )
    domain_total = domain_weights.shape[0]
    domain_index = jnp.arange(domain_total, dtype=jnp.int32)
    factor = (
        domain_weights
        * (row_total * seq_devices)
        / (domain_total * domain_counts.astype(jnp.float32))
    )
    picked = domain_ids.reshape(row_total)[:, None] == domain_index[None, :]
    row_scale = jnp.sum(jnp.where(picked, factor[None, :], 0.0), axis=1)
    grad_out = cot.reshape(row_total, model_width).astype(jnp.float32) * row_scale[:, None]
    grad_low = grad_out.astype(jnp.bfloat16)
    grad_down = outer_sum(mixed, grad_low)
    grad_mixed = back_product(grad_low, w_down)
    grad_gate = (grad_mixed * up_proj * gate_logit * (1.0 + gate_proj * (1.0 - gate_logit))).astype(
        jnp.bfloat16
    )
    grad_up = (grad_mixed * gate_act).astype(jnp.bfloat16)
    grad_mlp_gate = outer_sum(h_normed, grad_gate)
    grad_mlp_up = outer_sum(h_normed, grad_up)
    grad_hnorm = lax.psum(
        (back_product(grad_gate, w_gate) + back_product(grad_up, w_up)).astype(jnp.bfloat16), "head"
    ).astype(jnp.float32)
    grad_norm_two = jnp.sum(grad_hnorm * normed_two, axis=0)
    grad_resid = grad_out + norm_back(grad_hnorm, normed_two, scale_two, gain_two)
    grad_attn = grad_resid.astype(jnp.bfloat16)
    grad_wout = outer_sum(gated, grad_attn)
    grad_gated = back_product(grad_attn, w_out)
    grad_heads_flat = (grad_gated * gate_sig).astype(jnp.bfloat16)
    grad_gatepre = (grad_gated * attn_flat * gate_sig * (1.0 - gate_sig)).astype(jnp.bfloat16)
    grad_wgate_attn = outer_sum(x_normed, grad_gatepre)
    grad_heads = grad_heads_flat.reshape(
        sequences, local_rows, kv_local, group_size, head_dim
    ).transpose(0, 2, 3, 1, 4)
    row_delta = jnp.sum(grad_heads.astype(jnp.float32) * attn_heads, axis=-1)
    key_piece = lax.all_gather(key_seq, "seq", axis=1, tiled=True)
    value_piece = lax.all_gather(value_seq, "seq", axis=1, tiled=True)
    row_count = key_piece.shape[1]
    key_block = key_piece.reshape(sequences, row_count, kv_local, head_dim)
    value_block = value_piece.reshape(sequences, row_count, kv_local, head_dim)
    key_pos = positions(block_order, jnp.int32(0), row_count, block_rows)
    allowed = key_pos[None, :] <= query_pos[:, None]
    scores = jnp.einsum(
        "skgqd,spkd->skgqp", query_heads, key_block, preferred_element_type=jnp.float32
    )
    probs = jnp.where(
        allowed, jnp.exp(jnp.where(allowed, scores, -1e30) - log_total[..., None]), 0.0
    )
    grad_probs = jnp.einsum(
        "skgqd,spkd->skgqp", grad_heads, value_block, preferred_element_type=jnp.float32
    )
    grad_scores = (probs * (grad_probs - row_delta[..., None])).astype(jnp.bfloat16)
    grad_query = jnp.einsum(
        "skgqp,spkd->skgqd", grad_scores, key_block, preferred_element_type=jnp.float32
    )
    key_term = jnp.einsum(
        "skgqp,skgqd->spkd", grad_scores, query_heads, preferred_element_type=jnp.float32
    ).reshape(sequences, row_count, kv_local * head_dim)
    value_term = jnp.einsum(
        "skgqp,skgqd->spkd",
        probs.astype(jnp.bfloat16),
        grad_heads,
        preferred_element_type=jnp.float32,
    ).reshape(sequences, row_count, kv_local * head_dim)
    grad_keys = key_term
    grad_values = value_term
    grad_query, grad_keys, grad_values = (grad_query, grad_keys, grad_values)
    grad_key_own, grad_value_own = (
        lax.psum_scatter(
            grad_keys.astype(jnp.bfloat16), "seq", scatter_dimension=1, tiled=True
        ).astype(jnp.float32),
        lax.psum_scatter(
            grad_values.astype(jnp.bfloat16), "seq", scatter_dimension=1, tiled=True
        ).astype(jnp.float32),
    )
    grad_query_rows = grad_query.transpose(0, 3, 1, 2, 4).reshape(row_total, q_local, head_dim)
    grad_qgain_part = jnp.sum(grad_query_rows * query_normed * query_factor, axis=(0, 1))
    grad_query_raw = (
        norm_back(grad_query_rows, query_normed, query_scale, q_gain * query_factor)
        .astype(jnp.bfloat16)
        .reshape(row_total, q_local * head_dim)
    )
    grad_key_rows = grad_key_own.reshape(row_total, kv_local, head_dim)
    grad_kgain_part = jnp.sum(grad_key_rows * key_normed, axis=(0, 1))
    grad_key_raw = (
        norm_back(grad_key_rows, key_normed, key_scale, k_gain)
        .astype(jnp.bfloat16)
        .reshape(row_total, kv_local * head_dim)
    )
    grad_value_low = grad_value_own.reshape(row_total, kv_local * head_dim).astype(jnp.bfloat16)
    grad_xnorm_part = (
        back_product(grad_query_raw, w_query)
        + back_product(grad_key_raw, w_key)
        + back_product(grad_value_low, w_value)
        + back_product(grad_gatepre, w_gate_attn)
    )
    grad_xnorm, grad_qgain, grad_kgain = (
        lax.psum(grad_xnorm_part.astype(jnp.bfloat16), "head").astype(jnp.float32),
        lax.psum(grad_qgain_part.astype(jnp.bfloat16), "head").astype(jnp.float32),
        lax.psum(grad_kgain_part.astype(jnp.bfloat16), "head").astype(jnp.float32),
    )
    grad_norm_one = jnp.sum(grad_xnorm * normed_one, axis=0)
    x_grad = (
        (grad_resid + norm_back(grad_xnorm, normed_one, scale_one, gain_one))
        .astype(jnp.bfloat16)
        .reshape(sequences, local_rows, model_width)
    )
    grad_wquery = outer_sum(x_normed, grad_query_raw)
    grad_wkey = outer_sum(x_normed, grad_key_raw)
    grad_wvalue = outer_sum(x_normed, grad_value_low)
    all_totals = (
        lax.psum_scatter(
            grad_norm_one.astype(jnp.bfloat16), "seq", scatter_dimension=0, tiled=True
        ).astype(jnp.float32),
        lax.psum_scatter(
            grad_wquery.astype(jnp.bfloat16), "seq", scatter_dimension=0, tiled=True
        ).astype(jnp.float32),
        lax.psum_scatter(
            grad_wkey.astype(jnp.bfloat16), "seq", scatter_dimension=0, tiled=True
        ).astype(jnp.float32),
        lax.psum_scatter(
            grad_wvalue.astype(jnp.bfloat16), "seq", scatter_dimension=0, tiled=True
        ).astype(jnp.float32),
        lax.psum_scatter(
            grad_wgate_attn.astype(jnp.bfloat16), "seq", scatter_dimension=0, tiled=True
        ).astype(jnp.float32),
        lax.psum_scatter(
            grad_wout.astype(jnp.bfloat16), "seq", scatter_dimension=1, tiled=True
        ).astype(jnp.float32),
        lax.psum_scatter(
            grad_qgain.astype(jnp.bfloat16), "seq", scatter_dimension=0, tiled=True
        ).astype(jnp.float32),
        lax.psum_scatter(
            grad_kgain.astype(jnp.bfloat16), "seq", scatter_dimension=0, tiled=True
        ).astype(jnp.float32),
        lax.psum_scatter(
            grad_mlp_gate.astype(jnp.bfloat16), "seq", scatter_dimension=0, tiled=True
        ).astype(jnp.float32),
        lax.psum_scatter(
            grad_mlp_up.astype(jnp.bfloat16), "seq", scatter_dimension=0, tiled=True
        ).astype(jnp.float32),
        lax.psum_scatter(
            grad_down.astype(jnp.bfloat16), "seq", scatter_dimension=1, tiled=True
        ).astype(jnp.float32),
        lax.psum_scatter(
            grad_norm_two.astype(jnp.bfloat16), "seq", scatter_dimension=0, tiled=True
        ).astype(jnp.float32),
    )
    return (
        block_out,
        x_grad,
        all_totals[0],
        all_totals[1],
        all_totals[2],
        all_totals[3],
        all_totals[4],
        all_totals[5],
        all_totals[6],
        all_totals[7],
        all_totals[11],
        all_totals[8],
        all_totals[9],
        all_totals[10],
    )


def solution(mesh):
    fits = mesh.shape["seq"] == 8 and mesh.shape["head"] == 4
    return jax.shard_map(
        on_device if fits else on_device_plain,
        mesh=mesh,
        in_specs=(
            P(None, "seq", None),
            P(None, "seq", None),
            P(None, "seq"),
            P(),
            P(),
            P(),
            P(),
            P(None, "head"),
            P(None, "head"),
            P(None, "head"),
            P(None, "head"),
            P("head", None),
            P(),
            P(),
            P(),
            P(None, "head"),
            P(None, "head"),
            P("head", None),
        ),
        out_specs=(
            P(None, "seq", None),
            P(None, "seq", None),
            P("seq"),
            P("seq", "head"),
            P("seq", "head"),
            P("seq", "head"),
            P("seq", "head"),
            P("head", "seq"),
            P("seq"),
            P("seq"),
            P("seq"),
            P("seq", "head"),
            P("seq", "head"),
            P("head", "seq"),
        ),
        check_vma=False,
    )
```

```python
import jax
import jax.numpy as jnp
from jax import lax
from jax.experimental import pallas as pl
from jax.experimental.pallas import tpu as pltpu
from jax.sharding import PartitionSpec as P

epsilon = 1e-06


def norm_scale(value):
    return lax.rsqrt(jnp.mean(value * value, axis=-1, keepdims=True) + epsilon)


def norm_back(grad_in, normed, scale, gain):
    scaled = grad_in * gain
    return scale * (scaled - normed * jnp.mean(scaled * normed, axis=-1, keepdims=True))


def product(left, right):
    return jnp.dot(left, right, preferred_element_type=jnp.float32)


def outer_sum(left, right):
    return lax.dot_general(
        left, right, (((0,), (0,)), ((), ())), preferred_element_type=jnp.float32
    )


def back_product(left, right):
    return lax.dot_general(
        left, right, (((1,), (1,)), ((), ())), preferred_element_type=jnp.float32
    )


def low(value):
    return value.astype(jnp.bfloat16)


def wide(value):
    return value.astype(jnp.float32)


def positions(block_order, device, row_count, block_rows):
    stored = device * row_count + jnp.arange(row_count, dtype=jnp.int32)
    slots = stored // block_rows
    slot_index = jnp.arange(block_order.shape[0], dtype=jnp.int32)
    picked = jnp.sum(
        jnp.where(slots[:, None] == slot_index[None, :], block_order[None, :], 0), axis=1
    )
    return picked * block_rows + stored % block_rows


MESH = pl.DeviceIdType.MESH
TILE = 256


def other_z(z, t):
    low_z, high_z = lax.rem(z, 2), lax.div(z, 2)
    low_t, high_t = lax.rem(t, 2), lax.div(t, 2)
    return (low_z + low_t - 2 * low_z * low_t) + 2 * (high_z + high_t - 2 * high_z * high_t)


def dot_plain(left, right):
    return jnp.dot(left, right, preferred_element_type=jnp.float32)


def dot_rows(left, right):
    return lax.dot_general(
        left, right, (((1,), (1,)), ((), ())), preferred_element_type=jnp.float32
    )


def dot_first(left, right):
    return lax.dot_general(
        left, right, (((0,), (0,)), ((), ())), preferred_element_type=jnp.float32
    )


def back_kernel(
    h_hbm, cot_hbm, x_hbm, xt_hbm, q_hbm, kv_hbm, o_hbm, sig_hbm, y_hbm, qraw_hbm, kraw_hbm,
    wg_hbm, wu_hbm, wd_hbm, wo_hbm, wq_hbm, wk_hbm, wv_hbm, wga_hbm,
    factor_ref, lse_ref, kpos_ref, qpos_ref, n1_ref, n2_ref, qg_ref, kg_ref,
    block_out, x_out, dwd_out, dwg_out, dwu_out, dwo_out, dwga_out, dwq_out, dwk_out, dwv_out,
    norms_out, gains_out, dh_hbm, zlo_hbm, zhi_hbm,
    acts, lt, odd, csend, crecv, xrecv, fin, yrecv, lrecv, hrecv,
    zlo_send, zhi_send, stage, ostage, wide_a, wide_b, delta,
    vec, vec_got, gvec, gvec_got,
    ya_s, ya_r, zl_s, zl_r, zh_s, zh_r, lt_s, lt_r, lc_s, lc_r,
    c1_s, c1_r, x_s, x_r, c2_s, c2_r, ky_s, ky_r, kl_s, kl_r, kh_s, kh_r,
    nv_s, nv_r, gv_s, gv_r, st_sem, out_sem, misc, credit,
):
    seq, head = lax.axis_index("seq"), lax.axis_index("head")
    z, y = lax.div(seq, 2), lax.rem(seq, 2)
    c = lax.rem(head, 2)
    y_dev = {"seq": z * 2 + 1 - y}
    lo_dev = {"seq": other_z(z, 1) * 2 + y}
    hi_dev = {"seq": other_z(z, 2) * 2 + y}
    core_dev = {"head": head + 1 - 2 * c}
    x_dev = {"head": head + 2 - 4 * lax.div(head, 2)}
    tokens = cot_hbm.shape[0]
    rows = kpos_ref.shape[0] // 8
    seqs = tokens // rows
    hidden_tiles = wd_hbm.shape[0] // TILE
    ff_items = 3 * hidden_tiles
    width = cot_hbm.shape[1]
    epsilon_k = 1e-06

    barrier = pltpu.get_barrier_semaphore()
    for device in (y_dev, lo_dev, hi_dev, core_dev, x_dev):
        pl.semaphore_signal(barrier, inc=1, device_id=device, device_id_type=MESH)
    pl.semaphore_wait(barrier, 5)

    def remote(src, dst, send, recv, device):
        return pltpu.make_async_remote_copy(
            src_ref=src, dst_ref=dst, send_sem=send, recv_sem=recv, device_id=device, device_id_type=MESH
        )

    def act_copy(i):
        return remote(acts.at[i, 0], acts.at[i, 1], ya_s.at[i], ya_r.at[i], y_dev)

    def lt_copy(l):
        return remote(odd.at[l], lt.at[l, 1, pl.ds(2 * c, 2)], lt_s.at[l], lt_r.at[l], y_dev)

    def lt_relay(l):
        piece = lt.at[l, 1, pl.ds(2 * c, 2)]
        return remote(piece, piece, lc_s.at[l], lc_r.at[l], core_dev)

    def lt_relay_in(l):
        piece = lt.at[l, 1, pl.ds(2 - 2 * c, 2)]
        return remote(piece, piece, lc_s.at[l], lc_r.at[l], core_dev)

    def zlo_copy(i):
        return remote(zlo_send.at[lax.rem(i, 4)], zlo_hbm.at[i], zl_s.at[i], zl_r.at[i], lo_dev)

    def zhi_copy(i):
        return remote(zhi_send.at[lax.rem(i, 4)], zhi_hbm.at[i], zh_s.at[i], zh_r.at[i], hi_dev)

    def item_dot(i, l, t):
        return dot_plain(lt[l, 0, t], acts[i, 0]) + dot_plain(lt[l, 1, t], acts[i, 1])

    def stage_one(i, l):
        act_copy(i).wait_recv()

        @pl.when(i >= 4)
        def _():
            zlo_copy(i - 4).wait_send()

        slot = lax.rem(i, 4)
        for k in range(2):
            zlo_send[slot, k] = low(item_dot(i, l, 2 * k + 1))
        zlo_copy(i).start()

    def stage_two(i, l):
        zlo_copy(i).wait_recv()
        here = pltpu.make_async_copy(zlo_hbm.at[i, 1], stage.at[0], st_sem.at[0])
        here.start()

        @pl.when(i >= 4)
        def _():
            zhi_copy(i - 4).wait_send()

        total = item_dot(i, l, 2)
        here.wait()
        zhi_send[lax.rem(i, 4)] = low(total + wide(stage[0]))
        zhi_copy(i).start()

    def out_wait(i):
        slot = lax.rem(i, 2)
        pltpu.make_async_copy(ostage.at[slot], dwk_out, out_sem.at[slot]).wait()

    def stage_three(i, l, places):
        zhi_copy(i).wait_recv()
        one = pltpu.make_async_copy(zlo_hbm.at[i, 0], stage.at[1], st_sem.at[1])
        two = pltpu.make_async_copy(zhi_hbm.at[i], stage.at[2], st_sem.at[2])
        one.start()
        two.start()

        @pl.when(i >= 2)
        def _():
            out_wait(i - 2)

        total = item_dot(i, l, 0)
        one.wait()
        two.wait()
        total = total + wide(stage[1]) + wide(stage[2])
        slot = lax.rem(i, 2)
        for chosen, ref, n, turned in places:

            def put():
                at = pl.ds(pl.multiple_of(n * TILE, TILE), TILE)
                ostage[slot] = total.T if turned else total
                target = ref.at[at] if turned else ref.at[:, at]
                pltpu.make_async_copy(ostage.at[slot], target, out_sem.at[slot]).start()

            if chosen is None:
                put()
            else:
                pl.when(chosen)(put)

    def ff_l(i):
        return 1 - lax.div(lax.rem(i, 3) + 1, 2)

    def ff_places(i):
        kind, j = lax.rem(i, 3), lax.div(i, 3)
        return (
            (kind == 0, dwd_out, j, True),
            (kind == 1, dwg_out, j, False),
            (kind == 2, dwu_out, j, False),
        )

    late = (
        (3, dwo_out, 0, True),
        (3, dwo_out, 1, True),
        (2, dwga_out, 0, False),
        (2, dwga_out, 1, False),
        (2, dwq_out, 0, False),
        (2, dwq_out, 1, False),
        (2, dwk_out, 0, False),
        (2, dwv_out, 0, False),
    )
    item_count = ff_items + 8
    lead, lag = 4, 2

    def tick(k, steady=False):
        if steady or k + lead < item_count:
            act_copy(k + lead).start()
        for stage_of, i in ((stage_one, k), (stage_two, k - lag), (stage_three, k - 2 * lag)):
            if not steady and not 0 <= i < item_count:
                continue
            is_ff = steady or i < ff_items
            l = ff_l(i) if is_ff else late[i - ff_items][0]
            if stage_of is stage_three:
                if is_ff:
                    stage_three(i, l, ff_places(i))
                else:
                    _, ref, n, turned = late[i - ff_items]
                    stage_three(i, l, ((None, ref, n, turned),))
            else:
                stage_of(i, l)

    def spread(l, source):
        @pl.loop(0, 4)
        def _(t):
            at = pl.multiple_of((other_z(z, t) * 2 + y) * TILE, TILE)
            lt[l, 0, t] = source[:, pl.ds(at, TILE)].T

        @pl.loop(0, 2)
        def _(k):
            at = pl.multiple_of((other_z(z, 2 * c + k) * 2 + 1 - y) * TILE, TILE)
            odd[l, k] = source[:, pl.ds(at, TILE)].T

        lt_copy(l).start()

    def relay(l):
        lt_copy(l).wait_recv()
        lt_relay(l).start()

    def core_copy(k, b):
        return remote(csend.at[b], crecv.at[k % 2, b], c1_s.at[k, b], c1_r.at[k, b], core_dev)

    def x_copy(k, b):
        return remote(fin.at[k % 2, c * 4 + b], xrecv.at[k % 2, b], x_s.at[k, b], x_r.at[k, b], x_dev)

    def fin_copy(k, b):
        piece = fin.at[k % 2, c * 4 + b]
        return remote(piece, piece, c2_s.at[k, b], c2_r.at[k, b], core_dev)

    def fin_copy_in(k, b):
        piece = fin.at[k % 2, (1 - c) * 4 + b]
        return remote(piece, piece, c2_s.at[k, b], c2_r.at[k, b], core_dev)

    def reduce_start(k, loads, compute, hooks=()):
        def block_of(step):
            return lax.rem(c + 1 + step, 2) * 4 + lax.div(step, 2)

        for copy in loads(block_of(0), 0):
            copy.start()

        @pl.loop(0, 8)
        def _(step):
            slot, b = lax.rem(step, 2), lax.div(step, 2)

            @pl.when(step < 7)
            def _():
                for copy in loads(block_of(step + 1), 1 - slot):
                    copy.start()

            for copy in loads(block_of(step), slot):
                copy.wait()
            part = compute(slot)

            @pl.when(slot == 0)
            def _():
                csend[b] = low(part)
                core_copy(k, b).start()

            @pl.when(slot == 1)
            def _():
                core_copy(k, b).wait_recv()
                fin[k % 2, c * 4 + b] = low(part + wide(crecv[k % 2, b]))
                x_copy(k, b).start()

            for when, hook in hooks:
                pl.when(step == when)(hook)

        @pl.loop(0, 4)
        def _(b):
            core_copy(k, b).wait_send()

    def reduce_end(k):
        @pl.loop(0, 4)
        def _(b):
            x_copy(k, b).wait()
            fin[k % 2, c * 4 + b] = low(wide(fin[k % 2, c * 4 + b]) + wide(xrecv[k % 2, b]))
            fin_copy(k, b).start()

        @pl.loop(0, 4)
        def _(b):
            fin_copy_in(k, b).wait_recv()
            fin_copy(k, b).wait_send()

    def fin_rows(k, at, count):
        return jnp.concatenate([wide(fin[k % 2, n, pl.ds(at, count)]) for n in range(8)], axis=1)

    def rms(value):
        return lax.rsqrt(jnp.mean(value * value, axis=-1, keepdims=True) + epsilon_k)

    n_chunks = tokens // 128

    def first_phase(hbuf, cbuf, wgb, wub, wdb, sems, w_sems):
        def row_loads(r, slot):
            at = pl.ds(r * 128, 128)
            return (
                pltpu.make_async_copy(h_hbm.at[at], hbuf.at[slot], sems.at[slot, 0]),
                pltpu.make_async_copy(cot_hbm.at[at], cbuf.at[slot], sems.at[slot, 1]),
            )

        def tile_loads(j, slot):
            at = pl.ds(pl.multiple_of(j * TILE, TILE), TILE)
            return (
                pltpu.make_async_copy(wg_hbm.at[:, at], wgb.at[slot], w_sems.at[slot, 0]),
                pltpu.make_async_copy(wu_hbm.at[:, at], wub.at[slot], w_sems.at[slot, 1]),
                pltpu.make_async_copy(wd_hbm.at[at], wdb.at[slot], w_sems.at[slot, 2]),
            )

        for copy in row_loads(0, 0):
            copy.start()
        for copy in tile_loads(0, 0):
            copy.start()

        @pl.loop(0, n_chunks)
        def _(r):
            slot = lax.rem(r, 2)

            @pl.when(r < n_chunks - 1)
            def _():
                for copy in row_loads(r + 1, 1 - slot):
                    copy.start()

            for copy in row_loads(r, slot):
                copy.wait()
            value = hbuf[slot]
            at = pl.ds(pl.multiple_of(r * 128, 128), 128)
            wide_a[at] = low(value * rms(value) * n2_ref[...])
            wide_b[at] = low(wide(cbuf[slot]) * factor_ref[at])

        spread(1, wide_b)

        @pl.loop(0, hidden_tiles)
        def _(j):
            slot = lax.rem(j, 2)

            @pl.when(j < hidden_tiles - 1)
            def _():
                for copy in tile_loads(j + 1, 1 - slot):
                    copy.start()

            for copy in tile_loads(j, slot):
                copy.wait()

            @pl.loop(0, 2)
            def _(half):
                at = pl.ds(pl.multiple_of(half * (tokens // 2), 128), tokens // 2)
                a = dot_plain(wide_a[at], wgb[slot])
                u = dot_plain(wide_a[at], wub[slot])
                dm = dot_rows(wide_b[at], wdb[slot])
                sig = jax.nn.sigmoid(a)
                act = a * sig
                acts[3 * j, 0, at] = low(act * u)
                acts[3 * j + 1, 0, at] = low(dm * u * sig * (1.0 + a * (1.0 - sig)))
                acts[3 * j + 2, 0, at] = low(dm * act)

            @pl.when(j == 0)
            def _():
                act_copy(0).start()
                spread(0, wide_a)
                act_copy(1).start()
                act_copy(2).start()

            @pl.when(j == 1)
            def _():
                act_copy(3).start()

            @pl.when(j == 3)
            def _():
                relay(1)

    pl.run_scoped(
        first_phase,
        pltpu.VMEM((2, 128, width), jnp.float32),
        pltpu.VMEM((2, 128, width), jnp.bfloat16),
        pltpu.VMEM((2, width, TILE), jnp.bfloat16),
        pltpu.VMEM((2, width, TILE), jnp.bfloat16),
        pltpu.VMEM((2, TILE, width), jnp.bfloat16),
        pltpu.SemaphoreType.DMA((2, 2)),
        pltpu.SemaphoreType.DMA((2, 3)),
    )

    lt_relay_in(1).wait_recv()
    tick(0)

    def second_phase(wa, wb, sems):
        def loads(n, slot):
            at = pl.ds(pl.multiple_of(n * TILE, TILE), TILE)
            return (
                pltpu.make_async_copy(wg_hbm.at[at], wa.at[slot], sems.at[slot, 0]),
                pltpu.make_async_copy(wu_hbm.at[at], wb.at[slot], sems.at[slot, 1]),
            )

        def compute(slot):
            total = None
            for j in range(hidden_tiles):
                at = pl.ds(j * TILE, TILE)
                part = dot_rows(acts[3 * j + 1, 0], wa[slot, :, at])
                part += dot_rows(acts[3 * j + 2, 0], wb[slot, :, at])
                total = part if total is None else total + part
            return total

        reduce_start(0, loads, compute, ((5, lambda: relay(0)),))

    pl.run_scoped(
        second_phase,
        pltpu.VMEM((2, TILE, wg_hbm.shape[1]), jnp.bfloat16),
        pltpu.VMEM((2, TILE, wg_hbm.shape[1]), jnp.bfloat16),
        pltpu.SemaphoreType.DMA((2, 2)),
    )

    lt_relay_in(0).wait_recv()
    tick(1)

    def third_phase(wa, sems):
        def loads(n, slot):
            at = pl.ds(pl.multiple_of(n * TILE, TILE), TILE)
            return (pltpu.make_async_copy(wd_hbm.at[:, at], wa.at[slot], sems.at[slot]),)

        def compute(slot):
            total = None
            for j in range(hidden_tiles):
                part = dot_plain(acts[3 * j, 0], wa[slot, pl.ds(j * TILE, TILE)])
                total = part if total is None else total + part
            return total

        reduce_start(1, loads, compute)

    pl.run_scoped(
        third_phase,
        pltpu.VMEM((2, wd_hbm.shape[0], TILE), jnp.bfloat16),
        pltpu.SemaphoreType.DMA((2,)),
    )

    tick(2)

    base = ff_items
    for n in range(2):
        pltpu.make_async_copy(
            y_hbm.at[:, pl.ds(n * TILE, TILE)], acts.at[base + n, 0], misc.at[n]
        ).start()

    def xt_own(t):
        shard = other_z(z, t) * 2 + y
        return pltpu.make_async_copy(xt_hbm.at[shard], lt.at[2, 0, t], misc.at[2 + t])

    def xt_odd(k):
        shard = other_z(z, 2 * c + k) * 2 + 1 - y
        return pltpu.make_async_copy(xt_hbm.at[shard], odd.at[2, k], misc.at[6 + k])

    for t in range(4):
        xt_own(t).start()
    for k in range(2):
        xt_odd(k).start()
    for t in range(4):
        xt_own(t).wait()
    for k in range(2):
        xt_odd(k).wait()
    for n in range(2):
        pltpu.make_async_copy(
            y_hbm.at[:, pl.ds(n * TILE, TILE)], acts.at[base + n, 0], misc.at[n]
        ).wait()

    tick(3)
    reduce_end(0)

    def fourth_phase(hbuf, cbuf, dbuf, wob, obuf, sbuf, sems, d_sems, w_sems):
        def row_loads(r, slot):
            at = pl.ds(r * 128, 128)
            return (
                pltpu.make_async_copy(h_hbm.at[at], hbuf.at[slot], sems.at[slot, 0]),
                pltpu.make_async_copy(cot_hbm.at[at], cbuf.at[slot], sems.at[slot, 1]),
            )

        def spill(r, slot):
            return pltpu.make_async_copy(dbuf.at[slot], dh_hbm.at[pl.ds(r * 128, 128)], d_sems.at[slot])

        def tile_loads(n):
            at = pl.ds(n * TILE, TILE)
            return (
                pltpu.make_async_copy(wo_hbm.at[at], wob.at[n], w_sems.at[n, 0]),
                pltpu.make_async_copy(o_hbm.at[:, at], obuf.at[n], w_sems.at[n, 1]),
                pltpu.make_async_copy(sig_hbm.at[:, at], sbuf.at[n], w_sems.at[n, 2]),
            )

        for copy in row_loads(0, 0):
            copy.start()
        for n in range(2):
            for copy in tile_loads(n):
                copy.start()
        vec[0] = jnp.zeros_like(vec[0])

        @pl.loop(0, n_chunks)
        def _(r):
            slot = lax.rem(r, 2)

            @pl.when(r < n_chunks - 1)
            def _():
                for copy in row_loads(r + 1, 1 - slot):
                    copy.start()

            for copy in row_loads(r, slot):
                copy.wait()

            @pl.when(r >= 2)
            def _():
                spill(r - 2, slot).wait()

            at = pl.ds(pl.multiple_of(r * 128, 128), 128)
            value = hbuf[slot]
            scale = rms(value)
            normed = value * scale
            grad = fin_rows(0, pl.multiple_of(r * 128, 128), 128)
            vec[0, 1:2] += jnp.sum(grad * normed, axis=0, keepdims=True)
            scaled = grad * n2_ref[...]
            inner = jnp.mean(scaled * normed, axis=-1, keepdims=True)
            dh = wide(cbuf[slot]) * factor_ref[at] + scale * (scaled - normed * inner)
            dbuf[slot] = dh
            wide_a[at] = low(dh)
            spill(r, slot).start()

        spill(n_chunks - 2, n_chunks % 2).wait()
        spill(n_chunks - 1, (n_chunks - 1) % 2).wait()

        tick(4)
        ones = jnp.ones((8, 128), jnp.bfloat16)
        for n in range(2):
            for copy in tile_loads(n):
                copy.wait()
            dy = dot_rows(wide_a[...], wob[n])
            sig, o = sbuf[n], obuf[n]
            do = low(dy * sig)
            acts[base + 2 + n, 0] = low(dy * o * sig * (1.0 - sig))
            wide_b[:, n * TILE : (n + 1) * TILE] = do
            both = wide(do) * o
            for g in range(2):
                part = both[:, g * 128 : (g + 1) * 128]
                top = low(part)
                rest = low(part - wide(top))
                delta[n, g] = dot_rows(ones, top) + dot_rows(ones, rest)

        spread(3, wide_a)
        for device in (core_dev, x_dev):
            pl.semaphore_signal(credit, inc=1, device_id=device, device_id_type=MESH)

    pl.run_scoped(
        fourth_phase,
        pltpu.VMEM((2, 128, width), jnp.float32),
        pltpu.VMEM((2, 128, width), jnp.bfloat16),
        pltpu.VMEM((2, 128, width), jnp.float32),
        pltpu.VMEM((2, TILE, width), jnp.bfloat16),
        pltpu.VMEM((2, tokens, TILE), jnp.float32),
        pltpu.VMEM((2, tokens, TILE), jnp.float32),
        pltpu.SemaphoreType.DMA((2, 2)),
        pltpu.SemaphoreType.DMA((2,)),
        pltpu.SemaphoreType.DMA((2, 3)),
    )

    tick(5)

    def attention_back(keep, ysend, lsend, hsend, dq_ref, dkv_ref):
        def ky_copy(s):
            return remote(ysend.at[lax.rem(s, 2)], yrecv.at[s], ky_s.at[s], ky_r.at[s], y_dev)

        def kl_copy(s):
            return remote(lsend.at[s], lrecv.at[s], kl_s.at[s], kl_r.at[s], lo_dev)

        def kh_copy(s):
            return remote(hsend.at[s], hrecv.at[s], kh_s.at[s], kh_r.at[s], hi_dev)

        keys_total = kpos_ref.shape[0]

        def fifth_phase(qbuf, kvbuf, q_sem, sems):
            def kv_load(s, slot):
                return pltpu.make_async_copy(kv_hbm.at[s], kvbuf.at[slot], sems.at[slot])

            q_load = pltpu.make_async_copy(q_hbm, qbuf, q_sem)
            q_load.start()
            kv_load(0, 0).start()
            q_load.wait()

            @pl.loop(0, seqs)
            def _(s):
                slot = lax.rem(s, 2)

                @pl.when(s < seqs - 1)
                def _():
                    kv_load(s + 1, 1 - slot).start()

                kv_load(s, slot).wait()
                at = pl.ds(pl.multiple_of(s * rows, 128), rows)
                @pl.when(s >= 2)
                def _():
                    ky_copy(s - 2).wait_send()

                allowed = kpos_ref[...] <= qpos_ref[...]
                for n in range(2):
                    lanes = [slice((2 * n + g) * 128, (2 * n + g + 1) * 128) for g in range(2)]
                    key = kvbuf[slot, :, n * 128 : (n + 1) * 128]
                    value = kvbuf[slot, :, 256 + n * 128 : 256 + (n + 1) * 128]
                    q = jnp.concatenate([qbuf[at, lane] for lane in lanes], axis=0)
                    do = jnp.concatenate([wide_b[at, lane] for lane in lanes], axis=0)
                    drow = jnp.concatenate([delta[n, g, 0:1, at] for g in range(2)], axis=1)
                    scores = dot_rows(key, q)
                    probs = jnp.exp(jnp.where(allowed, scores - lse_ref[s, n], -1e30))
                    grad_probs = dot_rows(value, do)
                    ds = low(probs * (grad_probs - drow))
                    for start, grad in ((0, dot_plain(ds, q)), (256, dot_plain(low(probs), do))):
                        into = slice(start + n * 128, start + (n + 1) * 128)
                        for m in range(4):
                            keep[s, m, :, into] = grad[2 * m * rows : (2 * m + 1) * rows]
                            ysend[slot, m, :, into] = low(grad[(2 * m + 1) * rows : (2 * m + 2) * rows])
                    dq = dot_first(key, ds).T
                    for g in range(2):
                        dq_ref[at, lanes[g]] = dq[g * rows : (g + 1) * rows]

                ky_copy(s).start()
                tick(6 + s, True)

        pl.run_scoped(
            fifth_phase,
            pltpu.VMEM(q_hbm.shape, jnp.bfloat16),
            pltpu.VMEM((2, keys_total, 512), jnp.bfloat16),
            pltpu.SemaphoreType.DMA,
            pltpu.SemaphoreType.DMA((2,)),
        )

        lt_copy(2).start()
        relay(3)
        tick(6 + seqs)
        tick(7 + seqs)

        @pl.loop(0, seqs)
        def _(s):
            ky_copy(s).wait_recv()
            for m in range(4):
                keep[s, m] += wide(yrecv[s, m])
            for k in range(2):
                lsend[s, k] = low(keep[s, 2 * k + 1])
            kl_copy(s).start()

        tick(8 + seqs)

        def query_phase(rbuf, sem):
            load = pltpu.make_async_copy(qraw_hbm, rbuf, sem)
            load.start()
            load.wait()
            factor = 128.0**-0.5
            for hd in range(4):
                lane = slice(hd * 128, (hd + 1) * 128)
                raw = rbuf[:, lane]
                scale = rms(raw)
                normed = raw * scale
                grad = dq_ref[:, lane]
                gvec[0, 0:1, 0:128] = (
                    jnp.sum(grad * normed * factor, axis=0, keepdims=True)
                    + (gvec[0, 0:1, 0:128] if hd else 0.0)
                )
                scaled = grad * (qg_ref[...] * factor)
                out = scale * (scaled - normed * jnp.mean(scaled * normed, axis=-1, keepdims=True))
                acts[base + 4 + hd // 2, 0, :, (hd % 2) * 128 : (hd % 2 + 1) * 128] = low(out)

        gvec[0] = jnp.zeros_like(gvec[0])
        pl.run_scoped(query_phase, pltpu.VMEM(qraw_hbm.shape, jnp.float32), pltpu.SemaphoreType.DMA)

        @pl.loop(0, seqs)
        def _(s):
            kl_copy(s).wait_recv()
            for k in range(2):
                keep[s, 2 * k] += wide(lrecv[s, k])
            hsend[s] = low(keep[s, 2])
            kh_copy(s).start()

        tick(9 + seqs)
        relay(2)
        reduce_end(1)

        def out_phase(hbuf, obuf, sems, o_sems):
            def load(r, slot):
                return pltpu.make_async_copy(h_hbm.at[pl.ds(r * 128, 128)], hbuf.at[slot], sems.at[slot])

            def store(r, slot):
                return pltpu.make_async_copy(obuf.at[slot], block_out.at[pl.ds(r * 128, 128)], o_sems.at[slot])

            load(0, 0).start()

            @pl.loop(0, n_chunks)
            def _(r):
                slot = lax.rem(r, 2)

                @pl.when(r < n_chunks - 1)
                def _():
                    load(r + 1, 1 - slot).start()

                load(r, slot).wait()

                @pl.when(r >= 2)
                def _():
                    store(r - 2, slot).wait()

                obuf[slot] = low(hbuf[slot] + fin_rows(1, pl.multiple_of(r * 128, 128), 128))
                store(r, slot).start()

            store(n_chunks - 2, n_chunks % 2).wait()
            store(n_chunks - 1, (n_chunks - 1) % 2).wait()

        pl.run_scoped(
            out_phase,
            pltpu.VMEM((2, 128, width), jnp.float32),
            pltpu.VMEM((2, 128, width), jnp.bfloat16),
            pltpu.SemaphoreType.DMA((2,)),
            pltpu.SemaphoreType.DMA((2,)),
        )

        tick(10 + seqs)

        @pl.loop(0, seqs)
        def _(s):
            kh_copy(s).wait_recv()
            dkv_ref[pl.ds(pl.multiple_of(s * rows, 128), rows)] = keep[s, 0] + wide(hrecv[s])

        def key_phase(rbuf, sem):
            load = pltpu.make_async_copy(kraw_hbm, rbuf, sem)
            load.start()
            load.wait()
            for hd in range(2):
                lane = slice(hd * 128, (hd + 1) * 128)
                raw = rbuf[:, lane]
                scale = rms(raw)
                normed = raw * scale
                grad = dkv_ref[:, lane]
                gvec[0, 0:1, 128:256] = (
                    jnp.sum(grad * normed, axis=0, keepdims=True)
                    + (gvec[0, 0:1, 128:256] if hd else 0.0)
                )
                scaled = grad * kg_ref[...]
                out = scale * (scaled - normed * jnp.mean(scaled * normed, axis=-1, keepdims=True))
                acts[base + 6, 0, :, lane] = low(out)
            acts[base + 7, 0] = low(dkv_ref[:, 256:512])

        pl.run_scoped(key_phase, pltpu.VMEM(kraw_hbm.shape, jnp.float32), pltpu.SemaphoreType.DMA)

        @pl.loop(seqs - 2, seqs)
        def _(s):
            ky_copy(s).wait_send()

        @pl.loop(0, seqs)
        def _(s):
            kl_copy(s).wait_send()
            kh_copy(s).wait_send()

    pl.run_scoped(
        attention_back,
        pltpu.VMEM((seqs, 4, rows, 512), jnp.float32),
        pltpu.VMEM((2, 4, rows, 512), jnp.bfloat16),
        pltpu.VMEM((seqs, 2, rows, 512), jnp.bfloat16),
        pltpu.VMEM((seqs, rows, 512), jnp.bfloat16),
        pltpu.VMEM((tokens, 512), jnp.float32),
        pltpu.VMEM((tokens, 512), jnp.float32),
    )

    def sixth_phase(wb, sems):
        pieces = ((wga_hbm, base + 2, 2), (wq_hbm, base + 4, 2), (wk_hbm, base + 6, 1), (wv_hbm, base + 7, 1))

        def loads(n, slot):
            at = pl.ds(pl.multiple_of(n * TILE, TILE), TILE)
            out, start = [], 0
            for p, (ref, _, count) in enumerate(pieces):
                out.append(
                    pltpu.make_async_copy(
                        ref.at[at], wb.at[slot, :, pl.ds(start, count * TILE)], sems.at[slot, p]
                    )
                )
                start += count * TILE
            return out

        def compute(slot):
            total, start = None, 0
            for _, first, count in pieces:
                for n in range(count):
                    part = dot_rows(acts[first + n, 0], wb[slot, :, pl.ds(start, TILE)])
                    total = part if total is None else total + part
                    start += TILE
            return total

        pl.semaphore_wait(credit, 2)
        reduce_start(2, loads, compute, ((3, lambda: tick(11 + seqs)),))

    pl.run_scoped(
        sixth_phase,
        pltpu.VMEM((2, TILE, 6 * TILE), jnp.bfloat16),
        pltpu.SemaphoreType.DMA((2, 4)),
    )

    for step in range(5):
        device = (y_dev, lo_dev, hi_dev, core_dev, x_dev)[step]
        copy = remote(gvec.at[step], gvec_got.at[step], gv_s.at[step], gv_r.at[step], device)
        copy.start()
        copy.wait()
        gvec[step + 1] = gvec[step] + gvec_got[step]
    gains_out[...] = gvec[5]

    lt_relay_in(2).wait_recv()
    lt_relay_in(3).wait_recv()
    tick(12 + seqs)
    tick(13 + seqs)
    reduce_end(2)

    def last_phase(xbuf, dbuf, obuf, sems, o_sems):
        def loads(r, slot):
            at = pl.ds(r * 128, 128)
            return (
                pltpu.make_async_copy(x_hbm.at[at], xbuf.at[slot], sems.at[slot, 0]),
                pltpu.make_async_copy(dh_hbm.at[at], dbuf.at[slot], sems.at[slot, 1]),
            )

        def store(r, slot):
            return pltpu.make_async_copy(obuf.at[slot], x_out.at[pl.ds(r * 128, 128)], o_sems.at[slot])

        for copy in loads(0, 0):
            copy.start()

        @pl.loop(0, n_chunks)
        def _(r):
            slot = lax.rem(r, 2)

            @pl.when(r < n_chunks - 1)
            def _():
                for copy in loads(r + 1, 1 - slot):
                    copy.start()

            for copy in loads(r, slot):
                copy.wait()

            @pl.when(r >= 2)
            def _():
                store(r - 2, slot).wait()

            value = wide(xbuf[slot])
            scale = rms(value)
            normed = value * scale
            grad = fin_rows(2, pl.multiple_of(r * 128, 128), 128)
            vec[0, 0:1] += jnp.sum(grad * normed, axis=0, keepdims=True)
            scaled = grad * n1_ref[...]
            inner = jnp.mean(scaled * normed, axis=-1, keepdims=True)
            obuf[slot] = low(dbuf[slot] + scale * (scaled - normed * inner))
            store(r, slot).start()

        store(n_chunks - 2, n_chunks % 2).wait()
        store(n_chunks - 1, (n_chunks - 1) % 2).wait()

    pl.run_scoped(
        last_phase,
        pltpu.VMEM((2, 128, width), jnp.bfloat16),
        pltpu.VMEM((2, 128, width), jnp.float32),
        pltpu.VMEM((2, 128, width), jnp.bfloat16),
        pltpu.SemaphoreType.DMA((2, 2)),
        pltpu.SemaphoreType.DMA((2,)),
    )

    for step in range(3):
        device = (y_dev, lo_dev, hi_dev)[step]
        copy = remote(vec.at[step], vec_got.at[step], nv_s.at[step], nv_r.at[step], device)
        copy.start()
        copy.wait()
        vec[step + 1] = vec[step] + vec_got[step]
    norms_out[...] = vec[3]

    for k in range(14 + seqs, item_count + 2 * lag):
        tick(k)

    @pl.loop(0, item_count)
    def _(i):
        act_copy(i).wait_send()

    @pl.loop(item_count - 4, item_count)
    def _(i):
        zlo_copy(i).wait_send()
        zhi_copy(i).wait_send()

    @pl.loop(item_count - 2, item_count)
    def _(i):
        out_wait(i)

    for l in range(4):
        lt_copy(l).wait_send()
        lt_relay(l).wait_send()


def back_call(hbm, vmem, sizes):
    tokens, width, seqs, rows, keys_total, hidden = sizes
    count = 3 * (hidden // TILE) + 8
    bf, f32 = jnp.bfloat16, jnp.float32
    dma = pltpu.SemaphoreType.DMA
    scratch = [
        pltpu.VMEM((count, 2, tokens, TILE), bf),
        pltpu.VMEM((4, 2, 4, TILE, tokens), bf),
        pltpu.VMEM((4, 2, TILE, tokens), bf),
        pltpu.VMEM((4, tokens, TILE), bf),
        pltpu.VMEM((2, 4, tokens, TILE), bf),
        pltpu.VMEM((2, 4, tokens, TILE), bf),
        pltpu.VMEM((2, 8, tokens, TILE), bf),
        pltpu.VMEM((seqs, 4, rows, 512), bf),
        pltpu.VMEM((seqs, 2, rows, 512), bf),
        pltpu.VMEM((seqs, rows, 512), bf),
        pltpu.VMEM((4, 2, TILE, TILE), bf),
        pltpu.VMEM((4, TILE, TILE), bf),
        pltpu.VMEM((3, TILE, TILE), bf),
        pltpu.VMEM((2, TILE, TILE), f32),
        pltpu.VMEM((tokens, width), bf),
        pltpu.VMEM((tokens, width), bf),
        pltpu.VMEM((2, 2, 8, tokens), f32),
        pltpu.VMEM((4, 8, width), f32),
        pltpu.VMEM((3, 8, width), f32),
        pltpu.VMEM((6, 8, 256), f32),
        pltpu.VMEM((5, 8, 256), f32),
        *(dma((count,)) for _ in range(6)),
        *(dma((4,)) for _ in range(4)),
        *(dma((3, 4)) for _ in range(6)),
        *(dma((seqs,)) for _ in range(6)),
        dma((3,)), dma((3,)), dma((5,)), dma((5,)),
        dma((3,)), dma((2,)), dma((8,)), pltpu.SemaphoreType.REGULAR,
    ]
    any_spec = pl.BlockSpec(memory_space=pl.ANY)
    vmem_spec = pl.BlockSpec(memory_space=pltpu.VMEM)
    return pl.pallas_call(
        back_kernel,
        out_shape=[
            jax.ShapeDtypeStruct((tokens, width), bf),
            jax.ShapeDtypeStruct((tokens, width), bf),
            jax.ShapeDtypeStruct((hidden, TILE), f32),
            jax.ShapeDtypeStruct((TILE, hidden), f32),
            jax.ShapeDtypeStruct((TILE, hidden), f32),
            jax.ShapeDtypeStruct((512, TILE), f32),
            jax.ShapeDtypeStruct((TILE, 512), f32),
            jax.ShapeDtypeStruct((TILE, 512), f32),
            jax.ShapeDtypeStruct((TILE, TILE), f32),
            jax.ShapeDtypeStruct((TILE, TILE), f32),
            jax.ShapeDtypeStruct((8, width), f32),
            jax.ShapeDtypeStruct((8, 256), f32),
            jax.ShapeDtypeStruct((tokens, width), f32),
            jax.ShapeDtypeStruct((count, 2, TILE, TILE), bf),
            jax.ShapeDtypeStruct((count, TILE, TILE), bf),
        ],
        in_specs=[any_spec] * len(hbm) + [vmem_spec] * len(vmem),
        out_specs=[any_spec] * 10 + [vmem_spec] * 2 + [any_spec] * 3,
        scratch_shapes=scratch,
        compiler_params=pltpu.CompilerParams(
            collective_id=1, has_side_effects=True, vmem_limit_bytes=61 << 20
        ),
    )(*hbm, *vmem)


def forward_kernel(
    x_hbm, wq_hbm, wk_hbm, wv_hbm, wga_hbm, wo_hbm,
    n1_ref, qg_ref, kg_ref, kpos_ref, qpos_ref,
    h_out, xt_out, q_out, kv_out, o_out, sig_out, y_out, qraw_out, kraw_out, lse_ref,
    xv, xn, wqv, wkv, wvv, wgav, wov, kv, qv, qraw, kraw, sig, ov, yv, xtv, hv,
    csend, crecv, fin, xrecv,
    x_sem, w_sem, out_sem, h_sem, kz_s, kz_r, ky_s, ky_r, c1_s, c1_r, x_s, x_r, c2_s, c2_r,
):
    seq, head = lax.axis_index("seq"), lax.axis_index("head")
    z, y = lax.div(seq, 2), lax.rem(seq, 2)
    c = lax.rem(head, 2)
    y_dev = {"seq": z * 2 + 1 - y}
    z_dev = [None] + [{"seq": other_z(z, t) * 2 + y} for t in (1, 2, 3)]
    core_dev = {"head": head + 1 - 2 * c}
    x_dev = {"head": head + 2 - 4 * lax.div(head, 2)}
    seqs, slots, rows = kv.shape[0], kv.shape[1], kv.shape[2]
    tokens, width = x_hbm.shape
    half = width // 2
    epsilon_k = 1e-06

    def rms(value):
        return lax.rsqrt(jnp.mean(value * value, axis=-1, keepdims=True) + epsilon_k)

    def rows_at(s):
        return pl.ds(pl.multiple_of(s * rows, 128), rows)

    def x_load(s):
        return pltpu.make_async_copy(x_hbm.at[rows_at(s)], xv.at[rows_at(s)], x_sem.at[s])

    weight_loads = [
        pltpu.make_async_copy(src, dst, w_sem.at[i])
        for i, (src, dst) in enumerate(
            ((wk_hbm, wkv), (wv_hbm, wvv), (wq_hbm, wqv), (wga_hbm, wgav), (wo_hbm, wov))
        )
    ]
    for s in range(seqs):
        x_load(s).start()
    for load in weight_loads:
        load.start()

    barrier = pltpu.get_barrier_semaphore()
    for device in (y_dev, *z_dev[1:], core_dev, x_dev):
        pl.semaphore_signal(barrier, inc=1, device_id=device, device_id_type=MESH)
    pl.semaphore_wait(barrier, 6)

    def remote(src, dst, send, recv, device):
        return pltpu.make_async_remote_copy(
            src_ref=src, dst_ref=dst, send_sem=send, recv_sem=recv, device_id=device, device_id_type=MESH
        )

    def z_copy(s, t):
        return remote(kv.at[s, 0], kv.at[s, 2 * t], kz_s.at[s, t], kz_r.at[s, t], z_dev[t])

    def y_copy(s, t):
        return remote(kv.at[s, 2 * t], kv.at[s, 2 * t + 1], ky_s.at[s, t], ky_r.at[s, t], y_dev)

    def core_copy(s):
        return remote(csend.at[s], crecv.at[s], c1_s.at[s], c1_r.at[s], core_dev)

    def x_copy(s):
        return remote(fin.at[s, c], xrecv.at[s], x_s.at[s], x_r.at[s], x_dev)

    def fin_copy(s):
        return remote(fin.at[s, c], fin.at[s, c], c2_s.at[s], c2_r.at[s], core_dev)

    def fin_copy_in(s):
        piece = fin.at[s, 1 - c]
        return remote(piece, piece, c2_s.at[s], c2_r.at[s], core_dev)

    @pl.loop(0, seqs)
    def _(s):
        x_load(s).wait()
        at = rows_at(s)
        value = wide(xv[at])
        xn[at] = low(value * rms(value) * n1_ref[...])

    weight_loads[0].wait()
    weight_loads[1].wait()

    @pl.loop(0, seqs)
    def _(s):
        at = rows_at(s)
        raw = dot_plain(xn[at], wkv[...])
        kraw[at] = raw
        for n in range(2):
            lane = slice(n * 128, (n + 1) * 128)
            part = raw[:, lane]
            kv[s, 0, :, lane] = low(part * rms(part) * kg_ref[...])
        kv[s, 0, :, 256:512] = low(dot_plain(xn[at], wvv[...]))
        y_copy(s, 0).start()
        for t in (1, 2, 3):
            z_copy(s, t).start()

    outs = []

    def leave(src, dst):
        copy = pltpu.make_async_copy(src, dst, out_sem.at[len(outs)])
        copy.start()
        outs.append(copy)

    leave(kraw, kraw_out)

    def forward_keys(s):
        for t in (1, 2, 3):
            z_copy(s, t).wait_recv()
            y_copy(s, t).start()

    weight_loads[2].wait()
    weight_loads[3].wait()
    scale_q = 128.0**-0.5

    @pl.loop(0, seqs)
    def _(s):
        at = rows_at(s)
        raw = dot_plain(xn[at], wqv[...])
        qraw[at] = raw
        for n in range(4):
            lane = slice(n * 128, (n + 1) * 128)
            part = raw[:, lane]
            qv[at, lane] = low(part * rms(part) * (qg_ref[...] * scale_q))
        sig[at] = jax.nn.sigmoid(dot_plain(xn[at], wgav[...]))

    leave(qraw, qraw_out)
    leave(qv, q_out)
    leave(sig, sig_out)
    forward_keys(0)

    @pl.loop(0, width // TILE)
    def _(n):
        at = pl.ds(pl.multiple_of(n * TILE, TILE), TILE)
        xtv[n] = xn[:, at].T

    leave(xtv, xt_out)
    weight_loads[4].wait()

    def finish(s):
        x_copy(s).wait()
        fin[s, c] = low(wide(fin[s, c]) + wide(xrecv[s]))
        fin_copy(s).start()

    def h_store(s, slot):
        return pltpu.make_async_copy(hv.at[slot], h_out.at[rows_at(s)], h_sem.at[slot])

    def finish_rows(s):
        slot = lax.rem(s, 2)
        fin_copy_in(s).wait_recv()

        @pl.when(s >= 2)
        def _():
            h_store(s - 2, slot).wait()

        hv[slot, :, 0:half] = wide(xv[rows_at(s), 0:half]) + wide(fin[s, 0])
        hv[slot, :, half:width] = wide(xv[rows_at(s), half:width]) + wide(fin[s, 1])
        h_store(s, slot).start()

    @pl.loop(0, seqs)
    def _(s):
        @pl.when(s < seqs - 1)
        def _():
            forward_keys(s + 1)

        for t in range(4):
            y_copy(s, t).wait_recv()
        at = rows_at(s)
        allowed = kpos_ref[...] <= qpos_ref[...]
        for n in range(2):
            lanes = [slice((2 * n + g) * 128, (2 * n + g + 1) * 128) for g in range(2)]
            key = kv[s, :, :, n * 128 : (n + 1) * 128].reshape(slots * rows, 128)
            value = kv[s, :, :, 256 + n * 128 : 256 + (n + 1) * 128].reshape(slots * rows, 128)
            q = jnp.concatenate([qv[at, lane] for lane in lanes], axis=0)
            scores = jnp.where(allowed, dot_rows(key, q), -1e30)
            top = jnp.max(scores, axis=0, keepdims=True)
            probs = jnp.exp(scores - top)
            total = jnp.sum(probs, axis=0, keepdims=True)
            out = (dot_first(value, low(probs)) / total).T
            lse_ref[s, n] = top + jnp.log(total)
            for g in range(2):
                ov[at, lanes[g]] = out[g * rows : (g + 1) * rows]
        gated = low(ov[at] * sig[at])
        yv[at] = gated
        away = pl.ds(pl.multiple_of((1 - c) * half, 128), half)
        mine = pl.ds(pl.multiple_of(c * half, 128), half)
        csend[s] = low(dot_plain(gated, wov[:, away]))
        core_copy(s).start()
        part = dot_plain(gated, wov[:, mine])
        core_copy(s).wait_recv()
        fin[s, c] = low(part + wide(crecv[s]))
        x_copy(s).start()

        @pl.when(s >= 1)
        def _():
            finish(s - 1)

        @pl.when(s >= 2)
        def _():
            finish_rows(s - 2)

    leave(kv, kv_out)
    leave(ov, o_out)
    leave(yv, y_out)
    finish_rows(seqs - 2)
    finish(seqs - 1)
    finish_rows(seqs - 1)
    h_store(seqs - 2, seqs % 2).wait()
    h_store(seqs - 1, (seqs - 1) % 2).wait()
    for copy in outs:
        copy.wait()

    @pl.loop(0, seqs)
    def _(s):
        for t in (1, 2, 3):
            z_copy(s, t).wait_send()
        for t in range(4):
            y_copy(s, t).wait_send()
        core_copy(s).wait_send()
        fin_copy(s).wait_send()


def forward_call(hbm, vmem, sizes):
    tokens, width, seqs, rows, slots = sizes
    bf, f32 = jnp.bfloat16, jnp.float32
    dma = pltpu.SemaphoreType.DMA
    half = width // 2
    kv_shape = (seqs, slots, rows, 512)
    scratch = [
        pltpu.VMEM((tokens, width), bf),
        pltpu.VMEM((tokens, width), bf),
        pltpu.VMEM((width, 512), bf),
        pltpu.VMEM((width, 256), bf),
        pltpu.VMEM((width, 256), bf),
        pltpu.VMEM((width, 512), bf),
        pltpu.VMEM((512, width), bf),
        pltpu.VMEM(kv_shape, bf),
        pltpu.VMEM((tokens, 512), bf),
        pltpu.VMEM((tokens, 512), f32),
        pltpu.VMEM((tokens, 256), f32),
        pltpu.VMEM((tokens, 512), f32),
        pltpu.VMEM((tokens, 512), f32),
        pltpu.VMEM((tokens, 512), bf),
        pltpu.VMEM((width // TILE, TILE, tokens), bf),
        pltpu.VMEM((2, rows, width), f32),
        pltpu.VMEM((seqs, rows, half), bf),
        pltpu.VMEM((seqs, rows, half), bf),
        pltpu.VMEM((seqs, 2, rows, half), bf),
        pltpu.VMEM((seqs, rows, half), bf),
        dma((seqs,)), dma((5,)), dma((8,)), dma((2,)),
        *(dma((seqs, 4)) for _ in range(4)),
        *(dma((seqs,)) for _ in range(6)),
    ]
    any_spec = pl.BlockSpec(memory_space=pl.ANY)
    vmem_spec = pl.BlockSpec(memory_space=pltpu.VMEM)
    return pl.pallas_call(
        forward_kernel,
        out_shape=[
            jax.ShapeDtypeStruct((tokens, width), f32),
            jax.ShapeDtypeStruct((width // TILE, TILE, tokens), bf),
            jax.ShapeDtypeStruct((tokens, 512), bf),
            jax.ShapeDtypeStruct(kv_shape, bf),
            jax.ShapeDtypeStruct((tokens, 512), f32),
            jax.ShapeDtypeStruct((tokens, 512), f32),
            jax.ShapeDtypeStruct((tokens, 512), bf),
            jax.ShapeDtypeStruct((tokens, 512), f32),
            jax.ShapeDtypeStruct((tokens, 256), f32),
            jax.ShapeDtypeStruct((seqs, 2, 1, 2 * rows), f32),
        ],
        in_specs=[any_spec] * len(hbm) + [vmem_spec] * len(vmem),
        out_specs=[any_spec] * 9 + [vmem_spec],
        scratch_shapes=scratch,
        compiler_params=pltpu.CompilerParams(
            collective_id=2, has_side_effects=True, vmem_limit_bytes=60 << 20
        ),
    )(*hbm, *vmem)


def on_device(
    x_in,
    cot,
    domain_ids,
    domain_counts,
    domain_weights,
    block_order,
    norm1,
    w_query,
    w_key,
    w_value,
    w_gate_attn,
    w_out,
    query_gain,
    key_gain,
    norm2,
    w_gate,
    w_up,
    w_down,
):
    sequences, local_rows, width = x_in.shape
    row_total = sequences * local_rows
    head_dim = query_gain.shape[0]
    kv_local = w_key.shape[1] // head_dim
    q_local = w_query.shape[1] // head_dim
    group = q_local // kv_local
    devices = lax.axis_size("seq")
    own = lax.axis_index("seq")
    block_rows = local_rows * devices // block_order.shape[0]
    q_gain, k_gain = wide(query_gain), wide(key_gain)
    gain_one, gain_two = wide(norm1), wide(norm2)

    x_rows = x_in.reshape(row_total, width)
    query_pos = positions(block_order, own, local_rows, block_rows)
    key_pos = jnp.concatenate(
        [positions(block_order, own ^ j, local_rows, block_rows) for j in range(devices)]
    )
    key_column = key_pos[:, None]
    query_row = jnp.concatenate([query_pos] * group)[None, :]

    domain_total = domain_weights.shape[0]
    domain_index = jnp.arange(domain_total, dtype=jnp.int32)
    factor = domain_weights * (row_total * devices) / (domain_total * wide(domain_counts))
    picked = domain_ids.reshape(row_total)[:, None] == domain_index[None, :]
    row_scale = jnp.sum(jnp.where(picked, factor[None, :], 0.0), axis=1)

    h, xt, query, kv, attn, sig, gated, query_raw, key_raw, lse = forward_call(
        (x_rows, w_query, w_key, w_value, w_gate_attn, w_out),
        (gain_one[None, :], q_gain[None, :], k_gain[None, :], key_column, query_row),
        (row_total, width, sequences, local_rows, devices),
    )
    out, x_grad, down, gate, up, wout, wga, wquery, wkey, wvalue, norms, gains, *_ = back_call(
        (
            h,
            cot.reshape(row_total, width),
            x_rows,
            xt,
            query,
            kv.reshape(sequences, devices * local_rows, -1),
            attn,
            sig,
            gated,
            query_raw,
            key_raw,
            w_gate,
            w_up,
            w_down,
            w_out,
            w_query,
            w_key,
            w_value,
            w_gate_attn,
        ),
        (
            row_scale[:, None],
            lse,
            key_column,
            query_row,
            gain_one[None, :],
            gain_two[None, :],
            q_gain[None, :],
            k_gain[None, :],
        ),
        (row_total, width, sequences, local_rows, local_rows * devices, w_down.shape[0]),
    )

    def own_part(value):
        size = value.shape[0] // devices
        return lax.dynamic_slice_in_dim(value, own * size, size, 0)

    return (
        out.reshape(x_in.shape),
        x_grad.reshape(x_in.shape),
        own_part(norms[0]),
        wquery,
        wkey,
        wvalue,
        wga,
        wout,
        own_part(gains[0, :head_dim]),
        own_part(gains[0, head_dim:]),
        own_part(norms[1]),
        gate,
        up,
        down,
    )


def on_device_plain(
    x_in,
    cot,
    domain_ids,
    domain_counts,
    domain_weights,
    block_order,
    norm1,
    w_query,
    w_key,
    w_value,
    w_gate_attn,
    w_out,
    query_gain,
    key_gain,
    norm2,
    w_gate,
    w_up,
    w_down,
):
    sequences, local_rows, model_width = x_in.shape
    row_total = sequences * local_rows
    head_dim = query_gain.shape[0]
    kv_local = w_key.shape[1] // head_dim
    q_local = w_query.shape[1] // head_dim
    group_size = q_local // kv_local
    block_rows = local_rows // 2
    seq_devices = lax.axis_size("seq")
    first_row = lax.axis_index("seq") * local_rows
    query_pos = positions(block_order, first_row, local_rows, block_rows)
    query_factor = head_dim ** (-0.5)
    q_gain = query_gain.astype(jnp.float32)
    k_gain = key_gain.astype(jnp.float32)
    gain_one = norm1.astype(jnp.float32)
    gain_two = norm2.astype(jnp.float32)
    x_float = x_in.reshape(row_total, model_width).astype(jnp.float32)
    scale_one = norm_scale(x_float)
    normed_one = x_float * scale_one
    x_normed = (normed_one * gain_one).astype(jnp.bfloat16)
    query_raw = product(x_normed, w_query).reshape(row_total, q_local, head_dim)
    key_raw = product(x_normed, w_key).reshape(row_total, kv_local, head_dim)
    value_rows = product(x_normed, w_value).astype(jnp.bfloat16)
    gate_pre = product(x_normed, w_gate_attn)
    query_scale = norm_scale(query_raw)
    query_normed = query_raw * query_scale
    key_scale = norm_scale(key_raw)
    key_normed = key_raw * key_scale
    query = (query_normed * q_gain * query_factor).astype(jnp.bfloat16)
    key_rows = (key_normed * k_gain).astype(jnp.bfloat16)
    project_query_heads = query.reshape(
        sequences, local_rows, kv_local, group_size, head_dim
    ).transpose(0, 2, 3, 1, 4)
    (
        query_scale,
        query_normed,
        key_scale,
        key_normed,
        query_heads,
        key_rows,
        value_rows,
        gate_pre,
    ) = (
        query_scale,
        query_normed,
        key_scale,
        key_normed,
        project_query_heads,
        key_rows,
        value_rows,
        gate_pre,
    )
    key_seq = key_rows.reshape(sequences, local_rows, kv_local * head_dim)
    value_seq = value_rows.reshape(sequences, local_rows, kv_local * head_dim)
    stat_shape = (sequences, kv_local, group_size, local_rows)
    running_max = jnp.full(stat_shape, -1e30, jnp.float32)
    key_piece = lax.all_gather(key_seq, "seq", axis=1, tiled=True)
    value_piece = lax.all_gather(value_seq, "seq", axis=1, tiled=True)
    row_count = key_piece.shape[1]
    key_block = key_piece.reshape(sequences, row_count, kv_local, head_dim)
    value_block = value_piece.reshape(sequences, row_count, kv_local, head_dim)
    key_pos = positions(block_order, jnp.int32(0), row_count, block_rows)
    allowed = key_pos[None, :] <= query_pos[:, None]
    scores = jnp.einsum(
        "skgqd,spkd->skgqp", query_heads, key_block, preferred_element_type=jnp.float32
    )
    scores = jnp.where(allowed, scores, -1e30)
    new_max = jnp.maximum(running_max, jnp.max(scores, axis=-1))
    weights = jnp.where(allowed, jnp.exp(scores - new_max[..., None]), 0.0)
    running_sum = jnp.sum(weights, axis=-1)
    weighted = jnp.einsum(
        "skgqp,spkd->skgqd",
        weights.astype(jnp.bfloat16),
        value_block,
        preferred_element_type=jnp.float32,
    )
    running_max, running_sum, weighted = (new_max, running_sum, weighted)
    log_total = running_max + jnp.log(running_sum)
    attn_heads = weighted / running_sum[..., None]
    attn_flat = attn_heads.transpose(0, 3, 1, 2, 4).reshape(row_total, q_local * head_dim)
    gate_sig = jax.nn.sigmoid(gate_pre)
    gated = (attn_flat * gate_sig).astype(jnp.bfloat16)
    attn_sum = lax.psum(product(gated, w_out).astype(jnp.bfloat16), "head").astype(jnp.float32)
    residual = x_float + attn_sum
    scale_two = norm_scale(residual)
    normed_two = residual * scale_two
    h_normed = (normed_two * gain_two).astype(jnp.bfloat16)
    gate_proj = product(h_normed, w_gate)
    up_proj = product(h_normed, w_up)
    gate_logit = jax.nn.sigmoid(gate_proj)
    gate_act = gate_proj * gate_logit
    mixed = (gate_act * up_proj).astype(jnp.bfloat16)
    mlp_sum = lax.psum(product(mixed, w_down).astype(jnp.bfloat16), "head").astype(jnp.float32)
    block_out = (
        (residual + mlp_sum).astype(jnp.bfloat16).reshape(sequences, local_rows, model_width)
    )
    domain_total = domain_weights.shape[0]
    domain_index = jnp.arange(domain_total, dtype=jnp.int32)
    factor = (
        domain_weights
        * (row_total * seq_devices)
        / (domain_total * domain_counts.astype(jnp.float32))
    )
    picked = domain_ids.reshape(row_total)[:, None] == domain_index[None, :]
    row_scale = jnp.sum(jnp.where(picked, factor[None, :], 0.0), axis=1)
    grad_out = cot.reshape(row_total, model_width).astype(jnp.float32) * row_scale[:, None]
    grad_low = grad_out.astype(jnp.bfloat16)
    grad_down = outer_sum(mixed, grad_low)
    grad_mixed = back_product(grad_low, w_down)
    grad_gate = (grad_mixed * up_proj * gate_logit * (1.0 + gate_proj * (1.0 - gate_logit))).astype(
        jnp.bfloat16
    )
    grad_up = (grad_mixed * gate_act).astype(jnp.bfloat16)
    grad_mlp_gate = outer_sum(h_normed, grad_gate)
    grad_mlp_up = outer_sum(h_normed, grad_up)
    grad_hnorm = lax.psum(
        (back_product(grad_gate, w_gate) + back_product(grad_up, w_up)).astype(jnp.bfloat16), "head"
    ).astype(jnp.float32)
    grad_norm_two = jnp.sum(grad_hnorm * normed_two, axis=0)
    grad_resid = grad_out + norm_back(grad_hnorm, normed_two, scale_two, gain_two)
    grad_attn = grad_resid.astype(jnp.bfloat16)
    grad_wout = outer_sum(gated, grad_attn)
    grad_gated = back_product(grad_attn, w_out)
    grad_heads_flat = (grad_gated * gate_sig).astype(jnp.bfloat16)
    grad_gatepre = (grad_gated * attn_flat * gate_sig * (1.0 - gate_sig)).astype(jnp.bfloat16)
    grad_wgate_attn = outer_sum(x_normed, grad_gatepre)
    grad_heads = grad_heads_flat.reshape(
        sequences, local_rows, kv_local, group_size, head_dim
    ).transpose(0, 2, 3, 1, 4)
    row_delta = jnp.sum(grad_heads.astype(jnp.float32) * attn_heads, axis=-1)
    key_piece = lax.all_gather(key_seq, "seq", axis=1, tiled=True)
    value_piece = lax.all_gather(value_seq, "seq", axis=1, tiled=True)
    row_count = key_piece.shape[1]
    key_block = key_piece.reshape(sequences, row_count, kv_local, head_dim)
    value_block = value_piece.reshape(sequences, row_count, kv_local, head_dim)
    key_pos = positions(block_order, jnp.int32(0), row_count, block_rows)
    allowed = key_pos[None, :] <= query_pos[:, None]
    scores = jnp.einsum(
        "skgqd,spkd->skgqp", query_heads, key_block, preferred_element_type=jnp.float32
    )
    probs = jnp.where(
        allowed, jnp.exp(jnp.where(allowed, scores, -1e30) - log_total[..., None]), 0.0
    )
    grad_probs = jnp.einsum(
        "skgqd,spkd->skgqp", grad_heads, value_block, preferred_element_type=jnp.float32
    )
    grad_scores = (probs * (grad_probs - row_delta[..., None])).astype(jnp.bfloat16)
    grad_query = jnp.einsum(
        "skgqp,spkd->skgqd", grad_scores, key_block, preferred_element_type=jnp.float32
    )
    key_term = jnp.einsum(
        "skgqp,skgqd->spkd", grad_scores, query_heads, preferred_element_type=jnp.float32
    ).reshape(sequences, row_count, kv_local * head_dim)
    value_term = jnp.einsum(
        "skgqp,skgqd->spkd",
        probs.astype(jnp.bfloat16),
        grad_heads,
        preferred_element_type=jnp.float32,
    ).reshape(sequences, row_count, kv_local * head_dim)
    grad_keys = key_term
    grad_values = value_term
    grad_query, grad_keys, grad_values = (grad_query, grad_keys, grad_values)
    grad_key_own, grad_value_own = (
        lax.psum_scatter(
            grad_keys.astype(jnp.bfloat16), "seq", scatter_dimension=1, tiled=True
        ).astype(jnp.float32),
        lax.psum_scatter(
            grad_values.astype(jnp.bfloat16), "seq", scatter_dimension=1, tiled=True
        ).astype(jnp.float32),
    )
    grad_query_rows = grad_query.transpose(0, 3, 1, 2, 4).reshape(row_total, q_local, head_dim)
    grad_qgain_part = jnp.sum(grad_query_rows * query_normed * query_factor, axis=(0, 1))
    grad_query_raw = (
        norm_back(grad_query_rows, query_normed, query_scale, q_gain * query_factor)
        .astype(jnp.bfloat16)
        .reshape(row_total, q_local * head_dim)
    )
    grad_key_rows = grad_key_own.reshape(row_total, kv_local, head_dim)
    grad_kgain_part = jnp.sum(grad_key_rows * key_normed, axis=(0, 1))
    grad_key_raw = (
        norm_back(grad_key_rows, key_normed, key_scale, k_gain)
        .astype(jnp.bfloat16)
        .reshape(row_total, kv_local * head_dim)
    )
    grad_value_low = grad_value_own.reshape(row_total, kv_local * head_dim).astype(jnp.bfloat16)
    grad_xnorm_part = (
        back_product(grad_query_raw, w_query)
        + back_product(grad_key_raw, w_key)
        + back_product(grad_value_low, w_value)
        + back_product(grad_gatepre, w_gate_attn)
    )
    grad_xnorm, grad_qgain, grad_kgain = (
        lax.psum(grad_xnorm_part.astype(jnp.bfloat16), "head").astype(jnp.float32),
        lax.psum(grad_qgain_part.astype(jnp.bfloat16), "head").astype(jnp.float32),
        lax.psum(grad_kgain_part.astype(jnp.bfloat16), "head").astype(jnp.float32),
    )
    grad_norm_one = jnp.sum(grad_xnorm * normed_one, axis=0)
    x_grad = (
        (grad_resid + norm_back(grad_xnorm, normed_one, scale_one, gain_one))
        .astype(jnp.bfloat16)
        .reshape(sequences, local_rows, model_width)
    )
    grad_wquery = outer_sum(x_normed, grad_query_raw)
    grad_wkey = outer_sum(x_normed, grad_key_raw)
    grad_wvalue = outer_sum(x_normed, grad_value_low)
    all_totals = (
        lax.psum_scatter(
            grad_norm_one.astype(jnp.bfloat16), "seq", scatter_dimension=0, tiled=True
        ).astype(jnp.float32),
        lax.psum_scatter(
            grad_wquery.astype(jnp.bfloat16), "seq", scatter_dimension=0, tiled=True
        ).astype(jnp.float32),
        lax.psum_scatter(
            grad_wkey.astype(jnp.bfloat16), "seq", scatter_dimension=0, tiled=True
        ).astype(jnp.float32),
        lax.psum_scatter(
            grad_wvalue.astype(jnp.bfloat16), "seq", scatter_dimension=0, tiled=True
        ).astype(jnp.float32),
        lax.psum_scatter(
            grad_wgate_attn.astype(jnp.bfloat16), "seq", scatter_dimension=0, tiled=True
        ).astype(jnp.float32),
        lax.psum_scatter(
            grad_wout.astype(jnp.bfloat16), "seq", scatter_dimension=1, tiled=True
        ).astype(jnp.float32),
        lax.psum_scatter(
            grad_qgain.astype(jnp.bfloat16), "seq", scatter_dimension=0, tiled=True
        ).astype(jnp.float32),
        lax.psum_scatter(
            grad_kgain.astype(jnp.bfloat16), "seq", scatter_dimension=0, tiled=True
        ).astype(jnp.float32),
        lax.psum_scatter(
            grad_mlp_gate.astype(jnp.bfloat16), "seq", scatter_dimension=0, tiled=True
        ).astype(jnp.float32),
        lax.psum_scatter(
            grad_mlp_up.astype(jnp.bfloat16), "seq", scatter_dimension=0, tiled=True
        ).astype(jnp.float32),
        lax.psum_scatter(
            grad_down.astype(jnp.bfloat16), "seq", scatter_dimension=1, tiled=True
        ).astype(jnp.float32),
        lax.psum_scatter(
            grad_norm_two.astype(jnp.bfloat16), "seq", scatter_dimension=0, tiled=True
        ).astype(jnp.float32),
    )
    return (
        block_out,
        x_grad,
        all_totals[0],
        all_totals[1],
        all_totals[2],
        all_totals[3],
        all_totals[4],
        all_totals[5],
        all_totals[6],
        all_totals[7],
        all_totals[11],
        all_totals[8],
        all_totals[9],
        all_totals[10],
    )


def solution(mesh):
    fits = mesh.shape["seq"] == 8 and mesh.shape["head"] == 4
    return jax.shard_map(
        on_device if fits else on_device_plain,
        mesh=mesh,
        in_specs=(
            P(None, "seq", None),
            P(None, "seq", None),
            P(None, "seq"),
            P(),
            P(),
            P(),
            P(),
            P(None, "head"),
            P(None, "head"),
            P(None, "head"),
            P(None, "head"),
            P("head", None),
            P(),
            P(),
            P(),
            P(None, "head"),
            P(None, "head"),
            P("head", None),
        ),
        out_specs=(
            P(None, "seq", None),
            P(None, "seq", None),
            P("seq"),
            P("seq", "head"),
            P("seq", "head"),
            P("seq", "head"),
            P("seq", "head"),
            P("head", "seq"),
            P("seq"),
            P("seq"),
            P("seq"),
            P("seq", "head"),
            P("seq", "head"),
            P("head", "seq"),
        ),
        check_vma=False,
    )
```

```python
import jax
import jax.numpy as jnp
from jax import lax
from jax.experimental import pallas as pl
from jax.experimental.pallas import tpu as pltpu
from jax.sharding import PartitionSpec as P

epsilon = 1e-06


def norm_scale(value):
    return lax.rsqrt(jnp.mean(value * value, axis=-1, keepdims=True) + epsilon)


def norm_back(grad_in, normed, scale, gain):
    scaled = grad_in * gain
    return scale * (scaled - normed * jnp.mean(scaled * normed, axis=-1, keepdims=True))


def product(left, right):
    return jnp.dot(left, right, preferred_element_type=jnp.float32)


def outer_sum(left, right):
    return lax.dot_general(
        left, right, (((0,), (0,)), ((), ())), preferred_element_type=jnp.float32
    )


def back_product(left, right):
    return lax.dot_general(
        left, right, (((1,), (1,)), ((), ())), preferred_element_type=jnp.float32
    )


def low(value):
    return value.astype(jnp.bfloat16)


def wide(value):
    return value.astype(jnp.float32)


def positions(block_order, device, row_count, block_rows):
    stored = device * row_count + jnp.arange(row_count, dtype=jnp.int32)
    slots = stored // block_rows
    slot_index = jnp.arange(block_order.shape[0], dtype=jnp.int32)
    picked = jnp.sum(
        jnp.where(slots[:, None] == slot_index[None, :], block_order[None, :], 0), axis=1
    )
    return picked * block_rows + stored % block_rows


MESH = pl.DeviceIdType.MESH
TILE = 256


PLAN = {
    "p1.0": (
        ("a", 0),
    ),
    "p1.1": (
        ("r1", 1),
    ),
    "p1.3": (
        ("a", 1), ("r2", 1),
    ),
    "p1.4": (
        ("a", 2), ("r1", 0), ("s1", 0),
    ),
    "p1.5": (
        ("a", 3),
    ),
    "p2.0": (
        ("r2", 0),
    ),
    "p2.2": (
        ("s1", 1), ("a", 4), ("s2", 0), ("s1", 2),
    ),
    "p2.3": (
        ("s1", 3), ("a", 5),
    ),
    "p2.5": (
        ("s3", 0),
    ),
    "p2.6": (
        ("a", 6), ("s2", 1), ("s1", 4),
    ),
    "p3.0": (
        ("s4", 0), ("a", 7),
    ),
    "p3.2": (
        ("s3", 1), ("s2", 2), ("s1", 5),
    ),
    "p3.3": (
        ("a", 8),
    ),
    "p3.4": (
        ("s4", 1),
    ),
    "p3.6": (
        ("s2", 3), ("s1", 6), ("a", 9), ("s3", 2),
    ),
    "e0.3": (
        ("s4", 2), ("s3", 3), ("s2", 4), ("s1", 7), ("a", 10),
    ),
    "p4b": (
        ("s2", 5), ("s1", 8), ("a", 11), ("s3", 4),
    ),
    "p5.0": (
        ("s2", 6), ("s1", 9), ("s3", 5),
    ),
    "p5.1": (
        ("s2", 7), ("s1", 10), ("s3", 6),
    ),
    "p5.2": (
        ("ky", 0), ("s2", 8), ("s3", 7),
    ),
    "p5.3": (
        ("ky", 1), ("s2", 9), ("s3", 8),
    ),
    "qp": (
        ("s2", 10), ("s1", 11),
    ),
    "e1.2": (
        ("s3", 9),
    ),
    "e1.3": (
        ("s4", 3), ("s4", 4), ("s4", 5), ("ky", 2), ("s4", 6), ("s4", 7), ("s4", 8),
    ),
    "e1.4": (
        ("kl", 0),
    ),
    "op": (
        ("s3", 10), ("s4", 9), ("km", 0), ("kl", 1), ("ky", 3), ("s4", 10), ("r1", 3), ("a", 12), ("km", 1),
        ("s2", 11), ("r1", 2), ("a", 13), ("r2", 3), ("s3", 11), ("kl", 2), ("s1", 12), ("a", 14), ("r2", 2),
        ("s4", 11), ("s1", 13), ("a", 15), ("km", 2), ("kl", 3), ("s1", 14), ("a", 16), ("km", 3), ("s2", 12),
        ("s1", 15), ("a", 17),
    ),
    "p7.0": (
        ("a", 18), ("s3", 12), ("s2", 13), ("s1", 16),
    ),
    "p7.2": (
        ("a", 19), ("s4", 12),
    ),
    "p7.4": (
        ("s3", 13), ("s2", 14), ("s1", 17), ("a", 20),
    ),
    "p7.6": (
        ("s4", 13),
    ),
    "e2.1": (
        ("s2", 15), ("s1", 18), ("a", 21), ("s3", 14),
    ),
    "e2.2": (
        ("s4", 14), ("s3", 15), ("s2", 16), ("s1", 19), ("a", 22),
    ),
    "e2.3": (
        ("s4", 15),
    ),
    "lp": (
        ("s2", 17), ("s1", 20), ("a", 23), ("s3", 16),
    ),
    "vec": (
        ("s2", 18), ("s1", 21), ("a", 24), ("s3", 17), ("s4", 16), ("s4", 17), ("s2", 19), ("s1", 22),
        ("a", 25), ("s3", 18), ("s4", 18), ("s3", 19), ("s2", 20), ("s1", 23), ("s4", 19), ("s3", 20),
        ("s2", 21), ("s1", 24), ("s4", 20), ("s2", 22), ("s1", 25), ("s3", 21), ("s4", 21), ("s3", 22),
        ("s2", 23), ("s4", 22), ("s3", 23), ("s2", 24), ("s4", 23), ("s2", 25), ("s3", 24), ("s4", 24),
        ("s3", 25), ("s4", 25),
    ),
}


def other_z(z, t):
    low_z, high_z = lax.rem(z, 2), lax.div(z, 2)
    low_t, high_t = lax.rem(t, 2), lax.div(t, 2)
    return (low_z + low_t - 2 * low_z * low_t) + 2 * (high_z + high_t - 2 * high_z * high_t)


def dot_plain(left, right):
    return jnp.dot(left, right, preferred_element_type=jnp.float32)


def dot_rows(left, right):
    return lax.dot_general(
        left, right, (((1,), (1,)), ((), ())), preferred_element_type=jnp.float32
    )


def dot_first(left, right):
    return lax.dot_general(
        left, right, (((0,), (0,)), ((), ())), preferred_element_type=jnp.float32
    )


def back_kernel(
    h_hbm, cot_hbm, x_hbm, xt_hbm, q_hbm, kv_hbm, o_hbm, sig_hbm, y_hbm, qraw_hbm, kraw_hbm,
    wg_hbm, wu_hbm, wd_hbm, wo_hbm, wq_hbm, wk_hbm, wv_hbm, wga_hbm,
    factor_ref, lse_ref, kpos_ref, qpos_ref, n1_ref, n2_ref, qg_ref, kg_ref,
    block_out, x_out, dwd_out, dwg_out, dwu_out, dwo_out, dwga_out, dwq_out, dwk_out, dwv_out,
    norms_out, gains_out, dh_hbm, z1_hbm, z2_hbm, z3_hbm,
    acts, lt, odd, csend, crecv, xrecv, fin, yrecv, lrecv, mrecv, hrecv,
    zsend, stage, ostage, wide_a, wide_b, delta,
    vec, vec_got, gvec, gvec_got,
    ya_s, ya_r, z1_s, z1_r, z2_s, z2_r, z3_s, z3_r, lt_s, lt_r, lc_s, lc_r, lx_s, lx_r, lf_s, lf_r,
    c1_s, c1_r, x_s, x_r, c2_s, c2_r, ky_s, ky_r, kl_s, kl_r, km_s, km_r, kh_s, kh_r,
    nv_s, nv_r, gv_s, gv_r, st_sem, out_sem, misc, credit,
):
    seq, head = lax.axis_index("seq"), lax.axis_index("head")
    z, y = lax.div(seq, 2), lax.rem(seq, 2)
    c = lax.rem(head, 2)
    y_dev = {"seq": z * 2 + 1 - y}
    lo_dev = {"seq": other_z(z, 1) * 2 + y}
    hi_dev = {"seq": other_z(z, 2) * 2 + y}
    mid_dev = {"seq": (3 - z) * 2 + y}
    core_dev = {"head": head + 1 - 2 * c}
    x_dev = {"head": head + 2 - 4 * lax.div(head, 2)}
    at_end, inside = lax.rem(z, 3) == 0, lax.rem(z, 3) != 0
    tokens = cot_hbm.shape[0]
    rows = kpos_ref.shape[0] // 8
    seqs = tokens // rows
    hidden_tiles = wd_hbm.shape[0] // TILE
    ff_items = 3 * hidden_tiles
    width = cot_hbm.shape[1]
    epsilon_k = 1e-06

    barrier = pltpu.get_barrier_semaphore()
    for device in (y_dev, lo_dev, hi_dev, core_dev, x_dev):
        pl.semaphore_signal(barrier, inc=1, device_id=device, device_id_type=MESH)

    @pl.when(inside)
    def _():
        pl.semaphore_signal(barrier, inc=1, device_id=mid_dev, device_id_type=MESH)
        pl.semaphore_wait(barrier, 6)

    @pl.when(at_end)
    def _():
        pl.semaphore_wait(barrier, 5)


    def remote(src, dst, send, recv, device):
        return pltpu.make_async_remote_copy(
            src_ref=src, dst_ref=dst, send_sem=send, recv_sem=recv, device_id=device, device_id_type=MESH
        )

    def act_copy(i):
        return remote(acts.at[i, 0], acts.at[i, 1], ya_s.at[i], ya_r.at[i], y_dev)

    def lt_copy(l):
        return remote(odd.at[l], lt.at[l, 1, head], lt_s.at[l], lt_r.at[l], y_dev)

    x_head = head + 2 - 4 * lax.div(head, 2)
    core_head = head + 1 - 2 * c
    far_head = x_head + 1 - 2 * c

    def lt_core(l, part):
        piece = lt.at[l, 1, part]
        return remote(piece, piece, lc_s.at[l], lc_r.at[l], core_dev)

    def lt_x(l, part):
        piece = lt.at[l, 1, part]
        return remote(piece, piece, lx_s.at[l], lx_r.at[l], x_dev)

    def lt_far(l, part):
        piece = lt.at[l, 1, part]
        return remote(piece, piece, lf_s.at[l], lf_r.at[l], core_dev)

    def z1_copy(i):
        return remote(zsend.at[i % 4], z1_hbm.at[i], z1_s.at[i], z1_r.at[i], lo_dev)

    def z2_copy(i):
        return remote(zsend.at[i % 4, pl.ds(0, 2)], z2_hbm.at[i], z2_s.at[i], z2_r.at[i], mid_dev)

    def z3_copy(i):
        return remote(zsend.at[i % 4, 2], z3_hbm.at[i], z3_s.at[i], z3_r.at[i], lo_dev)

    def item_dot(i, l, first, last):
        count = (last - first) * TILE
        mine = dot_plain(lt[l, 0, first:last].reshape(count, tokens), acts[i, 0])
        return mine + dot_plain(lt[l, 1, first:last].reshape(count, tokens), acts[i, 1])

    def stage_load(src, slot):
        copy = pltpu.make_async_copy(src, stage.at[slot], st_sem.at[slot])
        copy.start()
        return copy

    def stage_one(i, l, place):
        act_copy(i).wait_recv()

        @pl.when(at_end)
        def _():
            if i >= 4:
                z1_copy(i - 4).wait_send()
            total = item_dot(i, l, 1, 4)
            for k in range(3):
                zsend[i % 4, k] = low(total[k * TILE : (k + 1) * TILE])
            z1_copy(i).start()

    def stage_two(i, l, place):
        @pl.when(inside)
        def _():
            z1_copy(i).wait_recv()
            loads = [stage_load(z1_hbm.at[i, k], k) for k in (1, 2)]
            if i >= 4:
                z2_copy(i - 4).wait_send()
            total = item_dot(i, l, 2, 4)
            for load in loads:
                load.wait()
            zsend[i % 4, 0] = low(total[:TILE] + wide(stage[2]))
            zsend[i % 4, 1] = low(total[TILE:] + wide(stage[1]))
            z2_copy(i).start()

    def out_wait(i):
        pltpu.make_async_copy(ostage.at[i % 2], dwk_out, out_sem.at[i % 2]).wait()

    def put(i, total, place):
        ref, n, turned = place
        if i >= 2:
            out_wait(i - 2)
        ostage[i % 2] = total.T if turned else total
        at = pl.ds(n * TILE, TILE)
        target = ref.at[at] if turned else ref.at[:, at]
        pltpu.make_async_copy(ostage.at[i % 2], target, out_sem.at[i % 2]).start()

    def stage_three(i, l, place):
        @pl.when(inside)
        def _():
            z2_copy(i).wait_recv()
            loads = [stage_load(z1_hbm.at[i, 0], 0), stage_load(z2_hbm.at[i, 0], 1), stage_load(z2_hbm.at[i, 1], 2)]
            if i >= 4:
                z3_copy(i - 4).wait_send()
            total = item_dot(i, l, 0, 2)
            for load in loads:
                load.wait()
            zsend[i % 4, 2] = low(total[TILE:] + wide(stage[1]))
            z3_copy(i).start()
            put(i, total[:TILE] + wide(stage[0]) + wide(stage[2]), place)

    def stage_four(i, l, place):
        @pl.when(at_end)
        def _():
            z3_copy(i).wait_recv()
            load = stage_load(z3_hbm.at[i], 3)
            total = item_dot(i, l, 0, 1)
            load.wait()
            put(i, total + wide(stage[3]), place)

    late = (
        (3, dwo_out, 0, True),
        (3, dwo_out, 1, True),
        (2, dwga_out, 0, False),
        (2, dwga_out, 1, False),
        (2, dwq_out, 0, False),
        (2, dwq_out, 1, False),
        (2, dwk_out, 0, False),
        (2, dwv_out, 0, False),
    )
    item_count = ff_items + 8
    shown = set()

    def item_step(stage_of, i):
        l = (1 if i % 3 == 0 else 0) if i < ff_items else late[i - ff_items][0]
        if stage_of is stage_one and l not in shown:
            shown.add(l)
            relay_in(l)
        if i < ff_items:
            place = ((dwd_out, dwg_out, dwu_out)[i % 3], i // 3, i % 3 == 0)
        else:
            place = late[i - ff_items][1:]
        stage_of(i, l, place)

    actions = {
        "a": lambda i: act_copy(i).start(),
        "s1": lambda i: item_step(stage_one, i),
        "s2": lambda i: item_step(stage_two, i),
        "s3": lambda i: item_step(stage_three, i),
        "s4": lambda i: item_step(stage_four, i),
        "r1": lambda l: relay_one(l),
        "r2": lambda l: relay_two(l),
    }

    def after(place):
        for name, i in PLAN.get(place, ()):
            actions[name](i)

    def after_step(place, step, count):
        for k in range(count):
            if f"{place}.{k}" in PLAN:
                pl.when(step == k)(lambda k=k: after(f"{place}.{k}"))

    def spread(l, source):
        @pl.loop(0, 4)
        def _(t):
            at = pl.multiple_of((other_z(z, t) * 2 + y) * TILE, TILE)
            lt[l, 0, t] = source[:, pl.ds(at, TILE)].T

        at = pl.multiple_of((other_z(z, head) * 2 + 1 - y) * TILE, TILE)
        odd[l] = source[:, pl.ds(at, TILE)].T

    def relay_one(l):
        lt_copy(l).wait_recv()
        lt_core(l, head).start()
        lt_x(l, head).start()

    def relay_two(l):
        lt_x(l, x_head).wait_recv()
        lt_far(l, x_head).start()

    def relay_in(l):
        lt_core(l, core_head).wait_recv()
        lt_far(l, far_head).wait_recv()

    def core_copy(k, b):
        return remote(csend.at[b], crecv.at[k % 2, b], c1_s.at[k, b], c1_r.at[k, b], core_dev)

    def x_copy(k, b):
        return remote(fin.at[k % 2, c * 4 + b], xrecv.at[k % 2, b], x_s.at[k, b], x_r.at[k, b], x_dev)

    def fin_copy(k, b):
        piece = fin.at[k % 2, c * 4 + b]
        return remote(piece, piece, c2_s.at[k, b], c2_r.at[k, b], core_dev)

    def fin_copy_in(k, b):
        piece = fin.at[k % 2, (1 - c) * 4 + b]
        return remote(piece, piece, c2_s.at[k, b], c2_r.at[k, b], core_dev)

    def reduce_start(k, loads, compute, place):
        def block_of(step):
            return lax.rem(c + 1 + step, 2) * 4 + lax.div(step, 2)

        for copy in loads(block_of(0), 0):
            copy.start()

        @pl.loop(0, 8)
        def _(step):
            slot, b = lax.rem(step, 2), lax.div(step, 2)

            @pl.when(step < 7)
            def _():
                for copy in loads(block_of(step + 1), 1 - slot):
                    copy.start()

            for copy in loads(block_of(step), slot):
                copy.wait()
            part = compute(slot)

            @pl.when(slot == 0)
            def _():
                csend[b] = low(part)
                core_copy(k, b).start()

            @pl.when(slot == 1)
            def _():
                core_copy(k, b).wait_recv()
                fin[k % 2, c * 4 + b] = low(part + wide(crecv[k % 2, b]))
                x_copy(k, b).start()

            after_step(place, step, 8)

        @pl.loop(0, 4)
        def _(b):
            core_copy(k, b).wait_send()

    def reduce_end(k):
        for b in range(4):
            x_copy(k, b).wait()
            fin[k % 2, c * 4 + b] = low(wide(fin[k % 2, c * 4 + b]) + wide(xrecv[k % 2, b]))
            fin_copy(k, b).start()
            after(f"e{k}.{b}")
        for b in range(4):
            fin_copy_in(k, b).wait_recv()
            fin_copy(k, b).wait_send()
        after(f"e{k}.4")

    def fin_rows(k, at, count):
        return jnp.concatenate([wide(fin[k % 2, n, pl.ds(at, count)]) for n in range(8)], axis=1)

    def rms(value):
        return lax.rsqrt(jnp.mean(value * value, axis=-1, keepdims=True) + epsilon_k)

    n_chunks = tokens // 128

    def first_phase(hbuf, cbuf, wgb, wub, wdb, sems, w_sems):
        def row_loads(r, slot):
            at = pl.ds(r * 128, 128)
            return (
                pltpu.make_async_copy(h_hbm.at[at], hbuf.at[slot], sems.at[slot, 0]),
                pltpu.make_async_copy(cot_hbm.at[at], cbuf.at[slot], sems.at[slot, 1]),
            )

        def tile_loads(j, slot):
            at = pl.ds(pl.multiple_of(j * TILE, TILE), TILE)
            return (
                pltpu.make_async_copy(wg_hbm.at[:, at], wgb.at[slot], w_sems.at[slot, 0]),
                pltpu.make_async_copy(wu_hbm.at[:, at], wub.at[slot], w_sems.at[slot, 1]),
                pltpu.make_async_copy(wd_hbm.at[at], wdb.at[slot], w_sems.at[slot, 2]),
            )

        for copy in row_loads(0, 0):
            copy.start()
        for copy in tile_loads(0, 0):
            copy.start()

        @pl.loop(0, n_chunks)
        def _(r):
            slot = lax.rem(r, 2)

            @pl.when(r < n_chunks - 1)
            def _():
                for copy in row_loads(r + 1, 1 - slot):
                    copy.start()

            for copy in row_loads(r, slot):
                copy.wait()
            value = hbuf[slot]
            at = pl.ds(pl.multiple_of(r * 128, 128), 128)
            wide_a[at] = low(value * rms(value) * n2_ref[...])
            wide_b[at] = low(wide(cbuf[slot]) * factor_ref[at])

        spread(1, wide_b)
        lt_copy(1).start()
        after("p0")

        @pl.loop(0, hidden_tiles)
        def _(j):
            slot = lax.rem(j, 2)

            @pl.when(j < hidden_tiles - 1)
            def _():
                for copy in tile_loads(j + 1, 1 - slot):
                    copy.start()

            for copy in tile_loads(j, slot):
                copy.wait()

            @pl.loop(0, 2)
            def _(half):
                at = pl.ds(pl.multiple_of(half * (tokens // 2), 128), tokens // 2)
                a = dot_plain(wide_a[at], wgb[slot])
                u = dot_plain(wide_a[at], wub[slot])
                dm = dot_rows(wide_b[at], wdb[slot])
                sig = jax.nn.sigmoid(a)
                act = a * sig
                acts[3 * j, 0, at] = low(act * u)
                acts[3 * j + 1, 0, at] = low(dm * u * sig * (1.0 + a * (1.0 - sig)))
                acts[3 * j + 2, 0, at] = low(dm * act)

            after_step("p1", j, 1)

            @pl.when(j == 0)
            def _():
                spread(0, wide_a)
                lt_copy(0).start()
                after("sp0")

            for k in range(1, hidden_tiles):
                if f"p1.{k}" in PLAN:
                    pl.when(j == k)(lambda k=k: after(f"p1.{k}"))

    pl.run_scoped(
        first_phase,
        pltpu.VMEM((2, 128, width), jnp.float32),
        pltpu.VMEM((2, 128, width), jnp.bfloat16),
        pltpu.VMEM((2, width, TILE), jnp.bfloat16),
        pltpu.VMEM((2, width, TILE), jnp.bfloat16),
        pltpu.VMEM((2, TILE, width), jnp.bfloat16),
        pltpu.SemaphoreType.DMA((2, 2)),
        pltpu.SemaphoreType.DMA((2, 3)),
    )

    def second_phase(wa, wb, sems):
        def loads(n, slot):
            at = pl.ds(pl.multiple_of(n * TILE, TILE), TILE)
            return (
                pltpu.make_async_copy(wg_hbm.at[at], wa.at[slot], sems.at[slot, 0]),
                pltpu.make_async_copy(wu_hbm.at[at], wb.at[slot], sems.at[slot, 1]),
            )

        def compute(slot):
            total = None
            for j in range(hidden_tiles):
                at = pl.ds(j * TILE, TILE)
                part = dot_rows(acts[3 * j + 1, 0], wa[slot, :, at])
                part += dot_rows(acts[3 * j + 2, 0], wb[slot, :, at])
                total = part if total is None else total + part
            return total

        reduce_start(0, loads, compute, "p2")

    pl.run_scoped(
        second_phase,
        pltpu.VMEM((2, TILE, wg_hbm.shape[1]), jnp.bfloat16),
        pltpu.VMEM((2, TILE, wg_hbm.shape[1]), jnp.bfloat16),
        pltpu.SemaphoreType.DMA((2, 2)),
    )

    def third_phase(wa, sems):
        def loads(n, slot):
            at = pl.ds(pl.multiple_of(n * TILE, TILE), TILE)
            return (pltpu.make_async_copy(wd_hbm.at[:, at], wa.at[slot], sems.at[slot]),)

        def compute(slot):
            total = None
            for j in range(hidden_tiles):
                part = dot_plain(acts[3 * j, 0], wa[slot, pl.ds(j * TILE, TILE)])
                total = part if total is None else total + part
            return total

        reduce_start(1, loads, compute, "p3")

    pl.run_scoped(
        third_phase,
        pltpu.VMEM((2, wd_hbm.shape[0], TILE), jnp.bfloat16),
        pltpu.SemaphoreType.DMA((2,)),
    )

    base = ff_items
    for n in range(2):
        pltpu.make_async_copy(
            y_hbm.at[:, pl.ds(n * TILE, TILE)], acts.at[base + n, 0], misc.at[n]
        ).start()

    def xt_own(t):
        shard = other_z(z, t) * 2 + y
        return pltpu.make_async_copy(xt_hbm.at[shard], lt.at[2, 0, t], misc.at[2 + t])

    def xt_odd():
        shard = other_z(z, head) * 2 + 1 - y
        return pltpu.make_async_copy(xt_hbm.at[shard], odd.at[2], misc.at[6])

    for t in range(4):
        xt_own(t).start()
    xt_odd().start()
    for t in range(4):
        xt_own(t).wait()
    xt_odd().wait()
    for n in range(2):
        pltpu.make_async_copy(
            y_hbm.at[:, pl.ds(n * TILE, TILE)], acts.at[base + n, 0], misc.at[n]
        ).wait()
    after("xt")
    reduce_end(0)

    def fourth_phase(hbuf, cbuf, dbuf, wob, obuf, sbuf, sems, d_sems, w_sems):
        def row_loads(r, slot):
            at = pl.ds(r * 128, 128)
            return (
                pltpu.make_async_copy(h_hbm.at[at], hbuf.at[slot], sems.at[slot, 0]),
                pltpu.make_async_copy(cot_hbm.at[at], cbuf.at[slot], sems.at[slot, 1]),
            )

        def spill(r, slot):
            return pltpu.make_async_copy(dbuf.at[slot], dh_hbm.at[pl.ds(r * 128, 128)], d_sems.at[slot])

        def tile_loads(n):
            at = pl.ds(n * TILE, TILE)
            return (
                pltpu.make_async_copy(wo_hbm.at[at], wob.at[n], w_sems.at[n, 0]),
                pltpu.make_async_copy(o_hbm.at[:, at], obuf.at[n], w_sems.at[n, 1]),
                pltpu.make_async_copy(sig_hbm.at[:, at], sbuf.at[n], w_sems.at[n, 2]),
            )

        for copy in row_loads(0, 0):
            copy.start()
        for n in range(2):
            for copy in tile_loads(n):
                copy.start()
        vec[0] = jnp.zeros_like(vec[0])

        @pl.loop(0, n_chunks)
        def _(r):
            slot = lax.rem(r, 2)

            @pl.when(r < n_chunks - 1)
            def _():
                for copy in row_loads(r + 1, 1 - slot):
                    copy.start()

            for copy in row_loads(r, slot):
                copy.wait()

            @pl.when(r >= 2)
            def _():
                spill(r - 2, slot).wait()

            at = pl.ds(pl.multiple_of(r * 128, 128), 128)
            value = hbuf[slot]
            scale = rms(value)
            normed = value * scale
            grad = fin_rows(0, pl.multiple_of(r * 128, 128), 128)
            vec[0, 1:2] += jnp.sum(grad * normed, axis=0, keepdims=True)
            scaled = grad * n2_ref[...]
            inner = jnp.mean(scaled * normed, axis=-1, keepdims=True)
            dh = wide(cbuf[slot]) * factor_ref[at] + scale * (scaled - normed * inner)
            dbuf[slot] = dh
            wide_a[at] = low(dh)
            spill(r, slot).start()

        spill(n_chunks - 2, n_chunks % 2).wait()
        spill(n_chunks - 1, (n_chunks - 1) % 2).wait()

        after("p4a")
        ones = jnp.ones((8, 128), jnp.bfloat16)
        for n in range(2):
            for copy in tile_loads(n):
                copy.wait()
            dy = dot_rows(wide_a[...], wob[n])
            sig, o = sbuf[n], obuf[n]
            do = low(dy * sig)
            acts[base + 2 + n, 0] = low(dy * o * sig * (1.0 - sig))
            wide_b[:, n * TILE : (n + 1) * TILE] = do
            both = wide(do) * o
            for g in range(2):
                part = both[:, g * 128 : (g + 1) * 128]
                top = low(part)
                rest = low(part - wide(top))
                delta[n, g] = dot_rows(ones, top) + dot_rows(ones, rest)

        spread(3, wide_a)
        after("p4b")
        for device in (core_dev, x_dev):
            pl.semaphore_signal(credit, inc=1, device_id=device, device_id_type=MESH)

    pl.run_scoped(
        fourth_phase,
        pltpu.VMEM((2, 128, width), jnp.float32),
        pltpu.VMEM((2, 128, width), jnp.bfloat16),
        pltpu.VMEM((2, 128, width), jnp.float32),
        pltpu.VMEM((2, TILE, width), jnp.bfloat16),
        pltpu.VMEM((2, tokens, TILE), jnp.float32),
        pltpu.VMEM((2, tokens, TILE), jnp.float32),
        pltpu.SemaphoreType.DMA((2, 2)),
        pltpu.SemaphoreType.DMA((2,)),
        pltpu.SemaphoreType.DMA((2, 3)),
    )

    def attention_back(keep, ysend, lsend, dq_ref, dkv_ref):
        def ky_copy(s):
            return remote(ysend.at[lax.rem(s, 2)], yrecv.at[s], ky_s.at[s], ky_r.at[s], y_dev)

        def kl_copy(s):
            return remote(lsend.at[s], lrecv.at[s], kl_s.at[s], kl_r.at[s], lo_dev)

        def km_copy(s):
            return remote(lsend.at[s, pl.ds(0, 2)], mrecv.at[s], km_s.at[s], km_r.at[s], mid_dev)

        def kh_copy(s):
            return remote(lsend.at[s, 2], hrecv.at[s], kh_s.at[s], kh_r.at[s], lo_dev)

        def ky_step(s):
            ky_copy(s).wait_recv()
            for m in range(4):
                keep[s, m] += wide(yrecv[s, m])

            @pl.when(at_end)
            def _():
                for k in range(3):
                    lsend[s, k] = low(keep[s, k + 1])
                kl_copy(s).start()

        def kl_step(s):
            @pl.when(inside)
            def _():
                kl_copy(s).wait_recv()
                keep[s, 0] += wide(lrecv[s, 0])
                lsend[s, 0] = low(keep[s, 2] + wide(lrecv[s, 2]))
                lsend[s, 1] = low(keep[s, 3] + wide(lrecv[s, 1]))
                km_copy(s).start()

        def km_step(s):
            @pl.when(inside)
            def _():
                km_copy(s).wait_recv()
                keep[s, 0] += wide(mrecv[s, 1])
                lsend[s, 2] = low(keep[s, 1] + wide(mrecv[s, 0]))
                kh_copy(s).start()

        actions["ky"] = ky_step
        actions["kl"] = kl_step
        actions["km"] = km_step
        keys_total = kpos_ref.shape[0]

        def fifth_phase(qbuf, kvbuf, q_sem, sems):
            def kv_load(s, slot):
                return pltpu.make_async_copy(kv_hbm.at[s], kvbuf.at[slot], sems.at[slot])

            q_load = pltpu.make_async_copy(q_hbm, qbuf, q_sem)
            q_load.start()
            kv_load(0, 0).start()
            q_load.wait()

            @pl.loop(0, seqs)
            def _(s):
                slot = lax.rem(s, 2)

                @pl.when(s < seqs - 1)
                def _():
                    kv_load(s + 1, 1 - slot).start()

                kv_load(s, slot).wait()
                at = pl.ds(pl.multiple_of(s * rows, 128), rows)
                @pl.when(s >= 2)
                def _():
                    ky_copy(s - 2).wait_send()

                allowed = kpos_ref[...] <= qpos_ref[...]
                for n in range(2):
                    lanes = [slice((2 * n + g) * 128, (2 * n + g + 1) * 128) for g in range(2)]
                    key = kvbuf[slot, :, n * 128 : (n + 1) * 128]
                    value = kvbuf[slot, :, 256 + n * 128 : 256 + (n + 1) * 128]
                    q = jnp.concatenate([qbuf[at, lane] for lane in lanes], axis=0)
                    do = jnp.concatenate([wide_b[at, lane] for lane in lanes], axis=0)
                    drow = jnp.concatenate([delta[n, g, 0:1, at] for g in range(2)], axis=1)
                    scores = dot_rows(key, q)
                    probs = jnp.exp(jnp.where(allowed, scores - lse_ref[s, n], -1e30))
                    grad_probs = dot_rows(value, do)
                    ds = low(probs * (grad_probs - drow))
                    for start, grad in ((0, dot_plain(ds, q)), (256, dot_plain(low(probs), do))):
                        into = slice(start + n * 128, start + (n + 1) * 128)
                        for m in range(4):
                            keep[s, m, :, into] = grad[2 * m * rows : (2 * m + 1) * rows]
                            ysend[slot, m, :, into] = low(grad[(2 * m + 1) * rows : (2 * m + 2) * rows])
                    dq = dot_first(key, ds).T
                    for g in range(2):
                        dq_ref[at, lanes[g]] = dq[g * rows : (g + 1) * rows]

                ky_copy(s).start()
                after_step("p5", s, seqs)

        pl.run_scoped(
            fifth_phase,
            pltpu.VMEM(q_hbm.shape, jnp.bfloat16),
            pltpu.VMEM((2, keys_total, 512), jnp.bfloat16),
            pltpu.SemaphoreType.DMA,
            pltpu.SemaphoreType.DMA((2,)),
        )

        lt_copy(3).start()
        lt_copy(2).start()
        after("sl3")

        def query_phase(rbuf, sem):
            load = pltpu.make_async_copy(qraw_hbm, rbuf, sem)
            load.start()
            load.wait()
            factor = 128.0**-0.5
            for hd in range(4):
                lane = slice(hd * 128, (hd + 1) * 128)
                raw = rbuf[:, lane]
                scale = rms(raw)
                normed = raw * scale
                grad = dq_ref[:, lane]
                gvec[0, 0:1, 0:128] = (
                    jnp.sum(grad * normed * factor, axis=0, keepdims=True)
                    + (gvec[0, 0:1, 0:128] if hd else 0.0)
                )
                scaled = grad * (qg_ref[...] * factor)
                out = scale * (scaled - normed * jnp.mean(scaled * normed, axis=-1, keepdims=True))
                acts[base + 4 + hd // 2, 0, :, (hd % 2) * 128 : (hd % 2 + 1) * 128] = low(out)

        gvec[0] = jnp.zeros_like(gvec[0])
        pl.run_scoped(query_phase, pltpu.VMEM(qraw_hbm.shape, jnp.float32), pltpu.SemaphoreType.DMA)

        after("qp")
        reduce_end(1)

        def out_phase(hbuf, obuf, sems, o_sems):
            def load(r, slot):
                return pltpu.make_async_copy(h_hbm.at[pl.ds(r * 128, 128)], hbuf.at[slot], sems.at[slot])

            def store(r, slot):
                return pltpu.make_async_copy(obuf.at[slot], block_out.at[pl.ds(r * 128, 128)], o_sems.at[slot])

            load(0, 0).start()

            @pl.loop(0, n_chunks)
            def _(r):
                slot = lax.rem(r, 2)

                @pl.when(r < n_chunks - 1)
                def _():
                    load(r + 1, 1 - slot).start()

                load(r, slot).wait()

                @pl.when(r >= 2)
                def _():
                    store(r - 2, slot).wait()

                obuf[slot] = low(hbuf[slot] + fin_rows(1, pl.multiple_of(r * 128, 128), 128))
                store(r, slot).start()

            store(n_chunks - 2, n_chunks % 2).wait()
            store(n_chunks - 1, (n_chunks - 1) % 2).wait()

        pl.run_scoped(
            out_phase,
            pltpu.VMEM((2, 128, width), jnp.float32),
            pltpu.VMEM((2, 128, width), jnp.bfloat16),
            pltpu.SemaphoreType.DMA((2,)),
            pltpu.SemaphoreType.DMA((2,)),
        )

        after("op")

        @pl.loop(0, seqs)
        def _(s):
            at = pl.ds(pl.multiple_of(s * rows, 128), rows)

            @pl.when(inside)
            def _():
                dkv_ref[at] = keep[s, 0]

            @pl.when(at_end)
            def _():
                kh_copy(s).wait_recv()
                dkv_ref[at] = keep[s, 0] + wide(hrecv[s])

        def key_phase(rbuf, sem):
            load = pltpu.make_async_copy(kraw_hbm, rbuf, sem)
            load.start()
            load.wait()
            for hd in range(2):
                lane = slice(hd * 128, (hd + 1) * 128)
                raw = rbuf[:, lane]
                scale = rms(raw)
                normed = raw * scale
                grad = dkv_ref[:, lane]
                gvec[0, 0:1, 128:256] = (
                    jnp.sum(grad * normed, axis=0, keepdims=True)
                    + (gvec[0, 0:1, 128:256] if hd else 0.0)
                )
                scaled = grad * kg_ref[...]
                out = scale * (scaled - normed * jnp.mean(scaled * normed, axis=-1, keepdims=True))
                acts[base + 6, 0, :, lane] = low(out)
            acts[base + 7, 0] = low(dkv_ref[:, 256:512])

        pl.run_scoped(key_phase, pltpu.VMEM(kraw_hbm.shape, jnp.float32), pltpu.SemaphoreType.DMA)
        after("kp")

        @pl.loop(seqs - 2, seqs)
        def _(s):
            ky_copy(s).wait_send()

        @pl.loop(0, seqs)
        def _(s):
            @pl.when(at_end)
            def _():
                kl_copy(s).wait_send()

            @pl.when(inside)
            def _():
                km_copy(s).wait_send()
                kh_copy(s).wait_send()

    pl.run_scoped(
        attention_back,
        pltpu.VMEM((seqs, 4, rows, 512), jnp.float32),
        pltpu.VMEM((2, 4, rows, 512), jnp.bfloat16),
        pltpu.VMEM((seqs, 3, rows, 512), jnp.bfloat16),
        pltpu.VMEM((tokens, 512), jnp.float32),
        pltpu.VMEM((tokens, 512), jnp.float32),
    )

    def sixth_phase(wb, sems):
        pieces = ((wga_hbm, base + 2, 2), (wq_hbm, base + 4, 2), (wk_hbm, base + 6, 1), (wv_hbm, base + 7, 1))

        def loads(n, slot):
            at = pl.ds(pl.multiple_of(n * TILE, TILE), TILE)
            out, start = [], 0
            for p, (ref, _, count) in enumerate(pieces):
                out.append(
                    pltpu.make_async_copy(
                        ref.at[at], wb.at[slot, :, pl.ds(start, count * TILE)], sems.at[slot, p]
                    )
                )
                start += count * TILE
            return out

        def compute(slot):
            total, start = None, 0
            for _, first, count in pieces:
                for n in range(count):
                    part = dot_rows(acts[first + n, 0], wb[slot, :, pl.ds(start, TILE)])
                    total = part if total is None else total + part
                    start += TILE
            return total

        pl.semaphore_wait(credit, 2)
        reduce_start(2, loads, compute, "p7")

    pl.run_scoped(
        sixth_phase,
        pltpu.VMEM((2, TILE, 6 * TILE), jnp.bfloat16),
        pltpu.SemaphoreType.DMA((2, 4)),
    )

    for step in range(5):
        device = (y_dev, lo_dev, hi_dev, core_dev, x_dev)[step]
        copy = remote(gvec.at[step], gvec_got.at[step], gv_s.at[step], gv_r.at[step], device)
        copy.start()
        copy.wait()
        gvec[step + 1] = gvec[step] + gvec_got[step]
    gains_out[...] = gvec[5]

    reduce_end(2)

    def last_phase(xbuf, dbuf, obuf, sems, o_sems):
        def loads(r, slot):
            at = pl.ds(r * 128, 128)
            return (
                pltpu.make_async_copy(x_hbm.at[at], xbuf.at[slot], sems.at[slot, 0]),
                pltpu.make_async_copy(dh_hbm.at[at], dbuf.at[slot], sems.at[slot, 1]),
            )

        def store(r, slot):
            return pltpu.make_async_copy(obuf.at[slot], x_out.at[pl.ds(r * 128, 128)], o_sems.at[slot])

        for copy in loads(0, 0):
            copy.start()

        @pl.loop(0, n_chunks)
        def _(r):
            slot = lax.rem(r, 2)

            @pl.when(r < n_chunks - 1)
            def _():
                for copy in loads(r + 1, 1 - slot):
                    copy.start()

            for copy in loads(r, slot):
                copy.wait()

            @pl.when(r >= 2)
            def _():
                store(r - 2, slot).wait()

            value = wide(xbuf[slot])
            scale = rms(value)
            normed = value * scale
            grad = fin_rows(2, pl.multiple_of(r * 128, 128), 128)
            vec[0, 0:1] += jnp.sum(grad * normed, axis=0, keepdims=True)
            scaled = grad * n1_ref[...]
            inner = jnp.mean(scaled * normed, axis=-1, keepdims=True)
            obuf[slot] = low(dbuf[slot] + scale * (scaled - normed * inner))
            store(r, slot).start()

        store(n_chunks - 2, n_chunks % 2).wait()
        store(n_chunks - 1, (n_chunks - 1) % 2).wait()

    pl.run_scoped(
        last_phase,
        pltpu.VMEM((2, 128, width), jnp.bfloat16),
        pltpu.VMEM((2, 128, width), jnp.float32),
        pltpu.VMEM((2, 128, width), jnp.bfloat16),
        pltpu.SemaphoreType.DMA((2, 2)),
        pltpu.SemaphoreType.DMA((2,)),
    )

    after("lp")
    for step in range(3):
        device = (y_dev, lo_dev, hi_dev)[step]
        copy = remote(vec.at[step], vec_got.at[step], nv_s.at[step], nv_r.at[step], device)
        copy.start()
        copy.wait()
        vec[step + 1] = vec[step] + vec_got[step]
    norms_out[...] = vec[3]

    after("vec")

    @pl.loop(0, item_count)
    def _(i):
        act_copy(i).wait_send()

    for i in range(item_count - 4, item_count):

        @pl.when(at_end)
        def _():
            z1_copy(i).wait_send()

        @pl.when(inside)
        def _():
            z2_copy(i).wait_send()
            z3_copy(i).wait_send()

    for i in range(item_count - 2, item_count):
        out_wait(i)

    for l in range(4):
        lt_copy(l).wait_send()
        lt_core(l, head).wait_send()
        lt_x(l, head).wait_send()
        lt_far(l, x_head).wait_send()


def back_call(hbm, vmem, sizes):
    tokens, width, seqs, rows, keys_total, hidden = sizes
    count = 3 * (hidden // TILE) + 8
    bf, f32 = jnp.bfloat16, jnp.float32
    dma = pltpu.SemaphoreType.DMA
    scratch = [
        pltpu.VMEM((count, 2, tokens, TILE), bf),
        pltpu.VMEM((4, 2, 4, TILE, tokens), bf),
        pltpu.VMEM((4, TILE, tokens), bf),
        pltpu.VMEM((4, tokens, TILE), bf),
        pltpu.VMEM((2, 4, tokens, TILE), bf),
        pltpu.VMEM((2, 4, tokens, TILE), bf),
        pltpu.VMEM((2, 8, tokens, TILE), bf),
        pltpu.VMEM((seqs, 4, rows, 512), bf),
        pltpu.VMEM((seqs, 3, rows, 512), bf),
        pltpu.VMEM((seqs, 2, rows, 512), bf),
        pltpu.VMEM((seqs, rows, 512), bf),
        pltpu.VMEM((4, 3, TILE, TILE), bf),
        pltpu.VMEM((4, TILE, TILE), bf),
        pltpu.VMEM((2, TILE, TILE), f32),
        pltpu.VMEM((tokens, width), bf),
        pltpu.VMEM((tokens, width), bf),
        pltpu.VMEM((2, 2, 8, tokens), f32),
        pltpu.VMEM((4, 8, width), f32),
        pltpu.VMEM((3, 8, width), f32),
        pltpu.VMEM((6, 8, 256), f32),
        pltpu.VMEM((5, 8, 256), f32),
        *(dma((count,)) for _ in range(8)),
        *(dma((4,)) for _ in range(8)),
        *(dma((3, 4)) for _ in range(6)),
        *(dma((seqs,)) for _ in range(8)),
        dma((3,)), dma((3,)), dma((5,)), dma((5,)),
        dma((4,)), dma((2,)), dma((8,)), pltpu.SemaphoreType.REGULAR,
    ]
    any_spec = pl.BlockSpec(memory_space=pl.ANY)
    vmem_spec = pl.BlockSpec(memory_space=pltpu.VMEM)
    return pl.pallas_call(
        back_kernel,
        out_shape=[
            jax.ShapeDtypeStruct((tokens, width), bf),
            jax.ShapeDtypeStruct((tokens, width), bf),
            jax.ShapeDtypeStruct((hidden, TILE), f32),
            jax.ShapeDtypeStruct((TILE, hidden), f32),
            jax.ShapeDtypeStruct((TILE, hidden), f32),
            jax.ShapeDtypeStruct((512, TILE), f32),
            jax.ShapeDtypeStruct((TILE, 512), f32),
            jax.ShapeDtypeStruct((TILE, 512), f32),
            jax.ShapeDtypeStruct((TILE, TILE), f32),
            jax.ShapeDtypeStruct((TILE, TILE), f32),
            jax.ShapeDtypeStruct((8, width), f32),
            jax.ShapeDtypeStruct((8, 256), f32),
            jax.ShapeDtypeStruct((tokens, width), f32),
            jax.ShapeDtypeStruct((count, 3, TILE, TILE), bf),
            jax.ShapeDtypeStruct((count, 2, TILE, TILE), bf),
            jax.ShapeDtypeStruct((count, TILE, TILE), bf),
        ],
        in_specs=[any_spec] * len(hbm) + [vmem_spec] * len(vmem),
        out_specs=[any_spec] * 10 + [vmem_spec] * 2 + [any_spec] * 4,
        scratch_shapes=scratch,
        compiler_params=pltpu.CompilerParams(
            collective_id=1, has_side_effects=True, vmem_limit_bytes=61 << 20
        ),
    )(*hbm, *vmem)


def forward_kernel(
    x_hbm, wq_hbm, wk_hbm, wv_hbm, wga_hbm, wo_hbm,
    n1_ref, qg_ref, kg_ref, kpos_ref, qpos_ref,
    h_out, xt_out, q_out, kv_out, o_out, sig_out, y_out, qraw_out, kraw_out, lse_ref,
    xv, xn, wqv, wkv, wvv, wgav, wov, kv, qv, qraw, kraw, sig, ov, yv, xtv, hv,
    csend, crecv, fin, xrecv,
    x_sem, w_sem, out_sem, h_sem, kz_s, kz_r, ky_s, ky_r, c1_s, c1_r, x_s, x_r, c2_s, c2_r,
):
    seq, head = lax.axis_index("seq"), lax.axis_index("head")
    z, y = lax.div(seq, 2), lax.rem(seq, 2)
    c = lax.rem(head, 2)
    y_dev = {"seq": z * 2 + 1 - y}
    z_dev = [None] + [{"seq": other_z(z, t) * 2 + y} for t in (1, 2, 3)]
    core_dev = {"head": head + 1 - 2 * c}
    x_dev = {"head": head + 2 - 4 * lax.div(head, 2)}
    seqs, slots, rows = kv.shape[0], kv.shape[1], kv.shape[2]
    tokens, width = x_hbm.shape
    half = width // 2
    epsilon_k = 1e-06

    def rms(value):
        return lax.rsqrt(jnp.mean(value * value, axis=-1, keepdims=True) + epsilon_k)

    def rows_at(s):
        return pl.ds(pl.multiple_of(s * rows, 128), rows)

    def x_load(s):
        return pltpu.make_async_copy(x_hbm.at[rows_at(s)], xv.at[rows_at(s)], x_sem.at[s])

    weight_loads = [
        pltpu.make_async_copy(src, dst, w_sem.at[i])
        for i, (src, dst) in enumerate(
            ((wk_hbm, wkv), (wv_hbm, wvv), (wq_hbm, wqv), (wga_hbm, wgav), (wo_hbm, wov))
        )
    ]
    for s in range(seqs):
        x_load(s).start()
    for load in weight_loads:
        load.start()

    barrier = pltpu.get_barrier_semaphore()
    for device in (y_dev, *z_dev[1:], core_dev, x_dev):
        pl.semaphore_signal(barrier, inc=1, device_id=device, device_id_type=MESH)
    pl.semaphore_wait(barrier, 6)

    def remote(src, dst, send, recv, device):
        return pltpu.make_async_remote_copy(
            src_ref=src, dst_ref=dst, send_sem=send, recv_sem=recv, device_id=device, device_id_type=MESH
        )

    def z_copy(s, t):
        return remote(kv.at[s, 0], kv.at[s, 2 * t], kz_s.at[s, t], kz_r.at[s, t], z_dev[t])

    def y_copy(s, t):
        return remote(kv.at[s, 2 * t], kv.at[s, 2 * t + 1], ky_s.at[s, t], ky_r.at[s, t], y_dev)

    def core_copy(s):
        return remote(csend.at[s], crecv.at[s], c1_s.at[s], c1_r.at[s], core_dev)

    def x_copy(s):
        return remote(fin.at[s, c], xrecv.at[s], x_s.at[s], x_r.at[s], x_dev)

    def fin_copy(s):
        return remote(fin.at[s, c], fin.at[s, c], c2_s.at[s], c2_r.at[s], core_dev)

    def fin_copy_in(s):
        piece = fin.at[s, 1 - c]
        return remote(piece, piece, c2_s.at[s], c2_r.at[s], core_dev)

    @pl.loop(0, seqs)
    def _(s):
        x_load(s).wait()
        at = rows_at(s)
        value = wide(xv[at])
        xn[at] = low(value * rms(value) * n1_ref[...])

    weight_loads[0].wait()
    weight_loads[1].wait()

    @pl.loop(0, seqs)
    def _(s):
        at = rows_at(s)
        raw = dot_plain(xn[at], wkv[...])
        kraw[at] = raw
        for n in range(2):
            lane = slice(n * 128, (n + 1) * 128)
            part = raw[:, lane]
            kv[s, 0, :, lane] = low(part * rms(part) * kg_ref[...])
        kv[s, 0, :, 256:512] = low(dot_plain(xn[at], wvv[...]))
        y_copy(s, 0).start()
        for t in (1, 2, 3):
            z_copy(s, t).start()

    outs = []

    def leave(src, dst):
        copy = pltpu.make_async_copy(src, dst, out_sem.at[len(outs)])
        copy.start()
        outs.append(copy)

    leave(kraw, kraw_out)

    def forward_keys(s):
        for t in (1, 2, 3):
            z_copy(s, t).wait_recv()
            y_copy(s, t).start()

    weight_loads[2].wait()
    weight_loads[3].wait()
    scale_q = 128.0**-0.5

    @pl.loop(0, seqs)
    def _(s):
        at = rows_at(s)
        raw = dot_plain(xn[at], wqv[...])
        qraw[at] = raw
        for n in range(4):
            lane = slice(n * 128, (n + 1) * 128)
            part = raw[:, lane]
            qv[at, lane] = low(part * rms(part) * (qg_ref[...] * scale_q))
        sig[at] = jax.nn.sigmoid(dot_plain(xn[at], wgav[...]))

    leave(qraw, qraw_out)
    leave(qv, q_out)
    leave(sig, sig_out)
    forward_keys(0)

    @pl.loop(0, width // TILE)
    def _(n):
        at = pl.ds(pl.multiple_of(n * TILE, TILE), TILE)
        xtv[n] = xn[:, at].T

    leave(xtv, xt_out)
    weight_loads[4].wait()

    def finish(s):
        x_copy(s).wait()
        fin[s, c] = low(wide(fin[s, c]) + wide(xrecv[s]))
        fin_copy(s).start()

    def h_store(s, slot):
        return pltpu.make_async_copy(hv.at[slot], h_out.at[rows_at(s)], h_sem.at[slot])

    def finish_rows(s):
        slot = lax.rem(s, 2)
        fin_copy_in(s).wait_recv()

        @pl.when(s >= 2)
        def _():
            h_store(s - 2, slot).wait()

        hv[slot, :, 0:half] = wide(xv[rows_at(s), 0:half]) + wide(fin[s, 0])
        hv[slot, :, half:width] = wide(xv[rows_at(s), half:width]) + wide(fin[s, 1])
        h_store(s, slot).start()

    @pl.loop(0, seqs)
    def _(s):
        @pl.when(s < seqs - 1)
        def _():
            forward_keys(s + 1)

        for t in range(4):
            y_copy(s, t).wait_recv()
        at = rows_at(s)
        allowed = kpos_ref[...] <= qpos_ref[...]
        for n in range(2):
            lanes = [slice((2 * n + g) * 128, (2 * n + g + 1) * 128) for g in range(2)]
            key = kv[s, :, :, n * 128 : (n + 1) * 128].reshape(slots * rows, 128)
            value = kv[s, :, :, 256 + n * 128 : 256 + (n + 1) * 128].reshape(slots * rows, 128)
            q = jnp.concatenate([qv[at, lane] for lane in lanes], axis=0)
            scores = jnp.where(allowed, dot_rows(key, q), -1e30)
            top = jnp.max(scores, axis=0, keepdims=True)
            probs = jnp.exp(scores - top)
            total = jnp.sum(probs, axis=0, keepdims=True)
            out = (dot_first(value, low(probs)) / total).T
            lse_ref[s, n] = top + jnp.log(total)
            for g in range(2):
                ov[at, lanes[g]] = out[g * rows : (g + 1) * rows]
        gated = low(ov[at] * sig[at])
        yv[at] = gated
        away = pl.ds(pl.multiple_of((1 - c) * half, 128), half)
        mine = pl.ds(pl.multiple_of(c * half, 128), half)
        csend[s] = low(dot_plain(gated, wov[:, away]))
        core_copy(s).start()
        part = dot_plain(gated, wov[:, mine])
        core_copy(s).wait_recv()
        fin[s, c] = low(part + wide(crecv[s]))
        x_copy(s).start()

        @pl.when(s >= 1)
        def _():
            finish(s - 1)

        @pl.when(s >= 2)
        def _():
            finish_rows(s - 2)

    leave(kv, kv_out)
    leave(ov, o_out)
    leave(yv, y_out)
    finish_rows(seqs - 2)
    finish(seqs - 1)
    finish_rows(seqs - 1)
    h_store(seqs - 2, seqs % 2).wait()
    h_store(seqs - 1, (seqs - 1) % 2).wait()
    for copy in outs:
        copy.wait()

    @pl.loop(0, seqs)
    def _(s):
        for t in (1, 2, 3):
            z_copy(s, t).wait_send()
        for t in range(4):
            y_copy(s, t).wait_send()
        core_copy(s).wait_send()
        fin_copy(s).wait_send()


def forward_call(hbm, vmem, sizes):
    tokens, width, seqs, rows, slots = sizes
    bf, f32 = jnp.bfloat16, jnp.float32
    dma = pltpu.SemaphoreType.DMA
    half = width // 2
    kv_shape = (seqs, slots, rows, 512)
    scratch = [
        pltpu.VMEM((tokens, width), bf),
        pltpu.VMEM((tokens, width), bf),
        pltpu.VMEM((width, 512), bf),
        pltpu.VMEM((width, 256), bf),
        pltpu.VMEM((width, 256), bf),
        pltpu.VMEM((width, 512), bf),
        pltpu.VMEM((512, width), bf),
        pltpu.VMEM(kv_shape, bf),
        pltpu.VMEM((tokens, 512), bf),
        pltpu.VMEM((tokens, 512), f32),
        pltpu.VMEM((tokens, 256), f32),
        pltpu.VMEM((tokens, 512), f32),
        pltpu.VMEM((tokens, 512), f32),
        pltpu.VMEM((tokens, 512), bf),
        pltpu.VMEM((width // TILE, TILE, tokens), bf),
        pltpu.VMEM((2, rows, width), f32),
        pltpu.VMEM((seqs, rows, half), bf),
        pltpu.VMEM((seqs, rows, half), bf),
        pltpu.VMEM((seqs, 2, rows, half), bf),
        pltpu.VMEM((seqs, rows, half), bf),
        dma((seqs,)), dma((5,)), dma((8,)), dma((2,)),
        *(dma((seqs, 4)) for _ in range(4)),
        *(dma((seqs,)) for _ in range(6)),
    ]
    any_spec = pl.BlockSpec(memory_space=pl.ANY)
    vmem_spec = pl.BlockSpec(memory_space=pltpu.VMEM)
    return pl.pallas_call(
        forward_kernel,
        out_shape=[
            jax.ShapeDtypeStruct((tokens, width), f32),
            jax.ShapeDtypeStruct((width // TILE, TILE, tokens), bf),
            jax.ShapeDtypeStruct((tokens, 512), bf),
            jax.ShapeDtypeStruct(kv_shape, bf),
            jax.ShapeDtypeStruct((tokens, 512), f32),
            jax.ShapeDtypeStruct((tokens, 512), f32),
            jax.ShapeDtypeStruct((tokens, 512), bf),
            jax.ShapeDtypeStruct((tokens, 512), f32),
            jax.ShapeDtypeStruct((tokens, 256), f32),
            jax.ShapeDtypeStruct((seqs, 2, 1, 2 * rows), f32),
        ],
        in_specs=[any_spec] * len(hbm) + [vmem_spec] * len(vmem),
        out_specs=[any_spec] * 9 + [vmem_spec],
        scratch_shapes=scratch,
        compiler_params=pltpu.CompilerParams(
            collective_id=2, has_side_effects=True, vmem_limit_bytes=60 << 20
        ),
    )(*hbm, *vmem)


def on_device(
    x_in,
    cot,
    domain_ids,
    domain_counts,
    domain_weights,
    block_order,
    norm1,
    w_query,
    w_key,
    w_value,
    w_gate_attn,
    w_out,
    query_gain,
    key_gain,
    norm2,
    w_gate,
    w_up,
    w_down,
):
    sequences, local_rows, width = x_in.shape
    row_total = sequences * local_rows
    head_dim = query_gain.shape[0]
    kv_local = w_key.shape[1] // head_dim
    q_local = w_query.shape[1] // head_dim
    group = q_local // kv_local
    devices = lax.axis_size("seq")
    own = lax.axis_index("seq")
    block_rows = local_rows * devices // block_order.shape[0]
    q_gain, k_gain = wide(query_gain), wide(key_gain)
    gain_one, gain_two = wide(norm1), wide(norm2)

    x_rows = x_in.reshape(row_total, width)
    query_pos = positions(block_order, own, local_rows, block_rows)
    key_pos = jnp.concatenate(
        [positions(block_order, own ^ j, local_rows, block_rows) for j in range(devices)]
    )
    key_column = key_pos[:, None]
    query_row = jnp.concatenate([query_pos] * group)[None, :]

    domain_total = domain_weights.shape[0]
    domain_index = jnp.arange(domain_total, dtype=jnp.int32)
    factor = domain_weights * (row_total * devices) / (domain_total * wide(domain_counts))
    picked = domain_ids.reshape(row_total)[:, None] == domain_index[None, :]
    row_scale = jnp.sum(jnp.where(picked, factor[None, :], 0.0), axis=1)

    h, xt, query, kv, attn, sig, gated, query_raw, key_raw, lse = forward_call(
        (x_rows, w_query, w_key, w_value, w_gate_attn, w_out),
        (gain_one[None, :], q_gain[None, :], k_gain[None, :], key_column, query_row),
        (row_total, width, sequences, local_rows, devices),
    )
    out, x_grad, down, gate, up, wout, wga, wquery, wkey, wvalue, norms, gains, *_ = back_call(
        (
            h,
            cot.reshape(row_total, width),
            x_rows,
            xt,
            query,
            kv.reshape(sequences, devices * local_rows, -1),
            attn,
            sig,
            gated,
            query_raw,
            key_raw,
            w_gate,
            w_up,
            w_down,
            w_out,
            w_query,
            w_key,
            w_value,
            w_gate_attn,
        ),
        (
            row_scale[:, None],
            lse,
            key_column,
            query_row,
            gain_one[None, :],
            gain_two[None, :],
            q_gain[None, :],
            k_gain[None, :],
        ),
        (row_total, width, sequences, local_rows, local_rows * devices, w_down.shape[0]),
    )

    def own_part(value):
        size = value.shape[0] // devices
        return lax.dynamic_slice_in_dim(value, own * size, size, 0)

    return (
        out.reshape(x_in.shape),
        x_grad.reshape(x_in.shape),
        own_part(norms[0]),
        wquery,
        wkey,
        wvalue,
        wga,
        wout,
        own_part(gains[0, :head_dim]),
        own_part(gains[0, head_dim:]),
        own_part(norms[1]),
        gate,
        up,
        down,
    )


def on_device_plain(
    x_in,
    cot,
    domain_ids,
    domain_counts,
    domain_weights,
    block_order,
    norm1,
    w_query,
    w_key,
    w_value,
    w_gate_attn,
    w_out,
    query_gain,
    key_gain,
    norm2,
    w_gate,
    w_up,
    w_down,
):
    sequences, local_rows, model_width = x_in.shape
    row_total = sequences * local_rows
    head_dim = query_gain.shape[0]
    kv_local = w_key.shape[1] // head_dim
    q_local = w_query.shape[1] // head_dim
    group_size = q_local // kv_local
    block_rows = local_rows // 2
    seq_devices = lax.axis_size("seq")
    first_row = lax.axis_index("seq") * local_rows
    query_pos = positions(block_order, first_row, local_rows, block_rows)
    query_factor = head_dim ** (-0.5)
    q_gain = query_gain.astype(jnp.float32)
    k_gain = key_gain.astype(jnp.float32)
    gain_one = norm1.astype(jnp.float32)
    gain_two = norm2.astype(jnp.float32)
    x_float = x_in.reshape(row_total, model_width).astype(jnp.float32)
    scale_one = norm_scale(x_float)
    normed_one = x_float * scale_one
    x_normed = (normed_one * gain_one).astype(jnp.bfloat16)
    query_raw = product(x_normed, w_query).reshape(row_total, q_local, head_dim)
    key_raw = product(x_normed, w_key).reshape(row_total, kv_local, head_dim)
    value_rows = product(x_normed, w_value).astype(jnp.bfloat16)
    gate_pre = product(x_normed, w_gate_attn)
    query_scale = norm_scale(query_raw)
    query_normed = query_raw * query_scale
    key_scale = norm_scale(key_raw)
    key_normed = key_raw * key_scale
    query = (query_normed * q_gain * query_factor).astype(jnp.bfloat16)
    key_rows = (key_normed * k_gain).astype(jnp.bfloat16)
    project_query_heads = query.reshape(
        sequences, local_rows, kv_local, group_size, head_dim
    ).transpose(0, 2, 3, 1, 4)
    (
        query_scale,
        query_normed,
        key_scale,
        key_normed,
        query_heads,
        key_rows,
        value_rows,
        gate_pre,
    ) = (
        query_scale,
        query_normed,
        key_scale,
        key_normed,
        project_query_heads,
        key_rows,
        value_rows,
        gate_pre,
    )
    key_seq = key_rows.reshape(sequences, local_rows, kv_local * head_dim)
    value_seq = value_rows.reshape(sequences, local_rows, kv_local * head_dim)
    stat_shape = (sequences, kv_local, group_size, local_rows)
    running_max = jnp.full(stat_shape, -1e30, jnp.float32)
    key_piece = lax.all_gather(key_seq, "seq", axis=1, tiled=True)
    value_piece = lax.all_gather(value_seq, "seq", axis=1, tiled=True)
    row_count = key_piece.shape[1]
    key_block = key_piece.reshape(sequences, row_count, kv_local, head_dim)
    value_block = value_piece.reshape(sequences, row_count, kv_local, head_dim)
    key_pos = positions(block_order, jnp.int32(0), row_count, block_rows)
    allowed = key_pos[None, :] <= query_pos[:, None]
    scores = jnp.einsum(
        "skgqd,spkd->skgqp", query_heads, key_block, preferred_element_type=jnp.float32
    )
    scores = jnp.where(allowed, scores, -1e30)
    new_max = jnp.maximum(running_max, jnp.max(scores, axis=-1))
    weights = jnp.where(allowed, jnp.exp(scores - new_max[..., None]), 0.0)
    running_sum = jnp.sum(weights, axis=-1)
    weighted = jnp.einsum(
        "skgqp,spkd->skgqd",
        weights.astype(jnp.bfloat16),
        value_block,
        preferred_element_type=jnp.float32,
    )
    running_max, running_sum, weighted = (new_max, running_sum, weighted)
    log_total = running_max + jnp.log(running_sum)
    attn_heads = weighted / running_sum[..., None]
    attn_flat = attn_heads.transpose(0, 3, 1, 2, 4).reshape(row_total, q_local * head_dim)
    gate_sig = jax.nn.sigmoid(gate_pre)
    gated = (attn_flat * gate_sig).astype(jnp.bfloat16)
    attn_sum = lax.psum(product(gated, w_out).astype(jnp.bfloat16), "head").astype(jnp.float32)
    residual = x_float + attn_sum
    scale_two = norm_scale(residual)
    normed_two = residual * scale_two
    h_normed = (normed_two * gain_two).astype(jnp.bfloat16)
    gate_proj = product(h_normed, w_gate)
    up_proj = product(h_normed, w_up)
    gate_logit = jax.nn.sigmoid(gate_proj)
    gate_act = gate_proj * gate_logit
    mixed = (gate_act * up_proj).astype(jnp.bfloat16)
    mlp_sum = lax.psum(product(mixed, w_down).astype(jnp.bfloat16), "head").astype(jnp.float32)
    block_out = (
        (residual + mlp_sum).astype(jnp.bfloat16).reshape(sequences, local_rows, model_width)
    )
    domain_total = domain_weights.shape[0]
    domain_index = jnp.arange(domain_total, dtype=jnp.int32)
    factor = (
        domain_weights
        * (row_total * seq_devices)
        / (domain_total * domain_counts.astype(jnp.float32))
    )
    picked = domain_ids.reshape(row_total)[:, None] == domain_index[None, :]
    row_scale = jnp.sum(jnp.where(picked, factor[None, :], 0.0), axis=1)
    grad_out = cot.reshape(row_total, model_width).astype(jnp.float32) * row_scale[:, None]
    grad_low = grad_out.astype(jnp.bfloat16)
    grad_down = outer_sum(mixed, grad_low)
    grad_mixed = back_product(grad_low, w_down)
    grad_gate = (grad_mixed * up_proj * gate_logit * (1.0 + gate_proj * (1.0 - gate_logit))).astype(
        jnp.bfloat16
    )
    grad_up = (grad_mixed * gate_act).astype(jnp.bfloat16)
    grad_mlp_gate = outer_sum(h_normed, grad_gate)
    grad_mlp_up = outer_sum(h_normed, grad_up)
    grad_hnorm = lax.psum(
        (back_product(grad_gate, w_gate) + back_product(grad_up, w_up)).astype(jnp.bfloat16), "head"
    ).astype(jnp.float32)
    grad_norm_two = jnp.sum(grad_hnorm * normed_two, axis=0)
    grad_resid = grad_out + norm_back(grad_hnorm, normed_two, scale_two, gain_two)
    grad_attn = grad_resid.astype(jnp.bfloat16)
    grad_wout = outer_sum(gated, grad_attn)
    grad_gated = back_product(grad_attn, w_out)
    grad_heads_flat = (grad_gated * gate_sig).astype(jnp.bfloat16)
    grad_gatepre = (grad_gated * attn_flat * gate_sig * (1.0 - gate_sig)).astype(jnp.bfloat16)
    grad_wgate_attn = outer_sum(x_normed, grad_gatepre)
    grad_heads = grad_heads_flat.reshape(
        sequences, local_rows, kv_local, group_size, head_dim
    ).transpose(0, 2, 3, 1, 4)
    row_delta = jnp.sum(grad_heads.astype(jnp.float32) * attn_heads, axis=-1)
    key_piece = lax.all_gather(key_seq, "seq", axis=1, tiled=True)
    value_piece = lax.all_gather(value_seq, "seq", axis=1, tiled=True)
    row_count = key_piece.shape[1]
    key_block = key_piece.reshape(sequences, row_count, kv_local, head_dim)
    value_block = value_piece.reshape(sequences, row_count, kv_local, head_dim)
    key_pos = positions(block_order, jnp.int32(0), row_count, block_rows)
    allowed = key_pos[None, :] <= query_pos[:, None]
    scores = jnp.einsum(
        "skgqd,spkd->skgqp", query_heads, key_block, preferred_element_type=jnp.float32
    )
    probs = jnp.where(
        allowed, jnp.exp(jnp.where(allowed, scores, -1e30) - log_total[..., None]), 0.0
    )
    grad_probs = jnp.einsum(
        "skgqd,spkd->skgqp", grad_heads, value_block, preferred_element_type=jnp.float32
    )
    grad_scores = (probs * (grad_probs - row_delta[..., None])).astype(jnp.bfloat16)
    grad_query = jnp.einsum(
        "skgqp,spkd->skgqd", grad_scores, key_block, preferred_element_type=jnp.float32
    )
    key_term = jnp.einsum(
        "skgqp,skgqd->spkd", grad_scores, query_heads, preferred_element_type=jnp.float32
    ).reshape(sequences, row_count, kv_local * head_dim)
    value_term = jnp.einsum(
        "skgqp,skgqd->spkd",
        probs.astype(jnp.bfloat16),
        grad_heads,
        preferred_element_type=jnp.float32,
    ).reshape(sequences, row_count, kv_local * head_dim)
    grad_keys = key_term
    grad_values = value_term
    grad_query, grad_keys, grad_values = (grad_query, grad_keys, grad_values)
    grad_key_own, grad_value_own = (
        lax.psum_scatter(
            grad_keys.astype(jnp.bfloat16), "seq", scatter_dimension=1, tiled=True
        ).astype(jnp.float32),
        lax.psum_scatter(
            grad_values.astype(jnp.bfloat16), "seq", scatter_dimension=1, tiled=True
        ).astype(jnp.float32),
    )
    grad_query_rows = grad_query.transpose(0, 3, 1, 2, 4).reshape(row_total, q_local, head_dim)
    grad_qgain_part = jnp.sum(grad_query_rows * query_normed * query_factor, axis=(0, 1))
    grad_query_raw = (
        norm_back(grad_query_rows, query_normed, query_scale, q_gain * query_factor)
        .astype(jnp.bfloat16)
        .reshape(row_total, q_local * head_dim)
    )
    grad_key_rows = grad_key_own.reshape(row_total, kv_local, head_dim)
    grad_kgain_part = jnp.sum(grad_key_rows * key_normed, axis=(0, 1))
    grad_key_raw = (
        norm_back(grad_key_rows, key_normed, key_scale, k_gain)
        .astype(jnp.bfloat16)
        .reshape(row_total, kv_local * head_dim)
    )
    grad_value_low = grad_value_own.reshape(row_total, kv_local * head_dim).astype(jnp.bfloat16)
    grad_xnorm_part = (
        back_product(grad_query_raw, w_query)
        + back_product(grad_key_raw, w_key)
        + back_product(grad_value_low, w_value)
        + back_product(grad_gatepre, w_gate_attn)
    )
    grad_xnorm, grad_qgain, grad_kgain = (
        lax.psum(grad_xnorm_part.astype(jnp.bfloat16), "head").astype(jnp.float32),
        lax.psum(grad_qgain_part.astype(jnp.bfloat16), "head").astype(jnp.float32),
        lax.psum(grad_kgain_part.astype(jnp.bfloat16), "head").astype(jnp.float32),
    )
    grad_norm_one = jnp.sum(grad_xnorm * normed_one, axis=0)
    x_grad = (
        (grad_resid + norm_back(grad_xnorm, normed_one, scale_one, gain_one))
        .astype(jnp.bfloat16)
        .reshape(sequences, local_rows, model_width)
    )
    grad_wquery = outer_sum(x_normed, grad_query_raw)
    grad_wkey = outer_sum(x_normed, grad_key_raw)
    grad_wvalue = outer_sum(x_normed, grad_value_low)
    all_totals = (
        lax.psum_scatter(
            grad_norm_one.astype(jnp.bfloat16), "seq", scatter_dimension=0, tiled=True
        ).astype(jnp.float32),
        lax.psum_scatter(
            grad_wquery.astype(jnp.bfloat16), "seq", scatter_dimension=0, tiled=True
        ).astype(jnp.float32),
        lax.psum_scatter(
            grad_wkey.astype(jnp.bfloat16), "seq", scatter_dimension=0, tiled=True
        ).astype(jnp.float32),
        lax.psum_scatter(
            grad_wvalue.astype(jnp.bfloat16), "seq", scatter_dimension=0, tiled=True
        ).astype(jnp.float32),
        lax.psum_scatter(
            grad_wgate_attn.astype(jnp.bfloat16), "seq", scatter_dimension=0, tiled=True
        ).astype(jnp.float32),
        lax.psum_scatter(
            grad_wout.astype(jnp.bfloat16), "seq", scatter_dimension=1, tiled=True
        ).astype(jnp.float32),
        lax.psum_scatter(
            grad_qgain.astype(jnp.bfloat16), "seq", scatter_dimension=0, tiled=True
        ).astype(jnp.float32),
        lax.psum_scatter(
            grad_kgain.astype(jnp.bfloat16), "seq", scatter_dimension=0, tiled=True
        ).astype(jnp.float32),
        lax.psum_scatter(
            grad_mlp_gate.astype(jnp.bfloat16), "seq", scatter_dimension=0, tiled=True
        ).astype(jnp.float32),
        lax.psum_scatter(
            grad_mlp_up.astype(jnp.bfloat16), "seq", scatter_dimension=0, tiled=True
        ).astype(jnp.float32),
        lax.psum_scatter(
            grad_down.astype(jnp.bfloat16), "seq", scatter_dimension=1, tiled=True
        ).astype(jnp.float32),
        lax.psum_scatter(
            grad_norm_two.astype(jnp.bfloat16), "seq", scatter_dimension=0, tiled=True
        ).astype(jnp.float32),
    )
    return (
        block_out,
        x_grad,
        all_totals[0],
        all_totals[1],
        all_totals[2],
        all_totals[3],
        all_totals[4],
        all_totals[5],
        all_totals[6],
        all_totals[7],
        all_totals[11],
        all_totals[8],
        all_totals[9],
        all_totals[10],
    )


def solution(mesh):
    fits = mesh.shape["seq"] == 8 and mesh.shape["head"] == 4
    return jax.shard_map(
        on_device if fits else on_device_plain,
        mesh=mesh,
        in_specs=(
            P(None, "seq", None),
            P(None, "seq", None),
            P(None, "seq"),
            P(),
            P(),
            P(),
            P(),
            P(None, "head"),
            P(None, "head"),
            P(None, "head"),
            P(None, "head"),
            P("head", None),
            P(),
            P(),
            P(),
            P(None, "head"),
            P(None, "head"),
            P("head", None),
        ),
        out_specs=(
            P(None, "seq", None),
            P(None, "seq", None),
            P("seq"),
            P("seq", "head"),
            P("seq", "head"),
            P("seq", "head"),
            P("seq", "head"),
            P("head", "seq"),
            P("seq"),
            P("seq"),
            P("seq"),
            P("seq", "head"),
            P("seq", "head"),
            P("head", "seq"),
        ),
        check_vma=False,
    )
```

```python
import jax
import jax.numpy as jnp
from jax import lax
from jax.experimental import pallas as pl
from jax.experimental.pallas import tpu as pltpu
from jax.sharding import PartitionSpec as P

epsilon = 1e-06


def norm_scale(value):
    return lax.rsqrt(jnp.mean(value * value, axis=-1, keepdims=True) + epsilon)


def norm_back(grad_in, normed, scale, gain):
    scaled = grad_in * gain
    return scale * (scaled - normed * jnp.mean(scaled * normed, axis=-1, keepdims=True))


def product(left, right):
    return jnp.dot(left, right, preferred_element_type=jnp.float32)


def outer_sum(left, right):
    return lax.dot_general(
        left, right, (((0,), (0,)), ((), ())), preferred_element_type=jnp.float32
    )


def back_product(left, right):
    return lax.dot_general(
        left, right, (((1,), (1,)), ((), ())), preferred_element_type=jnp.float32
    )


def low(value):
    return value.astype(jnp.bfloat16)


def wide(value):
    return value.astype(jnp.float32)


def positions(block_order, device, row_count, block_rows):
    stored = device * row_count + jnp.arange(row_count, dtype=jnp.int32)
    slots = stored // block_rows
    slot_index = jnp.arange(block_order.shape[0], dtype=jnp.int32)
    picked = jnp.sum(
        jnp.where(slots[:, None] == slot_index[None, :], block_order[None, :], 0), axis=1
    )
    return picked * block_rows + stored % block_rows


MESH = pl.DeviceIdType.MESH
TILE = 256


PLAN = {
    "p1.0": (
        ("a", 0),
    ),
    "p1.3": (
        ("a", 1), ("s1", 0),
    ),
    "p1.5": (
        ("a", 2), ("r1", 0),
    ),
    "p2.0": (
        ("a", 3), ("s1", 1),
    ),
    "p2.1": (
        ("s2", 0),
    ),
    "p2.2": (
        ("r2", 0), ("a", 4), ("s1", 2),
    ),
    "p2.4": (
        ("a", 5), ("s1", 3), ("s3", 0), ("s2", 1),
    ),
    "p2.6": (
        ("a", 6), ("s1", 4), ("s4", 0),
    ),
    "p3.0": (
        ("s2", 2), ("a", 7), ("s3", 1), ("s1", 5),
    ),
    "p3.2": (
        ("a", 8), ("s4", 1), ("s2", 3), ("s1", 6), ("s3", 2),
    ),
    "p3.4": (
        ("a", 9),
    ),
    "p3.6": (
        ("s2", 4), ("s1", 7), ("a", 10), ("s3", 3), ("s4", 2),
    ),
    "e0.3": (
        ("s4", 3), ("s2", 5), ("s1", 8), ("a", 11), ("s3", 4),
    ),
    "p4b": (
        ("s2", 6), ("s1", 9), ("a", 12), ("s3", 5),
    ),
    "p5.0": (
        ("s2", 7), ("s1", 10), ("s3", 6),
    ),
    "p5.1": (
        ("s2", 8), ("s1", 11), ("s3", 7),
    ),
    "p5.2": (
        ("ky", 0), ("s2", 9), ("s3", 8),
    ),
    "p5.3": (
        ("s2", 10), ("s1", 12), ("ky", 1), ("s3", 9),
    ),
    "qp": (
        ("s2", 11),
    ),
    "e1.3": (
        ("s4", 4), ("s4", 5), ("s3", 10), ("s4", 6), ("s4", 7), ("s4", 8), ("s4", 9), ("kl", 0), ("ky", 2),
    ),
    "op": (
        ("s3", 11), ("s4", 10), ("s2", 12), ("km", 0), ("ky", 3), ("s4", 11), ("a", 13), ("kl", 1), ("r1", 3),
        ("s3", 12), ("a", 14), ("r1", 2), ("s4", 12), ("kl", 2), ("km", 1), ("r2", 3), ("a", 15), ("s1", 13),
        ("r2", 2), ("a", 16), ("kl", 3), ("s1", 14), ("km", 2), ("a", 17), ("s1", 15), ("s2", 13), ("km", 3),
        ("a", 18), ("s1", 16),
    ),
    "kp": (
        ("a", 19), ("s2", 14), ("s1", 17), ("s3", 13),
    ),
    "p7.0": (
        ("a", 20),
    ),
    "p7.1": (
        ("s2", 15), ("s1", 18),
    ),
    "p7.2": (
        ("a", 21), ("s3", 14), ("s4", 13),
    ),
    "p7.4": (
        ("s2", 16), ("s1", 19), ("a", 22), ("s3", 15), ("s4", 14),
    ),
    "p7.7": (
        ("s2", 17), ("s1", 20), ("a", 23), ("s3", 16),
    ),
    "e2.1": (
        ("s4", 15),
    ),
    "e2.2": (
        ("s2", 18), ("s1", 21), ("a", 24), ("s3", 17),
    ),
    "e2.3": (
        ("s4", 16),
    ),
    "lp": (
        ("s2", 19), ("s1", 22), ("a", 25), ("s3", 18),
    ),
    "vec": (
        ("s2", 20), ("s1", 23), ("s4", 17), ("s3", 19), ("s4", 18), ("s2", 21), ("s1", 24), ("s4", 19),
        ("s3", 20), ("s2", 22), ("s1", 25), ("s3", 21), ("s4", 20), ("s4", 21), ("s2", 23), ("s3", 22),
        ("s4", 22), ("s2", 24), ("s3", 23), ("s4", 23), ("s2", 25), ("s3", 24), ("s4", 24), ("s3", 25),
        ("s4", 25),
    ),
}


def other_z(z, t):
    low_z, high_z = lax.rem(z, 2), lax.div(z, 2)
    low_t, high_t = lax.rem(t, 2), lax.div(t, 2)
    return (low_z + low_t - 2 * low_z * low_t) + 2 * (high_z + high_t - 2 * high_z * high_t)


def fill_bias(order_ref, bias, rows, z, y, seq):
    block = bias.shape[0] // order_ref.shape[0]
    each = rows // block
    lane = lax.broadcasted_iota(jnp.int32, (block, bias.shape[1]), 1)
    down = lax.broadcasted_iota(jnp.int32, (block, bias.shape[1]), 0)
    within = lax.rem(lane, rows)
    query = lax.rem(lane, block)
    for i in range(each):
        query += jnp.where(lax.div(within, block) == i, order_ref[seq * each + i] * block, 0)
    for j in range(8):
        other_y = 1 - y if j % 2 else y
        device = other_z(z, j // 2) * 2 + other_y
        for i in range(each):
            key = order_ref[device * each + i] * block + down
            bias[j * rows + i * block : j * rows + (i + 1) * block] = jnp.where(key <= query, 0.0, -1e30)


def fill_factor(ids_ref, counts_ref, weights_ref, factor, total):
    seqs, rows = ids_ref.shape
    domains = counts_ref.shape[0]
    across = jnp.zeros((seqs, rows), jnp.float32)
    ids = ids_ref[...]
    for d in range(domains):
        count = jnp.full((seqs, rows), counts_ref[d], jnp.int32).astype(jnp.float32)
        weight = jnp.full((seqs, rows), weights_ref[d], jnp.float32) * total / (domains * count)
        across = jnp.where(ids == d, weight, across)
    here = lax.broadcasted_iota(jnp.int32, (rows, rows), 0) == lax.broadcasted_iota(
        jnp.int32, (rows, rows), 1
    )
    for s in range(seqs):
        spread = jnp.where(here, across[s : s + 1], 0.0)
        factor[s * rows : (s + 1) * rows] = jnp.sum(spread, axis=1, keepdims=True)


def dot_plain(left, right):
    return jnp.dot(left, right, preferred_element_type=jnp.float32)


def dot_rows(left, right):
    return lax.dot_general(
        left, right, (((1,), (1,)), ((), ())), preferred_element_type=jnp.float32
    )


def dot_first(left, right):
    return lax.dot_general(
        left, right, (((0,), (0,)), ((), ())), preferred_element_type=jnp.float32
    )


def back_kernel(
    h_hbm, cot_hbm, x_hbm, xt_hbm, ltd_hbm, dm_hbm, q_hbm, kv_hbm, o_hbm, sig_hbm, y_hbm, qraw_hbm, kraw_hbm,
    wg_hbm, wu_hbm, wd_hbm, wo_hbm, wq_hbm, wk_hbm, wv_hbm, wga_hbm,
    ids_ref, lse_ref, n1_ref, n2_ref, qg_ref, kg_ref, order_ref, counts_ref, weights_ref,
    block_out, x_out, dwd_out, dwg_out, dwu_out, dwo_out, dwga_out, dwq_out, dwk_out, dwv_out,
    n1_out, n2_out, qg_out, kg_out, dh_hbm, z1_hbm, z2_hbm, z3_hbm,
    acts, lt, odd, csend, crecv, xrecv, fin, yrecv, lrecv, mrecv, hrecv,
    zsend, stage, ostage, wide_a, wide_b, delta,
    vec, vec_got, gvec, gvec_got, bias, factor_ref,
    ya_s, ya_r, z1_s, z1_r, z2_s, z2_r, z3_s, z3_r, lt_s, lt_r, lc_s, lc_r, lx_s, lx_r, lf_s, lf_r,
    c1_s, c1_r, x_s, x_r, c2_s, c2_r, ky_s, ky_r, kl_s, kl_r, km_s, km_r, kh_s, kh_r,
    nv_s, nv_r, gv_s, gv_r, st_sem, out_sem, misc, credit,
):
    seq, head = lax.axis_index("seq"), lax.axis_index("head")
    z, y = lax.div(seq, 2), lax.rem(seq, 2)
    c = lax.rem(head, 2)
    y_dev = {"seq": z * 2 + 1 - y}
    lo_dev = {"seq": other_z(z, 1) * 2 + y}
    hi_dev = {"seq": other_z(z, 2) * 2 + y}
    mid_dev = {"seq": (3 - z) * 2 + y}
    core_dev = {"head": head + 1 - 2 * c}
    x_dev = {"head": head + 2 - 4 * lax.div(head, 2)}
    at_end, inside = lax.rem(z, 3) == 0, lax.rem(z, 3) != 0
    tokens = cot_hbm.shape[0]
    rows = bias.shape[0] // 8
    seqs = tokens // rows
    hidden_tiles = wd_hbm.shape[0] // TILE
    ff_items = 3 * hidden_tiles
    width = cot_hbm.shape[1]
    epsilon_k = 1e-06

    barrier = pltpu.get_barrier_semaphore()
    for device in (y_dev, lo_dev, hi_dev, core_dev, x_dev):
        pl.semaphore_signal(barrier, inc=1, device_id=device, device_id_type=MESH)

    @pl.when(inside)
    def _():
        pl.semaphore_signal(barrier, inc=1, device_id=mid_dev, device_id_type=MESH)
        pl.semaphore_wait(barrier, 6)

    @pl.when(at_end)
    def _():
        pl.semaphore_wait(barrier, 5)


    fill_bias(order_ref, bias, rows, z, y, seq)
    fill_factor(ids_ref, counts_ref, weights_ref, factor_ref, float(tokens * 8))

    def remote(src, dst, send, recv, device):
        return pltpu.make_async_remote_copy(
            src_ref=src, dst_ref=dst, send_sem=send, recv_sem=recv, device_id=device, device_id_type=MESH
        )

    def act_copy(i):
        return remote(acts.at[i, 0], acts.at[i, 1], ya_s.at[i], ya_r.at[i], y_dev)

    def lt_copy(l):
        return remote(odd.at[l], lt.at[l, 1, head], lt_s.at[l], lt_r.at[l], y_dev)

    x_head = head + 2 - 4 * lax.div(head, 2)
    core_head = head + 1 - 2 * c
    far_head = x_head + 1 - 2 * c

    def lt_core(l, part):
        piece = lt.at[l, 1, part]
        return remote(piece, piece, lc_s.at[l], lc_r.at[l], core_dev)

    def lt_x(l, part):
        piece = lt.at[l, 1, part]
        return remote(piece, piece, lx_s.at[l], lx_r.at[l], x_dev)

    def lt_far(l, part):
        piece = lt.at[l, 1, part]
        return remote(piece, piece, lf_s.at[l], lf_r.at[l], core_dev)

    def z1_copy(i):
        return remote(zsend.at[i % 4], z1_hbm.at[i], z1_s.at[i], z1_r.at[i], lo_dev)

    def z2_copy(i):
        return remote(zsend.at[i % 4, pl.ds(0, 2)], z2_hbm.at[i], z2_s.at[i], z2_r.at[i], mid_dev)

    def z3_copy(i):
        return remote(zsend.at[i % 4, 2], z3_hbm.at[i], z3_s.at[i], z3_r.at[i], lo_dev)

    def item_dot(i, l, first, last):
        count = (last - first) * TILE
        mine = dot_plain(lt[l, 0, first:last].reshape(count, tokens), acts[i, 0])
        return mine + dot_plain(lt[l, 1, first:last].reshape(count, tokens), acts[i, 1])

    def stage_load(src, slot):
        copy = pltpu.make_async_copy(src, stage.at[slot], st_sem.at[slot])
        copy.start()
        return copy

    def stage_one(i, l, place):
        act_copy(i).wait_recv()

        @pl.when(at_end)
        def _():
            if i >= 4:
                z1_copy(i - 4).wait_send()
            total = item_dot(i, l, 1, 4)
            for k in range(3):
                zsend[i % 4, k] = low(total[k * TILE : (k + 1) * TILE])
            z1_copy(i).start()

    def stage_two(i, l, place):
        @pl.when(inside)
        def _():
            z1_copy(i).wait_recv()
            loads = [stage_load(z1_hbm.at[i, k], k) for k in (1, 2)]
            if i >= 4:
                z2_copy(i - 4).wait_send()
            total = item_dot(i, l, 2, 4)
            for load in loads:
                load.wait()
            zsend[i % 4, 0] = low(total[:TILE] + wide(stage[2]))
            zsend[i % 4, 1] = low(total[TILE:] + wide(stage[1]))
            z2_copy(i).start()

    def out_wait(i):
        pltpu.make_async_copy(ostage.at[i % 2], dwk_out, out_sem.at[i % 2]).wait()

    def put(i, total, place):
        ref, n, turned = place
        if i >= 2:
            out_wait(i - 2)
        ostage[i % 2] = total.T if turned else total
        at = pl.ds(n * TILE, TILE)
        target = ref.at[at] if turned else ref.at[:, at]
        pltpu.make_async_copy(ostage.at[i % 2], target, out_sem.at[i % 2]).start()

    def stage_three(i, l, place):
        @pl.when(inside)
        def _():
            z2_copy(i).wait_recv()
            loads = [stage_load(z1_hbm.at[i, 0], 0), stage_load(z2_hbm.at[i, 0], 1), stage_load(z2_hbm.at[i, 1], 2)]
            if i >= 4:
                z3_copy(i - 4).wait_send()
            total = item_dot(i, l, 0, 2)
            for load in loads:
                load.wait()
            zsend[i % 4, 2] = low(total[TILE:] + wide(stage[1]))
            z3_copy(i).start()
            put(i, total[:TILE] + wide(stage[0]) + wide(stage[2]), place)

    def stage_four(i, l, place):
        @pl.when(at_end)
        def _():
            z3_copy(i).wait_recv()
            load = stage_load(z3_hbm.at[i], 3)
            total = item_dot(i, l, 0, 1)
            load.wait()
            put(i, total + wide(stage[3]), place)

    def at_tile(j, kind):
        later = j // 3 if isinstance(j, int) else lax.div(j, 3)
        if kind == 0:
            return j + 2 * j * later
        return (2 + 2 * j + kind) * (1 - later) + (3 * j + kind) * later

    ff_kind = {at_tile(j, kind): (j, kind) for j in range(hidden_tiles) for kind in range(3)}
    late = (
        (3, dwo_out, 0, True),
        (3, dwo_out, 1, True),
        (2, dwga_out, 0, False),
        (2, dwga_out, 1, False),
        (2, dwq_out, 0, False),
        (2, dwq_out, 1, False),
        (2, dwk_out, 0, False),
        (2, dwv_out, 0, False),
    )
    item_count = ff_items + 8
    shown = set()
    ltd_load = pltpu.make_async_copy(ltd_hbm, lt.at[1], misc.at[7])

    def item_step(stage_of, i):
        l = (1 if ff_kind[i][1] == 0 else 0) if i < ff_items else late[i - ff_items][0]
        if stage_of is stage_one and l not in shown:
            shown.add(l)
            if l == 1:
                ltd_load.wait()
            else:
                relay_in(l)
        if i < ff_items:
            j, kind = ff_kind[i]
            place = ((dwd_out, dwg_out, dwu_out)[kind], j, kind == 0)
        else:
            place = late[i - ff_items][1:]
        stage_of(i, l, place)

    actions = {
        "a": lambda i: act_copy(i).start(),
        "s1": lambda i: item_step(stage_one, i),
        "s2": lambda i: item_step(stage_two, i),
        "s3": lambda i: item_step(stage_three, i),
        "s4": lambda i: item_step(stage_four, i),
        "r1": lambda l: relay_one(l),
        "r2": lambda l: relay_two(l),
    }

    def after(place):
        for name, i in PLAN.get(place, ()):
            actions[name](i)

    def after_step(place, step, count):
        for k in range(count):
            if f"{place}.{k}" in PLAN:
                pl.when(step == k)(lambda k=k: after(f"{place}.{k}"))

    def spread(l, source):
        @pl.loop(0, 4)
        def _(t):
            at = pl.multiple_of((other_z(z, t) * 2 + y) * TILE, TILE)
            lt[l, 0, t] = source[:, pl.ds(at, TILE)].T

        at = pl.multiple_of((other_z(z, head) * 2 + 1 - y) * TILE, TILE)
        odd[l] = source[:, pl.ds(at, TILE)].T

    def relay_one(l):
        lt_copy(l).wait_recv()
        lt_core(l, head).start()
        lt_x(l, head).start()

    def relay_two(l):
        lt_x(l, x_head).wait_recv()
        lt_far(l, x_head).start()

    def relay_in(l):
        lt_core(l, core_head).wait_recv()
        lt_far(l, far_head).wait_recv()

    def core_copy(k, b):
        return remote(csend.at[b], crecv.at[k % 2, b], c1_s.at[k, b], c1_r.at[k, b], core_dev)

    def x_copy(k, b):
        return remote(fin.at[k % 2, c * 4 + b], xrecv.at[k % 2, b], x_s.at[k, b], x_r.at[k, b], x_dev)

    def fin_copy(k, b):
        piece = fin.at[k % 2, c * 4 + b]
        return remote(piece, piece, c2_s.at[k, b], c2_r.at[k, b], core_dev)

    def fin_copy_in(k, b):
        piece = fin.at[k % 2, (1 - c) * 4 + b]
        return remote(piece, piece, c2_s.at[k, b], c2_r.at[k, b], core_dev)

    def reduce_start(k, loads, compute, place):
        def block_of(step):
            return lax.rem(c + 1 + step, 2) * 4 + lax.div(step, 2)

        for copy in loads(block_of(0), 0):
            copy.start()

        @pl.loop(0, 8)
        def _(step):
            slot, b = lax.rem(step, 2), lax.div(step, 2)

            @pl.when(step < 7)
            def _():
                for copy in loads(block_of(step + 1), 1 - slot):
                    copy.start()

            for copy in loads(block_of(step), slot):
                copy.wait()
            part = compute(slot)

            @pl.when(slot == 0)
            def _():
                csend[b] = low(part)
                core_copy(k, b).start()

            @pl.when(slot == 1)
            def _():
                core_copy(k, b).wait_recv()
                fin[k % 2, c * 4 + b] = low(part + wide(crecv[k % 2, b]))
                x_copy(k, b).start()

            after_step(place, step, 8)

        @pl.loop(0, 4)
        def _(b):
            core_copy(k, b).wait_send()

    def reduce_end(k):
        for b in range(4):
            x_copy(k, b).wait()
            fin[k % 2, c * 4 + b] = low(wide(fin[k % 2, c * 4 + b]) + wide(xrecv[k % 2, b]))
            fin_copy(k, b).start()
            after(f"e{k}.{b}")
        for b in range(4):
            fin_copy_in(k, b).wait_recv()
            fin_copy(k, b).wait_send()
        after(f"e{k}.4")

    def fin_rows(k, at, count):
        return jnp.concatenate([wide(fin[k % 2, n, pl.ds(at, count)]) for n in range(8)], axis=1)

    def rms(value):
        return lax.rsqrt(jnp.mean(value * value, axis=-1, keepdims=True) + epsilon_k)

    n_chunks = tokens // 128

    def first_phase(hbuf, wgb, wub, dmb, sems, w_sems):
        def row_load(r, slot):
            return pltpu.make_async_copy(h_hbm.at[pl.ds(r * 128, 128)], hbuf.at[slot], sems.at[slot])

        def tile_loads(j, slot):
            at = pl.ds(pl.multiple_of(j * TILE, TILE), TILE)
            return (
                pltpu.make_async_copy(wg_hbm.at[:, at], wgb.at[slot], w_sems.at[slot, 0]),
                pltpu.make_async_copy(wu_hbm.at[:, at], wub.at[slot], w_sems.at[slot, 1]),
                pltpu.make_async_copy(dm_hbm.at[j], dmb.at[slot], w_sems.at[slot, 2]),
            )

        row_load(0, 0).start()
        for copy in tile_loads(0, 0):
            copy.start()
        ltd_load.start()

        @pl.loop(0, n_chunks)
        def _(r):
            slot = lax.rem(r, 2)

            @pl.when(r < n_chunks - 1)
            def _():
                row_load(r + 1, 1 - slot).start()

            row_load(r, slot).wait()
            value = hbuf[slot]
            at = pl.ds(pl.multiple_of(r * 128, 128), 128)
            wide_a[at] = low(value * rms(value) * wide(n2_ref[...]))

        after("p0")

        @pl.loop(0, hidden_tiles)
        def _(j):
            slot = lax.rem(j, 2)

            @pl.when(j < hidden_tiles - 1)
            def _():
                for copy in tile_loads(j + 1, 1 - slot):
                    copy.start()

            for copy in tile_loads(j, slot):
                copy.wait()

            @pl.loop(0, 2)
            def _(half):
                at = pl.ds(pl.multiple_of(half * (tokens // 2), 128), tokens // 2)
                a = dot_plain(wide_a[at], wgb[slot])
                u = dot_plain(wide_a[at], wub[slot])
                dm = dmb[slot, at]
                sig = jax.nn.sigmoid(a)
                act = a * sig
                acts[at_tile(j, 0), 0, at] = low(act * u)
                acts[at_tile(j, 1), 0, at] = low(dm * u * sig * (1.0 + a * (1.0 - sig)))
                acts[at_tile(j, 2), 0, at] = low(dm * act)

            after_step("p1", j, 1)

            @pl.when(j == 0)
            def _():
                spread(0, wide_a)
                lt_copy(0).start()
                after("sp0")

            for k in range(1, hidden_tiles):
                if f"p1.{k}" in PLAN:
                    pl.when(j == k)(lambda k=k: after(f"p1.{k}"))

    pl.run_scoped(
        first_phase,
        pltpu.VMEM((2, 128, width), jnp.float32),
        pltpu.VMEM((2, width, TILE), jnp.bfloat16),
        pltpu.VMEM((2, width, TILE), jnp.bfloat16),
        pltpu.VMEM((2, tokens, TILE), jnp.float32),
        pltpu.SemaphoreType.DMA((2,)),
        pltpu.SemaphoreType.DMA((2, 3)),
    )

    def second_phase(wa, wb, sems):
        def loads(n, slot):
            at = pl.ds(pl.multiple_of(n * TILE, TILE), TILE)
            return (
                pltpu.make_async_copy(wg_hbm.at[at], wa.at[slot], sems.at[slot, 0]),
                pltpu.make_async_copy(wu_hbm.at[at], wb.at[slot], sems.at[slot, 1]),
            )

        def compute(slot):
            total = None
            for j in range(hidden_tiles):
                at = pl.ds(j * TILE, TILE)
                part = dot_rows(acts[at_tile(j, 1), 0], wa[slot, :, at])
                part += dot_rows(acts[at_tile(j, 2), 0], wb[slot, :, at])
                total = part if total is None else total + part
            return total

        reduce_start(0, loads, compute, "p2")

    pl.run_scoped(
        second_phase,
        pltpu.VMEM((2, TILE, wg_hbm.shape[1]), jnp.bfloat16),
        pltpu.VMEM((2, TILE, wg_hbm.shape[1]), jnp.bfloat16),
        pltpu.SemaphoreType.DMA((2, 2)),
    )

    def third_phase(wa, sems):
        def loads(n, slot):
            at = pl.ds(pl.multiple_of(n * TILE, TILE), TILE)
            return (pltpu.make_async_copy(wd_hbm.at[:, at], wa.at[slot], sems.at[slot]),)

        def compute(slot):
            total = None
            for j in range(hidden_tiles):
                part = dot_plain(acts[at_tile(j, 0), 0], wa[slot, pl.ds(j * TILE, TILE)])
                total = part if total is None else total + part
            return total

        reduce_start(1, loads, compute, "p3")

    pl.run_scoped(
        third_phase,
        pltpu.VMEM((2, wd_hbm.shape[0], TILE), jnp.bfloat16),
        pltpu.SemaphoreType.DMA((2,)),
    )

    base = ff_items
    for n in range(2):
        pltpu.make_async_copy(
            y_hbm.at[:, pl.ds(n * TILE, TILE)], acts.at[base + n, 0], misc.at[n]
        ).start()

    def xt_own(t):
        shard = other_z(z, t) * 2 + y
        return pltpu.make_async_copy(xt_hbm.at[shard], lt.at[2, 0, t], misc.at[2 + t])

    def xt_odd():
        shard = other_z(z, head) * 2 + 1 - y
        return pltpu.make_async_copy(xt_hbm.at[shard], odd.at[2], misc.at[6])

    for t in range(4):
        xt_own(t).start()
    xt_odd().start()
    for t in range(4):
        xt_own(t).wait()
    xt_odd().wait()
    for n in range(2):
        pltpu.make_async_copy(
            y_hbm.at[:, pl.ds(n * TILE, TILE)], acts.at[base + n, 0], misc.at[n]
        ).wait()
    after("xt")
    reduce_end(0)

    def fourth_phase(hbuf, cbuf, dbuf, wob, obuf, sbuf, sems, d_sems, w_sems):
        def row_loads(r, slot):
            at = pl.ds(r * 128, 128)
            return (
                pltpu.make_async_copy(h_hbm.at[at], hbuf.at[slot], sems.at[slot, 0]),
                pltpu.make_async_copy(cot_hbm.at[at], cbuf.at[slot], sems.at[slot, 1]),
            )

        def spill(r, slot):
            return pltpu.make_async_copy(dbuf.at[slot], dh_hbm.at[pl.ds(r * 128, 128)], d_sems.at[slot])

        def tile_loads(n):
            at = pl.ds(n * TILE, TILE)
            return (
                pltpu.make_async_copy(wo_hbm.at[at], wob.at[n], w_sems.at[n, 0]),
                pltpu.make_async_copy(o_hbm.at[:, at], obuf.at[n], w_sems.at[n, 1]),
                pltpu.make_async_copy(sig_hbm.at[:, at], sbuf.at[n], w_sems.at[n, 2]),
            )

        for copy in row_loads(0, 0):
            copy.start()
        for n in range(2):
            for copy in tile_loads(n):
                copy.start()
        vec[0] = jnp.zeros_like(vec[0])

        @pl.loop(0, n_chunks)
        def _(r):
            slot = lax.rem(r, 2)

            @pl.when(r < n_chunks - 1)
            def _():
                for copy in row_loads(r + 1, 1 - slot):
                    copy.start()

            for copy in row_loads(r, slot):
                copy.wait()

            @pl.when(r >= 2)
            def _():
                spill(r - 2, slot).wait()

            at = pl.ds(pl.multiple_of(r * 128, 128), 128)
            value = hbuf[slot]
            scale = rms(value)
            normed = value * scale
            grad = fin_rows(0, pl.multiple_of(r * 128, 128), 128)
            vec[0, 1:2] += jnp.sum(grad * normed, axis=0, keepdims=True)
            scaled = grad * wide(n2_ref[...])
            inner = jnp.mean(scaled * normed, axis=-1, keepdims=True)
            dh = wide(cbuf[slot]) * factor_ref[at] + scale * (scaled - normed * inner)
            dbuf[slot] = dh
            wide_a[at] = low(dh)
            spill(r, slot).start()

        spill(n_chunks - 2, n_chunks % 2).wait()
        spill(n_chunks - 1, (n_chunks - 1) % 2).wait()

        after("p4a")
        ones = jnp.ones((8, 128), jnp.bfloat16)
        for n in range(2):
            for copy in tile_loads(n):
                copy.wait()
            dy = dot_rows(wide_a[...], wob[n])
            sig, o = sbuf[n], obuf[n]
            do = low(dy * sig)
            acts[base + 2 + n, 0] = low(dy * o * sig * (1.0 - sig))
            wide_b[:, n * TILE : (n + 1) * TILE] = do
            both = wide(do) * o
            for g in range(2):
                part = both[:, g * 128 : (g + 1) * 128]
                top = low(part)
                rest = low(part - wide(top))
                delta[n, g] = dot_rows(ones, top) + dot_rows(ones, rest)

        spread(3, wide_a)
        after("p4b")
        for device in (core_dev, x_dev):
            pl.semaphore_signal(credit, inc=1, device_id=device, device_id_type=MESH)

    pl.run_scoped(
        fourth_phase,
        pltpu.VMEM((2, 128, width), jnp.float32),
        pltpu.VMEM((2, 128, width), jnp.bfloat16),
        pltpu.VMEM((2, 128, width), jnp.float32),
        pltpu.VMEM((2, TILE, width), jnp.bfloat16),
        pltpu.VMEM((2, tokens, TILE), jnp.float32),
        pltpu.VMEM((2, tokens, TILE), jnp.float32),
        pltpu.SemaphoreType.DMA((2, 2)),
        pltpu.SemaphoreType.DMA((2,)),
        pltpu.SemaphoreType.DMA((2, 3)),
    )

    def attention_back(keep, ysend, lsend, dq_ref, dkv_ref):
        def ky_copy(s):
            return remote(ysend.at[lax.rem(s, 2)], yrecv.at[s], ky_s.at[s], ky_r.at[s], y_dev)

        def kl_copy(s):
            return remote(lsend.at[s], lrecv.at[s], kl_s.at[s], kl_r.at[s], lo_dev)

        def km_copy(s):
            return remote(lsend.at[s, pl.ds(0, 2)], mrecv.at[s], km_s.at[s], km_r.at[s], mid_dev)

        def kh_copy(s):
            return remote(lsend.at[s, 2], hrecv.at[s], kh_s.at[s], kh_r.at[s], lo_dev)

        def ky_step(s):
            ky_copy(s).wait_recv()
            for m in range(4):
                keep[s, m] += wide(yrecv[s, m])

            @pl.when(at_end)
            def _():
                for k in range(3):
                    lsend[s, k] = low(keep[s, k + 1])
                kl_copy(s).start()

        def kl_step(s):
            @pl.when(inside)
            def _():
                kl_copy(s).wait_recv()
                keep[s, 0] += wide(lrecv[s, 0])
                lsend[s, 0] = low(keep[s, 2] + wide(lrecv[s, 2]))
                lsend[s, 1] = low(keep[s, 3] + wide(lrecv[s, 1]))
                km_copy(s).start()

        def km_step(s):
            @pl.when(inside)
            def _():
                km_copy(s).wait_recv()
                keep[s, 0] += wide(mrecv[s, 1])
                lsend[s, 2] = low(keep[s, 1] + wide(mrecv[s, 0]))
                kh_copy(s).start()

        actions["ky"] = ky_step
        actions["kl"] = kl_step
        actions["km"] = km_step
        keys_total = bias.shape[0]

        def fifth_phase(qbuf, kvbuf, q_sem, sems):
            def kv_load(s, slot):
                return pltpu.make_async_copy(kv_hbm.at[s], kvbuf.at[slot], sems.at[slot])

            q_load = pltpu.make_async_copy(q_hbm, qbuf, q_sem)
            q_load.start()
            kv_load(0, 0).start()
            q_load.wait()

            @pl.loop(0, seqs)
            def _(s):
                slot = lax.rem(s, 2)

                @pl.when(s < seqs - 1)
                def _():
                    kv_load(s + 1, 1 - slot).start()

                kv_load(s, slot).wait()
                at = pl.ds(pl.multiple_of(s * rows, 128), rows)
                @pl.when(s >= 2)
                def _():
                    ky_copy(s - 2).wait_send()

                for n in range(2):
                    lanes = [slice((2 * n + g) * 128, (2 * n + g + 1) * 128) for g in range(2)]
                    key = kvbuf[slot, :, n * 128 : (n + 1) * 128]
                    value = kvbuf[slot, :, 256 + n * 128 : 256 + (n + 1) * 128]
                    q = jnp.concatenate([qbuf[at, lane] for lane in lanes], axis=0)
                    do = jnp.concatenate([wide_b[at, lane] for lane in lanes], axis=0)
                    drow = jnp.concatenate([delta[n, g, 0:1, at] for g in range(2)], axis=1)
                    scores = dot_rows(key, q)
                    probs = jnp.exp(scores - lse_ref[s, n] + bias[...])
                    grad_probs = dot_rows(value, do)
                    ds = low(probs * (grad_probs - drow))
                    for start, grad in ((0, dot_plain(ds, q)), (256, dot_plain(low(probs), do))):
                        into = slice(start + n * 128, start + (n + 1) * 128)
                        for m in range(4):
                            keep[s, m, :, into] = grad[2 * m * rows : (2 * m + 1) * rows]
                            ysend[slot, m, :, into] = low(grad[(2 * m + 1) * rows : (2 * m + 2) * rows])
                    dq = dot_first(key, ds).T
                    for g in range(2):
                        dq_ref[at, lanes[g]] = dq[g * rows : (g + 1) * rows]

                ky_copy(s).start()
                after_step("p5", s, seqs)

        pl.run_scoped(
            fifth_phase,
            pltpu.VMEM(q_hbm.shape, jnp.bfloat16),
            pltpu.VMEM((2, keys_total, 512), jnp.bfloat16),
            pltpu.SemaphoreType.DMA,
            pltpu.SemaphoreType.DMA((2,)),
        )

        lt_copy(3).start()
        lt_copy(2).start()
        after("sl3")

        def query_phase(rbuf, sem):
            load = pltpu.make_async_copy(qraw_hbm, rbuf, sem)
            load.start()
            load.wait()
            factor = 128.0**-0.5
            for hd in range(4):
                lane = slice(hd * 128, (hd + 1) * 128)
                raw = rbuf[:, lane]
                scale = rms(raw)
                normed = raw * scale
                grad = dq_ref[:, lane]
                gvec[0, 0:1, 0:128] = (
                    jnp.sum(grad * normed * factor, axis=0, keepdims=True)
                    + (gvec[0, 0:1, 0:128] if hd else 0.0)
                )
                scaled = grad * (wide(qg_ref[...]) * factor)
                out = scale * (scaled - normed * jnp.mean(scaled * normed, axis=-1, keepdims=True))
                acts[base + 4 + hd // 2, 0, :, (hd % 2) * 128 : (hd % 2 + 1) * 128] = low(out)

        gvec[0] = jnp.zeros_like(gvec[0])
        pl.run_scoped(query_phase, pltpu.VMEM(qraw_hbm.shape, jnp.float32), pltpu.SemaphoreType.DMA)

        after("qp")
        reduce_end(1)

        def out_phase(hbuf, obuf, sems, o_sems):
            def load(r, slot):
                return pltpu.make_async_copy(h_hbm.at[pl.ds(r * 128, 128)], hbuf.at[slot], sems.at[slot])

            def store(r, slot):
                return pltpu.make_async_copy(obuf.at[slot], block_out.at[pl.ds(r * 128, 128)], o_sems.at[slot])

            load(0, 0).start()

            @pl.loop(0, n_chunks)
            def _(r):
                slot = lax.rem(r, 2)

                @pl.when(r < n_chunks - 1)
                def _():
                    load(r + 1, 1 - slot).start()

                load(r, slot).wait()

                @pl.when(r >= 2)
                def _():
                    store(r - 2, slot).wait()

                obuf[slot] = low(hbuf[slot] + fin_rows(1, pl.multiple_of(r * 128, 128), 128))
                store(r, slot).start()

            store(n_chunks - 2, n_chunks % 2).wait()
            store(n_chunks - 1, (n_chunks - 1) % 2).wait()

        pl.run_scoped(
            out_phase,
            pltpu.VMEM((2, 128, width), jnp.float32),
            pltpu.VMEM((2, 128, width), jnp.bfloat16),
            pltpu.SemaphoreType.DMA((2,)),
            pltpu.SemaphoreType.DMA((2,)),
        )

        after("op")

        @pl.loop(0, seqs)
        def _(s):
            at = pl.ds(pl.multiple_of(s * rows, 128), rows)

            @pl.when(inside)
            def _():
                dkv_ref[at] = keep[s, 0]

            @pl.when(at_end)
            def _():
                kh_copy(s).wait_recv()
                dkv_ref[at] = keep[s, 0] + wide(hrecv[s])

        def key_phase(rbuf, sem):
            load = pltpu.make_async_copy(kraw_hbm, rbuf, sem)
            load.start()
            load.wait()
            for hd in range(2):
                lane = slice(hd * 128, (hd + 1) * 128)
                raw = rbuf[:, lane]
                scale = rms(raw)
                normed = raw * scale
                grad = dkv_ref[:, lane]
                gvec[0, 0:1, 128:256] = (
                    jnp.sum(grad * normed, axis=0, keepdims=True)
                    + (gvec[0, 0:1, 128:256] if hd else 0.0)
                )
                scaled = grad * wide(kg_ref[...])
                out = scale * (scaled - normed * jnp.mean(scaled * normed, axis=-1, keepdims=True))
                acts[base + 6, 0, :, lane] = low(out)
            acts[base + 7, 0] = low(dkv_ref[:, 256:512])

        pl.run_scoped(key_phase, pltpu.VMEM(kraw_hbm.shape, jnp.float32), pltpu.SemaphoreType.DMA)
        after("kp")

        @pl.loop(seqs - 2, seqs)
        def _(s):
            ky_copy(s).wait_send()

        @pl.loop(0, seqs)
        def _(s):
            @pl.when(at_end)
            def _():
                kl_copy(s).wait_send()

            @pl.when(inside)
            def _():
                km_copy(s).wait_send()
                kh_copy(s).wait_send()

    pl.run_scoped(
        attention_back,
        pltpu.VMEM((seqs, 4, rows, 512), jnp.float32),
        pltpu.VMEM((2, 4, rows, 512), jnp.bfloat16),
        pltpu.VMEM((seqs, 3, rows, 512), jnp.bfloat16),
        pltpu.VMEM((tokens, 512), jnp.float32),
        pltpu.VMEM((tokens, 512), jnp.float32),
    )

    def sixth_phase(wb, sems):
        pieces = ((wga_hbm, base + 2, 2), (wq_hbm, base + 4, 2), (wk_hbm, base + 6, 1), (wv_hbm, base + 7, 1))

        def loads(n, slot):
            at = pl.ds(pl.multiple_of(n * TILE, TILE), TILE)
            out, start = [], 0
            for p, (ref, _, count) in enumerate(pieces):
                out.append(
                    pltpu.make_async_copy(
                        ref.at[at], wb.at[slot, :, pl.ds(start, count * TILE)], sems.at[slot, p]
                    )
                )
                start += count * TILE
            return out

        def compute(slot):
            total, start = None, 0
            for _, first, count in pieces:
                for n in range(count):
                    part = dot_rows(acts[first + n, 0], wb[slot, :, pl.ds(start, TILE)])
                    total = part if total is None else total + part
                    start += TILE
            return total

        pl.semaphore_wait(credit, 2)
        reduce_start(2, loads, compute, "p7")

    pl.run_scoped(
        sixth_phase,
        pltpu.VMEM((2, TILE, 6 * TILE), jnp.bfloat16),
        pltpu.SemaphoreType.DMA((2, 4)),
    )

    for step in range(5):
        device = (y_dev, lo_dev, hi_dev, core_dev, x_dev)[step]
        copy = remote(gvec.at[step], gvec_got.at[step], gv_s.at[step], gv_r.at[step], device)
        copy.start()
        copy.wait()
        gvec[step + 1] = gvec[step] + gvec_got[step]
    piece = qg_out.shape[1]
    turn = lax.rem(128 - seq * piece, 128)
    for out, at in ((qg_out, 0), (kg_out, 128)):
        out[...] = pltpu.roll(gvec[5, :, at : at + 128], turn, 1)[0:1, 0:piece]

    reduce_end(2)

    def last_phase(xbuf, dbuf, obuf, sems, o_sems):
        def loads(r, slot):
            at = pl.ds(r * 128, 128)
            return (
                pltpu.make_async_copy(x_hbm.at[at], xbuf.at[slot], sems.at[slot, 0]),
                pltpu.make_async_copy(dh_hbm.at[at], dbuf.at[slot], sems.at[slot, 1]),
            )

        def store(r, slot):
            return pltpu.make_async_copy(obuf.at[slot], x_out.at[pl.ds(r * 128, 128)], o_sems.at[slot])

        for copy in loads(0, 0):
            copy.start()

        @pl.loop(0, n_chunks)
        def _(r):
            slot = lax.rem(r, 2)

            @pl.when(r < n_chunks - 1)
            def _():
                for copy in loads(r + 1, 1 - slot):
                    copy.start()

            for copy in loads(r, slot):
                copy.wait()

            @pl.when(r >= 2)
            def _():
                store(r - 2, slot).wait()

            value = wide(xbuf[slot])
            scale = rms(value)
            normed = value * scale
            grad = fin_rows(2, pl.multiple_of(r * 128, 128), 128)
            vec[0, 0:1] += jnp.sum(grad * normed, axis=0, keepdims=True)
            scaled = grad * wide(n1_ref[...])
            inner = jnp.mean(scaled * normed, axis=-1, keepdims=True)
            obuf[slot] = low(dbuf[slot] + scale * (scaled - normed * inner))
            store(r, slot).start()

        store(n_chunks - 2, n_chunks % 2).wait()
        store(n_chunks - 1, (n_chunks - 1) % 2).wait()

    pl.run_scoped(
        last_phase,
        pltpu.VMEM((2, 128, width), jnp.bfloat16),
        pltpu.VMEM((2, 128, width), jnp.float32),
        pltpu.VMEM((2, 128, width), jnp.bfloat16),
        pltpu.SemaphoreType.DMA((2, 2)),
        pltpu.SemaphoreType.DMA((2,)),
    )

    after("lp")
    for step in range(3):
        device = (y_dev, lo_dev, hi_dev)[step]
        copy = remote(vec.at[step], vec_got.at[step], nv_s.at[step], nv_r.at[step], device)
        copy.start()
        copy.wait()
        vec[step + 1] = vec[step] + vec_got[step]
    own = pl.ds(pl.multiple_of(seq * TILE, TILE), TILE)
    n1_out[...] = vec[3, 0:1, own]
    n2_out[...] = vec[3, 1:2, own]

    after("vec")

    @pl.loop(0, item_count)
    def _(i):
        act_copy(i).wait_send()

    for i in range(item_count - 4, item_count):

        @pl.when(at_end)
        def _():
            z1_copy(i).wait_send()

        @pl.when(inside)
        def _():
            z2_copy(i).wait_send()
            z3_copy(i).wait_send()

    for i in range(item_count - 2, item_count):
        out_wait(i)

    for l in (0, 2, 3):
        lt_copy(l).wait_send()
        lt_core(l, head).wait_send()
        lt_x(l, head).wait_send()
        lt_far(l, x_head).wait_send()


def back_call(hbm, vmem, smem, sizes):
    tokens, width, seqs, rows, keys_total, hidden = sizes
    count = 3 * (hidden // TILE) + 8
    bf, f32 = jnp.bfloat16, jnp.float32
    dma = pltpu.SemaphoreType.DMA
    scratch = [
        pltpu.VMEM((count, 2, tokens, TILE), bf),
        pltpu.VMEM((4, 2, 4, TILE, tokens), bf),
        pltpu.VMEM((4, TILE, tokens), bf),
        pltpu.VMEM((4, tokens, TILE), bf),
        pltpu.VMEM((2, 4, tokens, TILE), bf),
        pltpu.VMEM((2, 4, tokens, TILE), bf),
        pltpu.VMEM((2, 8, tokens, TILE), bf),
        pltpu.VMEM((seqs, 4, rows, 512), bf),
        pltpu.VMEM((seqs, 3, rows, 512), bf),
        pltpu.VMEM((seqs, 2, rows, 512), bf),
        pltpu.VMEM((seqs, rows, 512), bf),
        pltpu.VMEM((4, 3, TILE, TILE), bf),
        pltpu.VMEM((4, TILE, TILE), bf),
        pltpu.VMEM((2, TILE, TILE), f32),
        pltpu.VMEM((tokens, width), bf),
        pltpu.VMEM((tokens, width), bf),
        pltpu.VMEM((2, 2, 8, tokens), f32),
        pltpu.VMEM((4, 8, width), f32),
        pltpu.VMEM((3, 8, width), f32),
        pltpu.VMEM((6, 8, 256), f32),
        pltpu.VMEM((5, 8, 256), f32),
        pltpu.VMEM((keys_total, 2 * rows), f32),
        pltpu.VMEM((tokens, 1), f32),
        *(dma((count,)) for _ in range(8)),
        *(dma((4,)) for _ in range(8)),
        *(dma((3, 4)) for _ in range(6)),
        *(dma((seqs,)) for _ in range(8)),
        dma((3,)), dma((3,)), dma((5,)), dma((5,)),
        dma((4,)), dma((2,)), dma((8,)), pltpu.SemaphoreType.REGULAR,
    ]
    any_spec = pl.BlockSpec(memory_space=pl.ANY)
    vmem_spec = pl.BlockSpec(memory_space=pltpu.VMEM)
    smem_spec = pl.BlockSpec(memory_space=pltpu.SMEM)
    return pl.pallas_call(
        back_kernel,
        out_shape=[
            jax.ShapeDtypeStruct((tokens, width), bf),
            jax.ShapeDtypeStruct((tokens, width), bf),
            jax.ShapeDtypeStruct((hidden, TILE), f32),
            jax.ShapeDtypeStruct((TILE, hidden), f32),
            jax.ShapeDtypeStruct((TILE, hidden), f32),
            jax.ShapeDtypeStruct((512, TILE), f32),
            jax.ShapeDtypeStruct((TILE, 512), f32),
            jax.ShapeDtypeStruct((TILE, 512), f32),
            jax.ShapeDtypeStruct((TILE, TILE), f32),
            jax.ShapeDtypeStruct((TILE, TILE), f32),
            jax.ShapeDtypeStruct((1, width // 8), f32),
            jax.ShapeDtypeStruct((1, width // 8), f32),
            jax.ShapeDtypeStruct((1, 16), f32),
            jax.ShapeDtypeStruct((1, 16), f32),
            jax.ShapeDtypeStruct((tokens, width), f32),
            jax.ShapeDtypeStruct((count, 3, TILE, TILE), bf),
            jax.ShapeDtypeStruct((count, 2, TILE, TILE), bf),
            jax.ShapeDtypeStruct((count, TILE, TILE), bf),
        ],
        in_specs=[any_spec] * len(hbm) + [vmem_spec] * len(vmem) + [smem_spec] * len(smem),
        out_specs=[any_spec] * 10 + [vmem_spec] * 4 + [any_spec] * 4,
        scratch_shapes=scratch,
        compiler_params=pltpu.CompilerParams(
            collective_id=1, has_side_effects=True, vmem_limit_bytes=61 << 20
        ),
    )(*hbm, *vmem, *smem)


def forward_kernel(
    x_hbm, wq_hbm, wk_hbm, wv_hbm, wga_hbm, wo_hbm, cot_hbm, wd_hbm,
    ids_ref, n1_ref, qg_ref, kg_ref, order_ref, counts_ref, weights_ref,
    h_out, xt_out, q_out, kv_out, o_out, sig_out, y_out, qraw_out, kraw_out, ltd_out, dm_out, lse_ref,
    xv, xn, wqv, wkv, wvv, wgav, wov, kv, qv, qraw, kraw, sig, ov, yv, xtv, hv,
    dout, ltd, odd, wdv, dmv, bias, factor_ref,
    csend, crecv, fin, xrecv,
    x_sem, w_sem, out_sem, h_sem, kz_s, kz_r, kf_s, ky_s, ky_r, l_sem, d_sem, m_sem, c1_s, c1_r, x_s, x_r, c2_s, c2_r,
):
    seq, head = lax.axis_index("seq"), lax.axis_index("head")
    z, y = lax.div(seq, 2), lax.rem(seq, 2)
    c = lax.rem(head, 2)
    y_dev = {"seq": z * 2 + 1 - y}
    lo_dev, mid_dev = {"seq": other_z(z, 1) * 2 + y}, {"seq": (3 - z) * 2 + y}
    at_end, inside = lax.rem(z, 3) == 0, lax.rem(z, 3) != 0
    core_dev = {"head": head + 1 - 2 * c}
    x_dev = {"head": head + 2 - 4 * lax.div(head, 2)}
    seqs, slots, rows = kv.shape[0], kv.shape[1], kv.shape[2]
    tokens, width = x_hbm.shape
    half = width // 2
    epsilon_k = 1e-06

    def rms(value):
        return lax.rsqrt(jnp.mean(value * value, axis=-1, keepdims=True) + epsilon_k)

    def rows_at(s):
        return pl.ds(pl.multiple_of(s * rows, 128), rows)

    def x_load(s):
        return pltpu.make_async_copy(x_hbm.at[rows_at(s)], xv.at[rows_at(s)], x_sem.at[s])

    weight_loads = [
        pltpu.make_async_copy(src, dst, w_sem.at[i])
        for i, (src, dst) in enumerate(
            ((wk_hbm, wkv), (wv_hbm, wvv), (wq_hbm, wqv), (wga_hbm, wgav), (wo_hbm, wov))
        )
    ]
    for s in range(seqs):
        x_load(s).start()
    for load in weight_loads:
        load.start()
    for s in range(seqs):
        pltpu.make_async_copy(cot_hbm.at[rows_at(s)], dout.at[rows_at(s)], d_sem.at[s]).start()

    barrier = pltpu.get_barrier_semaphore()
    for device in (y_dev, lo_dev, core_dev, x_dev):
        pl.semaphore_signal(barrier, inc=1, device_id=device, device_id_type=MESH)

    @pl.when(inside)
    def _():
        pl.semaphore_signal(barrier, inc=1, device_id=mid_dev, device_id_type=MESH)
        pl.semaphore_wait(barrier, 5)

    @pl.when(at_end)
    def _():
        pl.semaphore_wait(barrier, 4)

    def remote(src, dst, send, recv, device):
        return pltpu.make_async_remote_copy(
            src_ref=src, dst_ref=dst, send_sem=send, recv_sem=recv, device_id=device, device_id_type=MESH
        )

    def own_out(s):
        return remote(kv.at[s, 0], kv.at[s, 2], kz_s.at[s, 1], kz_r.at[s, 1], lo_dev)

    def own_over(s):
        return remote(kv.at[s, 0], kv.at[s, 6], kz_s.at[s, 3], kz_r.at[s, 3], mid_dev)

    def end_over(s):
        return remote(kv.at[s, 2], kv.at[s, 4], kz_s.at[s, 2], kz_r.at[s, 2], mid_dev)

    def mid_out(s):
        return remote(kv.at[s, 6], kv.at[s, 4], kf_s.at[s, 0], kz_r.at[s, 2], lo_dev)

    def far_out(s):
        return remote(kv.at[s, 4], kv.at[s, 6], kf_s.at[s, 1], kz_r.at[s, 3], lo_dev)

    def y_copy(s, t):
        return remote(kv.at[s, 2 * t], kv.at[s, 2 * t + 1], ky_s.at[s, t], ky_r.at[s, t], y_dev)

    def core_copy(s):
        return remote(csend.at[s], crecv.at[s], c1_s.at[s], c1_r.at[s], core_dev)

    def x_copy(s):
        return remote(fin.at[s, c], xrecv.at[s], x_s.at[s], x_r.at[s], x_dev)

    def fin_copy(s):
        return remote(fin.at[s, c], fin.at[s, c], c2_s.at[s], c2_r.at[s], core_dev)

    def fin_copy_in(s):
        piece = fin.at[s, 1 - c]
        return remote(piece, piece, c2_s.at[s], c2_r.at[s], core_dev)

    weight_loads[0].wait()
    weight_loads[1].wait()

    @pl.loop(0, seqs)
    def _(s):
        x_load(s).wait()
        at = rows_at(s)
        value = wide(xv[at])
        xn[at] = low(value * rms(value) * wide(n1_ref[...]))
        raw = dot_plain(xn[at], wkv[...])
        kraw[at] = raw
        for n in range(2):
            lane = slice(n * 128, (n + 1) * 128)
            part = raw[:, lane]
            kv[s, 0, :, lane] = low(part * rms(part) * wide(kg_ref[...]))
        kv[s, 0, :, 256:512] = low(dot_plain(xn[at], wvv[...]))
        y_copy(s, 0).start()
        own_out(s).start()

        @pl.when(inside)
        def _():
            own_over(s).start()

    outs = []

    def leave(src, dst):
        copy = pltpu.make_async_copy(src, dst, out_sem.at[len(outs)])
        copy.start()
        outs.append(copy)

    leave(kraw, kraw_out)

    def forward_keys(s):
        own_out(s).wait_recv()

        @pl.when(inside)
        def _():
            end_over(s).start()
            y_copy(s, 1).start()
            own_over(s).wait_recv()
            mid_out(s).start()
            y_copy(s, 3).start()
            end_over(s).wait_recv()
            far_out(s).start()
            y_copy(s, 2).start()

        @pl.when(at_end)
        def _():
            y_copy(s, 1).start()
            mid_out(s).wait_recv()
            y_copy(s, 2).start()
            far_out(s).wait_recv()
            y_copy(s, 3).start()

    hidden_tiles = wd_hbm.shape[0] // TILE

    def cot_load(s):
        return pltpu.make_async_copy(cot_hbm.at[rows_at(s)], dout.at[rows_at(s)], d_sem.at[s])

    def wd_load(j):
        at = pl.ds(pl.multiple_of(j * TILE, TILE), TILE)
        return pltpu.make_async_copy(wd_hbm.at[at], wdv.at[lax.rem(j, 2)], l_sem.at[lax.rem(j, 2)])

    def dm_store(j):
        return pltpu.make_async_copy(dmv.at[lax.rem(j, 2)], dm_out.at[j], m_sem.at[lax.rem(j, 2)])

    def spread_copy():
        return remote(odd, ltd.at[1, pl.ds(2 * c, 2)], l_sem.at[2], l_sem.at[3], y_dev)

    def relay_copy(part):
        piece = ltd.at[1, pl.ds(2 * part, 2)]
        return remote(piece, piece, l_sem.at[4], l_sem.at[5], core_dev)

    def dm_tile(j):
        @pl.when(j < hidden_tiles - 1)
        def _():
            wd_load(j + 1).start()

        wd_load(j).wait()

        @pl.when(j >= 2)
        def _():
            dm_store(j - 2).wait()

        dmv[lax.rem(j, 2)] = dot_rows(dout[...], wdv[lax.rem(j, 2)])
        dm_store(j).start()

    fill_bias(order_ref, bias, rows, z, y, seq)
    fill_factor(ids_ref, counts_ref, weights_ref, factor_ref, float(tokens * 8))

    weight_loads[2].wait()
    weight_loads[3].wait()
    scale_q = 128.0**-0.5

    @pl.loop(0, seqs)
    def _(s):
        at = rows_at(s)
        raw = dot_plain(xn[at], wqv[...])
        qraw[at] = raw
        for n in range(4):
            lane = slice(n * 128, (n + 1) * 128)
            part = raw[:, lane]
            qv[at, lane] = low(part * rms(part) * (wide(qg_ref[...]) * scale_q))
        sig[at] = jax.nn.sigmoid(dot_plain(xn[at], wgav[...]))

    leave(qraw, qraw_out)
    leave(qv, q_out)
    leave(sig, sig_out)
    forward_keys(0)

    @pl.loop(0, width // TILE)
    def _(n):
        at = pl.ds(pl.multiple_of(n * TILE, TILE), TILE)
        xtv[n] = xn[:, at].T

    leave(xtv, xt_out)
    wd_load(0).start()

    @pl.loop(0, seqs)
    def _(s):
        cot_load(s).wait()
        at = rows_at(s)
        dout[at] = low(wide(dout[at]) * factor_ref[at])

    @pl.loop(0, 4)
    def _(t):
        at = pl.multiple_of((other_z(z, t) * 2 + y) * TILE, TILE)
        ltd[0, t] = dout[:, pl.ds(at, TILE)].T

    @pl.loop(0, 2)
    def _(k):
        at = pl.multiple_of((other_z(z, 2 * c + k) * 2 + 1 - y) * TILE, TILE)
        odd[k] = dout[:, pl.ds(at, TILE)].T

    weight_loads[4].wait()

    def finish(s):
        x_copy(s).wait()
        fin[s, c] = low(wide(fin[s, c]) + wide(xrecv[s]))
        fin_copy(s).start()

    def h_store(s, slot):
        return pltpu.make_async_copy(hv.at[slot], h_out.at[rows_at(s)], h_sem.at[slot])

    def finish_rows(s):
        slot = lax.rem(s, 2)
        fin_copy_in(s).wait_recv()

        @pl.when(s >= 2)
        def _():
            h_store(s - 2, slot).wait()

        hv[slot, :, 0:half] = wide(xv[rows_at(s), 0:half]) + wide(fin[s, 0])
        hv[slot, :, half:width] = wide(xv[rows_at(s), half:width]) + wide(fin[s, 1])
        h_store(s, slot).start()

    @pl.loop(0, seqs)
    def _(s):
        @pl.when(s < seqs - 1)
        def _():
            forward_keys(s + 1)

            @pl.when(s == seqs - 2)
            def _():
                spread_copy().start()

            dm_tile(2 * s)
            dm_tile(2 * s + 1)

        for t in range(4):
            y_copy(s, t).wait_recv()
        at = rows_at(s)
        for n in range(2):
            lanes = [slice((2 * n + g) * 128, (2 * n + g + 1) * 128) for g in range(2)]
            key = kv[s, :, :, n * 128 : (n + 1) * 128].reshape(slots * rows, 128)
            value = kv[s, :, :, 256 + n * 128 : 256 + (n + 1) * 128].reshape(slots * rows, 128)
            q = jnp.concatenate([qv[at, lane] for lane in lanes], axis=0)
            scores = dot_rows(key, q) + bias[...]
            top = jnp.max(scores, axis=0, keepdims=True)
            probs = jnp.exp(scores - top)
            total = jnp.sum(probs, axis=0, keepdims=True)
            out = (dot_first(value, low(probs)) / total).T
            lse_ref[s, n] = top + jnp.log(total)
            for g in range(2):
                ov[at, lanes[g]] = out[g * rows : (g + 1) * rows]
        gated = low(ov[at] * sig[at])
        yv[at] = gated
        away = pl.ds(pl.multiple_of((1 - c) * half, 128), half)
        mine = pl.ds(pl.multiple_of(c * half, 128), half)
        csend[s] = low(dot_plain(gated, wov[:, away]))
        core_copy(s).start()
        part = dot_plain(gated, wov[:, mine])
        core_copy(s).wait_recv()
        fin[s, c] = low(part + wide(crecv[s]))
        x_copy(s).start()

        @pl.when(s >= 1)
        def _():
            finish(s - 1)

        @pl.when(s >= 2)
        def _():
            finish_rows(s - 2)

    leave(kv, kv_out)
    leave(ov, o_out)
    leave(yv, y_out)
    finish_rows(seqs - 2)
    spread_copy().wait_recv()
    relay_copy(c).start()
    finish(seqs - 1)
    finish_rows(seqs - 1)
    h_store(seqs - 2, seqs % 2).wait()
    h_store(seqs - 1, (seqs - 1) % 2).wait()
    relay_copy(1 - c).wait_recv()
    leave(ltd, ltd_out)
    spread_copy().wait_send()
    relay_copy(c).wait_send()
    dm_store(hidden_tiles - 2).wait()
    dm_store(hidden_tiles - 1).wait()
    for copy in outs:
        copy.wait()

    @pl.loop(0, seqs)
    def _(s):
        own_out(s).wait_send()

        @pl.when(inside)
        def _():
            for copy in (own_over, end_over, mid_out, far_out):
                copy(s).wait_send()

        for t in range(4):
            y_copy(s, t).wait_send()
        core_copy(s).wait_send()
        fin_copy(s).wait_send()


def forward_call(hbm, vmem, smem, sizes):
    tokens, width, seqs, rows, slots, hidden = sizes
    bf, f32 = jnp.bfloat16, jnp.float32
    dma = pltpu.SemaphoreType.DMA
    half = width // 2
    kv_shape = (seqs, slots, rows, 512)
    scratch = [
        pltpu.VMEM((tokens, width), bf),
        pltpu.VMEM((tokens, width), bf),
        pltpu.VMEM((width, 512), bf),
        pltpu.VMEM((width, 256), bf),
        pltpu.VMEM((width, 256), bf),
        pltpu.VMEM((width, 512), bf),
        pltpu.VMEM((512, width), bf),
        pltpu.VMEM(kv_shape, bf),
        pltpu.VMEM((tokens, 512), bf),
        pltpu.VMEM((tokens, 512), f32),
        pltpu.VMEM((tokens, 256), f32),
        pltpu.VMEM((tokens, 512), f32),
        pltpu.VMEM((tokens, 512), f32),
        pltpu.VMEM((tokens, 512), bf),
        pltpu.VMEM((width // TILE, TILE, tokens), bf),
        pltpu.VMEM((2, rows, width), f32),
        pltpu.VMEM((tokens, width), bf),
        pltpu.VMEM((2, 4, TILE, tokens), bf),
        pltpu.VMEM((2, TILE, tokens), bf),
        pltpu.VMEM((2, TILE, width), bf),
        pltpu.VMEM((2, tokens, TILE), f32),
        pltpu.VMEM((slots * rows, 2 * rows), f32),
        pltpu.VMEM((tokens, 1), f32),
        pltpu.VMEM((seqs, rows, half), bf),
        pltpu.VMEM((seqs, rows, half), bf),
        pltpu.VMEM((seqs, 2, rows, half), bf),
        pltpu.VMEM((seqs, rows, half), bf),
        dma((seqs,)), dma((5,)), dma((9,)), dma((2,)),
        *(dma((seqs, 4)) for _ in range(5)),
        dma((6,)), dma((seqs,)), dma((2,)),
        *(dma((seqs,)) for _ in range(6)),
    ]
    any_spec = pl.BlockSpec(memory_space=pl.ANY)
    vmem_spec = pl.BlockSpec(memory_space=pltpu.VMEM)
    smem_spec = pl.BlockSpec(memory_space=pltpu.SMEM)
    return pl.pallas_call(
        forward_kernel,
        out_shape=[
            jax.ShapeDtypeStruct((tokens, width), f32),
            jax.ShapeDtypeStruct((width // TILE, TILE, tokens), bf),
            jax.ShapeDtypeStruct((tokens, 512), bf),
            jax.ShapeDtypeStruct(kv_shape, bf),
            jax.ShapeDtypeStruct((tokens, 512), f32),
            jax.ShapeDtypeStruct((tokens, 512), f32),
            jax.ShapeDtypeStruct((tokens, 512), bf),
            jax.ShapeDtypeStruct((tokens, 512), f32),
            jax.ShapeDtypeStruct((tokens, 256), f32),
            jax.ShapeDtypeStruct((2, 4, TILE, tokens), bf),
            jax.ShapeDtypeStruct((hidden // TILE, tokens, TILE), f32),
            jax.ShapeDtypeStruct((seqs, 2, 1, 2 * rows), f32),
        ],
        in_specs=[any_spec] * len(hbm) + [vmem_spec] * len(vmem) + [smem_spec] * len(smem),
        out_specs=[any_spec] * 11 + [vmem_spec],
        scratch_shapes=scratch,
        compiler_params=pltpu.CompilerParams(
            collective_id=2, has_side_effects=True, vmem_limit_bytes=60 << 20
        ),
    )(*hbm, *vmem, *smem)


def on_device(
    x_in,
    cot,
    domain_ids,
    domain_counts,
    domain_weights,
    block_order,
    norm1,
    w_query,
    w_key,
    w_value,
    w_gate_attn,
    w_out,
    query_gain,
    key_gain,
    norm2,
    w_gate,
    w_up,
    w_down,
):
    sequences, local_rows, width = x_in.shape
    row_total = sequences * local_rows
    devices = lax.axis_size("seq")
    x_rows = x_in.reshape(row_total, width)
    scalars = (block_order, domain_counts, domain_weights)
    h, xt, query, kv, attn, sig, gated, query_raw, key_raw, ltd, dm, lse = forward_call(
        (x_rows, w_query, w_key, w_value, w_gate_attn, w_out, cot.reshape(row_total, width), w_down),
        (domain_ids, norm1[None, :], query_gain[None, :], key_gain[None, :]),
        scalars,
        (row_total, width, sequences, local_rows, devices, w_down.shape[0]),
    )
    out, x_grad, down, gate, up, wout, wga, wquery, wkey, wvalue, *small = back_call(
        (
            h,
            cot.reshape(row_total, width),
            x_rows,
            xt,
            ltd,
            dm,
            query,
            kv.reshape(sequences, devices * local_rows, -1),
            attn,
            sig,
            gated,
            query_raw,
            key_raw,
            w_gate,
            w_up,
            w_down,
            w_out,
            w_query,
            w_key,
            w_value,
            w_gate_attn,
        ),
        (
            domain_ids,
            lse,
            norm1[None, :],
            norm2[None, :],
            query_gain[None, :],
            key_gain[None, :],
        ),
        scalars,
        (row_total, width, sequences, local_rows, local_rows * devices, w_down.shape[0]),
    )

    return (
        out.reshape(x_in.shape),
        x_grad.reshape(x_in.shape),
        small[0].reshape(-1),
        wquery,
        wkey,
        wvalue,
        wga,
        wout,
        small[2].reshape(-1),
        small[3].reshape(-1),
        small[1].reshape(-1),
        gate,
        up,
        down,
    )


def on_device_plain(
    x_in,
    cot,
    domain_ids,
    domain_counts,
    domain_weights,
    block_order,
    norm1,
    w_query,
    w_key,
    w_value,
    w_gate_attn,
    w_out,
    query_gain,
    key_gain,
    norm2,
    w_gate,
    w_up,
    w_down,
):
    sequences, local_rows, model_width = x_in.shape
    row_total = sequences * local_rows
    head_dim = query_gain.shape[0]
    kv_local = w_key.shape[1] // head_dim
    q_local = w_query.shape[1] // head_dim
    group_size = q_local // kv_local
    block_rows = local_rows // 2
    seq_devices = lax.axis_size("seq")
    first_row = lax.axis_index("seq") * local_rows
    query_pos = positions(block_order, first_row, local_rows, block_rows)
    query_factor = head_dim ** (-0.5)
    q_gain = query_gain.astype(jnp.float32)
    k_gain = key_gain.astype(jnp.float32)
    gain_one = norm1.astype(jnp.float32)
    gain_two = norm2.astype(jnp.float32)
    x_float = x_in.reshape(row_total, model_width).astype(jnp.float32)
    scale_one = norm_scale(x_float)
    normed_one = x_float * scale_one
    x_normed = (normed_one * gain_one).astype(jnp.bfloat16)
    query_raw = product(x_normed, w_query).reshape(row_total, q_local, head_dim)
    key_raw = product(x_normed, w_key).reshape(row_total, kv_local, head_dim)
    value_rows = product(x_normed, w_value).astype(jnp.bfloat16)
    gate_pre = product(x_normed, w_gate_attn)
    query_scale = norm_scale(query_raw)
    query_normed = query_raw * query_scale
    key_scale = norm_scale(key_raw)
    key_normed = key_raw * key_scale
    query = (query_normed * q_gain * query_factor).astype(jnp.bfloat16)
    key_rows = (key_normed * k_gain).astype(jnp.bfloat16)
    project_query_heads = query.reshape(
        sequences, local_rows, kv_local, group_size, head_dim
    ).transpose(0, 2, 3, 1, 4)
    (
        query_scale,
        query_normed,
        key_scale,
        key_normed,
        query_heads,
        key_rows,
        value_rows,
        gate_pre,
    ) = (
        query_scale,
        query_normed,
        key_scale,
        key_normed,
        project_query_heads,
        key_rows,
        value_rows,
        gate_pre,
    )
    key_seq = key_rows.reshape(sequences, local_rows, kv_local * head_dim)
    value_seq = value_rows.reshape(sequences, local_rows, kv_local * head_dim)
    stat_shape = (sequences, kv_local, group_size, local_rows)
    running_max = jnp.full(stat_shape, -1e30, jnp.float32)
    key_piece = lax.all_gather(key_seq, "seq", axis=1, tiled=True)
    value_piece = lax.all_gather(value_seq, "seq", axis=1, tiled=True)
    row_count = key_piece.shape[1]
    key_block = key_piece.reshape(sequences, row_count, kv_local, head_dim)
    value_block = value_piece.reshape(sequences, row_count, kv_local, head_dim)
    key_pos = positions(block_order, jnp.int32(0), row_count, block_rows)
    allowed = key_pos[None, :] <= query_pos[:, None]
    scores = jnp.einsum(
        "skgqd,spkd->skgqp", query_heads, key_block, preferred_element_type=jnp.float32
    )
    scores = jnp.where(allowed, scores, -1e30)
    new_max = jnp.maximum(running_max, jnp.max(scores, axis=-1))
    weights = jnp.where(allowed, jnp.exp(scores - new_max[..., None]), 0.0)
    running_sum = jnp.sum(weights, axis=-1)
    weighted = jnp.einsum(
        "skgqp,spkd->skgqd",
        weights.astype(jnp.bfloat16),
        value_block,
        preferred_element_type=jnp.float32,
    )
    running_max, running_sum, weighted = (new_max, running_sum, weighted)
    log_total = running_max + jnp.log(running_sum)
    attn_heads = weighted / running_sum[..., None]
    attn_flat = attn_heads.transpose(0, 3, 1, 2, 4).reshape(row_total, q_local * head_dim)
    gate_sig = jax.nn.sigmoid(gate_pre)
    gated = (attn_flat * gate_sig).astype(jnp.bfloat16)
    attn_sum = lax.psum(product(gated, w_out).astype(jnp.bfloat16), "head").astype(jnp.float32)
    residual = x_float + attn_sum
    scale_two = norm_scale(residual)
    normed_two = residual * scale_two
    h_normed = (normed_two * gain_two).astype(jnp.bfloat16)
    gate_proj = product(h_normed, w_gate)
    up_proj = product(h_normed, w_up)
    gate_logit = jax.nn.sigmoid(gate_proj)
    gate_act = gate_proj * gate_logit
    mixed = (gate_act * up_proj).astype(jnp.bfloat16)
    mlp_sum = lax.psum(product(mixed, w_down).astype(jnp.bfloat16), "head").astype(jnp.float32)
    block_out = (
        (residual + mlp_sum).astype(jnp.bfloat16).reshape(sequences, local_rows, model_width)
    )
    domain_total = domain_weights.shape[0]
    domain_index = jnp.arange(domain_total, dtype=jnp.int32)
    factor = (
        domain_weights
        * (row_total * seq_devices)
        / (domain_total * domain_counts.astype(jnp.float32))
    )
    picked = domain_ids.reshape(row_total)[:, None] == domain_index[None, :]
    row_scale = jnp.sum(jnp.where(picked, factor[None, :], 0.0), axis=1)
    grad_out = cot.reshape(row_total, model_width).astype(jnp.float32) * row_scale[:, None]
    grad_low = grad_out.astype(jnp.bfloat16)
    grad_down = outer_sum(mixed, grad_low)
    grad_mixed = back_product(grad_low, w_down)
    grad_gate = (grad_mixed * up_proj * gate_logit * (1.0 + gate_proj * (1.0 - gate_logit))).astype(
        jnp.bfloat16
    )
    grad_up = (grad_mixed * gate_act).astype(jnp.bfloat16)
    grad_mlp_gate = outer_sum(h_normed, grad_gate)
    grad_mlp_up = outer_sum(h_normed, grad_up)
    grad_hnorm = lax.psum(
        (back_product(grad_gate, w_gate) + back_product(grad_up, w_up)).astype(jnp.bfloat16), "head"
    ).astype(jnp.float32)
    grad_norm_two = jnp.sum(grad_hnorm * normed_two, axis=0)
    grad_resid = grad_out + norm_back(grad_hnorm, normed_two, scale_two, gain_two)
    grad_attn = grad_resid.astype(jnp.bfloat16)
    grad_wout = outer_sum(gated, grad_attn)
    grad_gated = back_product(grad_attn, w_out)
    grad_heads_flat = (grad_gated * gate_sig).astype(jnp.bfloat16)
    grad_gatepre = (grad_gated * attn_flat * gate_sig * (1.0 - gate_sig)).astype(jnp.bfloat16)
    grad_wgate_attn = outer_sum(x_normed, grad_gatepre)
    grad_heads = grad_heads_flat.reshape(
        sequences, local_rows, kv_local, group_size, head_dim
    ).transpose(0, 2, 3, 1, 4)
    row_delta = jnp.sum(grad_heads.astype(jnp.float32) * attn_heads, axis=-1)
    key_piece = lax.all_gather(key_seq, "seq", axis=1, tiled=True)
    value_piece = lax.all_gather(value_seq, "seq", axis=1, tiled=True)
    row_count = key_piece.shape[1]
    key_block = key_piece.reshape(sequences, row_count, kv_local, head_dim)
    value_block = value_piece.reshape(sequences, row_count, kv_local, head_dim)
    key_pos = positions(block_order, jnp.int32(0), row_count, block_rows)
    allowed = key_pos[None, :] <= query_pos[:, None]
    scores = jnp.einsum(
        "skgqd,spkd->skgqp", query_heads, key_block, preferred_element_type=jnp.float32
    )
    probs = jnp.where(
        allowed, jnp.exp(jnp.where(allowed, scores, -1e30) - log_total[..., None]), 0.0
    )
    grad_probs = jnp.einsum(
        "skgqd,spkd->skgqp", grad_heads, value_block, preferred_element_type=jnp.float32
    )
    grad_scores = (probs * (grad_probs - row_delta[..., None])).astype(jnp.bfloat16)
    grad_query = jnp.einsum(
        "skgqp,spkd->skgqd", grad_scores, key_block, preferred_element_type=jnp.float32
    )
    key_term = jnp.einsum(
        "skgqp,skgqd->spkd", grad_scores, query_heads, preferred_element_type=jnp.float32
    ).reshape(sequences, row_count, kv_local * head_dim)
    value_term = jnp.einsum(
        "skgqp,skgqd->spkd",
        probs.astype(jnp.bfloat16),
        grad_heads,
        preferred_element_type=jnp.float32,
    ).reshape(sequences, row_count, kv_local * head_dim)
    grad_keys = key_term
    grad_values = value_term
    grad_query, grad_keys, grad_values = (grad_query, grad_keys, grad_values)
    grad_key_own, grad_value_own = (
        lax.psum_scatter(
            grad_keys.astype(jnp.bfloat16), "seq", scatter_dimension=1, tiled=True
        ).astype(jnp.float32),
        lax.psum_scatter(
            grad_values.astype(jnp.bfloat16), "seq", scatter_dimension=1, tiled=True
        ).astype(jnp.float32),
    )
    grad_query_rows = grad_query.transpose(0, 3, 1, 2, 4).reshape(row_total, q_local, head_dim)
    grad_qgain_part = jnp.sum(grad_query_rows * query_normed * query_factor, axis=(0, 1))
    grad_query_raw = (
        norm_back(grad_query_rows, query_normed, query_scale, q_gain * query_factor)
        .astype(jnp.bfloat16)
        .reshape(row_total, q_local * head_dim)
    )
    grad_key_rows = grad_key_own.reshape(row_total, kv_local, head_dim)
    grad_kgain_part = jnp.sum(grad_key_rows * key_normed, axis=(0, 1))
    grad_key_raw = (
        norm_back(grad_key_rows, key_normed, key_scale, k_gain)
        .astype(jnp.bfloat16)
        .reshape(row_total, kv_local * head_dim)
    )
    grad_value_low = grad_value_own.reshape(row_total, kv_local * head_dim).astype(jnp.bfloat16)
    grad_xnorm_part = (
        back_product(grad_query_raw, w_query)
        + back_product(grad_key_raw, w_key)
        + back_product(grad_value_low, w_value)
        + back_product(grad_gatepre, w_gate_attn)
    )
    grad_xnorm, grad_qgain, grad_kgain = (
        lax.psum(grad_xnorm_part.astype(jnp.bfloat16), "head").astype(jnp.float32),
        lax.psum(grad_qgain_part.astype(jnp.bfloat16), "head").astype(jnp.float32),
        lax.psum(grad_kgain_part.astype(jnp.bfloat16), "head").astype(jnp.float32),
    )
    grad_norm_one = jnp.sum(grad_xnorm * normed_one, axis=0)
    x_grad = (
        (grad_resid + norm_back(grad_xnorm, normed_one, scale_one, gain_one))
        .astype(jnp.bfloat16)
        .reshape(sequences, local_rows, model_width)
    )
    grad_wquery = outer_sum(x_normed, grad_query_raw)
    grad_wkey = outer_sum(x_normed, grad_key_raw)
    grad_wvalue = outer_sum(x_normed, grad_value_low)
    all_totals = (
        lax.psum_scatter(
            grad_norm_one.astype(jnp.bfloat16), "seq", scatter_dimension=0, tiled=True
        ).astype(jnp.float32),
        lax.psum_scatter(
            grad_wquery.astype(jnp.bfloat16), "seq", scatter_dimension=0, tiled=True
        ).astype(jnp.float32),
        lax.psum_scatter(
            grad_wkey.astype(jnp.bfloat16), "seq", scatter_dimension=0, tiled=True
        ).astype(jnp.float32),
        lax.psum_scatter(
            grad_wvalue.astype(jnp.bfloat16), "seq", scatter_dimension=0, tiled=True
        ).astype(jnp.float32),
        lax.psum_scatter(
            grad_wgate_attn.astype(jnp.bfloat16), "seq", scatter_dimension=0, tiled=True
        ).astype(jnp.float32),
        lax.psum_scatter(
            grad_wout.astype(jnp.bfloat16), "seq", scatter_dimension=1, tiled=True
        ).astype(jnp.float32),
        lax.psum_scatter(
            grad_qgain.astype(jnp.bfloat16), "seq", scatter_dimension=0, tiled=True
        ).astype(jnp.float32),
        lax.psum_scatter(
            grad_kgain.astype(jnp.bfloat16), "seq", scatter_dimension=0, tiled=True
        ).astype(jnp.float32),
        lax.psum_scatter(
            grad_mlp_gate.astype(jnp.bfloat16), "seq", scatter_dimension=0, tiled=True
        ).astype(jnp.float32),
        lax.psum_scatter(
            grad_mlp_up.astype(jnp.bfloat16), "seq", scatter_dimension=0, tiled=True
        ).astype(jnp.float32),
        lax.psum_scatter(
            grad_down.astype(jnp.bfloat16), "seq", scatter_dimension=1, tiled=True
        ).astype(jnp.float32),
        lax.psum_scatter(
            grad_norm_two.astype(jnp.bfloat16), "seq", scatter_dimension=0, tiled=True
        ).astype(jnp.float32),
    )
    return (
        block_out,
        x_grad,
        all_totals[0],
        all_totals[1],
        all_totals[2],
        all_totals[3],
        all_totals[4],
        all_totals[5],
        all_totals[6],
        all_totals[7],
        all_totals[11],
        all_totals[8],
        all_totals[9],
        all_totals[10],
    )


def solution(mesh):
    fits = mesh.shape["seq"] == 8 and mesh.shape["head"] == 4
    return jax.shard_map(
        on_device if fits else on_device_plain,
        mesh=mesh,
        in_specs=(
            P(None, "seq", None),
            P(None, "seq", None),
            P(None, "seq"),
            P(),
            P(),
            P(),
            P(),
            P(None, "head"),
            P(None, "head"),
            P(None, "head"),
            P(None, "head"),
            P("head", None),
            P(),
            P(),
            P(),
            P(None, "head"),
            P(None, "head"),
            P("head", None),
        ),
        out_specs=(
            P(None, "seq", None),
            P(None, "seq", None),
            P("seq"),
            P("seq", "head"),
            P("seq", "head"),
            P("seq", "head"),
            P("seq", "head"),
            P("head", "seq"),
            P("seq"),
            P("seq"),
            P("seq"),
            P("seq", "head"),
            P("seq", "head"),
            P("head", "seq"),
        ),
        check_vma=False,
    )
```

```python
import functools

import jax
import jax.numpy as jnp
from jax import lax
from jax.experimental import pallas as pl
from jax.experimental.pallas import tpu as pltpu
from jax.sharding import PartitionSpec as P

epsilon = 1e-06


def norm_scale(value):
    return lax.rsqrt(jnp.mean(value * value, axis=-1, keepdims=True) + epsilon)


def norm_back(grad_in, normed, scale, gain):
    scaled = grad_in * gain
    return scale * (scaled - normed * jnp.mean(scaled * normed, axis=-1, keepdims=True))


def product(left, right):
    return jnp.dot(left, right, preferred_element_type=jnp.float32)


def outer_sum(left, right):
    return lax.dot_general(
        left, right, (((0,), (0,)), ((), ())), preferred_element_type=jnp.float32
    )


def back_product(left, right):
    return lax.dot_general(
        left, right, (((1,), (1,)), ((), ())), preferred_element_type=jnp.float32
    )


def low(value):
    return value.astype(jnp.bfloat16)


def wide(value):
    return value.astype(jnp.float32)


def positions(block_order, device, row_count, block_rows):
    stored = device * row_count + jnp.arange(row_count, dtype=jnp.int32)
    slots = stored // block_rows
    slot_index = jnp.arange(block_order.shape[0], dtype=jnp.int32)
    picked = jnp.sum(
        jnp.where(slots[:, None] == slot_index[None, :], block_order[None, :], 0), axis=1
    )
    return picked * block_rows + stored % block_rows


MESH = pl.DeviceIdType.MESH
TILE = 256


PLAN = {
    "p1.0": (
        ("a", 0),
    ),
    "p1.3": (
        ("a", 1), ("s1", 0),
    ),
    "p1.5": (
        ("a", 2), ("r1", 0),
    ),
    "p2.0": (
        ("a", 3), ("s1", 1),
    ),
    "p2.1": (
        ("s2", 0),
    ),
    "p2.2": (
        ("r2", 0), ("a", 4), ("s1", 2),
    ),
    "p2.4": (
        ("a", 5), ("s1", 3), ("s3", 0), ("s2", 1),
    ),
    "p2.6": (
        ("a", 6), ("s1", 4), ("s4", 0),
    ),
    "p3.0": (
        ("s2", 2), ("a", 7), ("s3", 1), ("s1", 5),
    ),
    "p3.2": (
        ("a", 8), ("s4", 1), ("s2", 3), ("s1", 6), ("s3", 2),
    ),
    "p3.4": (
        ("a", 9),
    ),
    "p3.6": (
        ("s2", 4), ("s1", 7), ("a", 10), ("s3", 3), ("s4", 2),
    ),
    "e0.3": (
        ("s4", 3), ("s2", 5), ("s1", 8), ("a", 11), ("s3", 4),
    ),
    "p4b": (
        ("s2", 6), ("s1", 9), ("a", 12), ("s3", 5),
    ),
    "p5.0": (
        ("s2", 7), ("s1", 10), ("s3", 6),
    ),
    "p5.1": (
        ("s2", 8), ("s1", 11), ("s3", 7),
    ),
    "p5.2": (
        ("ky", 0), ("s2", 9), ("s3", 8),
    ),
    "p5.3": (
        ("s2", 10), ("s1", 12), ("ky", 1), ("s3", 9),
    ),
    "qp": (
        ("s2", 11),
    ),
    "e1.3": (
        ("s4", 4), ("s4", 5), ("s3", 10), ("s4", 6), ("s4", 7), ("s4", 8), ("s4", 9), ("kl", 0), ("ky", 2),
    ),
    "op": (
        ("s3", 11), ("s4", 10), ("s2", 12), ("km", 0), ("ky", 3), ("s4", 11), ("a", 13), ("kl", 1), ("r1", 3),
        ("s3", 12), ("a", 14), ("r1", 2), ("s4", 12), ("kl", 2), ("km", 1), ("r2", 3), ("a", 15), ("s1", 13),
        ("r2", 2), ("a", 16), ("kl", 3), ("s1", 14), ("km", 2), ("a", 17), ("s1", 15), ("s2", 13), ("km", 3),
        ("a", 18), ("s1", 16),
    ),
    "kp": (
        ("a", 19), ("s2", 14), ("s1", 17), ("s3", 13),
    ),
    "p7.0": (
        ("a", 20),
    ),
    "p7.1": (
        ("s2", 15), ("s1", 18),
    ),
    "p7.2": (
        ("a", 21), ("s3", 14), ("s4", 13),
    ),
    "p7.4": (
        ("s2", 16), ("s1", 19), ("a", 22), ("s3", 15), ("s4", 14),
    ),
    "p7.7": (
        ("s2", 17), ("s1", 20), ("a", 23), ("s3", 16),
    ),
    "e2.1": (
        ("s4", 15),
    ),
    "e2.2": (
        ("s2", 18), ("s1", 21), ("a", 24), ("s3", 17),
    ),
    "e2.3": (
        ("s4", 16),
    ),
    "lp": (
        ("s2", 19), ("s1", 22), ("a", 25), ("s3", 18),
    ),
    "vec": (
        ("s2", 20), ("s1", 23), ("s4", 17), ("s3", 19), ("s4", 18), ("s2", 21), ("s1", 24), ("s4", 19),
        ("s3", 20), ("s2", 22), ("s1", 25), ("s3", 21), ("s4", 20), ("s4", 21), ("s2", 23), ("s3", 22),
        ("s4", 22), ("s2", 24), ("s3", 23), ("s4", 23), ("s2", 25), ("s3", 24), ("s4", 24), ("s3", 25),
        ("s4", 25),
    ),
}


def other_z(z, t):
    low_z, high_z = lax.rem(z, 2), lax.div(z, 2)
    low_t, high_t = lax.rem(t, 2), lax.div(t, 2)
    return (low_z + low_t - 2 * low_z * low_t) + 2 * (high_z + high_t - 2 * high_z * high_t)


def fill_bias(order_ref, bias, rows, z, y, seq):
    block = bias.shape[0] // order_ref.shape[0]
    each = rows // block
    lane = lax.broadcasted_iota(jnp.int32, (block, bias.shape[1]), 1)
    down = lax.broadcasted_iota(jnp.int32, (block, bias.shape[1]), 0)
    within = lax.rem(lane, rows)
    query = lax.rem(lane, block)
    for i in range(each):
        query += jnp.where(lax.div(within, block) == i, order_ref[seq * each + i] * block, 0)
    for j in range(8):
        other_y = 1 - y if j % 2 else y
        device = other_z(z, j // 2) * 2 + other_y
        for i in range(each):
            key = order_ref[device * each + i] * block + down
            bias[j * rows + i * block : j * rows + (i + 1) * block] = jnp.where(key <= query, 0.0, -1e30)


def fill_factor(ids_ref, counts_ref, weights_ref, factor, total):
    seqs, rows = ids_ref.shape
    domains = counts_ref.shape[0]
    across = jnp.zeros((seqs, rows), jnp.float32)
    ids = ids_ref[...]
    for d in range(domains):
        count = jnp.full((seqs, rows), counts_ref[d], jnp.int32).astype(jnp.float32)
        weight = jnp.full((seqs, rows), weights_ref[d], jnp.float32) * total / (domains * count)
        across = jnp.where(ids == d, weight, across)
    here = lax.broadcasted_iota(jnp.int32, (rows, rows), 0) == lax.broadcasted_iota(
        jnp.int32, (rows, rows), 1
    )
    for s in range(seqs):
        spread = jnp.where(here, across[s : s + 1], 0.0)
        factor[s * rows : (s + 1) * rows] = jnp.sum(spread, axis=1, keepdims=True)


def dot_plain(left, right):
    return jnp.dot(left, right, preferred_element_type=jnp.float32)


def dot_rows(left, right):
    return lax.dot_general(
        left, right, (((1,), (1,)), ((), ())), preferred_element_type=jnp.float32
    )


def dot_first(left, right):
    return lax.dot_general(
        left, right, (((0,), (0,)), ((), ())), preferred_element_type=jnp.float32
    )


def back_kernel(
    h_hbm, cot_hbm, x_hbm, xt_hbm, ltd_hbm, dm_hbm, q_hbm, kv_hbm, o_hbm, sig_hbm, y_hbm, qraw_hbm, kraw_hbm,
    wg_hbm, wu_hbm, wd_hbm, wo_hbm, wq_hbm, wk_hbm, wv_hbm, wga_hbm,
    ids_ref, lse_ref, n1_ref, n2_ref, qg_ref, kg_ref, order_ref, counts_ref, weights_ref,
    block_out, x_out, dwd_out, dwg_out, dwu_out, dwo_out, dwga_out, dwq_out, dwk_out, dwv_out,
    n1_out, n2_out, qg_out, kg_out, dh_hbm, z1_hbm, z2_hbm, z3_hbm,
    acts, lt, odd, csend, crecv, xrecv, fin, yrecv, lrecv, mrecv, hrecv,
    zsend, stage, ostage, wide_a, wide_b, delta,
    vec, vec_got, gvec, gvec_got, bias, factor_ref,
    ya_s, ya_r, z1_s, z1_r, z2_s, z2_r, z3_s, z3_r, lt_s, lt_r, lc_s, lc_r, lx_s, lx_r, lf_s, lf_r,
    c1_s, c1_r, x_s, x_r, c2_s, c2_r, ky_s, ky_r, kl_s, kl_r, km_s, km_r, kh_s, kh_r,
    nv_s, nv_r, gv_s, gv_r, st_sem, out_sem, misc, credit,
):
    seq, head = lax.axis_index("seq"), lax.axis_index("head")
    z, y = lax.div(seq, 2), lax.rem(seq, 2)
    c = lax.rem(head, 2)
    y_dev = {"seq": z * 2 + 1 - y}
    lo_dev = {"seq": other_z(z, 1) * 2 + y}
    hi_dev = {"seq": other_z(z, 2) * 2 + y}
    mid_dev = {"seq": (3 - z) * 2 + y}
    core_dev = {"head": head + 1 - 2 * c}
    x_dev = {"head": head + 2 - 4 * lax.div(head, 2)}
    at_end, inside = lax.rem(z, 3) == 0, lax.rem(z, 3) != 0
    tokens = cot_hbm.shape[0]
    rows = bias.shape[0] // 8
    seqs = tokens // rows
    hidden_tiles = wd_hbm.shape[0] // TILE
    ff_items = 3 * hidden_tiles
    width = cot_hbm.shape[1]
    epsilon_k = 1e-06

    barrier = pltpu.get_barrier_semaphore()
    for device in (y_dev, lo_dev, hi_dev, core_dev, x_dev):
        pl.semaphore_signal(barrier, inc=1, device_id=device, device_id_type=MESH)

    @pl.when(inside)
    def _():
        pl.semaphore_signal(barrier, inc=1, device_id=mid_dev, device_id_type=MESH)
        pl.semaphore_wait(barrier, 6)

    @pl.when(at_end)
    def _():
        pl.semaphore_wait(barrier, 5)


    def remote(src, dst, send, recv, device):
        return pltpu.make_async_remote_copy(
            src_ref=src, dst_ref=dst, send_sem=send, recv_sem=recv, device_id=device, device_id_type=MESH
        )

    def act_copy(i):
        return remote(acts.at[i, 0], acts.at[i, 1], ya_s.at[i], ya_r.at[i], y_dev)

    def lt_copy(l):
        return remote(odd.at[l], lt.at[l, 1, head], lt_s.at[l], lt_r.at[l], y_dev)

    x_head = head + 2 - 4 * lax.div(head, 2)
    core_head = head + 1 - 2 * c
    far_head = x_head + 1 - 2 * c

    def lt_core(l, part):
        piece = lt.at[l, 1, part]
        return remote(piece, piece, lc_s.at[l], lc_r.at[l], core_dev)

    def lt_x(l, part):
        piece = lt.at[l, 1, part]
        return remote(piece, piece, lx_s.at[l], lx_r.at[l], x_dev)

    def lt_far(l, part):
        piece = lt.at[l, 1, part]
        return remote(piece, piece, lf_s.at[l], lf_r.at[l], core_dev)

    def z1_copy(i):
        return remote(zsend.at[i % 4], z1_hbm.at[i], z1_s.at[i], z1_r.at[i], lo_dev)

    def z2_copy(i):
        return remote(zsend.at[i % 4, pl.ds(0, 2)], z2_hbm.at[i], z2_s.at[i], z2_r.at[i], mid_dev)

    def z3_copy(i):
        return remote(zsend.at[i % 4, 2], z3_hbm.at[i], z3_s.at[i], z3_r.at[i], lo_dev)

    def item_dot(i, l, first, last):
        count = (last - first) * TILE
        mine = dot_plain(lt[l, 0, first:last].reshape(count, tokens), acts[i, 0])
        return mine + dot_plain(lt[l, 1, first:last].reshape(count, tokens), acts[i, 1])

    def stage_load(src, slot):
        copy = pltpu.make_async_copy(src, stage.at[slot], st_sem.at[slot])
        copy.start()
        return copy

    def stage_one(i, l, place):
        act_copy(i).wait_recv()

        @pl.when(at_end)
        def _():
            if i >= 4:
                z1_copy(i - 4).wait_send()
            total = item_dot(i, l, 1, 4)
            for k in range(3):
                zsend[i % 4, k] = low(total[k * TILE : (k + 1) * TILE])
            z1_copy(i).start()

    def stage_two(i, l, place):
        @pl.when(inside)
        def _():
            z1_copy(i).wait_recv()
            loads = [stage_load(z1_hbm.at[i, k], k) for k in (1, 2)]
            if i >= 4:
                z2_copy(i - 4).wait_send()
            total = item_dot(i, l, 2, 4)
            for load in loads:
                load.wait()
            zsend[i % 4, 0] = low(total[:TILE] + wide(stage[2]))
            zsend[i % 4, 1] = low(total[TILE:] + wide(stage[1]))
            z2_copy(i).start()

    def out_wait(i):
        pltpu.make_async_copy(ostage.at[i % 2], dwk_out, out_sem.at[i % 2]).wait()

    def put(i, total, place):
        ref, n, turned = place
        if i >= 2:
            out_wait(i - 2)
        ostage[i % 2] = total.T if turned else total
        at = pl.ds(n * TILE, TILE)
        target = ref.at[at] if turned else ref.at[:, at]
        pltpu.make_async_copy(ostage.at[i % 2], target, out_sem.at[i % 2]).start()

    def stage_three(i, l, place):
        @pl.when(inside)
        def _():
            z2_copy(i).wait_recv()
            loads = [stage_load(z1_hbm.at[i, 0], 0), stage_load(z2_hbm.at[i, 0], 1), stage_load(z2_hbm.at[i, 1], 2)]
            if i >= 4:
                z3_copy(i - 4).wait_send()
            total = item_dot(i, l, 0, 2)
            for load in loads:
                load.wait()
            zsend[i % 4, 2] = low(total[TILE:] + wide(stage[1]))
            z3_copy(i).start()
            put(i, total[:TILE] + wide(stage[0]) + wide(stage[2]), place)

    def stage_four(i, l, place):
        @pl.when(at_end)
        def _():
            z3_copy(i).wait_recv()
            load = stage_load(z3_hbm.at[i], 3)
            total = item_dot(i, l, 0, 1)
            load.wait()
            put(i, total + wide(stage[3]), place)

    def at_tile(j, kind):
        later = j // 3 if isinstance(j, int) else lax.div(j, 3)
        if kind == 0:
            return j + 2 * j * later
        return (2 + 2 * j + kind) * (1 - later) + (3 * j + kind) * later

    ff_kind = {at_tile(j, kind): (j, kind) for j in range(hidden_tiles) for kind in range(3)}
    late = (
        (3, dwo_out, 0, True),
        (3, dwo_out, 1, True),
        (2, dwga_out, 0, False),
        (2, dwga_out, 1, False),
        (2, dwq_out, 0, False),
        (2, dwq_out, 1, False),
        (2, dwk_out, 0, False),
        (2, dwv_out, 0, False),
    )
    item_count = ff_items + 8
    shown = set()
    ltd_load = pltpu.make_async_copy(ltd_hbm, lt.at[1], misc.at[7])

    def item_step(stage_of, i):
        l = (1 if ff_kind[i][1] == 0 else 0) if i < ff_items else late[i - ff_items][0]
        if stage_of is stage_one and l not in shown:
            shown.add(l)
            if l == 1:
                ltd_load.wait()
            else:
                relay_in(l)
        if i < ff_items:
            j, kind = ff_kind[i]
            place = ((dwd_out, dwg_out, dwu_out)[kind], j, kind == 0)
        else:
            place = late[i - ff_items][1:]
        stage_of(i, l, place)

    actions = {
        "a": lambda i: act_copy(i).start(),
        "s1": lambda i: item_step(stage_one, i),
        "s2": lambda i: item_step(stage_two, i),
        "s3": lambda i: item_step(stage_three, i),
        "s4": lambda i: item_step(stage_four, i),
        "r1": lambda l: relay_one(l),
        "r2": lambda l: relay_two(l),
    }

    def after(place):
        for name, i in PLAN.get(place, ()):
            actions[name](i)

    def after_step(place, step, count):
        for k in range(count):
            if f"{place}.{k}" in PLAN:
                pl.when(step == k)(lambda k=k: after(f"{place}.{k}"))

    def spread(l, source):
        @pl.loop(0, 4)
        def _(t):
            at = pl.multiple_of((other_z(z, t) * 2 + y) * TILE, TILE)
            lt[l, 0, t] = source[:, pl.ds(at, TILE)].T

        at = pl.multiple_of((other_z(z, head) * 2 + 1 - y) * TILE, TILE)
        odd[l] = source[:, pl.ds(at, TILE)].T

    def relay_one(l):
        lt_copy(l).wait_recv()
        lt_core(l, head).start()
        lt_x(l, head).start()

    def relay_two(l):
        lt_x(l, x_head).wait_recv()
        lt_far(l, x_head).start()

    def relay_in(l):
        lt_core(l, core_head).wait_recv()
        lt_far(l, far_head).wait_recv()

    def core_copy(k, b):
        return remote(csend.at[b], crecv.at[k % 2, b], c1_s.at[k, b], c1_r.at[k, b], core_dev)

    def x_copy(k, b):
        return remote(fin.at[k % 2, c * 4 + b], xrecv.at[k % 2, b], x_s.at[k, b], x_r.at[k, b], x_dev)

    def fin_copy(k, b):
        piece = fin.at[k % 2, c * 4 + b]
        return remote(piece, piece, c2_s.at[k, b], c2_r.at[k, b], core_dev)

    def fin_copy_in(k, b):
        piece = fin.at[k % 2, (1 - c) * 4 + b]
        return remote(piece, piece, c2_s.at[k, b], c2_r.at[k, b], core_dev)

    def reduce_start(k, loads, compute, place):
        def block_of(step):
            return lax.rem(c + 1 + step, 2) * 4 + lax.div(step, 2)

        for copy in loads(block_of(0), 0):
            copy.start()

        @pl.loop(0, 8)
        def _(step):
            slot, b = lax.rem(step, 2), lax.div(step, 2)

            @pl.when(step < 7)
            def _():
                for copy in loads(block_of(step + 1), 1 - slot):
                    copy.start()

            for copy in loads(block_of(step), slot):
                copy.wait()
            part = compute(slot)

            @pl.when(slot == 0)
            def _():
                csend[b] = low(part)
                core_copy(k, b).start()

            @pl.when(slot == 1)
            def _():
                core_copy(k, b).wait_recv()
                fin[k % 2, c * 4 + b] = low(part + wide(crecv[k % 2, b]))
                x_copy(k, b).start()

            after_step(place, step, 8)

        @pl.loop(0, 4)
        def _(b):
            core_copy(k, b).wait_send()

    def reduce_end(k):
        for b in range(4):
            x_copy(k, b).wait()
            fin[k % 2, c * 4 + b] = low(wide(fin[k % 2, c * 4 + b]) + wide(xrecv[k % 2, b]))
            fin_copy(k, b).start()
            after(f"e{k}.{b}")
        for b in range(4):
            fin_copy_in(k, b).wait_recv()
            fin_copy(k, b).wait_send()
        after(f"e{k}.4")

    def fin_rows(k, at, count):
        return jnp.concatenate([wide(fin[k % 2, n, pl.ds(at, count)]) for n in range(8)], axis=1)

    def rms(value):
        return lax.rsqrt(jnp.mean(value * value, axis=-1, keepdims=True) + epsilon_k)

    n_chunks = tokens // 128

    def first_phase(hbuf, wgb, wub, dmb, sems, w_sems):
        def row_load(r, slot):
            return pltpu.make_async_copy(h_hbm.at[pl.ds(r * 128, 128)], hbuf.at[slot], sems.at[slot])

        def tile_loads(j, slot):
            at = pl.ds(pl.multiple_of(j * TILE, TILE), TILE)
            return (
                pltpu.make_async_copy(wg_hbm.at[:, at], wgb.at[slot], w_sems.at[slot, 0]),
                pltpu.make_async_copy(wu_hbm.at[:, at], wub.at[slot], w_sems.at[slot, 1]),
                pltpu.make_async_copy(dm_hbm.at[j], dmb.at[slot], w_sems.at[slot, 2]),
            )

        row_load(0, 0).start()
        for copy in tile_loads(0, 0):
            copy.start()
        ltd_load.start()

        @pl.loop(0, n_chunks)
        def _(r):
            slot = lax.rem(r, 2)

            @pl.when(r < n_chunks - 1)
            def _():
                row_load(r + 1, 1 - slot).start()

            row_load(r, slot).wait()
            value = hbuf[slot]
            at = pl.ds(pl.multiple_of(r * 128, 128), 128)
            wide_a[at] = low(value * rms(value) * wide(n2_ref[...]))

        after("p0")

        @pl.loop(0, hidden_tiles)
        def _(j):
            slot = lax.rem(j, 2)

            @pl.when(j < hidden_tiles - 1)
            def _():
                for copy in tile_loads(j + 1, 1 - slot):
                    copy.start()

            for copy in tile_loads(j, slot):
                copy.wait()

            @pl.loop(0, 2)
            def _(half):
                at = pl.ds(pl.multiple_of(half * (tokens // 2), 128), tokens // 2)
                a = dot_plain(wide_a[at], wgb[slot])
                u = dot_plain(wide_a[at], wub[slot])
                dm = dmb[slot, at]
                sig = jax.nn.sigmoid(a)
                act = a * sig
                acts[at_tile(j, 0), 0, at] = low(act * u)
                acts[at_tile(j, 1), 0, at] = low(dm * u * sig * (1.0 + a * (1.0 - sig)))
                acts[at_tile(j, 2), 0, at] = low(dm * act)

            after_step("p1", j, 1)

            @pl.when(j == 0)
            def _():
                spread(0, wide_a)
                lt_copy(0).start()
                after("sp0")

            for k in range(1, hidden_tiles):
                if f"p1.{k}" in PLAN:
                    pl.when(j == k)(lambda k=k: after(f"p1.{k}"))

    pl.run_scoped(
        first_phase,
        pltpu.VMEM((2, 128, width), jnp.float32),
        pltpu.VMEM((2, width, TILE), jnp.bfloat16),
        pltpu.VMEM((2, width, TILE), jnp.bfloat16),
        pltpu.VMEM((2, tokens, TILE), jnp.float32),
        pltpu.SemaphoreType.DMA((2,)),
        pltpu.SemaphoreType.DMA((2, 3)),
    )

    def second_phase(wa, wb, sems):
        def loads(n, slot):
            at = pl.ds(pl.multiple_of(n * TILE, TILE), TILE)
            return (
                pltpu.make_async_copy(wg_hbm.at[at], wa.at[slot], sems.at[slot, 0]),
                pltpu.make_async_copy(wu_hbm.at[at], wb.at[slot], sems.at[slot, 1]),
            )

        def compute(slot):
            total = None
            for j in range(hidden_tiles):
                at = pl.ds(j * TILE, TILE)
                part = dot_rows(acts[at_tile(j, 1), 0], wa[slot, :, at])
                part += dot_rows(acts[at_tile(j, 2), 0], wb[slot, :, at])
                total = part if total is None else total + part
            return total

        reduce_start(0, loads, compute, "p2")

    pl.run_scoped(
        second_phase,
        pltpu.VMEM((2, TILE, wg_hbm.shape[1]), jnp.bfloat16),
        pltpu.VMEM((2, TILE, wg_hbm.shape[1]), jnp.bfloat16),
        pltpu.SemaphoreType.DMA((2, 2)),
    )

    def third_phase(wa, sems):
        def loads(n, slot):
            at = pl.ds(pl.multiple_of(n * TILE, TILE), TILE)
            return (pltpu.make_async_copy(wd_hbm.at[:, at], wa.at[slot], sems.at[slot]),)

        def compute(slot):
            total = None
            for j in range(hidden_tiles):
                part = dot_plain(acts[at_tile(j, 0), 0], wa[slot, pl.ds(j * TILE, TILE)])
                total = part if total is None else total + part
            return total

        reduce_start(1, loads, compute, "p3")

    pl.run_scoped(
        third_phase,
        pltpu.VMEM((2, wd_hbm.shape[0], TILE), jnp.bfloat16),
        pltpu.SemaphoreType.DMA((2,)),
    )

    base = ff_items
    for n in range(2):
        pltpu.make_async_copy(
            y_hbm.at[:, pl.ds(n * TILE, TILE)], acts.at[base + n, 0], misc.at[n]
        ).start()

    def xt_own(t):
        shard = other_z(z, t) * 2 + y
        return pltpu.make_async_copy(xt_hbm.at[shard], lt.at[2, 0, t], misc.at[2 + t])

    def xt_odd():
        shard = other_z(z, head) * 2 + 1 - y
        return pltpu.make_async_copy(xt_hbm.at[shard], odd.at[2], misc.at[6])

    for t in range(4):
        xt_own(t).start()
    xt_odd().start()
    for t in range(4):
        xt_own(t).wait()
    xt_odd().wait()
    for n in range(2):
        pltpu.make_async_copy(
            y_hbm.at[:, pl.ds(n * TILE, TILE)], acts.at[base + n, 0], misc.at[n]
        ).wait()
    fill_bias(order_ref, bias, rows, z, y, seq)
    fill_factor(ids_ref, counts_ref, weights_ref, factor_ref, float(tokens * 8))
    after("xt")
    reduce_end(0)

    def fourth_phase(hbuf, cbuf, dbuf, wob, obuf, sbuf, sems, d_sems, w_sems):
        def row_loads(r, slot):
            at = pl.ds(r * 128, 128)
            return (
                pltpu.make_async_copy(h_hbm.at[at], hbuf.at[slot], sems.at[slot, 0]),
                pltpu.make_async_copy(cot_hbm.at[at], cbuf.at[slot], sems.at[slot, 1]),
            )

        def spill(r, slot):
            return pltpu.make_async_copy(dbuf.at[slot], dh_hbm.at[pl.ds(r * 128, 128)], d_sems.at[slot])

        def tile_loads(n):
            at = pl.ds(n * TILE, TILE)
            return (
                pltpu.make_async_copy(wo_hbm.at[at], wob.at[n], w_sems.at[n, 0]),
                pltpu.make_async_copy(o_hbm.at[:, at], obuf.at[n], w_sems.at[n, 1]),
                pltpu.make_async_copy(sig_hbm.at[:, at], sbuf.at[n], w_sems.at[n, 2]),
            )

        for copy in row_loads(0, 0):
            copy.start()
        for n in range(2):
            for copy in tile_loads(n):
                copy.start()
        vec[0] = jnp.zeros_like(vec[0])

        @pl.loop(0, n_chunks)
        def _(r):
            slot = lax.rem(r, 2)

            @pl.when(r < n_chunks - 1)
            def _():
                for copy in row_loads(r + 1, 1 - slot):
                    copy.start()

            for copy in row_loads(r, slot):
                copy.wait()

            @pl.when(r >= 2)
            def _():
                spill(r - 2, slot).wait()

            at = pl.ds(pl.multiple_of(r * 128, 128), 128)
            value = hbuf[slot]
            scale = rms(value)
            normed = value * scale
            grad = fin_rows(0, pl.multiple_of(r * 128, 128), 128)
            vec[0, 1:2] += jnp.sum(grad * normed, axis=0, keepdims=True)
            scaled = grad * wide(n2_ref[...])
            inner = jnp.mean(scaled * normed, axis=-1, keepdims=True)
            dh = wide(cbuf[slot]) * factor_ref[at] + scale * (scaled - normed * inner)
            dbuf[slot] = dh
            wide_a[at] = low(dh)
            spill(r, slot).start()

        spill(n_chunks - 2, n_chunks % 2).wait()
        spill(n_chunks - 1, (n_chunks - 1) % 2).wait()

        after("p4a")
        ones = jnp.ones((8, 128), jnp.bfloat16)
        for n in range(2):
            for copy in tile_loads(n):
                copy.wait()
            dy = dot_rows(wide_a[...], wob[n])
            sig, o = sbuf[n], obuf[n]
            do = low(dy * sig)
            acts[base + 2 + n, 0] = low(dy * o * sig * (1.0 - sig))
            wide_b[:, n * TILE : (n + 1) * TILE] = do
            both = wide(do) * o
            for g in range(2):
                part = both[:, g * 128 : (g + 1) * 128]
                top = low(part)
                rest = low(part - wide(top))
                delta[n, g] = dot_rows(ones, top) + dot_rows(ones, rest)

        spread(3, wide_a)
        after("p4b")
        for device in (core_dev, x_dev):
            pl.semaphore_signal(credit, inc=1, device_id=device, device_id_type=MESH)

    pl.run_scoped(
        fourth_phase,
        pltpu.VMEM((2, 128, width), jnp.float32),
        pltpu.VMEM((2, 128, width), jnp.bfloat16),
        pltpu.VMEM((2, 128, width), jnp.float32),
        pltpu.VMEM((2, TILE, width), jnp.bfloat16),
        pltpu.VMEM((2, tokens, TILE), jnp.float32),
        pltpu.VMEM((2, tokens, TILE), jnp.float32),
        pltpu.SemaphoreType.DMA((2, 2)),
        pltpu.SemaphoreType.DMA((2,)),
        pltpu.SemaphoreType.DMA((2, 3)),
    )

    def attention_back(keep, ysend, lsend, dq_ref, dkv_ref):
        def ky_copy(s):
            return remote(ysend.at[lax.rem(s, 2)], yrecv.at[s], ky_s.at[s], ky_r.at[s], y_dev)

        def kl_copy(s):
            return remote(lsend.at[s], lrecv.at[s], kl_s.at[s], kl_r.at[s], lo_dev)

        def km_copy(s):
            return remote(lsend.at[s, pl.ds(0, 2)], mrecv.at[s], km_s.at[s], km_r.at[s], mid_dev)

        def kh_copy(s):
            return remote(lsend.at[s, 2], hrecv.at[s], kh_s.at[s], kh_r.at[s], lo_dev)

        def ky_step(s):
            ky_copy(s).wait_recv()
            for m in range(4):
                keep[s, m] += wide(yrecv[s, m])

            @pl.when(at_end)
            def _():
                for k in range(3):
                    lsend[s, k] = low(keep[s, k + 1])
                kl_copy(s).start()

        def kl_step(s):
            @pl.when(inside)
            def _():
                kl_copy(s).wait_recv()
                keep[s, 0] += wide(lrecv[s, 0])
                lsend[s, 0] = low(keep[s, 2] + wide(lrecv[s, 2]))
                lsend[s, 1] = low(keep[s, 3] + wide(lrecv[s, 1]))
                km_copy(s).start()

        def km_step(s):
            @pl.when(inside)
            def _():
                km_copy(s).wait_recv()
                keep[s, 0] += wide(mrecv[s, 1])
                lsend[s, 2] = low(keep[s, 1] + wide(mrecv[s, 0]))
                kh_copy(s).start()

        actions["ky"] = ky_step
        actions["kl"] = kl_step
        actions["km"] = km_step
        keys_total = bias.shape[0]

        def fifth_phase(qbuf, kvbuf, q_sem, sems):
            def kv_load(s, slot):
                return pltpu.make_async_copy(kv_hbm.at[s], kvbuf.at[slot], sems.at[slot])

            q_load = pltpu.make_async_copy(q_hbm, qbuf, q_sem)
            q_load.start()
            kv_load(0, 0).start()
            q_load.wait()

            @pl.loop(0, seqs)
            def _(s):
                slot = lax.rem(s, 2)

                @pl.when(s < seqs - 1)
                def _():
                    kv_load(s + 1, 1 - slot).start()

                kv_load(s, slot).wait()
                at = pl.ds(pl.multiple_of(s * rows, 128), rows)
                @pl.when(s >= 2)
                def _():
                    ky_copy(s - 2).wait_send()

                for n in range(2):
                    lanes = [slice((2 * n + g) * 128, (2 * n + g + 1) * 128) for g in range(2)]
                    key = kvbuf[slot, :, n * 128 : (n + 1) * 128]
                    value = kvbuf[slot, :, 256 + n * 128 : 256 + (n + 1) * 128]
                    q = jnp.concatenate([qbuf[at, lane] for lane in lanes], axis=0)
                    do = jnp.concatenate([wide_b[at, lane] for lane in lanes], axis=0)
                    drow = jnp.concatenate([delta[n, g, 0:1, at] for g in range(2)], axis=1)
                    scores = dot_rows(key, q)
                    probs = jnp.exp(scores - lse_ref[s, n] + bias[...])
                    grad_probs = dot_rows(value, do)
                    ds = low(probs * (grad_probs - drow))
                    for start, grad in ((0, dot_plain(ds, q)), (256, dot_plain(low(probs), do))):
                        into = slice(start + n * 128, start + (n + 1) * 128)
                        for m in range(4):
                            keep[s, m, :, into] = grad[2 * m * rows : (2 * m + 1) * rows]
                            ysend[slot, m, :, into] = low(grad[(2 * m + 1) * rows : (2 * m + 2) * rows])
                    dq = dot_first(key, ds).T
                    for g in range(2):
                        dq_ref[at, lanes[g]] = dq[g * rows : (g + 1) * rows]

                ky_copy(s).start()
                after_step("p5", s, seqs)

        pl.run_scoped(
            fifth_phase,
            pltpu.VMEM(q_hbm.shape, jnp.bfloat16),
            pltpu.VMEM((2, keys_total, 512), jnp.bfloat16),
            pltpu.SemaphoreType.DMA,
            pltpu.SemaphoreType.DMA((2,)),
        )

        lt_copy(3).start()
        lt_copy(2).start()
        after("sl3")

        def query_phase(rbuf, sem):
            load = pltpu.make_async_copy(qraw_hbm, rbuf, sem)
            load.start()
            load.wait()
            factor = 128.0**-0.5
            for hd in range(4):
                lane = slice(hd * 128, (hd + 1) * 128)
                raw = rbuf[:, lane]
                scale = rms(raw)
                normed = raw * scale
                grad = dq_ref[:, lane]
                gvec[0, 0:1, 0:128] = (
                    jnp.sum(grad * normed * factor, axis=0, keepdims=True)
                    + (gvec[0, 0:1, 0:128] if hd else 0.0)
                )
                scaled = grad * (wide(qg_ref[...]) * factor)
                out = scale * (scaled - normed * jnp.mean(scaled * normed, axis=-1, keepdims=True))
                acts[base + 4 + hd // 2, 0, :, (hd % 2) * 128 : (hd % 2 + 1) * 128] = low(out)

        gvec[0] = jnp.zeros_like(gvec[0])
        pl.run_scoped(query_phase, pltpu.VMEM(qraw_hbm.shape, jnp.float32), pltpu.SemaphoreType.DMA)

        after("qp")
        reduce_end(1)

        def out_phase(hbuf, obuf, sems, o_sems):
            def load(r, slot):
                return pltpu.make_async_copy(h_hbm.at[pl.ds(r * 128, 128)], hbuf.at[slot], sems.at[slot])

            def store(r, slot):
                return pltpu.make_async_copy(obuf.at[slot], block_out.at[pl.ds(r * 128, 128)], o_sems.at[slot])

            load(0, 0).start()

            @pl.loop(0, n_chunks)
            def _(r):
                slot = lax.rem(r, 2)

                @pl.when(r < n_chunks - 1)
                def _():
                    load(r + 1, 1 - slot).start()

                load(r, slot).wait()

                @pl.when(r >= 2)
                def _():
                    store(r - 2, slot).wait()

                obuf[slot] = low(hbuf[slot] + fin_rows(1, pl.multiple_of(r * 128, 128), 128))
                store(r, slot).start()

            store(n_chunks - 2, n_chunks % 2).wait()
            store(n_chunks - 1, (n_chunks - 1) % 2).wait()

        pl.run_scoped(
            out_phase,
            pltpu.VMEM((2, 128, width), jnp.float32),
            pltpu.VMEM((2, 128, width), jnp.bfloat16),
            pltpu.SemaphoreType.DMA((2,)),
            pltpu.SemaphoreType.DMA((2,)),
        )

        after("op")

        @pl.loop(0, seqs)
        def _(s):
            at = pl.ds(pl.multiple_of(s * rows, 128), rows)

            @pl.when(inside)
            def _():
                dkv_ref[at] = keep[s, 0]

            @pl.when(at_end)
            def _():
                kh_copy(s).wait_recv()
                dkv_ref[at] = keep[s, 0] + wide(hrecv[s])

        def key_phase(rbuf, sem):
            load = pltpu.make_async_copy(kraw_hbm, rbuf, sem)
            load.start()
            load.wait()
            for hd in range(2):
                lane = slice(hd * 128, (hd + 1) * 128)
                raw = rbuf[:, lane]
                scale = rms(raw)
                normed = raw * scale
                grad = dkv_ref[:, lane]
                gvec[0, 0:1, 128:256] = (
                    jnp.sum(grad * normed, axis=0, keepdims=True)
                    + (gvec[0, 0:1, 128:256] if hd else 0.0)
                )
                scaled = grad * wide(kg_ref[...])
                out = scale * (scaled - normed * jnp.mean(scaled * normed, axis=-1, keepdims=True))
                acts[base + 6, 0, :, lane] = low(out)
            acts[base + 7, 0] = low(dkv_ref[:, 256:512])

        pl.run_scoped(key_phase, pltpu.VMEM(kraw_hbm.shape, jnp.float32), pltpu.SemaphoreType.DMA)
        after("kp")

        @pl.loop(seqs - 2, seqs)
        def _(s):
            ky_copy(s).wait_send()

        @pl.loop(0, seqs)
        def _(s):
            @pl.when(at_end)
            def _():
                kl_copy(s).wait_send()

            @pl.when(inside)
            def _():
                km_copy(s).wait_send()
                kh_copy(s).wait_send()

    pl.run_scoped(
        attention_back,
        pltpu.VMEM((seqs, 4, rows, 512), jnp.float32),
        pltpu.VMEM((2, 4, rows, 512), jnp.bfloat16),
        pltpu.VMEM((seqs, 3, rows, 512), jnp.bfloat16),
        pltpu.VMEM((tokens, 512), jnp.float32),
        pltpu.VMEM((tokens, 512), jnp.float32),
    )

    def sixth_phase(wb, sems):
        pieces = ((wga_hbm, base + 2, 2), (wq_hbm, base + 4, 2), (wk_hbm, base + 6, 1), (wv_hbm, base + 7, 1))

        def loads(n, slot):
            at = pl.ds(pl.multiple_of(n * TILE, TILE), TILE)
            out, start = [], 0
            for p, (ref, _, count) in enumerate(pieces):
                out.append(
                    pltpu.make_async_copy(
                        ref.at[at], wb.at[slot, :, pl.ds(start, count * TILE)], sems.at[slot, p]
                    )
                )
                start += count * TILE
            return out

        def compute(slot):
            total, start = None, 0
            for _, first, count in pieces:
                for n in range(count):
                    part = dot_rows(acts[first + n, 0], wb[slot, :, pl.ds(start, TILE)])
                    total = part if total is None else total + part
                    start += TILE
            return total

        pl.semaphore_wait(credit, 2)
        reduce_start(2, loads, compute, "p7")

    pl.run_scoped(
        sixth_phase,
        pltpu.VMEM((2, TILE, 6 * TILE), jnp.bfloat16),
        pltpu.SemaphoreType.DMA((2, 4)),
    )

    for step in range(5):
        device = (y_dev, lo_dev, hi_dev, core_dev, x_dev)[step]
        copy = remote(gvec.at[step], gvec_got.at[step], gv_s.at[step], gv_r.at[step], device)
        copy.start()
        copy.wait()
        gvec[step + 1] = gvec[step] + gvec_got[step]
    piece = qg_out.shape[1]
    turn = lax.rem(128 - seq * piece, 128)
    for out, at in ((qg_out, 0), (kg_out, 128)):
        out[...] = pltpu.roll(gvec[5, :, at : at + 128], turn, 1)[0:1, 0:piece]

    reduce_end(2)

    def last_phase(xbuf, dbuf, obuf, sems, o_sems):
        def loads(r, slot):
            at = pl.ds(r * 128, 128)
            return (
                pltpu.make_async_copy(x_hbm.at[at], xbuf.at[slot], sems.at[slot, 0]),
                pltpu.make_async_copy(dh_hbm.at[at], dbuf.at[slot], sems.at[slot, 1]),
            )

        def store(r, slot):
            return pltpu.make_async_copy(obuf.at[slot], x_out.at[pl.ds(r * 128, 128)], o_sems.at[slot])

        for copy in loads(0, 0):
            copy.start()

        @pl.loop(0, n_chunks)
        def _(r):
            slot = lax.rem(r, 2)

            @pl.when(r < n_chunks - 1)
            def _():
                for copy in loads(r + 1, 1 - slot):
                    copy.start()

            for copy in loads(r, slot):
                copy.wait()

            @pl.when(r >= 2)
            def _():
                store(r - 2, slot).wait()

            value = wide(xbuf[slot])
            scale = rms(value)
            normed = value * scale
            grad = fin_rows(2, pl.multiple_of(r * 128, 128), 128)
            vec[0, 0:1] += jnp.sum(grad * normed, axis=0, keepdims=True)
            scaled = grad * wide(n1_ref[...])
            inner = jnp.mean(scaled * normed, axis=-1, keepdims=True)
            obuf[slot] = low(dbuf[slot] + scale * (scaled - normed * inner))
            store(r, slot).start()

        store(n_chunks - 2, n_chunks % 2).wait()
        store(n_chunks - 1, (n_chunks - 1) % 2).wait()

    pl.run_scoped(
        last_phase,
        pltpu.VMEM((2, 128, width), jnp.bfloat16),
        pltpu.VMEM((2, 128, width), jnp.float32),
        pltpu.VMEM((2, 128, width), jnp.bfloat16),
        pltpu.SemaphoreType.DMA((2, 2)),
        pltpu.SemaphoreType.DMA((2,)),
    )

    after("lp")
    for step in range(3):
        device = (y_dev, lo_dev, hi_dev)[step]
        copy = remote(vec.at[step], vec_got.at[step], nv_s.at[step], nv_r.at[step], device)
        copy.start()
        copy.wait()
        vec[step + 1] = vec[step] + vec_got[step]
    own = pl.ds(pl.multiple_of(seq * TILE, TILE), TILE)
    n1_out[...] = vec[3, 0:1, own]
    n2_out[...] = vec[3, 1:2, own]

    after("vec")

    @pl.loop(0, item_count)
    def _(i):
        act_copy(i).wait_send()

    for i in range(item_count - 4, item_count):

        @pl.when(at_end)
        def _():
            z1_copy(i).wait_send()

        @pl.when(inside)
        def _():
            z2_copy(i).wait_send()
            z3_copy(i).wait_send()

    for i in range(item_count - 2, item_count):
        out_wait(i)

    for l in (0, 2, 3):
        lt_copy(l).wait_send()
        lt_core(l, head).wait_send()
        lt_x(l, head).wait_send()
        lt_far(l, x_head).wait_send()


def back_call(hbm, vmem, smem, sizes):
    tokens, width, seqs, rows, keys_total, hidden = sizes
    count = 3 * (hidden // TILE) + 8
    bf, f32 = jnp.bfloat16, jnp.float32
    dma = pltpu.SemaphoreType.DMA
    scratch = [
        pltpu.VMEM((count, 2, tokens, TILE), bf),
        pltpu.VMEM((4, 2, 4, TILE, tokens), bf),
        pltpu.VMEM((4, TILE, tokens), bf),
        pltpu.VMEM((4, tokens, TILE), bf),
        pltpu.VMEM((2, 4, tokens, TILE), bf),
        pltpu.VMEM((2, 4, tokens, TILE), bf),
        pltpu.VMEM((2, 8, tokens, TILE), bf),
        pltpu.VMEM((seqs, 4, rows, 512), bf),
        pltpu.VMEM((seqs, 3, rows, 512), bf),
        pltpu.VMEM((seqs, 2, rows, 512), bf),
        pltpu.VMEM((seqs, rows, 512), bf),
        pltpu.VMEM((4, 3, TILE, TILE), bf),
        pltpu.VMEM((4, TILE, TILE), bf),
        pltpu.VMEM((2, TILE, TILE), f32),
        pltpu.VMEM((tokens, width), bf),
        pltpu.VMEM((tokens, width), bf),
        pltpu.VMEM((2, 2, 8, tokens), f32),
        pltpu.VMEM((4, 8, width), f32),
        pltpu.VMEM((3, 8, width), f32),
        pltpu.VMEM((6, 8, 256), f32),
        pltpu.VMEM((5, 8, 256), f32),
        pltpu.VMEM((keys_total, 2 * rows), f32),
        pltpu.VMEM((tokens, 1), f32),
        *(dma((count,)) for _ in range(8)),
        *(dma((4,)) for _ in range(8)),
        *(dma((3, 4)) for _ in range(6)),
        *(dma((seqs,)) for _ in range(8)),
        dma((3,)), dma((3,)), dma((5,)), dma((5,)),
        dma((4,)), dma((2,)), dma((8,)), pltpu.SemaphoreType.REGULAR,
    ]
    any_spec = pl.BlockSpec(memory_space=pl.ANY)
    vmem_spec = pl.BlockSpec(memory_space=pltpu.VMEM)
    smem_spec = pl.BlockSpec(memory_space=pltpu.SMEM)
    return pl.pallas_call(
        back_kernel,
        out_shape=[
            jax.ShapeDtypeStruct((tokens, width), bf),
            jax.ShapeDtypeStruct((tokens, width), bf),
            jax.ShapeDtypeStruct((hidden, TILE), f32),
            jax.ShapeDtypeStruct((TILE, hidden), f32),
            jax.ShapeDtypeStruct((TILE, hidden), f32),
            jax.ShapeDtypeStruct((512, TILE), f32),
            jax.ShapeDtypeStruct((TILE, 512), f32),
            jax.ShapeDtypeStruct((TILE, 512), f32),
            jax.ShapeDtypeStruct((TILE, TILE), f32),
            jax.ShapeDtypeStruct((TILE, TILE), f32),
            jax.ShapeDtypeStruct((1, width // 8), f32),
            jax.ShapeDtypeStruct((1, width // 8), f32),
            jax.ShapeDtypeStruct((1, 16), f32),
            jax.ShapeDtypeStruct((1, 16), f32),
            jax.ShapeDtypeStruct((tokens, width), f32),
            jax.ShapeDtypeStruct((count, 3, TILE, TILE), bf),
            jax.ShapeDtypeStruct((count, 2, TILE, TILE), bf),
            jax.ShapeDtypeStruct((count, TILE, TILE), bf),
        ],
        in_specs=[any_spec] * len(hbm) + [vmem_spec] * len(vmem) + [smem_spec] * len(smem),
        out_specs=[any_spec] * 10 + [vmem_spec] * 4 + [any_spec] * 4,
        scratch_shapes=scratch,
        compiler_params=pltpu.CompilerParams(
            collective_id=1, has_side_effects=True, vmem_limit_bytes=61 << 20
        ),
    )(*hbm, *vmem, *smem)


def hand_over_kernel(count, *refs):
    src, dst, held, sems = refs[:count], refs[count : 2 * count], refs[2 * count : -1], refs[-1]
    into = [pltpu.make_async_copy(src[i], held[i], sems.at[0, i]) for i in range(count)]
    out = [pltpu.make_async_copy(held[i], dst[i], sems.at[1, i]) for i in range(count)]
    for copy in into:
        copy.start()
    for i in range(count):
        into[i].wait()
        out[i].start()
    for copy in out:
        copy.wait()


def hand_over(arrays):
    any_spec = pl.BlockSpec(memory_space=pl.ANY)
    count = len(arrays)
    return pl.pallas_call(
        functools.partial(hand_over_kernel, count),
        out_shape=[jax.ShapeDtypeStruct(a.shape, a.dtype) for a in arrays],
        in_specs=[any_spec] * count,
        out_specs=[any_spec] * count,
        scratch_shapes=[
            *(pltpu.VMEM(a.shape, a.dtype) for a in arrays),
            pltpu.SemaphoreType.DMA((2, count)),
        ],
        compiler_params=pltpu.CompilerParams(vmem_limit_bytes=61 << 20),
    )(*arrays)


def forward_kernel(
    x_hbm, wq_hbm, wk_hbm, wv_hbm, wga_hbm, wo_hbm, cot_hbm, wd_hbm,
    ids_ref, n1_ref, qg_ref, kg_ref, order_ref, counts_ref, weights_ref,
    h_out, xt_out, q_out, kv_out, o_out, sig_out, y_out, qraw_out, kraw_out, ltd_out, dm_out, lse_ref,
    xv, xn, wqv, wkv, wvv, wgav, wov, kv, qv, qraw, kraw, sig, ov, yv, xtv, hv,
    dout, ltd, odd, wdv, dmv, bias, factor_ref,
    csend, crecv, fin, xrecv,
    x_sem, w_sem, out_sem, h_sem, kz_s, kz_r, kf_s, ky_s, ky_r, l_sem, d_sem, m_sem, c1_s, c1_r, x_s, x_r, c2_s, c2_r,
):
    seq, head = lax.axis_index("seq"), lax.axis_index("head")
    z, y = lax.div(seq, 2), lax.rem(seq, 2)
    c = lax.rem(head, 2)
    y_dev = {"seq": z * 2 + 1 - y}
    lo_dev, mid_dev = {"seq": other_z(z, 1) * 2 + y}, {"seq": (3 - z) * 2 + y}
    at_end, inside = lax.rem(z, 3) == 0, lax.rem(z, 3) != 0
    core_dev = {"head": head + 1 - 2 * c}
    x_dev = {"head": head + 2 - 4 * lax.div(head, 2)}
    seqs, slots, rows = kv.shape[0], kv.shape[1], kv.shape[2]
    tokens, width = x_hbm.shape
    half = width // 2
    epsilon_k = 1e-06

    def rms(value):
        return lax.rsqrt(jnp.mean(value * value, axis=-1, keepdims=True) + epsilon_k)

    def rows_at(s):
        return pl.ds(pl.multiple_of(s * rows, 128), rows)

    def x_load(s):
        return pltpu.make_async_copy(x_hbm.at[rows_at(s)], xv.at[rows_at(s)], x_sem.at[s])

    weight_loads = [
        pltpu.make_async_copy(src, dst, w_sem.at[i])
        for i, (src, dst) in enumerate(
            ((wk_hbm, wkv), (wv_hbm, wvv), (wq_hbm, wqv), (wga_hbm, wgav), (wo_hbm, wov))
        )
    ]
    for s in range(seqs):
        x_load(s).start()
    for load in weight_loads:
        load.start()
    for s in range(seqs):
        pltpu.make_async_copy(cot_hbm.at[rows_at(s)], dout.at[rows_at(s)], d_sem.at[s]).start()

    barrier = pltpu.get_barrier_semaphore()
    for device in (y_dev, lo_dev, core_dev, x_dev):
        pl.semaphore_signal(barrier, inc=1, device_id=device, device_id_type=MESH)

    @pl.when(inside)
    def _():
        pl.semaphore_signal(barrier, inc=1, device_id=mid_dev, device_id_type=MESH)
        pl.semaphore_wait(barrier, 5)

    @pl.when(at_end)
    def _():
        pl.semaphore_wait(barrier, 4)

    def remote(src, dst, send, recv, device):
        return pltpu.make_async_remote_copy(
            src_ref=src, dst_ref=dst, send_sem=send, recv_sem=recv, device_id=device, device_id_type=MESH
        )

    def own_out(s):
        return remote(kv.at[s, 0], kv.at[s, 2], kz_s.at[s, 1], kz_r.at[s, 1], lo_dev)

    def own_over(s):
        return remote(kv.at[s, 0], kv.at[s, 6], kz_s.at[s, 3], kz_r.at[s, 3], mid_dev)

    def end_over(s):
        return remote(kv.at[s, 2], kv.at[s, 4], kz_s.at[s, 2], kz_r.at[s, 2], mid_dev)

    def mid_out(s):
        return remote(kv.at[s, 6], kv.at[s, 4], kf_s.at[s, 0], kz_r.at[s, 2], lo_dev)

    def far_out(s):
        return remote(kv.at[s, 4], kv.at[s, 6], kf_s.at[s, 1], kz_r.at[s, 3], lo_dev)

    def y_copy(s, t):
        return remote(kv.at[s, 2 * t], kv.at[s, 2 * t + 1], ky_s.at[s, t], ky_r.at[s, t], y_dev)

    def core_copy(s):
        return remote(csend.at[s], crecv.at[s], c1_s.at[s], c1_r.at[s], core_dev)

    def x_copy(s):
        return remote(fin.at[s, c], xrecv.at[s], x_s.at[s], x_r.at[s], x_dev)

    def fin_copy(s):
        return remote(fin.at[s, c], fin.at[s, c], c2_s.at[s], c2_r.at[s], core_dev)

    def fin_copy_in(s):
        piece = fin.at[s, 1 - c]
        return remote(piece, piece, c2_s.at[s], c2_r.at[s], core_dev)

    weight_loads[0].wait()
    weight_loads[1].wait()

    @pl.loop(0, seqs)
    def _(s):
        x_load(s).wait()
        at = rows_at(s)
        value = wide(xv[at])
        xn[at] = low(value * rms(value) * wide(n1_ref[...]))
        raw = dot_plain(xn[at], wkv[...])
        kraw[at] = raw
        for n in range(2):
            lane = slice(n * 128, (n + 1) * 128)
            part = raw[:, lane]
            kv[s, 0, :, lane] = low(part * rms(part) * wide(kg_ref[...]))
        kv[s, 0, :, 256:512] = low(dot_plain(xn[at], wvv[...]))
        y_copy(s, 0).start()
        own_out(s).start()

        @pl.when(inside)
        def _():
            own_over(s).start()

    outs = []

    def leave(src, dst):
        copy = pltpu.make_async_copy(src, dst, out_sem.at[len(outs)])
        copy.start()
        outs.append(copy)

    leave(kraw, kraw_out)

    def forward_keys(s):
        own_out(s).wait_recv()

        @pl.when(inside)
        def _():
            end_over(s).start()
            y_copy(s, 1).start()
            own_over(s).wait_recv()
            mid_out(s).start()
            y_copy(s, 3).start()
            end_over(s).wait_recv()
            far_out(s).start()
            y_copy(s, 2).start()

        @pl.when(at_end)
        def _():
            y_copy(s, 1).start()
            mid_out(s).wait_recv()
            y_copy(s, 2).start()
            far_out(s).wait_recv()
            y_copy(s, 3).start()

    hidden_tiles = wd_hbm.shape[0] // TILE

    def cot_load(s):
        return pltpu.make_async_copy(cot_hbm.at[rows_at(s)], dout.at[rows_at(s)], d_sem.at[s])

    def wd_load(j):
        at = pl.ds(pl.multiple_of(j * TILE, TILE), TILE)
        return pltpu.make_async_copy(wd_hbm.at[at], wdv.at[lax.rem(j, 2)], l_sem.at[lax.rem(j, 2)])

    def dm_store(j):
        return pltpu.make_async_copy(dmv.at[lax.rem(j, 2)], dm_out.at[j], m_sem.at[lax.rem(j, 2)])

    def spread_copy():
        return remote(odd, ltd.at[1, pl.ds(2 * c, 2)], l_sem.at[2], l_sem.at[3], y_dev)

    def relay_copy(part):
        piece = ltd.at[1, pl.ds(2 * part, 2)]
        return remote(piece, piece, l_sem.at[4], l_sem.at[5], core_dev)

    def dm_tile(j):
        @pl.when(j < hidden_tiles - 1)
        def _():
            wd_load(j + 1).start()

        wd_load(j).wait()

        @pl.when(j >= 2)
        def _():
            dm_store(j - 2).wait()

        dmv[lax.rem(j, 2)] = dot_rows(dout[...], wdv[lax.rem(j, 2)])
        dm_store(j).start()

    fill_bias(order_ref, bias, rows, z, y, seq)
    fill_factor(ids_ref, counts_ref, weights_ref, factor_ref, float(tokens * 8))

    weight_loads[2].wait()
    weight_loads[3].wait()
    scale_q = 128.0**-0.5

    @pl.loop(0, seqs)
    def _(s):
        at = rows_at(s)
        raw = dot_plain(xn[at], wqv[...])
        qraw[at] = raw
        for n in range(4):
            lane = slice(n * 128, (n + 1) * 128)
            part = raw[:, lane]
            qv[at, lane] = low(part * rms(part) * (wide(qg_ref[...]) * scale_q))
        sig[at] = jax.nn.sigmoid(dot_plain(xn[at], wgav[...]))

    leave(qraw, qraw_out)
    leave(qv, q_out)
    leave(sig, sig_out)
    forward_keys(0)

    @pl.loop(0, width // TILE)
    def _(n):
        at = pl.ds(pl.multiple_of(n * TILE, TILE), TILE)
        xtv[n] = xn[:, at].T

    leave(xtv, xt_out)
    wd_load(0).start()

    @pl.loop(0, seqs)
    def _(s):
        cot_load(s).wait()
        at = rows_at(s)
        dout[at] = low(wide(dout[at]) * factor_ref[at])

    @pl.loop(0, 4)
    def _(t):
        at = pl.multiple_of((other_z(z, t) * 2 + y) * TILE, TILE)
        ltd[0, t] = dout[:, pl.ds(at, TILE)].T

    @pl.loop(0, 2)
    def _(k):
        at = pl.multiple_of((other_z(z, 2 * c + k) * 2 + 1 - y) * TILE, TILE)
        odd[k] = dout[:, pl.ds(at, TILE)].T

    weight_loads[4].wait()

    def finish(s):
        x_copy(s).wait()
        fin[s, c] = low(wide(fin[s, c]) + wide(xrecv[s]))
        fin_copy(s).start()

    def h_store(s, slot):
        return pltpu.make_async_copy(hv.at[slot], h_out.at[rows_at(s)], h_sem.at[slot])

    def finish_rows(s):
        slot = lax.rem(s, 2)
        fin_copy_in(s).wait_recv()

        @pl.when(s >= 2)
        def _():
            h_store(s - 2, slot).wait()

        hv[slot, :, 0:half] = wide(xv[rows_at(s), 0:half]) + wide(fin[s, 0])
        hv[slot, :, half:width] = wide(xv[rows_at(s), half:width]) + wide(fin[s, 1])
        h_store(s, slot).start()

    @pl.loop(0, seqs)
    def _(s):
        @pl.when(s < seqs - 1)
        def _():
            forward_keys(s + 1)

            @pl.when(s == seqs - 2)
            def _():
                spread_copy().start()

            dm_tile(2 * s)
            dm_tile(2 * s + 1)

        for t in range(4):
            y_copy(s, t).wait_recv()
        at = rows_at(s)
        for n in range(2):
            lanes = [slice((2 * n + g) * 128, (2 * n + g + 1) * 128) for g in range(2)]
            key = kv[s, :, :, n * 128 : (n + 1) * 128].reshape(slots * rows, 128)
            value = kv[s, :, :, 256 + n * 128 : 256 + (n + 1) * 128].reshape(slots * rows, 128)
            q = jnp.concatenate([qv[at, lane] for lane in lanes], axis=0)
            scores = dot_rows(key, q) + bias[...]
            top = jnp.max(scores, axis=0, keepdims=True)
            probs = jnp.exp(scores - top)
            total = jnp.sum(probs, axis=0, keepdims=True)
            out = (dot_first(value, low(probs)) / total).T
            lse_ref[s, n] = top + jnp.log(total)
            for g in range(2):
                ov[at, lanes[g]] = out[g * rows : (g + 1) * rows]
        gated = low(ov[at] * sig[at])
        yv[at] = gated
        away = pl.ds(pl.multiple_of((1 - c) * half, 128), half)
        mine = pl.ds(pl.multiple_of(c * half, 128), half)
        csend[s] = low(dot_plain(gated, wov[:, away]))
        core_copy(s).start()
        part = dot_plain(gated, wov[:, mine])
        core_copy(s).wait_recv()
        fin[s, c] = low(part + wide(crecv[s]))
        x_copy(s).start()

        @pl.when(s >= 1)
        def _():
            finish(s - 1)

        @pl.when(s >= 2)
        def _():
            finish_rows(s - 2)

    leave(kv, kv_out)
    leave(ov, o_out)
    leave(yv, y_out)
    finish_rows(seqs - 2)
    spread_copy().wait_recv()
    relay_copy(c).start()
    finish(seqs - 1)
    finish_rows(seqs - 1)
    h_store(seqs - 2, seqs % 2).wait()
    h_store(seqs - 1, (seqs - 1) % 2).wait()
    relay_copy(1 - c).wait_recv()
    leave(ltd, ltd_out)
    spread_copy().wait_send()
    relay_copy(c).wait_send()
    dm_store(hidden_tiles - 2).wait()
    dm_store(hidden_tiles - 1).wait()
    for copy in outs:
        copy.wait()

    @pl.loop(0, seqs)
    def _(s):
        own_out(s).wait_send()

        @pl.when(inside)
        def _():
            for copy in (own_over, end_over, mid_out, far_out):
                copy(s).wait_send()

        for t in range(4):
            y_copy(s, t).wait_send()
        core_copy(s).wait_send()
        fin_copy(s).wait_send()


def forward_call(hbm, vmem, smem, sizes):
    tokens, width, seqs, rows, slots, hidden = sizes
    bf, f32 = jnp.bfloat16, jnp.float32
    dma = pltpu.SemaphoreType.DMA
    half = width // 2
    kv_shape = (seqs, slots, rows, 512)
    scratch = [
        pltpu.VMEM((tokens, width), bf),
        pltpu.VMEM((tokens, width), bf),
        pltpu.VMEM((width, 512), bf),
        pltpu.VMEM((width, 256), bf),
        pltpu.VMEM((width, 256), bf),
        pltpu.VMEM((width, 512), bf),
        pltpu.VMEM((512, width), bf),
        pltpu.VMEM(kv_shape, bf),
        pltpu.VMEM((tokens, 512), bf),
        pltpu.VMEM((tokens, 512), f32),
        pltpu.VMEM((tokens, 256), f32),
        pltpu.VMEM((tokens, 512), f32),
        pltpu.VMEM((tokens, 512), f32),
        pltpu.VMEM((tokens, 512), bf),
        pltpu.VMEM((width // TILE, TILE, tokens), bf),
        pltpu.VMEM((2, rows, width), f32),
        pltpu.VMEM((tokens, width), bf),
        pltpu.VMEM((2, 4, TILE, tokens), bf),
        pltpu.VMEM((2, TILE, tokens), bf),
        pltpu.VMEM((2, TILE, width), bf),
        pltpu.VMEM((2, tokens, TILE), f32),
        pltpu.VMEM((slots * rows, 2 * rows), f32),
        pltpu.VMEM((tokens, 1), f32),
        pltpu.VMEM((seqs, rows, half), bf),
        pltpu.VMEM((seqs, rows, half), bf),
        pltpu.VMEM((seqs, 2, rows, half), bf),
        pltpu.VMEM((seqs, rows, half), bf),
        dma((seqs,)), dma((5,)), dma((9,)), dma((2,)),
        *(dma((seqs, 4)) for _ in range(5)),
        dma((6,)), dma((seqs,)), dma((2,)),
        *(dma((seqs,)) for _ in range(6)),
    ]
    any_spec = pl.BlockSpec(memory_space=pl.ANY)
    vmem_spec = pl.BlockSpec(memory_space=pltpu.VMEM)
    smem_spec = pl.BlockSpec(memory_space=pltpu.SMEM)
    return pl.pallas_call(
        forward_kernel,
        out_shape=[
            jax.ShapeDtypeStruct((tokens, width), f32),
            jax.ShapeDtypeStruct((width // TILE, TILE, tokens), bf),
            jax.ShapeDtypeStruct((tokens, 512), bf),
            jax.ShapeDtypeStruct(kv_shape, bf),
            jax.ShapeDtypeStruct((tokens, 512), f32),
            jax.ShapeDtypeStruct((tokens, 512), f32),
            jax.ShapeDtypeStruct((tokens, 512), bf),
            jax.ShapeDtypeStruct((tokens, 512), f32),
            jax.ShapeDtypeStruct((tokens, 256), f32),
            jax.ShapeDtypeStruct((2, 4, TILE, tokens), bf),
            jax.ShapeDtypeStruct((hidden // TILE, tokens, TILE), f32),
            jax.ShapeDtypeStruct((seqs, 2, 1, 2 * rows), f32),
        ],
        in_specs=[any_spec] * len(hbm) + [vmem_spec] * len(vmem) + [smem_spec] * len(smem),
        out_specs=[any_spec] * 11 + [vmem_spec],
        scratch_shapes=scratch,
        compiler_params=pltpu.CompilerParams(
            collective_id=2, has_side_effects=True, vmem_limit_bytes=60 << 20
        ),
    )(*hbm, *vmem, *smem)


def on_device(
    x_in,
    cot,
    domain_ids,
    domain_counts,
    domain_weights,
    block_order,
    norm1,
    w_query,
    w_key,
    w_value,
    w_gate_attn,
    w_out,
    query_gain,
    key_gain,
    norm2,
    w_gate,
    w_up,
    w_down,
):
    sequences, local_rows, width = x_in.shape
    row_total = sequences * local_rows
    devices = lax.axis_size("seq")
    x_rows = x_in.reshape(row_total, width)
    scalars = (block_order, domain_counts, domain_weights)
    h, xt, query, kv, attn, sig, gated, query_raw, key_raw, ltd, dm, lse = forward_call(
        (x_rows, w_query, w_key, w_value, w_gate_attn, w_out, cot.reshape(row_total, width), w_down),
        (domain_ids, norm1[None, :], query_gain[None, :], key_gain[None, :]),
        scalars,
        (row_total, width, sequences, local_rows, devices, w_down.shape[0]),
    )
    out, x_grad, down, gate, up, wout, wga, wquery, wkey, wvalue, *small = back_call(
        (
            h,
            cot.reshape(row_total, width),
            x_rows,
            xt,
            ltd,
            dm,
            query,
            kv.reshape(sequences, devices * local_rows, -1),
            attn,
            sig,
            gated,
            query_raw,
            key_raw,
            w_gate,
            w_up,
            w_down,
            w_out,
            w_query,
            w_key,
            w_value,
            w_gate_attn,
        ),
        (
            domain_ids,
            lse,
            norm1[None, :],
            norm2[None, :],
            query_gain[None, :],
            key_gain[None, :],
        ),
        scalars,
        (row_total, width, sequences, local_rows, local_rows * devices, w_down.shape[0]),
    )

    out, x_grad, down, gate, up, wout, wga, wquery, wkey, wvalue, *small = hand_over(
        (out, x_grad, down, gate, up, wout, wga, wquery, wkey, wvalue, *small[:4])
    )
    return (
        out.reshape(x_in.shape),
        x_grad.reshape(x_in.shape),
        small[0].reshape(-1),
        wquery,
        wkey,
        wvalue,
        wga,
        wout,
        small[2].reshape(-1),
        small[3].reshape(-1),
        small[1].reshape(-1),
        gate,
        up,
        down,
    )


def on_device_plain(
    x_in,
    cot,
    domain_ids,
    domain_counts,
    domain_weights,
    block_order,
    norm1,
    w_query,
    w_key,
    w_value,
    w_gate_attn,
    w_out,
    query_gain,
    key_gain,
    norm2,
    w_gate,
    w_up,
    w_down,
):
    sequences, local_rows, model_width = x_in.shape
    row_total = sequences * local_rows
    head_dim = query_gain.shape[0]
    kv_local = w_key.shape[1] // head_dim
    q_local = w_query.shape[1] // head_dim
    group_size = q_local // kv_local
    block_rows = local_rows // 2
    seq_devices = lax.axis_size("seq")
    first_row = lax.axis_index("seq") * local_rows
    query_pos = positions(block_order, first_row, local_rows, block_rows)
    query_factor = head_dim ** (-0.5)
    q_gain = query_gain.astype(jnp.float32)
    k_gain = key_gain.astype(jnp.float32)
    gain_one = norm1.astype(jnp.float32)
    gain_two = norm2.astype(jnp.float32)
    x_float = x_in.reshape(row_total, model_width).astype(jnp.float32)
    scale_one = norm_scale(x_float)
    normed_one = x_float * scale_one
    x_normed = (normed_one * gain_one).astype(jnp.bfloat16)
    query_raw = product(x_normed, w_query).reshape(row_total, q_local, head_dim)
    key_raw = product(x_normed, w_key).reshape(row_total, kv_local, head_dim)
    value_rows = product(x_normed, w_value).astype(jnp.bfloat16)
    gate_pre = product(x_normed, w_gate_attn)
    query_scale = norm_scale(query_raw)
    query_normed = query_raw * query_scale
    key_scale = norm_scale(key_raw)
    key_normed = key_raw * key_scale
    query = (query_normed * q_gain * query_factor).astype(jnp.bfloat16)
    key_rows = (key_normed * k_gain).astype(jnp.bfloat16)
    project_query_heads = query.reshape(
        sequences, local_rows, kv_local, group_size, head_dim
    ).transpose(0, 2, 3, 1, 4)
    (
        query_scale,
        query_normed,
        key_scale,
        key_normed,
        query_heads,
        key_rows,
        value_rows,
        gate_pre,
    ) = (
        query_scale,
        query_normed,
        key_scale,
        key_normed,
        project_query_heads,
        key_rows,
        value_rows,
        gate_pre,
    )
    key_seq = key_rows.reshape(sequences, local_rows, kv_local * head_dim)
    value_seq = value_rows.reshape(sequences, local_rows, kv_local * head_dim)
    stat_shape = (sequences, kv_local, group_size, local_rows)
    running_max = jnp.full(stat_shape, -1e30, jnp.float32)
    key_piece = lax.all_gather(key_seq, "seq", axis=1, tiled=True)
    value_piece = lax.all_gather(value_seq, "seq", axis=1, tiled=True)
    row_count = key_piece.shape[1]
    key_block = key_piece.reshape(sequences, row_count, kv_local, head_dim)
    value_block = value_piece.reshape(sequences, row_count, kv_local, head_dim)
    key_pos = positions(block_order, jnp.int32(0), row_count, block_rows)
    allowed = key_pos[None, :] <= query_pos[:, None]
    scores = jnp.einsum(
        "skgqd,spkd->skgqp", query_heads, key_block, preferred_element_type=jnp.float32
    )
    scores = jnp.where(allowed, scores, -1e30)
    new_max = jnp.maximum(running_max, jnp.max(scores, axis=-1))
    weights = jnp.where(allowed, jnp.exp(scores - new_max[..., None]), 0.0)
    running_sum = jnp.sum(weights, axis=-1)
    weighted = jnp.einsum(
        "skgqp,spkd->skgqd",
        weights.astype(jnp.bfloat16),
        value_block,
        preferred_element_type=jnp.float32,
    )
    running_max, running_sum, weighted = (new_max, running_sum, weighted)
    log_total = running_max + jnp.log(running_sum)
    attn_heads = weighted / running_sum[..., None]
    attn_flat = attn_heads.transpose(0, 3, 1, 2, 4).reshape(row_total, q_local * head_dim)
    gate_sig = jax.nn.sigmoid(gate_pre)
    gated = (attn_flat * gate_sig).astype(jnp.bfloat16)
    attn_sum = lax.psum(product(gated, w_out).astype(jnp.bfloat16), "head").astype(jnp.float32)
    residual = x_float + attn_sum
    scale_two = norm_scale(residual)
    normed_two = residual * scale_two
    h_normed = (normed_two * gain_two).astype(jnp.bfloat16)
    gate_proj = product(h_normed, w_gate)
    up_proj = product(h_normed, w_up)
    gate_logit = jax.nn.sigmoid(gate_proj)
    gate_act = gate_proj * gate_logit
    mixed = (gate_act * up_proj).astype(jnp.bfloat16)
    mlp_sum = lax.psum(product(mixed, w_down).astype(jnp.bfloat16), "head").astype(jnp.float32)
    block_out = (
        (residual + mlp_sum).astype(jnp.bfloat16).reshape(sequences, local_rows, model_width)
    )
    domain_total = domain_weights.shape[0]
    domain_index = jnp.arange(domain_total, dtype=jnp.int32)
    factor = (
        domain_weights
        * (row_total * seq_devices)
        / (domain_total * domain_counts.astype(jnp.float32))
    )
    picked = domain_ids.reshape(row_total)[:, None] == domain_index[None, :]
    row_scale = jnp.sum(jnp.where(picked, factor[None, :], 0.0), axis=1)
    grad_out = cot.reshape(row_total, model_width).astype(jnp.float32) * row_scale[:, None]
    grad_low = grad_out.astype(jnp.bfloat16)
    grad_down = outer_sum(mixed, grad_low)
    grad_mixed = back_product(grad_low, w_down)
    grad_gate = (grad_mixed * up_proj * gate_logit * (1.0 + gate_proj * (1.0 - gate_logit))).astype(
        jnp.bfloat16
    )
    grad_up = (grad_mixed * gate_act).astype(jnp.bfloat16)
    grad_mlp_gate = outer_sum(h_normed, grad_gate)
    grad_mlp_up = outer_sum(h_normed, grad_up)
    grad_hnorm = lax.psum(
        (back_product(grad_gate, w_gate) + back_product(grad_up, w_up)).astype(jnp.bfloat16), "head"
    ).astype(jnp.float32)
    grad_norm_two = jnp.sum(grad_hnorm * normed_two, axis=0)
    grad_resid = grad_out + norm_back(grad_hnorm, normed_two, scale_two, gain_two)
    grad_attn = grad_resid.astype(jnp.bfloat16)
    grad_wout = outer_sum(gated, grad_attn)
    grad_gated = back_product(grad_attn, w_out)
    grad_heads_flat = (grad_gated * gate_sig).astype(jnp.bfloat16)
    grad_gatepre = (grad_gated * attn_flat * gate_sig * (1.0 - gate_sig)).astype(jnp.bfloat16)
    grad_wgate_attn = outer_sum(x_normed, grad_gatepre)
    grad_heads = grad_heads_flat.reshape(
        sequences, local_rows, kv_local, group_size, head_dim
    ).transpose(0, 2, 3, 1, 4)
    row_delta = jnp.sum(grad_heads.astype(jnp.float32) * attn_heads, axis=-1)
    key_piece = lax.all_gather(key_seq, "seq", axis=1, tiled=True)
    value_piece = lax.all_gather(value_seq, "seq", axis=1, tiled=True)
    row_count = key_piece.shape[1]
    key_block = key_piece.reshape(sequences, row_count, kv_local, head_dim)
    value_block = value_piece.reshape(sequences, row_count, kv_local, head_dim)
    key_pos = positions(block_order, jnp.int32(0), row_count, block_rows)
    allowed = key_pos[None, :] <= query_pos[:, None]
    scores = jnp.einsum(
        "skgqd,spkd->skgqp", query_heads, key_block, preferred_element_type=jnp.float32
    )
    probs = jnp.where(
        allowed, jnp.exp(jnp.where(allowed, scores, -1e30) - log_total[..., None]), 0.0
    )
    grad_probs = jnp.einsum(
        "skgqd,spkd->skgqp", grad_heads, value_block, preferred_element_type=jnp.float32
    )
    grad_scores = (probs * (grad_probs - row_delta[..., None])).astype(jnp.bfloat16)
    grad_query = jnp.einsum(
        "skgqp,spkd->skgqd", grad_scores, key_block, preferred_element_type=jnp.float32
    )
    key_term = jnp.einsum(
        "skgqp,skgqd->spkd", grad_scores, query_heads, preferred_element_type=jnp.float32
    ).reshape(sequences, row_count, kv_local * head_dim)
    value_term = jnp.einsum(
        "skgqp,skgqd->spkd",
        probs.astype(jnp.bfloat16),
        grad_heads,
        preferred_element_type=jnp.float32,
    ).reshape(sequences, row_count, kv_local * head_dim)
    grad_keys = key_term
    grad_values = value_term
    grad_query, grad_keys, grad_values = (grad_query, grad_keys, grad_values)
    grad_key_own, grad_value_own = (
        lax.psum_scatter(
            grad_keys.astype(jnp.bfloat16), "seq", scatter_dimension=1, tiled=True
        ).astype(jnp.float32),
        lax.psum_scatter(
            grad_values.astype(jnp.bfloat16), "seq", scatter_dimension=1, tiled=True
        ).astype(jnp.float32),
    )
    grad_query_rows = grad_query.transpose(0, 3, 1, 2, 4).reshape(row_total, q_local, head_dim)
    grad_qgain_part = jnp.sum(grad_query_rows * query_normed * query_factor, axis=(0, 1))
    grad_query_raw = (
        norm_back(grad_query_rows, query_normed, query_scale, q_gain * query_factor)
        .astype(jnp.bfloat16)
        .reshape(row_total, q_local * head_dim)
    )
    grad_key_rows = grad_key_own.reshape(row_total, kv_local, head_dim)
    grad_kgain_part = jnp.sum(grad_key_rows * key_normed, axis=(0, 1))
    grad_key_raw = (
        norm_back(grad_key_rows, key_normed, key_scale, k_gain)
        .astype(jnp.bfloat16)
        .reshape(row_total, kv_local * head_dim)
    )
    grad_value_low = grad_value_own.reshape(row_total, kv_local * head_dim).astype(jnp.bfloat16)
    grad_xnorm_part = (
        back_product(grad_query_raw, w_query)
        + back_product(grad_key_raw, w_key)
        + back_product(grad_value_low, w_value)
        + back_product(grad_gatepre, w_gate_attn)
    )
    grad_xnorm, grad_qgain, grad_kgain = (
        lax.psum(grad_xnorm_part.astype(jnp.bfloat16), "head").astype(jnp.float32),
        lax.psum(grad_qgain_part.astype(jnp.bfloat16), "head").astype(jnp.float32),
        lax.psum(grad_kgain_part.astype(jnp.bfloat16), "head").astype(jnp.float32),
    )
    grad_norm_one = jnp.sum(grad_xnorm * normed_one, axis=0)
    x_grad = (
        (grad_resid + norm_back(grad_xnorm, normed_one, scale_one, gain_one))
        .astype(jnp.bfloat16)
        .reshape(sequences, local_rows, model_width)
    )
    grad_wquery = outer_sum(x_normed, grad_query_raw)
    grad_wkey = outer_sum(x_normed, grad_key_raw)
    grad_wvalue = outer_sum(x_normed, grad_value_low)
    all_totals = (
        lax.psum_scatter(
            grad_norm_one.astype(jnp.bfloat16), "seq", scatter_dimension=0, tiled=True
        ).astype(jnp.float32),
        lax.psum_scatter(
            grad_wquery.astype(jnp.bfloat16), "seq", scatter_dimension=0, tiled=True
        ).astype(jnp.float32),
        lax.psum_scatter(
            grad_wkey.astype(jnp.bfloat16), "seq", scatter_dimension=0, tiled=True
        ).astype(jnp.float32),
        lax.psum_scatter(
            grad_wvalue.astype(jnp.bfloat16), "seq", scatter_dimension=0, tiled=True
        ).astype(jnp.float32),
        lax.psum_scatter(
            grad_wgate_attn.astype(jnp.bfloat16), "seq", scatter_dimension=0, tiled=True
        ).astype(jnp.float32),
        lax.psum_scatter(
            grad_wout.astype(jnp.bfloat16), "seq", scatter_dimension=1, tiled=True
        ).astype(jnp.float32),
        lax.psum_scatter(
            grad_qgain.astype(jnp.bfloat16), "seq", scatter_dimension=0, tiled=True
        ).astype(jnp.float32),
        lax.psum_scatter(
            grad_kgain.astype(jnp.bfloat16), "seq", scatter_dimension=0, tiled=True
        ).astype(jnp.float32),
        lax.psum_scatter(
            grad_mlp_gate.astype(jnp.bfloat16), "seq", scatter_dimension=0, tiled=True
        ).astype(jnp.float32),
        lax.psum_scatter(
            grad_mlp_up.astype(jnp.bfloat16), "seq", scatter_dimension=0, tiled=True
        ).astype(jnp.float32),
        lax.psum_scatter(
            grad_down.astype(jnp.bfloat16), "seq", scatter_dimension=1, tiled=True
        ).astype(jnp.float32),
        lax.psum_scatter(
            grad_norm_two.astype(jnp.bfloat16), "seq", scatter_dimension=0, tiled=True
        ).astype(jnp.float32),
    )
    return (
        block_out,
        x_grad,
        all_totals[0],
        all_totals[1],
        all_totals[2],
        all_totals[3],
        all_totals[4],
        all_totals[5],
        all_totals[6],
        all_totals[7],
        all_totals[11],
        all_totals[8],
        all_totals[9],
        all_totals[10],
    )


def solution(mesh):
    fits = mesh.shape["seq"] == 8 and mesh.shape["head"] == 4
    return jax.shard_map(
        on_device if fits else on_device_plain,
        mesh=mesh,
        in_specs=(
            P(None, "seq", None),
            P(None, "seq", None),
            P(None, "seq"),
            P(),
            P(),
            P(),
            P(),
            P(None, "head"),
            P(None, "head"),
            P(None, "head"),
            P(None, "head"),
            P("head", None),
            P(),
            P(),
            P(),
            P(None, "head"),
            P(None, "head"),
            P("head", None),
        ),
        out_specs=(
            P(None, "seq", None),
            P(None, "seq", None),
            P("seq"),
            P("seq", "head"),
            P("seq", "head"),
            P("seq", "head"),
            P("seq", "head"),
            P("head", "seq"),
            P("seq"),
            P("seq"),
            P("seq"),
            P("seq", "head"),
            P("seq", "head"),
            P("head", "seq"),
        ),
        check_vma=False,
    )
```

```python
import functools

import jax
import jax.numpy as jnp
from jax import lax
from jax.experimental import pallas as pl
from jax.experimental.pallas import tpu as pltpu
from jax.sharding import PartitionSpec as P

epsilon = 1e-06


def norm_scale(value):
    return lax.rsqrt(jnp.mean(value * value, axis=-1, keepdims=True) + epsilon)


def norm_back(grad_in, normed, scale, gain):
    scaled = grad_in * gain
    return scale * (scaled - normed * jnp.mean(scaled * normed, axis=-1, keepdims=True))


def product(left, right):
    return jnp.dot(left, right, preferred_element_type=jnp.float32)


def outer_sum(left, right):
    return lax.dot_general(
        left, right, (((0,), (0,)), ((), ())), preferred_element_type=jnp.float32
    )


def back_product(left, right):
    return lax.dot_general(
        left, right, (((1,), (1,)), ((), ())), preferred_element_type=jnp.float32
    )


def low(value):
    return value.astype(jnp.bfloat16)


def wide(value):
    return value.astype(jnp.float32)


def positions(block_order, device, row_count, block_rows):
    stored = device * row_count + jnp.arange(row_count, dtype=jnp.int32)
    slots = stored // block_rows
    slot_index = jnp.arange(block_order.shape[0], dtype=jnp.int32)
    picked = jnp.sum(
        jnp.where(slots[:, None] == slot_index[None, :], block_order[None, :], 0), axis=1
    )
    return picked * block_rows + stored % block_rows


MESH = pl.DeviceIdType.MESH
TILE = 256


PLAN = {
    "p1.0": (
        ("a", 0),
    ),
    "p1.3": (
        ("a", 1), ("s1", 0),
    ),
    "p1.5": (
        ("a", 2), ("r1", 0),
    ),
    "p2.0": (
        ("a", 3), ("s1", 1),
    ),
    "p2.1": (
        ("s2", 0),
    ),
    "p2.2": (
        ("r2", 0), ("a", 4), ("s1", 2),
    ),
    "p2.4": (
        ("a", 5), ("s3", 0), ("s2", 1), ("s1", 3),
    ),
    "p2.6": (
        ("a", 6), ("s4", 0),
    ),
    "p2.7": (
        ("s2", 2), ("s1", 4), ("a", 7), ("s3", 1),
    ),
    "p3.2": (
        ("s2", 3), ("s1", 5), ("a", 8), ("s3", 2), ("s4", 1),
    ),
    "p3.6": (
        ("s2", 4), ("s1", 6), ("a", 9), ("s3", 3), ("s4", 2),
    ),
    "e0.3": (
        ("s2", 5), ("s1", 7), ("a", 10), ("s3", 4), ("s4", 3),
    ),
    "p4b": (
        ("s2", 6), ("s1", 8), ("a", 11), ("s3", 5),
    ),
    "p5.0": (
        ("s2", 7), ("s1", 9), ("s3", 6),
    ),
    "p5.1": (
        ("s2", 8), ("s1", 10), ("s3", 7),
    ),
    "p5.2": (
        ("ky", 0), ("s2", 9), ("s1", 11), ("s3", 8),
    ),
    "p5.3": (
        ("ky", 1), ("s2", 10), ("s3", 9),
    ),
    "qp": (
        ("kl", 0),
    ),
    "e1.3": (
        ("s4", 4), ("s4", 5), ("s4", 6), ("s4", 7), ("s4", 8), ("s4", 9), ("s3", 10), ("ky", 2), ("s2", 11),
    ),
    "op": (
        ("km", 0), ("s4", 10), ("kl", 1), ("s3", 11), ("ky", 3), ("a", 12), ("r1", 3), ("s4", 11), ("kl", 2),
        ("km", 1), ("a", 13), ("r1", 2), ("r2", 3), ("kl", 3), ("km", 2), ("a", 14), ("s1", 12), ("r2", 2),
        ("a", 15), ("s1", 13), ("km", 3), ("a", 16), ("s2", 12), ("s1", 14),
    ),
    "kp": (
        ("a", 17),
    ),
    "p7.0": (
        ("s2", 13), ("s1", 15), ("a", 18), ("s3", 12),
    ),
    "p7.3": (
        ("s2", 14), ("s1", 16), ("a", 19), ("s3", 13),
    ),
    "p7.4": (
        ("s4", 12),
    ),
    "p7.6": (
        ("s2", 15), ("s1", 17), ("a", 20), ("s3", 14), ("s4", 13),
    ),
    "e2.2": (
        ("s2", 16), ("s1", 18), ("a", 21), ("s3", 15), ("s4", 14),
    ),
    "e2.3": (
        ("s4", 15), ("s2", 17), ("s1", 19), ("a", 22), ("s3", 16),
    ),
    "vec": (
        ("s2", 18), ("s1", 20), ("a", 23), ("s3", 17), ("s4", 16), ("s2", 19), ("s1", 21), ("a", 24),
        ("s4", 17), ("s3", 18), ("s2", 20), ("s1", 22), ("a", 25), ("s3", 19), ("s4", 18), ("s2", 21),
        ("s1", 23), ("s3", 20), ("s4", 19), ("s4", 20), ("s2", 22), ("s1", 24), ("s3", 21), ("s4", 21),
        ("s2", 23), ("s1", 25), ("s3", 22), ("s2", 24), ("s4", 22), ("s3", 23), ("s4", 23), ("s2", 25),
        ("s3", 24), ("s4", 24), ("s3", 25), ("s4", 25),
    ),
}


def other_z(z, t):
    low_z, high_z = lax.rem(z, 2), lax.div(z, 2)
    low_t, high_t = lax.rem(t, 2), lax.div(t, 2)
    return (low_z + low_t - 2 * low_z * low_t) + 2 * (high_z + high_t - 2 * high_z * high_t)


def fill_bias(order_ref, bias, rows, z, y, seq):
    block = bias.shape[0] // order_ref.shape[0]
    each = rows // block
    lane = lax.broadcasted_iota(jnp.int32, (block, bias.shape[1]), 1)
    down = lax.broadcasted_iota(jnp.int32, (block, bias.shape[1]), 0)
    within = lax.rem(lane, rows)
    query = lax.rem(lane, block)
    for i in range(each):
        query += jnp.where(lax.div(within, block) == i, order_ref[seq * each + i] * block, 0)
    for j in range(8):
        other_y = 1 - y if j % 2 else y
        device = other_z(z, j // 2) * 2 + other_y
        for i in range(each):
            key = order_ref[device * each + i] * block + down
            bias[j * rows + i * block : j * rows + (i + 1) * block] = jnp.where(key <= query, 0.0, -1e30)


def fill_factor(ids_ref, counts_ref, weights_ref, factor, total):
    seqs, rows = ids_ref.shape
    domains = counts_ref.shape[0]
    across = jnp.zeros((seqs, rows), jnp.float32)
    ids = ids_ref[...]
    for d in range(domains):
        count = jnp.full((seqs, rows), counts_ref[d], jnp.int32).astype(jnp.float32)
        weight = jnp.full((seqs, rows), weights_ref[d], jnp.float32) * total / (domains * count)
        across = jnp.where(ids == d, weight, across)
    here = lax.broadcasted_iota(jnp.int32, (rows, rows), 0) == lax.broadcasted_iota(
        jnp.int32, (rows, rows), 1
    )
    for s in range(seqs):
        spread = jnp.where(here, across[s : s + 1], 0.0)
        factor[s * rows : (s + 1) * rows] = jnp.sum(spread, axis=1, keepdims=True)


def dot_plain(left, right):
    return jnp.dot(left, right, preferred_element_type=jnp.float32)


def dot_rows(left, right):
    return lax.dot_general(
        left, right, (((1,), (1,)), ((), ())), preferred_element_type=jnp.float32
    )


def dot_first(left, right):
    return lax.dot_general(
        left, right, (((0,), (0,)), ((), ())), preferred_element_type=jnp.float32
    )


def back_kernel(
    h_hbm, cot_hbm, x_hbm, xt_hbm, ltd_hbm, dm_hbm, q_hbm, kv_hbm, o_hbm, sig_hbm, y_hbm, qraw_hbm, kraw_hbm,
    wg_hbm, wu_hbm, wd_hbm, wo_hbm, wq_hbm, wk_hbm, wv_hbm, wga_hbm,
    ids_ref, lse_ref, n1_ref, n2_ref, qg_ref, kg_ref, order_ref, counts_ref, weights_ref,
    block_out, x_out, dwd_out, dwg_out, dwu_out, dwo_out, dwga_out, dwq_out, dwk_out, dwv_out,
    n1_out, n2_out, qg_out, kg_out, dh_hbm, z1_hbm, z2_hbm, z3_hbm,
    acts, lt, odd, csend, crecv, xrecv, fin, yrecv, lrecv, mrecv, hrecv,
    zsend, stage, ostage, wide_a, wide_b, delta,
    vec, vec_got, gvec, gvec_got, bias, factor_ref,
    ya_s, ya_r, z1_s, z1_r, z2_s, z2_r, z3_s, z3_r, lt_s, lt_r, lc_s, lc_r, lx_s, lx_r, lf_s, lf_r,
    c1_s, c1_r, x_s, x_r, c2_s, c2_r, ky_s, ky_r, kl_s, kl_r, km_s, km_r, kh_s, kh_r,
    nv_s, nv_r, gv_s, gv_r, st_sem, out_sem, misc, credit,
):
    seq, head = lax.axis_index("seq"), lax.axis_index("head")
    z, y = lax.div(seq, 2), lax.rem(seq, 2)
    c = lax.rem(head, 2)
    y_dev = {"seq": z * 2 + 1 - y}
    lo_dev = {"seq": other_z(z, 1) * 2 + y}
    hi_dev = {"seq": other_z(z, 2) * 2 + y}
    mid_dev = {"seq": (3 - z) * 2 + y}
    core_dev = {"head": head + 1 - 2 * c}
    x_dev = {"head": head + 2 - 4 * lax.div(head, 2)}
    at_end, inside = lax.rem(z, 3) == 0, lax.rem(z, 3) != 0
    tokens = cot_hbm.shape[0]
    rows = bias.shape[0] // 8
    seqs = tokens // rows
    hidden_tiles = wd_hbm.shape[0] // TILE
    ff_items = 3 * hidden_tiles
    width = cot_hbm.shape[1]
    epsilon_k = 1e-06

    barrier = pltpu.get_barrier_semaphore()
    for device in (y_dev, lo_dev, hi_dev, core_dev, x_dev):
        pl.semaphore_signal(barrier, inc=1, device_id=device, device_id_type=MESH)

    @pl.when(inside)
    def _():
        pl.semaphore_signal(barrier, inc=1, device_id=mid_dev, device_id_type=MESH)
        pl.semaphore_wait(barrier, 6)

    @pl.when(at_end)
    def _():
        pl.semaphore_wait(barrier, 5)


    def remote(src, dst, send, recv, device):
        return pltpu.make_async_remote_copy(
            src_ref=src, dst_ref=dst, send_sem=send, recv_sem=recv, device_id=device, device_id_type=MESH
        )

    def act_copy(i):
        return remote(acts.at[i, 0], acts.at[i, 1], ya_s.at[i], ya_r.at[i], y_dev)

    def lt_copy(l):
        return remote(odd.at[l], lt.at[l, 1, head], lt_s.at[l], lt_r.at[l], y_dev)

    x_head = head + 2 - 4 * lax.div(head, 2)
    core_head = head + 1 - 2 * c
    far_head = x_head + 1 - 2 * c

    def lt_core(l, part):
        piece = lt.at[l, 1, part]
        return remote(piece, piece, lc_s.at[l], lc_r.at[l], core_dev)

    def lt_x(l, part):
        piece = lt.at[l, 1, part]
        return remote(piece, piece, lx_s.at[l], lx_r.at[l], x_dev)

    def lt_far(l, part):
        piece = lt.at[l, 1, part]
        return remote(piece, piece, lf_s.at[l], lf_r.at[l], core_dev)

    def z1_copy(i):
        return remote(zsend.at[i % 4], z1_hbm.at[i], z1_s.at[i], z1_r.at[i], lo_dev)

    def z2_copy(i):
        return remote(zsend.at[i % 4, pl.ds(0, 2)], z2_hbm.at[i], z2_s.at[i], z2_r.at[i], mid_dev)

    def z3_copy(i):
        return remote(zsend.at[i % 4, 2], z3_hbm.at[i], z3_s.at[i], z3_r.at[i], lo_dev)

    def item_dot(i, l, first, last):
        count = (last - first) * TILE
        mine = dot_plain(lt[l, 0, first:last].reshape(count, tokens), acts[i, 0])
        return mine + dot_plain(lt[l, 1, first:last].reshape(count, tokens), acts[i, 1])

    def stage_load(src, slot):
        copy = pltpu.make_async_copy(src, stage.at[slot], st_sem.at[slot])
        copy.start()
        return copy

    def stage_one(i, l, place):
        act_copy(i).wait_recv()

        @pl.when(at_end)
        def _():
            if i >= 4:
                z1_copy(i - 4).wait_send()
            total = item_dot(i, l, 1, 4)
            for k in range(3):
                zsend[i % 4, k] = low(total[k * TILE : (k + 1) * TILE])
            z1_copy(i).start()

    def stage_two(i, l, place):
        @pl.when(inside)
        def _():
            z1_copy(i).wait_recv()
            loads = [stage_load(z1_hbm.at[i, k], k) for k in (1, 2)]
            if i >= 4:
                z2_copy(i - 4).wait_send()
            total = item_dot(i, l, 2, 4)
            for load in loads:
                load.wait()
            zsend[i % 4, 0] = low(total[:TILE] + wide(stage[2]))
            zsend[i % 4, 1] = low(total[TILE:] + wide(stage[1]))
            z2_copy(i).start()

    def out_wait(i):
        pltpu.make_async_copy(ostage.at[i % 2], dwk_out, out_sem.at[i % 2]).wait()

    def put(i, total, place):
        ref, n, turned = place
        if i >= 2:
            out_wait(i - 2)
        ostage[i % 2] = total.T if turned else total
        at = pl.ds(n * TILE, TILE)
        target = ref.at[at] if turned else ref.at[:, at]
        pltpu.make_async_copy(ostage.at[i % 2], target, out_sem.at[i % 2]).start()

    def stage_three(i, l, place):
        @pl.when(inside)
        def _():
            z2_copy(i).wait_recv()
            loads = [stage_load(z1_hbm.at[i, 0], 0), stage_load(z2_hbm.at[i, 0], 1), stage_load(z2_hbm.at[i, 1], 2)]
            if i >= 4:
                z3_copy(i - 4).wait_send()
            total = item_dot(i, l, 0, 2)
            for load in loads:
                load.wait()
            zsend[i % 4, 2] = low(total[TILE:] + wide(stage[1]))
            z3_copy(i).start()
            put(i, total[:TILE] + wide(stage[0]) + wide(stage[2]), place)

    def stage_four(i, l, place):
        @pl.when(at_end)
        def _():
            z3_copy(i).wait_recv()
            load = stage_load(z3_hbm.at[i], 3)
            total = item_dot(i, l, 0, 1)
            load.wait()
            put(i, total + wide(stage[3]), place)

    def at_tile(j, kind):
        later = j // 3 if isinstance(j, int) else lax.div(j, 3)
        if kind == 0:
            return j + 2 * j * later
        return (2 + 2 * j + kind) * (1 - later) + (3 * j + kind) * later

    ff_kind = {at_tile(j, kind): (j, kind) for j in range(hidden_tiles) for kind in range(3)}
    late = (
        (3, dwo_out, 0, True),
        (3, dwo_out, 1, True),
        (2, dwga_out, 0, False),
        (2, dwga_out, 1, False),
        (2, dwq_out, 0, False),
        (2, dwq_out, 1, False),
        (2, dwk_out, 0, False),
        (2, dwv_out, 0, False),
    )
    item_count = ff_items + 8
    shown = set()
    ltd_load = pltpu.make_async_copy(ltd_hbm, lt.at[1], misc.at[7])

    def item_step(stage_of, i):
        l = (1 if ff_kind[i][1] == 0 else 0) if i < ff_items else late[i - ff_items][0]
        if stage_of is stage_one and l not in shown:
            shown.add(l)
            if l == 1:
                ltd_load.wait()
            else:
                relay_in(l)
        if i < ff_items:
            j, kind = ff_kind[i]
            place = ((dwd_out, dwg_out, dwu_out)[kind], j, kind == 0)
        else:
            place = late[i - ff_items][1:]
        stage_of(i, l, place)

    actions = {
        "a": lambda i: act_copy(i).start(),
        "s1": lambda i: item_step(stage_one, i),
        "s2": lambda i: item_step(stage_two, i),
        "s3": lambda i: item_step(stage_three, i),
        "s4": lambda i: item_step(stage_four, i),
        "r1": lambda l: relay_one(l),
        "r2": lambda l: relay_two(l),
    }

    def after(place):
        for name, i in PLAN.get(place, ()):
            actions[name](i)

    def after_step(place, step, count):
        for k in range(count):
            if f"{place}.{k}" in PLAN:
                pl.when(step == k)(lambda k=k: after(f"{place}.{k}"))

    def spread(l, source):
        @pl.loop(0, 4)
        def _(t):
            at = pl.multiple_of((other_z(z, t) * 2 + y) * TILE, TILE)
            lt[l, 0, t] = source[:, pl.ds(at, TILE)].T

        at = pl.multiple_of((other_z(z, head) * 2 + 1 - y) * TILE, TILE)
        odd[l] = source[:, pl.ds(at, TILE)].T

    def relay_one(l):
        lt_copy(l).wait_recv()
        lt_core(l, head).start()
        lt_x(l, head).start()

    def relay_two(l):
        lt_x(l, x_head).wait_recv()
        lt_far(l, x_head).start()

    def relay_in(l):
        lt_core(l, core_head).wait_recv()
        lt_far(l, far_head).wait_recv()

    def core_copy(k, b):
        return remote(csend.at[b], crecv.at[k % 2, b], c1_s.at[k, b], c1_r.at[k, b], core_dev)

    def x_copy(k, b):
        return remote(fin.at[k % 2, c * 4 + b], xrecv.at[k % 2, b], x_s.at[k, b], x_r.at[k, b], x_dev)

    def fin_copy(k, b):
        piece = fin.at[k % 2, c * 4 + b]
        return remote(piece, piece, c2_s.at[k, b], c2_r.at[k, b], core_dev)

    def fin_copy_in(k, b):
        piece = fin.at[k % 2, (1 - c) * 4 + b]
        return remote(piece, piece, c2_s.at[k, b], c2_r.at[k, b], core_dev)

    def reduce_start(k, loads, compute, place):
        def block_of(step):
            return lax.rem(c + 1 + step, 2) * 4 + lax.div(step, 2)

        for copy in loads(block_of(0), 0):
            copy.start()

        @pl.loop(0, 8)
        def _(step):
            slot, b = lax.rem(step, 2), lax.div(step, 2)

            @pl.when(step < 7)
            def _():
                for copy in loads(block_of(step + 1), 1 - slot):
                    copy.start()

            for copy in loads(block_of(step), slot):
                copy.wait()
            part = compute(slot)

            @pl.when(slot == 0)
            def _():
                csend[b] = low(part)
                core_copy(k, b).start()

            @pl.when(slot == 1)
            def _():
                core_copy(k, b).wait_recv()
                fin[k % 2, c * 4 + b] = low(part + wide(crecv[k % 2, b]))
                x_copy(k, b).start()

            after_step(place, step, 8)

        @pl.loop(0, 4)
        def _(b):
            core_copy(k, b).wait_send()

    def reduce_end(k):
        for b in range(4):
            x_copy(k, b).wait()
            fin[k % 2, c * 4 + b] = low(wide(fin[k % 2, c * 4 + b]) + wide(xrecv[k % 2, b]))
            fin_copy(k, b).start()
            after(f"e{k}.{b}")
        for b in range(4):
            fin_copy_in(k, b).wait_recv()
            fin_copy(k, b).wait_send()
        after(f"e{k}.4")

    def fin_rows(k, at, count):
        return jnp.concatenate([wide(fin[k % 2, n, pl.ds(at, count)]) for n in range(8)], axis=1)

    def rms(value):
        return lax.rsqrt(jnp.mean(value * value, axis=-1, keepdims=True) + epsilon_k)

    n_chunks = tokens // 128

    def first_phase(hbuf, wgb, wub, dmb, sems, w_sems):
        def row_load(r, slot):
            return pltpu.make_async_copy(h_hbm.at[pl.ds(r * 128, 128)], hbuf.at[slot], sems.at[slot])

        def tile_loads(j, slot):
            at = pl.ds(pl.multiple_of(j * TILE, TILE), TILE)
            return (
                pltpu.make_async_copy(wg_hbm.at[:, at], wgb.at[slot], w_sems.at[slot, 0]),
                pltpu.make_async_copy(wu_hbm.at[:, at], wub.at[slot], w_sems.at[slot, 1]),
                pltpu.make_async_copy(dm_hbm.at[j], dmb.at[slot], w_sems.at[slot, 2]),
            )

        row_load(0, 0).start()
        for copy in tile_loads(0, 0):
            copy.start()
        ltd_load.start()

        @pl.loop(0, n_chunks)
        def _(r):
            slot = lax.rem(r, 2)

            @pl.when(r < n_chunks - 1)
            def _():
                row_load(r + 1, 1 - slot).start()

            row_load(r, slot).wait()
            value = hbuf[slot]
            at = pl.ds(pl.multiple_of(r * 128, 128), 128)
            wide_a[at] = low(value * rms(value) * wide(n2_ref[...]))

        after("p0")

        @pl.loop(0, hidden_tiles)
        def _(j):
            slot = lax.rem(j, 2)

            @pl.when(j < hidden_tiles - 1)
            def _():
                for copy in tile_loads(j + 1, 1 - slot):
                    copy.start()

            for copy in tile_loads(j, slot):
                copy.wait()

            @pl.loop(0, 2)
            def _(half):
                at = pl.ds(pl.multiple_of(half * (tokens // 2), 128), tokens // 2)
                a = dot_plain(wide_a[at], wgb[slot])
                u = dot_plain(wide_a[at], wub[slot])
                dm = dmb[slot, at]
                sig = jax.nn.sigmoid(a)
                act = a * sig
                acts[at_tile(j, 0), 0, at] = low(act * u)
                acts[at_tile(j, 1), 0, at] = low(dm * u * sig * (1.0 + a * (1.0 - sig)))
                acts[at_tile(j, 2), 0, at] = low(dm * act)

            after_step("p1", j, 1)

            @pl.when(j == 0)
            def _():
                spread(0, wide_a)
                lt_copy(0).start()
                after("sp0")

            for k in range(1, hidden_tiles):
                if f"p1.{k}" in PLAN:
                    pl.when(j == k)(lambda k=k: after(f"p1.{k}"))

    pl.run_scoped(
        first_phase,
        pltpu.VMEM((2, 128, width), jnp.float32),
        pltpu.VMEM((2, width, TILE), jnp.bfloat16),
        pltpu.VMEM((2, width, TILE), jnp.bfloat16),
        pltpu.VMEM((2, tokens, TILE), jnp.float32),
        pltpu.SemaphoreType.DMA((2,)),
        pltpu.SemaphoreType.DMA((2, 3)),
    )

    def second_phase(wa, wb, sems):
        def loads(n, slot):
            at = pl.ds(pl.multiple_of(n * TILE, TILE), TILE)
            return (
                pltpu.make_async_copy(wg_hbm.at[at], wa.at[slot], sems.at[slot, 0]),
                pltpu.make_async_copy(wu_hbm.at[at], wb.at[slot], sems.at[slot, 1]),
            )

        def compute(slot):
            total = None
            for j in range(hidden_tiles):
                at = pl.ds(j * TILE, TILE)
                part = dot_rows(acts[at_tile(j, 1), 0], wa[slot, :, at])
                part += dot_rows(acts[at_tile(j, 2), 0], wb[slot, :, at])
                total = part if total is None else total + part
            return total

        reduce_start(0, loads, compute, "p2")

    pl.run_scoped(
        second_phase,
        pltpu.VMEM((2, TILE, wg_hbm.shape[1]), jnp.bfloat16),
        pltpu.VMEM((2, TILE, wg_hbm.shape[1]), jnp.bfloat16),
        pltpu.SemaphoreType.DMA((2, 2)),
    )

    def third_phase(wa, sems):
        def loads(n, slot):
            at = pl.ds(pl.multiple_of(n * TILE, TILE), TILE)
            return (pltpu.make_async_copy(wd_hbm.at[:, at], wa.at[slot], sems.at[slot]),)

        def compute(slot):
            total = None
            for j in range(hidden_tiles):
                part = dot_plain(acts[at_tile(j, 0), 0], wa[slot, pl.ds(j * TILE, TILE)])
                total = part if total is None else total + part
            return total

        reduce_start(1, loads, compute, "p3")

    pl.run_scoped(
        third_phase,
        pltpu.VMEM((2, wd_hbm.shape[0], TILE), jnp.bfloat16),
        pltpu.SemaphoreType.DMA((2,)),
    )

    base = ff_items
    for n in range(2):
        pltpu.make_async_copy(
            y_hbm.at[:, pl.ds(n * TILE, TILE)], acts.at[base + n, 0], misc.at[n]
        ).start()

    def xt_own(t):
        shard = other_z(z, t) * 2 + y
        return pltpu.make_async_copy(xt_hbm.at[shard], lt.at[2, 0, t], misc.at[2 + t])

    def xt_odd():
        shard = other_z(z, head) * 2 + 1 - y
        return pltpu.make_async_copy(xt_hbm.at[shard], odd.at[2], misc.at[6])

    for t in range(4):
        xt_own(t).start()
    xt_odd().start()
    for t in range(4):
        xt_own(t).wait()
    xt_odd().wait()
    for n in range(2):
        pltpu.make_async_copy(
            y_hbm.at[:, pl.ds(n * TILE, TILE)], acts.at[base + n, 0], misc.at[n]
        ).wait()
    fill_bias(order_ref, bias, rows, z, y, seq)
    fill_factor(ids_ref, counts_ref, weights_ref, factor_ref, float(tokens * 8))
    after("xt")
    reduce_end(0)

    def fourth_phase(hbuf, cbuf, dbuf, wob, obuf, sbuf, sems, d_sems, w_sems):
        def row_loads(r, slot):
            at = pl.ds(r * 128, 128)
            return (
                pltpu.make_async_copy(h_hbm.at[at], hbuf.at[slot], sems.at[slot, 0]),
                pltpu.make_async_copy(cot_hbm.at[at], cbuf.at[slot], sems.at[slot, 1]),
            )

        def spill(r, slot):
            return pltpu.make_async_copy(dbuf.at[slot], dh_hbm.at[pl.ds(r * 128, 128)], d_sems.at[slot])

        def tile_loads(n):
            at = pl.ds(n * TILE, TILE)
            return (
                pltpu.make_async_copy(wo_hbm.at[at], wob.at[n], w_sems.at[n, 0]),
                pltpu.make_async_copy(o_hbm.at[:, at], obuf.at[n], w_sems.at[n, 1]),
                pltpu.make_async_copy(sig_hbm.at[:, at], sbuf.at[n], w_sems.at[n, 2]),
            )

        for copy in row_loads(0, 0):
            copy.start()
        for n in range(2):
            for copy in tile_loads(n):
                copy.start()
        vec[0] = jnp.zeros_like(vec[0])

        @pl.loop(0, n_chunks)
        def _(r):
            slot = lax.rem(r, 2)

            @pl.when(r < n_chunks - 1)
            def _():
                for copy in row_loads(r + 1, 1 - slot):
                    copy.start()

            for copy in row_loads(r, slot):
                copy.wait()

            @pl.when(r >= 2)
            def _():
                spill(r - 2, slot).wait()

            at = pl.ds(pl.multiple_of(r * 128, 128), 128)
            value = hbuf[slot]
            scale = rms(value)
            normed = value * scale
            grad = fin_rows(0, pl.multiple_of(r * 128, 128), 128)
            vec[0, 1:2] += jnp.sum(grad * normed, axis=0, keepdims=True)
            scaled = grad * wide(n2_ref[...])
            inner = jnp.mean(scaled * normed, axis=-1, keepdims=True)
            dh = wide(cbuf[slot]) * factor_ref[at] + scale * (scaled - normed * inner)
            dbuf[slot] = dh
            wide_a[at] = low(dh)
            spill(r, slot).start()

        spill(n_chunks - 2, n_chunks % 2).wait()
        spill(n_chunks - 1, (n_chunks - 1) % 2).wait()

        after("p4a")
        ones = jnp.ones((8, 128), jnp.bfloat16)
        for n in range(2):
            for copy in tile_loads(n):
                copy.wait()
            dy = dot_rows(wide_a[...], wob[n])
            sig, o = sbuf[n], obuf[n]
            do = low(dy * sig)
            acts[base + 2 + n, 0] = low(dy * o * sig * (1.0 - sig))
            wide_b[:, n * TILE : (n + 1) * TILE] = do
            both = wide(do) * o
            for g in range(2):
                part = both[:, g * 128 : (g + 1) * 128]
                top = low(part)
                rest = low(part - wide(top))
                delta[n, g] = dot_rows(ones, top) + dot_rows(ones, rest)

        spread(3, wide_a)
        after("p4b")
        for device in (core_dev, x_dev):
            pl.semaphore_signal(credit, inc=1, device_id=device, device_id_type=MESH)

    pl.run_scoped(
        fourth_phase,
        pltpu.VMEM((2, 128, width), jnp.float32),
        pltpu.VMEM((2, 128, width), jnp.bfloat16),
        pltpu.VMEM((2, 128, width), jnp.float32),
        pltpu.VMEM((2, TILE, width), jnp.bfloat16),
        pltpu.VMEM((2, tokens, TILE), jnp.float32),
        pltpu.VMEM((2, tokens, TILE), jnp.float32),
        pltpu.SemaphoreType.DMA((2, 2)),
        pltpu.SemaphoreType.DMA((2,)),
        pltpu.SemaphoreType.DMA((2, 3)),
    )

    def attention_back(keep, ysend, lsend, dq_ref, dkv_ref):
        def ky_copy(s):
            return remote(ysend.at[lax.rem(s, 2)], yrecv.at[s], ky_s.at[s], ky_r.at[s], y_dev)

        def kl_copy(s):
            return remote(lsend.at[s], lrecv.at[s], kl_s.at[s], kl_r.at[s], lo_dev)

        def km_copy(s):
            return remote(lsend.at[s, pl.ds(0, 2)], mrecv.at[s], km_s.at[s], km_r.at[s], mid_dev)

        def kh_copy(s):
            return remote(lsend.at[s, 2], hrecv.at[s], kh_s.at[s], kh_r.at[s], lo_dev)

        def ky_step(s):
            ky_copy(s).wait_recv()
            for m in range(4):
                keep[s, m] += wide(yrecv[s, m])

            @pl.when(at_end)
            def _():
                for k in range(3):
                    lsend[s, k] = low(keep[s, k + 1])
                kl_copy(s).start()

        def kl_step(s):
            @pl.when(inside)
            def _():
                kl_copy(s).wait_recv()
                keep[s, 0] += wide(lrecv[s, 0])
                lsend[s, 0] = low(keep[s, 2] + wide(lrecv[s, 2]))
                lsend[s, 1] = low(keep[s, 3] + wide(lrecv[s, 1]))
                km_copy(s).start()

        def km_step(s):
            @pl.when(inside)
            def _():
                km_copy(s).wait_recv()
                keep[s, 0] += wide(mrecv[s, 1])
                lsend[s, 2] = low(keep[s, 1] + wide(mrecv[s, 0]))
                kh_copy(s).start()

        actions["ky"] = ky_step
        actions["kl"] = kl_step
        actions["km"] = km_step
        keys_total = bias.shape[0]

        def fifth_phase(qbuf, kvbuf, q_sem, sems):
            def kv_load(s, slot):
                return pltpu.make_async_copy(kv_hbm.at[s], kvbuf.at[slot], sems.at[slot])

            q_load = pltpu.make_async_copy(q_hbm, qbuf, q_sem)
            q_load.start()
            kv_load(0, 0).start()
            q_load.wait()

            @pl.loop(0, seqs)
            def _(s):
                slot = lax.rem(s, 2)

                @pl.when(s < seqs - 1)
                def _():
                    kv_load(s + 1, 1 - slot).start()

                kv_load(s, slot).wait()
                at = pl.ds(pl.multiple_of(s * rows, 128), rows)
                @pl.when(s >= 2)
                def _():
                    ky_copy(s - 2).wait_send()

                for n in range(2):
                    lanes = [slice((2 * n + g) * 128, (2 * n + g + 1) * 128) for g in range(2)]
                    key = kvbuf[slot, :, n * 128 : (n + 1) * 128]
                    value = kvbuf[slot, :, 256 + n * 128 : 256 + (n + 1) * 128]
                    q = jnp.concatenate([qbuf[at, lane] for lane in lanes], axis=0)
                    do = jnp.concatenate([wide_b[at, lane] for lane in lanes], axis=0)
                    drow = jnp.concatenate([delta[n, g, 0:1, at] for g in range(2)], axis=1)
                    scores = dot_rows(key, q)
                    probs = jnp.exp(scores - lse_ref[s, n] + bias[...])
                    grad_probs = dot_rows(value, do)
                    ds = low(probs * (grad_probs - drow))
                    for start, grad in ((0, dot_plain(ds, q)), (256, dot_plain(low(probs), do))):
                        into = slice(start + n * 128, start + (n + 1) * 128)
                        for m in range(4):
                            keep[s, m, :, into] = grad[2 * m * rows : (2 * m + 1) * rows]
                            ysend[slot, m, :, into] = low(grad[(2 * m + 1) * rows : (2 * m + 2) * rows])
                    dq = dot_first(key, ds).T
                    for g in range(2):
                        dq_ref[at, lanes[g]] = dq[g * rows : (g + 1) * rows]

                ky_copy(s).start()
                after_step("p5", s, seqs)

        pl.run_scoped(
            fifth_phase,
            pltpu.VMEM(q_hbm.shape, jnp.bfloat16),
            pltpu.VMEM((2, keys_total, 512), jnp.bfloat16),
            pltpu.SemaphoreType.DMA,
            pltpu.SemaphoreType.DMA((2,)),
        )

        lt_copy(3).start()
        lt_copy(2).start()
        after("sl3")

        def query_phase(rbuf, sem):
            load = pltpu.make_async_copy(qraw_hbm, rbuf, sem)
            load.start()
            load.wait()
            factor = 128.0**-0.5
            for hd in range(4):
                lane = slice(hd * 128, (hd + 1) * 128)
                raw = rbuf[:, lane]
                scale = rms(raw)
                normed = raw * scale
                grad = dq_ref[:, lane]
                gvec[0, 0:1, 0:128] = (
                    jnp.sum(grad * normed * factor, axis=0, keepdims=True)
                    + (gvec[0, 0:1, 0:128] if hd else 0.0)
                )
                scaled = grad * (wide(qg_ref[...]) * factor)
                out = scale * (scaled - normed * jnp.mean(scaled * normed, axis=-1, keepdims=True))
                acts[base + 4 + hd // 2, 0, :, (hd % 2) * 128 : (hd % 2 + 1) * 128] = low(out)

        gvec[0] = jnp.zeros_like(gvec[0])
        pl.run_scoped(query_phase, pltpu.VMEM(qraw_hbm.shape, jnp.float32), pltpu.SemaphoreType.DMA)

        after("qp")
        reduce_end(1)

        def out_phase(hbuf, obuf, sems, o_sems):
            def load(r, slot):
                return pltpu.make_async_copy(h_hbm.at[pl.ds(r * 128, 128)], hbuf.at[slot], sems.at[slot])

            def store(r, slot):
                return pltpu.make_async_copy(obuf.at[slot], block_out.at[pl.ds(r * 128, 128)], o_sems.at[slot])

            load(0, 0).start()

            @pl.loop(0, n_chunks)
            def _(r):
                slot = lax.rem(r, 2)

                @pl.when(r < n_chunks - 1)
                def _():
                    load(r + 1, 1 - slot).start()

                load(r, slot).wait()

                @pl.when(r >= 2)
                def _():
                    store(r - 2, slot).wait()

                obuf[slot] = low(hbuf[slot] + fin_rows(1, pl.multiple_of(r * 128, 128), 128))
                store(r, slot).start()

            store(n_chunks - 2, n_chunks % 2).wait()
            store(n_chunks - 1, (n_chunks - 1) % 2).wait()

        pl.run_scoped(
            out_phase,
            pltpu.VMEM((2, 128, width), jnp.float32),
            pltpu.VMEM((2, 128, width), jnp.bfloat16),
            pltpu.SemaphoreType.DMA((2,)),
            pltpu.SemaphoreType.DMA((2,)),
        )

        after("op")

        @pl.loop(0, seqs)
        def _(s):
            at = pl.ds(pl.multiple_of(s * rows, 128), rows)

            @pl.when(inside)
            def _():
                dkv_ref[at] = keep[s, 0]

            @pl.when(at_end)
            def _():
                kh_copy(s).wait_recv()
                dkv_ref[at] = keep[s, 0] + wide(hrecv[s])

        def key_phase(rbuf, sem):
            load = pltpu.make_async_copy(kraw_hbm, rbuf, sem)
            load.start()
            load.wait()
            for hd in range(2):
                lane = slice(hd * 128, (hd + 1) * 128)
                raw = rbuf[:, lane]
                scale = rms(raw)
                normed = raw * scale
                grad = dkv_ref[:, lane]
                gvec[0, 0:1, 128:256] = (
                    jnp.sum(grad * normed, axis=0, keepdims=True)
                    + (gvec[0, 0:1, 128:256] if hd else 0.0)
                )
                scaled = grad * wide(kg_ref[...])
                out = scale * (scaled - normed * jnp.mean(scaled * normed, axis=-1, keepdims=True))
                acts[base + 6, 0, :, lane] = low(out)
            acts[base + 7, 0] = low(dkv_ref[:, 256:512])

        pl.run_scoped(key_phase, pltpu.VMEM(kraw_hbm.shape, jnp.float32), pltpu.SemaphoreType.DMA)
        after("kp")

        @pl.loop(seqs - 2, seqs)
        def _(s):
            ky_copy(s).wait_send()

        @pl.loop(0, seqs)
        def _(s):
            @pl.when(at_end)
            def _():
                kl_copy(s).wait_send()

            @pl.when(inside)
            def _():
                km_copy(s).wait_send()
                kh_copy(s).wait_send()

    pl.run_scoped(
        attention_back,
        pltpu.VMEM((seqs, 4, rows, 512), jnp.float32),
        pltpu.VMEM((2, 4, rows, 512), jnp.bfloat16),
        pltpu.VMEM((seqs, 3, rows, 512), jnp.bfloat16),
        pltpu.VMEM((tokens, 512), jnp.float32),
        pltpu.VMEM((tokens, 512), jnp.float32),
    )

    def sixth_phase(wb, sems):
        pieces = ((wga_hbm, base + 2, 2), (wq_hbm, base + 4, 2), (wk_hbm, base + 6, 1), (wv_hbm, base + 7, 1))

        def loads(n, slot):
            at = pl.ds(pl.multiple_of(n * TILE, TILE), TILE)
            out, start = [], 0
            for p, (ref, _, count) in enumerate(pieces):
                out.append(
                    pltpu.make_async_copy(
                        ref.at[at], wb.at[slot, :, pl.ds(start, count * TILE)], sems.at[slot, p]
                    )
                )
                start += count * TILE
            return out

        def compute(slot):
            total, start = None, 0
            for _, first, count in pieces:
                for n in range(count):
                    part = dot_rows(acts[first + n, 0], wb[slot, :, pl.ds(start, TILE)])
                    total = part if total is None else total + part
                    start += TILE
            return total

        pl.semaphore_wait(credit, 2)
        reduce_start(2, loads, compute, "p7")

    pl.run_scoped(
        sixth_phase,
        pltpu.VMEM((2, TILE, 6 * TILE), jnp.bfloat16),
        pltpu.SemaphoreType.DMA((2, 4)),
    )

    for step in range(5):
        device = (y_dev, lo_dev, hi_dev, core_dev, x_dev)[step]
        copy = remote(gvec.at[step], gvec_got.at[step], gv_s.at[step], gv_r.at[step], device)
        copy.start()
        copy.wait()
        gvec[step + 1] = gvec[step] + gvec_got[step]
    piece = qg_out.shape[1]
    turn = lax.rem(128 - seq * piece, 128)
    for out, at in ((qg_out, 0), (kg_out, 128)):
        out[...] = pltpu.roll(gvec[5, :, at : at + 128], turn, 1)[0:1, 0:piece]

    reduce_end(2)

    def last_phase(xbuf, dbuf, obuf, sems, o_sems):
        def loads(r, slot):
            at = pl.ds(r * 128, 128)
            return (
                pltpu.make_async_copy(x_hbm.at[at], xbuf.at[slot], sems.at[slot, 0]),
                pltpu.make_async_copy(dh_hbm.at[at], dbuf.at[slot], sems.at[slot, 1]),
            )

        def store(r, slot):
            return pltpu.make_async_copy(obuf.at[slot], x_out.at[pl.ds(r * 128, 128)], o_sems.at[slot])

        for copy in loads(0, 0):
            copy.start()

        @pl.loop(0, n_chunks)
        def _(r):
            slot = lax.rem(r, 2)

            @pl.when(r < n_chunks - 1)
            def _():
                for copy in loads(r + 1, 1 - slot):
                    copy.start()

            for copy in loads(r, slot):
                copy.wait()

            @pl.when(r >= 2)
            def _():
                store(r - 2, slot).wait()

            value = wide(xbuf[slot])
            scale = rms(value)
            normed = value * scale
            grad = fin_rows(2, pl.multiple_of(r * 128, 128), 128)
            vec[0, 0:1] += jnp.sum(grad * normed, axis=0, keepdims=True)
            scaled = grad * wide(n1_ref[...])
            inner = jnp.mean(scaled * normed, axis=-1, keepdims=True)
            obuf[slot] = low(dbuf[slot] + scale * (scaled - normed * inner))
            store(r, slot).start()

        store(n_chunks - 2, n_chunks % 2).wait()
        store(n_chunks - 1, (n_chunks - 1) % 2).wait()

    pl.run_scoped(
        last_phase,
        pltpu.VMEM((2, 128, width), jnp.bfloat16),
        pltpu.VMEM((2, 128, width), jnp.float32),
        pltpu.VMEM((2, 128, width), jnp.bfloat16),
        pltpu.SemaphoreType.DMA((2, 2)),
        pltpu.SemaphoreType.DMA((2,)),
    )

    after("lp")
    for step in range(3):
        device = (y_dev, lo_dev, hi_dev)[step]
        copy = remote(vec.at[step], vec_got.at[step], nv_s.at[step], nv_r.at[step], device)
        copy.start()
        copy.wait()
        vec[step + 1] = vec[step] + vec_got[step]
    own = pl.ds(pl.multiple_of(seq * TILE, TILE), TILE)
    n1_out[...] = vec[3, 0:1, own]
    n2_out[...] = vec[3, 1:2, own]

    after("vec")

    @pl.loop(0, item_count)
    def _(i):
        act_copy(i).wait_send()

    for i in range(item_count - 4, item_count):

        @pl.when(at_end)
        def _():
            z1_copy(i).wait_send()

        @pl.when(inside)
        def _():
            z2_copy(i).wait_send()
            z3_copy(i).wait_send()

    for i in range(item_count - 2, item_count):
        out_wait(i)

    for l in (0, 2, 3):
        lt_copy(l).wait_send()
        lt_core(l, head).wait_send()
        lt_x(l, head).wait_send()
        lt_far(l, x_head).wait_send()


def back_call(hbm, vmem, smem, sizes):
    tokens, width, seqs, rows, keys_total, hidden = sizes
    count = 3 * (hidden // TILE) + 8
    bf, f32 = jnp.bfloat16, jnp.float32
    dma = pltpu.SemaphoreType.DMA
    scratch = [
        pltpu.VMEM((count, 2, tokens, TILE), bf),
        pltpu.VMEM((4, 2, 4, TILE, tokens), bf),
        pltpu.VMEM((4, TILE, tokens), bf),
        pltpu.VMEM((4, tokens, TILE), bf),
        pltpu.VMEM((2, 4, tokens, TILE), bf),
        pltpu.VMEM((2, 4, tokens, TILE), bf),
        pltpu.VMEM((2, 8, tokens, TILE), bf),
        pltpu.VMEM((seqs, 4, rows, 512), bf),
        pltpu.VMEM((seqs, 3, rows, 512), bf),
        pltpu.VMEM((seqs, 2, rows, 512), bf),
        pltpu.VMEM((seqs, rows, 512), bf),
        pltpu.VMEM((4, 3, TILE, TILE), bf),
        pltpu.VMEM((4, TILE, TILE), bf),
        pltpu.VMEM((2, TILE, TILE), f32),
        pltpu.VMEM((tokens, width), bf),
        pltpu.VMEM((tokens, width), bf),
        pltpu.VMEM((2, 2, 8, tokens), f32),
        pltpu.VMEM((4, 8, width), f32),
        pltpu.VMEM((3, 8, width), f32),
        pltpu.VMEM((6, 8, 256), f32),
        pltpu.VMEM((5, 8, 256), f32),
        pltpu.VMEM((keys_total, 2 * rows), f32),
        pltpu.VMEM((tokens, 1), f32),
        *(dma((count,)) for _ in range(8)),
        *(dma((4,)) for _ in range(8)),
        *(dma((3, 4)) for _ in range(6)),
        *(dma((seqs,)) for _ in range(8)),
        dma((3,)), dma((3,)), dma((5,)), dma((5,)),
        dma((4,)), dma((2,)), dma((8,)), pltpu.SemaphoreType.REGULAR,
    ]
    any_spec = pl.BlockSpec(memory_space=pl.ANY)
    vmem_spec = pl.BlockSpec(memory_space=pltpu.VMEM)
    smem_spec = pl.BlockSpec(memory_space=pltpu.SMEM)
    return pl.pallas_call(
        back_kernel,
        out_shape=[
            jax.ShapeDtypeStruct((tokens, width), bf),
            jax.ShapeDtypeStruct((tokens, width), bf),
            jax.ShapeDtypeStruct((hidden, TILE), f32),
            jax.ShapeDtypeStruct((TILE, hidden), f32),
            jax.ShapeDtypeStruct((TILE, hidden), f32),
            jax.ShapeDtypeStruct((512, TILE), f32),
            jax.ShapeDtypeStruct((TILE, 512), f32),
            jax.ShapeDtypeStruct((TILE, 512), f32),
            jax.ShapeDtypeStruct((TILE, TILE), f32),
            jax.ShapeDtypeStruct((TILE, TILE), f32),
            jax.ShapeDtypeStruct((1, width // 8), f32),
            jax.ShapeDtypeStruct((1, width // 8), f32),
            jax.ShapeDtypeStruct((1, 16), f32),
            jax.ShapeDtypeStruct((1, 16), f32),
            jax.ShapeDtypeStruct((tokens, width), f32),
            jax.ShapeDtypeStruct((count, 3, TILE, TILE), bf),
            jax.ShapeDtypeStruct((count, 2, TILE, TILE), bf),
            jax.ShapeDtypeStruct((count, TILE, TILE), bf),
        ],
        in_specs=[any_spec] * len(hbm) + [vmem_spec] * len(vmem) + [smem_spec] * len(smem),
        out_specs=[any_spec] * 10 + [vmem_spec] * 4 + [any_spec] * 4,
        scratch_shapes=scratch,
        compiler_params=pltpu.CompilerParams(
            collective_id=1, has_side_effects=True, vmem_limit_bytes=61 << 20
        ),
    )(*hbm, *vmem, *smem)


def hand_over_kernel(count, *refs):
    src, dst, held, sems = refs[:count], refs[count : 2 * count], refs[2 * count : -1], refs[-1]
    into = [pltpu.make_async_copy(src[i], held[i], sems.at[0, i]) for i in range(count)]
    out = [pltpu.make_async_copy(held[i], dst[i], sems.at[1, i]) for i in range(count)]
    for copy in into:
        copy.start()
    for i in range(count):
        into[i].wait()
        out[i].start()
    for copy in out:
        copy.wait()


def hand_over(arrays):
    any_spec = pl.BlockSpec(memory_space=pl.ANY)
    count = len(arrays)
    return pl.pallas_call(
        functools.partial(hand_over_kernel, count),
        out_shape=[jax.ShapeDtypeStruct(a.shape, a.dtype) for a in arrays],
        in_specs=[any_spec] * count,
        out_specs=[any_spec] * count,
        scratch_shapes=[
            *(pltpu.VMEM(a.shape, a.dtype) for a in arrays),
            pltpu.SemaphoreType.DMA((2, count)),
        ],
        compiler_params=pltpu.CompilerParams(vmem_limit_bytes=61 << 20),
    )(*arrays)


def forward_kernel(
    x_hbm, wq_hbm, wk_hbm, wv_hbm, wga_hbm, wo_hbm, cot_hbm, wd_hbm,
    ids_ref, n1_ref, qg_ref, kg_ref, order_ref, counts_ref, weights_ref,
    h_out, xt_out, q_out, kv_out, o_out, sig_out, y_out, qraw_out, kraw_out, ltd_out, dm_out, lse_ref,
    xv, xn, wqv, wkv, wvv, wgav, wov, kv, qv, qraw, kraw, sig, ov, yv, xtv, hv,
    dout, ltd, odd, wdv, dmv, bias, factor_ref,
    csend, crecv, fin, xrecv,
    x_sem, w_sem, out_sem, h_sem, kz_s, kz_r, kf_s, ky_s, ky_r, l_sem, d_sem, m_sem, c1_s, c1_r, x_s, x_r, c2_s, c2_r,
):
    seq, head = lax.axis_index("seq"), lax.axis_index("head")
    z, y = lax.div(seq, 2), lax.rem(seq, 2)
    c = lax.rem(head, 2)
    y_dev = {"seq": z * 2 + 1 - y}
    lo_dev, mid_dev = {"seq": other_z(z, 1) * 2 + y}, {"seq": (3 - z) * 2 + y}
    at_end, inside = lax.rem(z, 3) == 0, lax.rem(z, 3) != 0
    core_dev = {"head": head + 1 - 2 * c}
    x_dev = {"head": head + 2 - 4 * lax.div(head, 2)}
    seqs, slots, rows = kv.shape[0], kv.shape[1], kv.shape[2]
    tokens, width = x_hbm.shape
    half = width // 2
    epsilon_k = 1e-06

    def rms(value):
        return lax.rsqrt(jnp.mean(value * value, axis=-1, keepdims=True) + epsilon_k)

    def rows_at(s):
        return pl.ds(pl.multiple_of(s * rows, 128), rows)

    def x_load(s):
        return pltpu.make_async_copy(x_hbm.at[rows_at(s)], xv.at[rows_at(s)], x_sem.at[s])

    weight_loads = [
        pltpu.make_async_copy(src, dst, w_sem.at[i])
        for i, (src, dst) in enumerate(
            ((wk_hbm, wkv), (wv_hbm, wvv), (wq_hbm, wqv), (wga_hbm, wgav), (wo_hbm, wov))
        )
    ]
    for s in range(seqs):
        x_load(s).start()
    for load in weight_loads:
        load.start()
    for s in range(seqs):
        pltpu.make_async_copy(cot_hbm.at[rows_at(s)], dout.at[rows_at(s)], d_sem.at[s]).start()

    barrier = pltpu.get_barrier_semaphore()
    for device in (y_dev, lo_dev, core_dev, x_dev):
        pl.semaphore_signal(barrier, inc=1, device_id=device, device_id_type=MESH)

    @pl.when(inside)
    def _():
        pl.semaphore_signal(barrier, inc=1, device_id=mid_dev, device_id_type=MESH)
        pl.semaphore_wait(barrier, 5)

    @pl.when(at_end)
    def _():
        pl.semaphore_wait(barrier, 4)

    def remote(src, dst, send, recv, device):
        return pltpu.make_async_remote_copy(
            src_ref=src, dst_ref=dst, send_sem=send, recv_sem=recv, device_id=device, device_id_type=MESH
        )

    def own_out(s):
        return remote(kv.at[s, 0], kv.at[s, 2], kz_s.at[s, 1], kz_r.at[s, 1], lo_dev)

    def own_over(s):
        return remote(kv.at[s, 0], kv.at[s, 6], kz_s.at[s, 3], kz_r.at[s, 3], mid_dev)

    def end_over(s):
        return remote(kv.at[s, 2], kv.at[s, 4], kz_s.at[s, 2], kz_r.at[s, 2], mid_dev)

    def mid_out(s):
        return remote(kv.at[s, 6], kv.at[s, 4], kf_s.at[s, 0], kz_r.at[s, 2], lo_dev)

    def far_out(s):
        return remote(kv.at[s, 4], kv.at[s, 6], kf_s.at[s, 1], kz_r.at[s, 3], lo_dev)

    def y_copy(s, t):
        return remote(kv.at[s, 2 * t], kv.at[s, 2 * t + 1], ky_s.at[s, t], ky_r.at[s, t], y_dev)

    def core_copy(s):
        return remote(csend.at[s], crecv.at[s], c1_s.at[s], c1_r.at[s], core_dev)

    def x_copy(s):
        return remote(fin.at[s, c], xrecv.at[s], x_s.at[s], x_r.at[s], x_dev)

    def fin_copy(s):
        return remote(fin.at[s, c], fin.at[s, c], c2_s.at[s], c2_r.at[s], core_dev)

    def fin_copy_in(s):
        piece = fin.at[s, 1 - c]
        return remote(piece, piece, c2_s.at[s], c2_r.at[s], core_dev)

    weight_loads[0].wait()
    weight_loads[1].wait()

    @pl.loop(0, seqs)
    def _(s):
        x_load(s).wait()
        at = rows_at(s)
        value = wide(xv[at])
        xn[at] = low(value * rms(value) * wide(n1_ref[...]))
        raw = dot_plain(xn[at], wkv[...])
        kraw[at] = raw
        for n in range(2):
            lane = slice(n * 128, (n + 1) * 128)
            part = raw[:, lane]
            kv[s, 0, :, lane] = low(part * rms(part) * wide(kg_ref[...]))
        kv[s, 0, :, 256:512] = low(dot_plain(xn[at], wvv[...]))
        y_copy(s, 0).start()
        own_out(s).start()

        @pl.when(inside)
        def _():
            own_over(s).start()

    outs = []

    def leave(src, dst):
        copy = pltpu.make_async_copy(src, dst, out_sem.at[len(outs)])
        copy.start()
        outs.append(copy)

    leave(kraw, kraw_out)

    def forward_keys(s):
        own_out(s).wait_recv()

        @pl.when(inside)
        def _():
            end_over(s).start()
            y_copy(s, 1).start()
            own_over(s).wait_recv()
            mid_out(s).start()
            y_copy(s, 3).start()
            end_over(s).wait_recv()
            far_out(s).start()
            y_copy(s, 2).start()

        @pl.when(at_end)
        def _():
            y_copy(s, 1).start()
            mid_out(s).wait_recv()
            y_copy(s, 2).start()
            far_out(s).wait_recv()
            y_copy(s, 3).start()

    hidden_tiles = wd_hbm.shape[0] // TILE

    def cot_load(s):
        return pltpu.make_async_copy(cot_hbm.at[rows_at(s)], dout.at[rows_at(s)], d_sem.at[s])

    def wd_load(j):
        at = pl.ds(pl.multiple_of(j * TILE, TILE), TILE)
        return pltpu.make_async_copy(wd_hbm.at[at], wdv.at[lax.rem(j, 2)], l_sem.at[lax.rem(j, 2)])

    def dm_store(j):
        return pltpu.make_async_copy(dmv.at[lax.rem(j, 2)], dm_out.at[j], m_sem.at[lax.rem(j, 2)])

    def spread_copy():
        return remote(odd, ltd.at[1, pl.ds(2 * c, 2)], l_sem.at[2], l_sem.at[3], y_dev)

    def relay_copy(part):
        piece = ltd.at[1, pl.ds(2 * part, 2)]
        return remote(piece, piece, l_sem.at[4], l_sem.at[5], core_dev)

    def dm_tile(j):
        @pl.when(j < hidden_tiles - 1)
        def _():
            wd_load(j + 1).start()

        wd_load(j).wait()

        @pl.when(j >= 2)
        def _():
            dm_store(j - 2).wait()

        dmv[lax.rem(j, 2)] = dot_rows(dout[...], wdv[lax.rem(j, 2)])
        dm_store(j).start()

    fill_bias(order_ref, bias, rows, z, y, seq)
    fill_factor(ids_ref, counts_ref, weights_ref, factor_ref, float(tokens * 8))

    weight_loads[2].wait()
    weight_loads[3].wait()
    scale_q = 128.0**-0.5

    @pl.loop(0, seqs)
    def _(s):
        at = rows_at(s)
        raw = dot_plain(xn[at], wqv[...])
        qraw[at] = raw
        for n in range(4):
            lane = slice(n * 128, (n + 1) * 128)
            part = raw[:, lane]
            qv[at, lane] = low(part * rms(part) * (wide(qg_ref[...]) * scale_q))
        sig[at] = jax.nn.sigmoid(dot_plain(xn[at], wgav[...]))

    leave(qraw, qraw_out)
    leave(qv, q_out)
    leave(sig, sig_out)
    forward_keys(0)

    @pl.loop(0, width // TILE)
    def _(n):
        at = pl.ds(pl.multiple_of(n * TILE, TILE), TILE)
        xtv[n] = xn[:, at].T

    leave(xtv, xt_out)
    wd_load(0).start()

    @pl.loop(0, seqs)
    def _(s):
        cot_load(s).wait()
        at = rows_at(s)
        dout[at] = low(wide(dout[at]) * factor_ref[at])

    @pl.loop(0, 4)
    def _(t):
        at = pl.multiple_of((other_z(z, t) * 2 + y) * TILE, TILE)
        ltd[0, t] = dout[:, pl.ds(at, TILE)].T

    @pl.loop(0, 2)
    def _(k):
        at = pl.multiple_of((other_z(z, 2 * c + k) * 2 + 1 - y) * TILE, TILE)
        odd[k] = dout[:, pl.ds(at, TILE)].T

    weight_loads[4].wait()

    def finish(s):
        x_copy(s).wait()
        fin[s, c] = low(wide(fin[s, c]) + wide(xrecv[s]))
        fin_copy(s).start()

    def h_store(s, slot):
        return pltpu.make_async_copy(hv.at[slot], h_out.at[rows_at(s)], h_sem.at[slot])

    def finish_rows(s):
        slot = lax.rem(s, 2)
        fin_copy_in(s).wait_recv()

        @pl.when(s >= 2)
        def _():
            h_store(s - 2, slot).wait()

        hv[slot, :, 0:half] = wide(xv[rows_at(s), 0:half]) + wide(fin[s, 0])
        hv[slot, :, half:width] = wide(xv[rows_at(s), half:width]) + wide(fin[s, 1])
        h_store(s, slot).start()

    @pl.loop(0, seqs)
    def _(s):
        @pl.when(s < seqs - 1)
        def _():
            forward_keys(s + 1)

            @pl.when(s == seqs - 2)
            def _():
                spread_copy().start()

            dm_tile(2 * s)
            dm_tile(2 * s + 1)

        for t in range(4):
            y_copy(s, t).wait_recv()
        at = rows_at(s)
        for n in range(2):
            lanes = [slice((2 * n + g) * 128, (2 * n + g + 1) * 128) for g in range(2)]
            key = kv[s, :, :, n * 128 : (n + 1) * 128].reshape(slots * rows, 128)
            value = kv[s, :, :, 256 + n * 128 : 256 + (n + 1) * 128].reshape(slots * rows, 128)
            q = jnp.concatenate([qv[at, lane] for lane in lanes], axis=0)
            scores = dot_rows(key, q) + bias[...]
            top = jnp.max(scores, axis=0, keepdims=True)
            probs = jnp.exp(scores - top)
            total = jnp.sum(probs, axis=0, keepdims=True)
            out = (dot_first(value, low(probs)) / total).T
            lse_ref[s, n] = top + jnp.log(total)
            for g in range(2):
                ov[at, lanes[g]] = out[g * rows : (g + 1) * rows]
        gated = low(ov[at] * sig[at])
        yv[at] = gated
        away = pl.ds(pl.multiple_of((1 - c) * half, 128), half)
        mine = pl.ds(pl.multiple_of(c * half, 128), half)
        csend[s] = low(dot_plain(gated, wov[:, away]))
        core_copy(s).start()
        part = dot_plain(gated, wov[:, mine])
        core_copy(s).wait_recv()
        fin[s, c] = low(part + wide(crecv[s]))
        x_copy(s).start()

        @pl.when(s >= 1)
        def _():
            finish(s - 1)

        @pl.when(s >= 2)
        def _():
            finish_rows(s - 2)

    leave(kv, kv_out)
    leave(ov, o_out)
    leave(yv, y_out)
    finish_rows(seqs - 2)
    spread_copy().wait_recv()
    relay_copy(c).start()
    finish(seqs - 1)
    finish_rows(seqs - 1)
    h_store(seqs - 2, seqs % 2).wait()
    h_store(seqs - 1, (seqs - 1) % 2).wait()
    relay_copy(1 - c).wait_recv()
    leave(ltd, ltd_out)
    spread_copy().wait_send()
    relay_copy(c).wait_send()
    dm_store(hidden_tiles - 2).wait()
    dm_store(hidden_tiles - 1).wait()
    for copy in outs:
        copy.wait()

    @pl.loop(0, seqs)
    def _(s):
        own_out(s).wait_send()

        @pl.when(inside)
        def _():
            for copy in (own_over, end_over, mid_out, far_out):
                copy(s).wait_send()

        for t in range(4):
            y_copy(s, t).wait_send()
        core_copy(s).wait_send()
        fin_copy(s).wait_send()


def forward_call(hbm, vmem, smem, sizes):
    tokens, width, seqs, rows, slots, hidden = sizes
    bf, f32 = jnp.bfloat16, jnp.float32
    dma = pltpu.SemaphoreType.DMA
    half = width // 2
    kv_shape = (seqs, slots, rows, 512)
    scratch = [
        pltpu.VMEM((tokens, width), bf),
        pltpu.VMEM((tokens, width), bf),
        pltpu.VMEM((width, 512), bf),
        pltpu.VMEM((width, 256), bf),
        pltpu.VMEM((width, 256), bf),
        pltpu.VMEM((width, 512), bf),
        pltpu.VMEM((512, width), bf),
        pltpu.VMEM(kv_shape, bf),
        pltpu.VMEM((tokens, 512), bf),
        pltpu.VMEM((tokens, 512), f32),
        pltpu.VMEM((tokens, 256), f32),
        pltpu.VMEM((tokens, 512), f32),
        pltpu.VMEM((tokens, 512), f32),
        pltpu.VMEM((tokens, 512), bf),
        pltpu.VMEM((width // TILE, TILE, tokens), bf),
        pltpu.VMEM((2, rows, width), f32),
        pltpu.VMEM((tokens, width), bf),
        pltpu.VMEM((2, 4, TILE, tokens), bf),
        pltpu.VMEM((2, TILE, tokens), bf),
        pltpu.VMEM((2, TILE, width), bf),
        pltpu.VMEM((2, tokens, TILE), f32),
        pltpu.VMEM((slots * rows, 2 * rows), f32),
        pltpu.VMEM((tokens, 1), f32),
        pltpu.VMEM((seqs, rows, half), bf),
        pltpu.VMEM((seqs, rows, half), bf),
        pltpu.VMEM((seqs, 2, rows, half), bf),
        pltpu.VMEM((seqs, rows, half), bf),
        dma((seqs,)), dma((5,)), dma((9,)), dma((2,)),
        *(dma((seqs, 4)) for _ in range(5)),
        dma((6,)), dma((seqs,)), dma((2,)),
        *(dma((seqs,)) for _ in range(6)),
    ]
    any_spec = pl.BlockSpec(memory_space=pl.ANY)
    vmem_spec = pl.BlockSpec(memory_space=pltpu.VMEM)
    smem_spec = pl.BlockSpec(memory_space=pltpu.SMEM)
    return pl.pallas_call(
        forward_kernel,
        out_shape=[
            jax.ShapeDtypeStruct((tokens, width), f32),
            jax.ShapeDtypeStruct((width // TILE, TILE, tokens), bf),
            jax.ShapeDtypeStruct((tokens, 512), bf),
            jax.ShapeDtypeStruct(kv_shape, bf),
            jax.ShapeDtypeStruct((tokens, 512), f32),
            jax.ShapeDtypeStruct((tokens, 512), f32),
            jax.ShapeDtypeStruct((tokens, 512), bf),
            jax.ShapeDtypeStruct((tokens, 512), f32),
            jax.ShapeDtypeStruct((tokens, 256), f32),
            jax.ShapeDtypeStruct((2, 4, TILE, tokens), bf),
            jax.ShapeDtypeStruct((hidden // TILE, tokens, TILE), f32),
            jax.ShapeDtypeStruct((seqs, 2, 1, 2 * rows), f32),
        ],
        in_specs=[any_spec] * len(hbm) + [vmem_spec] * len(vmem) + [smem_spec] * len(smem),
        out_specs=[any_spec] * 11 + [vmem_spec],
        scratch_shapes=scratch,
        compiler_params=pltpu.CompilerParams(
            collective_id=2, has_side_effects=True, vmem_limit_bytes=60 << 20
        ),
    )(*hbm, *vmem, *smem)


def on_device(
    x_in,
    cot,
    domain_ids,
    domain_counts,
    domain_weights,
    block_order,
    norm1,
    w_query,
    w_key,
    w_value,
    w_gate_attn,
    w_out,
    query_gain,
    key_gain,
    norm2,
    w_gate,
    w_up,
    w_down,
):
    sequences, local_rows, width = x_in.shape
    row_total = sequences * local_rows
    devices = lax.axis_size("seq")
    x_rows = x_in.reshape(row_total, width)
    scalars = (block_order, domain_counts, domain_weights)
    h, xt, query, kv, attn, sig, gated, query_raw, key_raw, ltd, dm, lse = forward_call(
        (x_rows, w_query, w_key, w_value, w_gate_attn, w_out, cot.reshape(row_total, width), w_down),
        (domain_ids, norm1[None, :], query_gain[None, :], key_gain[None, :]),
        scalars,
        (row_total, width, sequences, local_rows, devices, w_down.shape[0]),
    )
    out, x_grad, down, gate, up, wout, wga, wquery, wkey, wvalue, *small = back_call(
        (
            h,
            cot.reshape(row_total, width),
            x_rows,
            xt,
            ltd,
            dm,
            query,
            kv.reshape(sequences, devices * local_rows, -1),
            attn,
            sig,
            gated,
            query_raw,
            key_raw,
            w_gate,
            w_up,
            w_down,
            w_out,
            w_query,
            w_key,
            w_value,
            w_gate_attn,
        ),
        (
            domain_ids,
            lse,
            norm1[None, :],
            norm2[None, :],
            query_gain[None, :],
            key_gain[None, :],
        ),
        scalars,
        (row_total, width, sequences, local_rows, local_rows * devices, w_down.shape[0]),
    )

    out, x_grad, down, gate, up, wout, wga, wquery, wkey, wvalue, *small = hand_over(
        (out, x_grad, down, gate, up, wout, wga, wquery, wkey, wvalue, *small[:4])
    )
    return (
        out.reshape(x_in.shape),
        x_grad.reshape(x_in.shape),
        small[0].reshape(-1),
        wquery,
        wkey,
        wvalue,
        wga,
        wout,
        small[2].reshape(-1),
        small[3].reshape(-1),
        small[1].reshape(-1),
        gate,
        up,
        down,
    )


def on_device_plain(
    x_in,
    cot,
    domain_ids,
    domain_counts,
    domain_weights,
    block_order,
    norm1,
    w_query,
    w_key,
    w_value,
    w_gate_attn,
    w_out,
    query_gain,
    key_gain,
    norm2,
    w_gate,
    w_up,
    w_down,
):
    sequences, local_rows, model_width = x_in.shape
    row_total = sequences * local_rows
    head_dim = query_gain.shape[0]
    kv_local = w_key.shape[1] // head_dim
    q_local = w_query.shape[1] // head_dim
    group_size = q_local // kv_local
    block_rows = local_rows // 2
    seq_devices = lax.axis_size("seq")
    first_row = lax.axis_index("seq") * local_rows
    query_pos = positions(block_order, first_row, local_rows, block_rows)
    query_factor = head_dim ** (-0.5)
    q_gain = query_gain.astype(jnp.float32)
    k_gain = key_gain.astype(jnp.float32)
    gain_one = norm1.astype(jnp.float32)
    gain_two = norm2.astype(jnp.float32)
    x_float = x_in.reshape(row_total, model_width).astype(jnp.float32)
    scale_one = norm_scale(x_float)
    normed_one = x_float * scale_one
    x_normed = (normed_one * gain_one).astype(jnp.bfloat16)
    query_raw = product(x_normed, w_query).reshape(row_total, q_local, head_dim)
    key_raw = product(x_normed, w_key).reshape(row_total, kv_local, head_dim)
    value_rows = product(x_normed, w_value).astype(jnp.bfloat16)
    gate_pre = product(x_normed, w_gate_attn)
    query_scale = norm_scale(query_raw)
    query_normed = query_raw * query_scale
    key_scale = norm_scale(key_raw)
    key_normed = key_raw * key_scale
    query = (query_normed * q_gain * query_factor).astype(jnp.bfloat16)
    key_rows = (key_normed * k_gain).astype(jnp.bfloat16)
    project_query_heads = query.reshape(
        sequences, local_rows, kv_local, group_size, head_dim
    ).transpose(0, 2, 3, 1, 4)
    (
        query_scale,
        query_normed,
        key_scale,
        key_normed,
        query_heads,
        key_rows,
        value_rows,
        gate_pre,
    ) = (
        query_scale,
        query_normed,
        key_scale,
        key_normed,
        project_query_heads,
        key_rows,
        value_rows,
        gate_pre,
    )
    key_seq = key_rows.reshape(sequences, local_rows, kv_local * head_dim)
    value_seq = value_rows.reshape(sequences, local_rows, kv_local * head_dim)
    stat_shape = (sequences, kv_local, group_size, local_rows)
    running_max = jnp.full(stat_shape, -1e30, jnp.float32)
    key_piece = lax.all_gather(key_seq, "seq", axis=1, tiled=True)
    value_piece = lax.all_gather(value_seq, "seq", axis=1, tiled=True)
    row_count = key_piece.shape[1]
    key_block = key_piece.reshape(sequences, row_count, kv_local, head_dim)
    value_block = value_piece.reshape(sequences, row_count, kv_local, head_dim)
    key_pos = positions(block_order, jnp.int32(0), row_count, block_rows)
    allowed = key_pos[None, :] <= query_pos[:, None]
    scores = jnp.einsum(
        "skgqd,spkd->skgqp", query_heads, key_block, preferred_element_type=jnp.float32
    )
    scores = jnp.where(allowed, scores, -1e30)
    new_max = jnp.maximum(running_max, jnp.max(scores, axis=-1))
    weights = jnp.where(allowed, jnp.exp(scores - new_max[..., None]), 0.0)
    running_sum = jnp.sum(weights, axis=-1)
    weighted = jnp.einsum(
        "skgqp,spkd->skgqd",
        weights.astype(jnp.bfloat16),
        value_block,
        preferred_element_type=jnp.float32,
    )
    running_max, running_sum, weighted = (new_max, running_sum, weighted)
    log_total = running_max + jnp.log(running_sum)
    attn_heads = weighted / running_sum[..., None]
    attn_flat = attn_heads.transpose(0, 3, 1, 2, 4).reshape(row_total, q_local * head_dim)
    gate_sig = jax.nn.sigmoid(gate_pre)
    gated = (attn_flat * gate_sig).astype(jnp.bfloat16)
    attn_sum = lax.psum(product(gated, w_out).astype(jnp.bfloat16), "head").astype(jnp.float32)
    residual = x_float + attn_sum
    scale_two = norm_scale(residual)
    normed_two = residual * scale_two
    h_normed = (normed_two * gain_two).astype(jnp.bfloat16)
    gate_proj = product(h_normed, w_gate)
    up_proj = product(h_normed, w_up)
    gate_logit = jax.nn.sigmoid(gate_proj)
    gate_act = gate_proj * gate_logit
    mixed = (gate_act * up_proj).astype(jnp.bfloat16)
    mlp_sum = lax.psum(product(mixed, w_down).astype(jnp.bfloat16), "head").astype(jnp.float32)
    block_out = (
        (residual + mlp_sum).astype(jnp.bfloat16).reshape(sequences, local_rows, model_width)
    )
    domain_total = domain_weights.shape[0]
    domain_index = jnp.arange(domain_total, dtype=jnp.int32)
    factor = (
        domain_weights
        * (row_total * seq_devices)
        / (domain_total * domain_counts.astype(jnp.float32))
    )
    picked = domain_ids.reshape(row_total)[:, None] == domain_index[None, :]
    row_scale = jnp.sum(jnp.where(picked, factor[None, :], 0.0), axis=1)
    grad_out = cot.reshape(row_total, model_width).astype(jnp.float32) * row_scale[:, None]
    grad_low = grad_out.astype(jnp.bfloat16)
    grad_down = outer_sum(mixed, grad_low)
    grad_mixed = back_product(grad_low, w_down)
    grad_gate = (grad_mixed * up_proj * gate_logit * (1.0 + gate_proj * (1.0 - gate_logit))).astype(
        jnp.bfloat16
    )
    grad_up = (grad_mixed * gate_act).astype(jnp.bfloat16)
    grad_mlp_gate = outer_sum(h_normed, grad_gate)
    grad_mlp_up = outer_sum(h_normed, grad_up)
    grad_hnorm = lax.psum(
        (back_product(grad_gate, w_gate) + back_product(grad_up, w_up)).astype(jnp.bfloat16), "head"
    ).astype(jnp.float32)
    grad_norm_two = jnp.sum(grad_hnorm * normed_two, axis=0)
    grad_resid = grad_out + norm_back(grad_hnorm, normed_two, scale_two, gain_two)
    grad_attn = grad_resid.astype(jnp.bfloat16)
    grad_wout = outer_sum(gated, grad_attn)
    grad_gated = back_product(grad_attn, w_out)
    grad_heads_flat = (grad_gated * gate_sig).astype(jnp.bfloat16)
    grad_gatepre = (grad_gated * attn_flat * gate_sig * (1.0 - gate_sig)).astype(jnp.bfloat16)
    grad_wgate_attn = outer_sum(x_normed, grad_gatepre)
    grad_heads = grad_heads_flat.reshape(
        sequences, local_rows, kv_local, group_size, head_dim
    ).transpose(0, 2, 3, 1, 4)
    row_delta = jnp.sum(grad_heads.astype(jnp.float32) * attn_heads, axis=-1)
    key_piece = lax.all_gather(key_seq, "seq", axis=1, tiled=True)
    value_piece = lax.all_gather(value_seq, "seq", axis=1, tiled=True)
    row_count = key_piece.shape[1]
    key_block = key_piece.reshape(sequences, row_count, kv_local, head_dim)
    value_block = value_piece.reshape(sequences, row_count, kv_local, head_dim)
    key_pos = positions(block_order, jnp.int32(0), row_count, block_rows)
    allowed = key_pos[None, :] <= query_pos[:, None]
    scores = jnp.einsum(
        "skgqd,spkd->skgqp", query_heads, key_block, preferred_element_type=jnp.float32
    )
    probs = jnp.where(
        allowed, jnp.exp(jnp.where(allowed, scores, -1e30) - log_total[..., None]), 0.0
    )
    grad_probs = jnp.einsum(
        "skgqd,spkd->skgqp", grad_heads, value_block, preferred_element_type=jnp.float32
    )
    grad_scores = (probs * (grad_probs - row_delta[..., None])).astype(jnp.bfloat16)
    grad_query = jnp.einsum(
        "skgqp,spkd->skgqd", grad_scores, key_block, preferred_element_type=jnp.float32
    )
    key_term = jnp.einsum(
        "skgqp,skgqd->spkd", grad_scores, query_heads, preferred_element_type=jnp.float32
    ).reshape(sequences, row_count, kv_local * head_dim)
    value_term = jnp.einsum(
        "skgqp,skgqd->spkd",
        probs.astype(jnp.bfloat16),
        grad_heads,
        preferred_element_type=jnp.float32,
    ).reshape(sequences, row_count, kv_local * head_dim)
    grad_keys = key_term
    grad_values = value_term
    grad_query, grad_keys, grad_values = (grad_query, grad_keys, grad_values)
    grad_key_own, grad_value_own = (
        lax.psum_scatter(
            grad_keys.astype(jnp.bfloat16), "seq", scatter_dimension=1, tiled=True
        ).astype(jnp.float32),
        lax.psum_scatter(
            grad_values.astype(jnp.bfloat16), "seq", scatter_dimension=1, tiled=True
        ).astype(jnp.float32),
    )
    grad_query_rows = grad_query.transpose(0, 3, 1, 2, 4).reshape(row_total, q_local, head_dim)
    grad_qgain_part = jnp.sum(grad_query_rows * query_normed * query_factor, axis=(0, 1))
    grad_query_raw = (
        norm_back(grad_query_rows, query_normed, query_scale, q_gain * query_factor)
        .astype(jnp.bfloat16)
        .reshape(row_total, q_local * head_dim)
    )
    grad_key_rows = grad_key_own.reshape(row_total, kv_local, head_dim)
    grad_kgain_part = jnp.sum(grad_key_rows * key_normed, axis=(0, 1))
    grad_key_raw = (
        norm_back(grad_key_rows, key_normed, key_scale, k_gain)
        .astype(jnp.bfloat16)
        .reshape(row_total, kv_local * head_dim)
    )
    grad_value_low = grad_value_own.reshape(row_total, kv_local * head_dim).astype(jnp.bfloat16)
    grad_xnorm_part = (
        back_product(grad_query_raw, w_query)
        + back_product(grad_key_raw, w_key)
        + back_product(grad_value_low, w_value)
        + back_product(grad_gatepre, w_gate_attn)
    )
    grad_xnorm, grad_qgain, grad_kgain = (
        lax.psum(grad_xnorm_part.astype(jnp.bfloat16), "head").astype(jnp.float32),
        lax.psum(grad_qgain_part.astype(jnp.bfloat16), "head").astype(jnp.float32),
        lax.psum(grad_kgain_part.astype(jnp.bfloat16), "head").astype(jnp.float32),
    )
    grad_norm_one = jnp.sum(grad_xnorm * normed_one, axis=0)
    x_grad = (
        (grad_resid + norm_back(grad_xnorm, normed_one, scale_one, gain_one))
        .astype(jnp.bfloat16)
        .reshape(sequences, local_rows, model_width)
    )
    grad_wquery = outer_sum(x_normed, grad_query_raw)
    grad_wkey = outer_sum(x_normed, grad_key_raw)
    grad_wvalue = outer_sum(x_normed, grad_value_low)
    all_totals = (
        lax.psum_scatter(
            grad_norm_one.astype(jnp.bfloat16), "seq", scatter_dimension=0, tiled=True
        ).astype(jnp.float32),
        lax.psum_scatter(
            grad_wquery.astype(jnp.bfloat16), "seq", scatter_dimension=0, tiled=True
        ).astype(jnp.float32),
        lax.psum_scatter(
            grad_wkey.astype(jnp.bfloat16), "seq", scatter_dimension=0, tiled=True
        ).astype(jnp.float32),
        lax.psum_scatter(
            grad_wvalue.astype(jnp.bfloat16), "seq", scatter_dimension=0, tiled=True
        ).astype(jnp.float32),
        lax.psum_scatter(
            grad_wgate_attn.astype(jnp.bfloat16), "seq", scatter_dimension=0, tiled=True
        ).astype(jnp.float32),
        lax.psum_scatter(
            grad_wout.astype(jnp.bfloat16), "seq", scatter_dimension=1, tiled=True
        ).astype(jnp.float32),
        lax.psum_scatter(
            grad_qgain.astype(jnp.bfloat16), "seq", scatter_dimension=0, tiled=True
        ).astype(jnp.float32),
        lax.psum_scatter(
            grad_kgain.astype(jnp.bfloat16), "seq", scatter_dimension=0, tiled=True
        ).astype(jnp.float32),
        lax.psum_scatter(
            grad_mlp_gate.astype(jnp.bfloat16), "seq", scatter_dimension=0, tiled=True
        ).astype(jnp.float32),
        lax.psum_scatter(
            grad_mlp_up.astype(jnp.bfloat16), "seq", scatter_dimension=0, tiled=True
        ).astype(jnp.float32),
        lax.psum_scatter(
            grad_down.astype(jnp.bfloat16), "seq", scatter_dimension=1, tiled=True
        ).astype(jnp.float32),
        lax.psum_scatter(
            grad_norm_two.astype(jnp.bfloat16), "seq", scatter_dimension=0, tiled=True
        ).astype(jnp.float32),
    )
    return (
        block_out,
        x_grad,
        all_totals[0],
        all_totals[1],
        all_totals[2],
        all_totals[3],
        all_totals[4],
        all_totals[5],
        all_totals[6],
        all_totals[7],
        all_totals[11],
        all_totals[8],
        all_totals[9],
        all_totals[10],
    )


def solution(mesh):
    fits = mesh.shape["seq"] == 8 and mesh.shape["head"] == 4
    return jax.shard_map(
        on_device if fits else on_device_plain,
        mesh=mesh,
        in_specs=(
            P(None, "seq", None),
            P(None, "seq", None),
            P(None, "seq"),
            P(),
            P(),
            P(),
            P(),
            P(None, "head"),
            P(None, "head"),
            P(None, "head"),
            P(None, "head"),
            P("head", None),
            P(),
            P(),
            P(),
            P(None, "head"),
            P(None, "head"),
            P("head", None),
        ),
        out_specs=(
            P(None, "seq", None),
            P(None, "seq", None),
            P("seq"),
            P("seq", "head"),
            P("seq", "head"),
            P("seq", "head"),
            P("seq", "head"),
            P("head", "seq"),
            P("seq"),
            P("seq"),
            P("seq"),
            P("seq", "head"),
            P("seq", "head"),
            P("head", "seq"),
        ),
        check_vma=False,
    )
```

```python
import functools

import jax
import jax.numpy as jnp
from jax import lax
from jax.experimental import pallas as pl
from jax.experimental.pallas import tpu as pltpu
from jax.sharding import PartitionSpec as P

epsilon = 1e-06


def norm_scale(value):
    return lax.rsqrt(jnp.mean(value * value, axis=-1, keepdims=True) + epsilon)


def norm_back(grad_in, normed, scale, gain):
    scaled = grad_in * gain
    return scale * (scaled - normed * jnp.mean(scaled * normed, axis=-1, keepdims=True))


def product(left, right):
    return jnp.dot(left, right, preferred_element_type=jnp.float32)


def outer_sum(left, right):
    return lax.dot_general(
        left, right, (((0,), (0,)), ((), ())), preferred_element_type=jnp.float32
    )


def back_product(left, right):
    return lax.dot_general(
        left, right, (((1,), (1,)), ((), ())), preferred_element_type=jnp.float32
    )


def low(value):
    return value.astype(jnp.bfloat16)


def wide(value):
    return value.astype(jnp.float32)


def positions(block_order, device, row_count, block_rows):
    stored = device * row_count + jnp.arange(row_count, dtype=jnp.int32)
    slots = stored // block_rows
    slot_index = jnp.arange(block_order.shape[0], dtype=jnp.int32)
    picked = jnp.sum(
        jnp.where(slots[:, None] == slot_index[None, :], block_order[None, :], 0), axis=1
    )
    return picked * block_rows + stored % block_rows


MESH = pl.DeviceIdType.MESH
TILE = 256


PLAN = {
    "p1.0": (
        ("a", 0),
    ),
    "p1.3": (
        ("a", 1), ("s1", 0),
    ),
    "p1.5": (
        ("a", 2), ("r1", 0),
    ),
    "p2.1": (
        ("a", 3), ("s1", 1), ("s2", 0),
    ),
    "p2.2": (
        ("r2", 0),
    ),
    "p2.3": (
        ("a", 4), ("s1", 2),
    ),
    "p2.4": (
        ("s3", 0),
    ),
    "p2.5": (
        ("a", 5), ("s2", 1), ("s1", 3),
    ),
    "p2.6": (
        ("s4", 0),
    ),
    "p2.7": (
        ("a", 6),
    ),
    "p3.0": (
        ("s2", 2), ("s1", 4), ("s3", 1), ("a", 7),
    ),
    "p3.4": (
        ("s4", 1), ("s2", 3), ("s1", 5), ("a", 8), ("s3", 2),
    ),
    "e0.3": (
        ("s2", 4), ("s1", 6), ("a", 9), ("s3", 3), ("s4", 2),
    ),
    "p4a": (
        ("s2", 5), ("s1", 7), ("a", 10), ("s3", 4),
    ),
    "p4b": (
        ("s2", 6), ("s1", 8), ("a", 11), ("s3", 5),
    ),
    "p5.0": (
        ("s2", 7), ("s1", 9), ("s3", 6),
    ),
    "p5.2": (
        ("s2", 8), ("ky", 0), ("s1", 10), ("s3", 7),
    ),
    "p5.3": (
        ("s2", 9), ("s1", 11), ("s3", 8),
    ),
    "qp": (
        ("kl", 0), ("ky", 1),
    ),
    "e1.3": (
        ("s4", 3), ("s4", 4), ("s4", 5), ("s3", 9), ("s4", 6), ("s4", 7), ("s4", 8), ("s2", 10),
    ),
    "op": (
        ("km", 0), ("ky", 2), ("s4", 9), ("s2", 11), ("s3", 10), ("ky", 3), ("s4", 10), ("kl", 1), ("s3", 11),
        ("r1", 3), ("a", 12), ("s4", 11), ("r1", 2), ("km", 1), ("a", 13), ("kl", 2), ("r2", 3), ("s1", 12),
        ("a", 14), ("r2", 2), ("km", 2), ("kl", 3), ("s1", 13), ("a", 15), ("a", 16), ("s2", 12), ("km", 3),
        ("s1", 14), ("a", 17),
    ),
    "kp": (
        ("s2", 13), ("s1", 15), ("s3", 12), ("a", 18),
    ),
    "p7.2": (
        ("s4", 12), ("s2", 14), ("s1", 16), ("a", 19), ("s3", 13),
    ),
    "p7.6": (
        ("s2", 15), ("s1", 17), ("a", 20), ("s3", 14),
    ),
    "e2.1": (
        ("s4", 13), ("s4", 14), ("s2", 16), ("s1", 18), ("a", 21), ("s3", 15),
    ),
    "e2.3": (
        ("s4", 15), ("s2", 17), ("s1", 19), ("a", 22), ("s3", 16),
    ),
    "vec": (
        ("s2", 18), ("s1", 20), ("a", 23), ("s3", 17), ("s4", 16), ("s2", 19), ("s1", 21), ("a", 24),
        ("s4", 17), ("s3", 18), ("s2", 20), ("s1", 22), ("a", 25), ("s3", 19), ("s4", 18), ("s4", 19),
        ("s2", 21), ("s1", 23), ("s3", 20), ("s4", 20), ("s2", 22), ("s1", 24), ("s3", 21), ("s4", 21),
        ("s2", 23), ("s1", 25), ("s3", 22), ("s4", 22), ("s2", 24), ("s3", 23), ("s4", 23), ("s2", 25),
        ("s3", 24), ("s4", 24), ("s3", 25), ("s4", 25),
    ),
}


def other_z(z, t):
    low_z, high_z = lax.rem(z, 2), lax.div(z, 2)
    low_t, high_t = lax.rem(t, 2), lax.div(t, 2)
    return (low_z + low_t - 2 * low_z * low_t) + 2 * (high_z + high_t - 2 * high_z * high_t)


def fill_bias(order_ref, bias, rows, z, y, seq):
    block = bias.shape[0] // order_ref.shape[0]
    each = rows // block
    lane = lax.broadcasted_iota(jnp.int32, (block, bias.shape[1]), 1)
    down = lax.broadcasted_iota(jnp.int32, (block, bias.shape[1]), 0)
    within = lax.rem(lane, rows)
    query = lax.rem(lane, block)
    for i in range(each):
        query += jnp.where(lax.div(within, block) == i, order_ref[seq * each + i] * block, 0)
    for j in range(8):
        other_y = 1 - y if j % 2 else y
        device = other_z(z, j // 2) * 2 + other_y
        for i in range(each):
            key = order_ref[device * each + i] * block + down
            bias[j * rows + i * block : j * rows + (i + 1) * block] = jnp.where(key <= query, 0.0, -1e30)


def fill_factor(ids_ref, counts_ref, weights_ref, factor, total):
    seqs, rows = ids_ref.shape
    domains = counts_ref.shape[0]
    across = jnp.zeros((seqs, rows), jnp.float32)
    ids = ids_ref[...]
    for d in range(domains):
        count = jnp.full((seqs, rows), counts_ref[d], jnp.int32).astype(jnp.float32)
        weight = jnp.full((seqs, rows), weights_ref[d], jnp.float32) * total / (domains * count)
        across = jnp.where(ids == d, weight, across)
    here = lax.broadcasted_iota(jnp.int32, (rows, rows), 0) == lax.broadcasted_iota(
        jnp.int32, (rows, rows), 1
    )
    for s in range(seqs):
        spread = jnp.where(here, across[s : s + 1], 0.0)
        factor[s * rows : (s + 1) * rows] = jnp.sum(spread, axis=1, keepdims=True)


def dot_plain(left, right):
    return jnp.dot(left, right, preferred_element_type=jnp.float32)


def dot_rows(left, right):
    return lax.dot_general(
        left, right, (((1,), (1,)), ((), ())), preferred_element_type=jnp.float32
    )


def dot_first(left, right):
    return lax.dot_general(
        left, right, (((0,), (0,)), ((), ())), preferred_element_type=jnp.float32
    )


def back_kernel(
    h_hbm, cot_hbm, x_hbm, xt_hbm, ltd_hbm, dm_hbm, q_hbm, kv_hbm, o_hbm, sig_hbm, y_hbm, qraw_hbm, kraw_hbm,
    wg_hbm, wu_hbm, wd_hbm, wo_hbm, wq_hbm, wk_hbm, wv_hbm, wga_hbm,
    ids_ref, lse_ref, n1_ref, n2_ref, qg_ref, kg_ref, order_ref, counts_ref, weights_ref,
    block_out, x_out, dwd_out, dwg_out, dwu_out, dwo_out, dwga_out, dwq_out, dwk_out, dwv_out,
    n1_out, n2_out, qg_out, kg_out, dh_hbm, z1_hbm, z2_hbm, z3_hbm,
    acts, lt, odd, csend, crecv, xrecv, fin, yrecv, lrecv, mrecv, hrecv,
    zsend, stage, ostage, wide_a, wide_b, delta,
    vec, vec_got, gvec, gvec_got, bias, factor_ref,
    ya_s, ya_r, z1_s, z1_r, z2_s, z2_r, z3_s, z3_r, lt_s, lt_r, lc_s, lc_r, lx_s, lx_r, lf_s, lf_r,
    c1_s, c1_r, x_s, x_r, c2_s, c2_r, ky_s, ky_r, kl_s, kl_r, km_s, km_r, kh_s, kh_r,
    nv_s, nv_r, gv_s, gv_r, st_sem, out_sem, misc, credit,
):
    seq, head = lax.axis_index("seq"), lax.axis_index("head")
    z, y = lax.div(seq, 2), lax.rem(seq, 2)
    c = lax.rem(head, 2)
    y_dev = {"seq": z * 2 + 1 - y}
    lo_dev = {"seq": other_z(z, 1) * 2 + y}
    hi_dev = {"seq": other_z(z, 2) * 2 + y}
    mid_dev = {"seq": (3 - z) * 2 + y}
    core_dev = {"head": head + 1 - 2 * c}
    x_dev = {"head": head + 2 - 4 * lax.div(head, 2)}
    at_end, inside = lax.rem(z, 3) == 0, lax.rem(z, 3) != 0
    tokens = cot_hbm.shape[0]
    rows = bias.shape[0] // 8
    seqs = tokens // rows
    hidden_tiles = wd_hbm.shape[0] // TILE
    ff_items = 3 * hidden_tiles
    width = cot_hbm.shape[1]
    epsilon_k = 1e-06

    barrier = pltpu.get_barrier_semaphore()
    for device in (y_dev, lo_dev, hi_dev, core_dev, x_dev):
        pl.semaphore_signal(barrier, inc=1, device_id=device, device_id_type=MESH)

    @pl.when(inside)
    def _():
        pl.semaphore_signal(barrier, inc=1, device_id=mid_dev, device_id_type=MESH)
        pl.semaphore_wait(barrier, 6)

    @pl.when(at_end)
    def _():
        pl.semaphore_wait(barrier, 5)


    def remote(src, dst, send, recv, device):
        return pltpu.make_async_remote_copy(
            src_ref=src, dst_ref=dst, send_sem=send, recv_sem=recv, device_id=device, device_id_type=MESH
        )

    def act_copy(i):
        return remote(acts.at[i, 0], acts.at[i, 1], ya_s.at[i], ya_r.at[i], y_dev)

    def lt_copy(l):
        return remote(odd.at[l], lt.at[l, 1, head], lt_s.at[l], lt_r.at[l], y_dev)

    x_head = head + 2 - 4 * lax.div(head, 2)
    core_head = head + 1 - 2 * c
    far_head = x_head + 1 - 2 * c

    def lt_core(l, part):
        piece = lt.at[l, 1, part]
        return remote(piece, piece, lc_s.at[l], lc_r.at[l], core_dev)

    def lt_x(l, part):
        piece = lt.at[l, 1, part]
        return remote(piece, piece, lx_s.at[l], lx_r.at[l], x_dev)

    def lt_far(l, part):
        piece = lt.at[l, 1, part]
        return remote(piece, piece, lf_s.at[l], lf_r.at[l], core_dev)

    def z1_copy(i):
        return remote(zsend.at[i % 4], z1_hbm.at[i], z1_s.at[i], z1_r.at[i], lo_dev)

    def z2_copy(i):
        return remote(zsend.at[i % 4, pl.ds(0, 2)], z2_hbm.at[i], z2_s.at[i], z2_r.at[i], mid_dev)

    def z3_copy(i):
        return remote(zsend.at[i % 4, 2], z3_hbm.at[i], z3_s.at[i], z3_r.at[i], lo_dev)

    def item_dot(i, l, first, last):
        count = (last - first) * TILE
        mine = dot_plain(lt[l, 0, first:last].reshape(count, tokens), acts[i, 0])
        return mine + dot_plain(lt[l, 1, first:last].reshape(count, tokens), acts[i, 1])

    def stage_load(src, slot):
        copy = pltpu.make_async_copy(src, stage.at[slot], st_sem.at[slot])
        copy.start()
        return copy

    def stage_one(i, l, place):
        act_copy(i).wait_recv()

        @pl.when(at_end)
        def _():
            if i >= 4:
                z1_copy(i - 4).wait_send()
            total = item_dot(i, l, 1, 4)
            for k in range(3):
                zsend[i % 4, k] = low(total[k * TILE : (k + 1) * TILE])
            z1_copy(i).start()

    def stage_two(i, l, place):
        @pl.when(inside)
        def _():
            z1_copy(i).wait_recv()
            loads = [stage_load(z1_hbm.at[i, k], k) for k in (1, 2)]
            if i >= 4:
                z2_copy(i - 4).wait_send()
            total = item_dot(i, l, 2, 4)
            for load in loads:
                load.wait()
            zsend[i % 4, 0] = low(total[:TILE] + wide(stage[2]))
            zsend[i % 4, 1] = low(total[TILE:] + wide(stage[1]))
            z2_copy(i).start()

    def out_wait(i):
        pltpu.make_async_copy(ostage.at[i % 2], dwk_out, out_sem.at[i % 2]).wait()

    def put(i, total, place):
        ref, n, turned = place
        if i >= 2:
            out_wait(i - 2)
        ostage[i % 2] = total.T if turned else total
        at = pl.ds(n * TILE, TILE)
        target = ref.at[at] if turned else ref.at[:, at]
        pltpu.make_async_copy(ostage.at[i % 2], target, out_sem.at[i % 2]).start()

    def stage_three(i, l, place):
        @pl.when(inside)
        def _():
            z2_copy(i).wait_recv()
            loads = [stage_load(z1_hbm.at[i, 0], 0), stage_load(z2_hbm.at[i, 0], 1), stage_load(z2_hbm.at[i, 1], 2)]
            if i >= 4:
                z3_copy(i - 4).wait_send()
            total = item_dot(i, l, 0, 2)
            for load in loads:
                load.wait()
            zsend[i % 4, 2] = low(total[TILE:] + wide(stage[1]))
            z3_copy(i).start()
            put(i, total[:TILE] + wide(stage[0]) + wide(stage[2]), place)

    def stage_four(i, l, place):
        @pl.when(at_end)
        def _():
            z3_copy(i).wait_recv()
            load = stage_load(z3_hbm.at[i], 3)
            total = item_dot(i, l, 0, 1)
            load.wait()
            put(i, total + wide(stage[3]), place)

    def at_tile(j, kind):
        later = j // 3 if isinstance(j, int) else lax.div(j, 3)
        if kind == 0:
            return j + 2 * j * later
        return (2 + 2 * j + kind) * (1 - later) + (3 * j + kind) * later

    ff_kind = {at_tile(j, kind): (j, kind) for j in range(hidden_tiles) for kind in range(3)}
    late = (
        (3, dwo_out, 0, True),
        (3, dwo_out, 1, True),
        (2, dwga_out, 0, False),
        (2, dwga_out, 1, False),
        (2, dwq_out, 0, False),
        (2, dwq_out, 1, False),
        (2, dwk_out, 0, False),
        (2, dwv_out, 0, False),
    )
    item_count = ff_items + 8
    shown = set()
    ltd_load = pltpu.make_async_copy(ltd_hbm, lt.at[1], misc.at[7])

    def item_step(stage_of, i):
        l = (1 if ff_kind[i][1] == 0 else 0) if i < ff_items else late[i - ff_items][0]
        if stage_of is stage_one and l not in shown:
            shown.add(l)
            if l == 1:
                ltd_load.wait()
            else:
                relay_in(l)
        if i < ff_items:
            j, kind = ff_kind[i]
            place = ((dwd_out, dwg_out, dwu_out)[kind], j, kind == 0)
        else:
            place = late[i - ff_items][1:]
        stage_of(i, l, place)

    actions = {
        "a": lambda i: act_copy(i).start(),
        "s1": lambda i: item_step(stage_one, i),
        "s2": lambda i: item_step(stage_two, i),
        "s3": lambda i: item_step(stage_three, i),
        "s4": lambda i: item_step(stage_four, i),
        "r1": lambda l: relay_one(l),
        "r2": lambda l: relay_two(l),
    }

    def after(place):
        for name, i in PLAN.get(place, ()):
            actions[name](i)

    def after_step(place, step, count):
        for k in range(count):
            if f"{place}.{k}" in PLAN:
                pl.when(step == k)(lambda k=k: after(f"{place}.{k}"))

    def spread(l, source):
        @pl.loop(0, 4)
        def _(t):
            at = pl.multiple_of((other_z(z, t) * 2 + y) * TILE, TILE)
            lt[l, 0, t] = source[:, pl.ds(at, TILE)].T

        at = pl.multiple_of((other_z(z, head) * 2 + 1 - y) * TILE, TILE)
        odd[l] = source[:, pl.ds(at, TILE)].T

    def relay_one(l):
        lt_copy(l).wait_recv()
        lt_core(l, head).start()
        lt_x(l, head).start()

    def relay_two(l):
        lt_x(l, x_head).wait_recv()
        lt_far(l, x_head).start()

    def relay_in(l):
        lt_core(l, core_head).wait_recv()
        lt_far(l, far_head).wait_recv()

    def core_copy(k, b):
        return remote(csend.at[b], crecv.at[k % 2, b], c1_s.at[k, b], c1_r.at[k, b], core_dev)

    def x_copy(k, b):
        return remote(fin.at[k % 2, c * 4 + b], xrecv.at[k % 2, b], x_s.at[k, b], x_r.at[k, b], x_dev)

    def fin_copy(k, b):
        piece = fin.at[k % 2, c * 4 + b]
        return remote(piece, piece, c2_s.at[k, b], c2_r.at[k, b], core_dev)

    def fin_copy_in(k, b):
        piece = fin.at[k % 2, (1 - c) * 4 + b]
        return remote(piece, piece, c2_s.at[k, b], c2_r.at[k, b], core_dev)

    def reduce_start(k, loads, compute, place):
        def block_of(step):
            return lax.rem(c + 1 + step, 2) * 4 + lax.div(step, 2)

        for copy in loads(block_of(0), 0):
            copy.start()

        @pl.loop(0, 8)
        def _(step):
            slot, b = lax.rem(step, 2), lax.div(step, 2)

            @pl.when(step < 7)
            def _():
                for copy in loads(block_of(step + 1), 1 - slot):
                    copy.start()

            for copy in loads(block_of(step), slot):
                copy.wait()
            part = compute(slot)

            @pl.when(slot == 0)
            def _():
                csend[b] = low(part)
                core_copy(k, b).start()

            @pl.when(slot == 1)
            def _():
                core_copy(k, b).wait_recv()
                fin[k % 2, c * 4 + b] = low(part + wide(crecv[k % 2, b]))
                x_copy(k, b).start()

            after_step(place, step, 8)

        @pl.loop(0, 4)
        def _(b):
            core_copy(k, b).wait_send()

    def reduce_end(k):
        for b in range(4):
            x_copy(k, b).wait()
            fin[k % 2, c * 4 + b] = low(wide(fin[k % 2, c * 4 + b]) + wide(xrecv[k % 2, b]))
            fin_copy(k, b).start()
            after(f"e{k}.{b}")
        for b in range(4):
            fin_copy_in(k, b).wait_recv()
            fin_copy(k, b).wait_send()
        after(f"e{k}.4")

    def fin_rows(k, at, count):
        return jnp.concatenate([wide(fin[k % 2, n, pl.ds(at, count)]) for n in range(8)], axis=1)

    def rms(value):
        return lax.rsqrt(jnp.mean(value * value, axis=-1, keepdims=True) + epsilon_k)

    n_chunks = tokens // 128

    def first_phase(hbuf, wgb, wub, dmb, sems, w_sems):
        def row_load(r, slot):
            return pltpu.make_async_copy(h_hbm.at[pl.ds(r * 128, 128)], hbuf.at[slot], sems.at[slot])

        def tile_loads(j, slot):
            at = pl.ds(pl.multiple_of(j * TILE, TILE), TILE)
            return (
                pltpu.make_async_copy(wg_hbm.at[:, at], wgb.at[slot], w_sems.at[slot, 0]),
                pltpu.make_async_copy(wu_hbm.at[:, at], wub.at[slot], w_sems.at[slot, 1]),
                pltpu.make_async_copy(dm_hbm.at[j], dmb.at[slot], w_sems.at[slot, 2]),
            )

        row_load(0, 0).start()
        for copy in tile_loads(0, 0):
            copy.start()
        ltd_load.start()

        @pl.loop(0, n_chunks)
        def _(r):
            slot = lax.rem(r, 2)

            @pl.when(r < n_chunks - 1)
            def _():
                row_load(r + 1, 1 - slot).start()

            row_load(r, slot).wait()
            value = hbuf[slot]
            at = pl.ds(pl.multiple_of(r * 128, 128), 128)
            wide_a[at] = low(value * rms(value) * wide(n2_ref[...]))

        after("p0")

        @pl.loop(0, hidden_tiles)
        def _(j):
            slot = lax.rem(j, 2)

            @pl.when(j < hidden_tiles - 1)
            def _():
                for copy in tile_loads(j + 1, 1 - slot):
                    copy.start()

            for copy in tile_loads(j, slot):
                copy.wait()

            @pl.loop(0, 2)
            def _(half):
                at = pl.ds(pl.multiple_of(half * (tokens // 2), 128), tokens // 2)
                a = dot_plain(wide_a[at], wgb[slot])
                u = dot_plain(wide_a[at], wub[slot])
                dm = dmb[slot, at]
                sig = jax.nn.sigmoid(a)
                act = a * sig
                acts[at_tile(j, 0), 0, at] = low(act * u)
                acts[at_tile(j, 1), 0, at] = low(dm * u * sig * (1.0 + a * (1.0 - sig)))
                acts[at_tile(j, 2), 0, at] = low(dm * act)

            after_step("p1", j, 1)

            @pl.when(j == 0)
            def _():
                spread(0, wide_a)
                lt_copy(0).start()
                after("sp0")

            for k in range(1, hidden_tiles):
                if f"p1.{k}" in PLAN:
                    pl.when(j == k)(lambda k=k: after(f"p1.{k}"))

    pl.run_scoped(
        first_phase,
        pltpu.VMEM((2, 128, width), jnp.float32),
        pltpu.VMEM((2, width, TILE), jnp.bfloat16),
        pltpu.VMEM((2, width, TILE), jnp.bfloat16),
        pltpu.VMEM((2, tokens, TILE), jnp.float32),
        pltpu.SemaphoreType.DMA((2,)),
        pltpu.SemaphoreType.DMA((2, 3)),
    )

    def second_phase(wa, wb, sems):
        def loads(n, slot):
            at = pl.ds(pl.multiple_of(n * TILE, TILE), TILE)
            return (
                pltpu.make_async_copy(wg_hbm.at[at], wa.at[slot], sems.at[slot, 0]),
                pltpu.make_async_copy(wu_hbm.at[at], wb.at[slot], sems.at[slot, 1]),
            )

        def compute(slot):
            total = None
            for j in range(hidden_tiles):
                at = pl.ds(j * TILE, TILE)
                part = dot_rows(acts[at_tile(j, 1), 0], wa[slot, :, at])
                part += dot_rows(acts[at_tile(j, 2), 0], wb[slot, :, at])
                total = part if total is None else total + part
            return total

        reduce_start(0, loads, compute, "p2")

    pl.run_scoped(
        second_phase,
        pltpu.VMEM((2, TILE, wg_hbm.shape[1]), jnp.bfloat16),
        pltpu.VMEM((2, TILE, wg_hbm.shape[1]), jnp.bfloat16),
        pltpu.SemaphoreType.DMA((2, 2)),
    )

    def third_phase(wa, sems):
        def loads(n, slot):
            at = pl.ds(pl.multiple_of(n * TILE, TILE), TILE)
            return (pltpu.make_async_copy(wd_hbm.at[:, at], wa.at[slot], sems.at[slot]),)

        def compute(slot):
            total = None
            for j in range(hidden_tiles):
                part = dot_plain(acts[at_tile(j, 0), 0], wa[slot, pl.ds(j * TILE, TILE)])
                total = part if total is None else total + part
            return total

        reduce_start(1, loads, compute, "p3")

    pl.run_scoped(
        third_phase,
        pltpu.VMEM((2, wd_hbm.shape[0], TILE), jnp.bfloat16),
        pltpu.SemaphoreType.DMA((2,)),
    )

    base = ff_items
    for n in range(2):
        pltpu.make_async_copy(
            y_hbm.at[:, pl.ds(n * TILE, TILE)], acts.at[base + n, 0], misc.at[n]
        ).start()

    def xt_own(t):
        shard = other_z(z, t) * 2 + y
        return pltpu.make_async_copy(xt_hbm.at[shard], lt.at[2, 0, t], misc.at[2 + t])

    def xt_odd():
        shard = other_z(z, head) * 2 + 1 - y
        return pltpu.make_async_copy(xt_hbm.at[shard], odd.at[2], misc.at[6])

    for t in range(4):
        xt_own(t).start()
    xt_odd().start()
    for t in range(4):
        xt_own(t).wait()
    xt_odd().wait()
    for n in range(2):
        pltpu.make_async_copy(
            y_hbm.at[:, pl.ds(n * TILE, TILE)], acts.at[base + n, 0], misc.at[n]
        ).wait()
    fill_bias(order_ref, bias, rows, z, y, seq)
    fill_factor(ids_ref, counts_ref, weights_ref, factor_ref, float(tokens * 8))
    after("xt")
    reduce_end(0)

    def fourth_phase(hbuf, cbuf, dbuf, wob, obuf, sbuf, sems, d_sems, w_sems):
        def row_loads(r, slot):
            at = pl.ds(r * 128, 128)
            return (
                pltpu.make_async_copy(h_hbm.at[at], hbuf.at[slot], sems.at[slot, 0]),
                pltpu.make_async_copy(cot_hbm.at[at], cbuf.at[slot], sems.at[slot, 1]),
            )

        def spill(r, slot):
            return pltpu.make_async_copy(dbuf.at[slot], dh_hbm.at[pl.ds(r * 128, 128)], d_sems.at[slot])

        def tile_loads(n):
            at = pl.ds(n * TILE, TILE)
            return (
                pltpu.make_async_copy(wo_hbm.at[at], wob.at[n], w_sems.at[n, 0]),
                pltpu.make_async_copy(o_hbm.at[:, at], obuf.at[n], w_sems.at[n, 1]),
                pltpu.make_async_copy(sig_hbm.at[:, at], sbuf.at[n], w_sems.at[n, 2]),
            )

        for copy in row_loads(0, 0):
            copy.start()
        for n in range(2):
            for copy in tile_loads(n):
                copy.start()
        vec[0] = jnp.zeros_like(vec[0])

        @pl.loop(0, n_chunks)
        def _(r):
            slot = lax.rem(r, 2)

            @pl.when(r < n_chunks - 1)
            def _():
                for copy in row_loads(r + 1, 1 - slot):
                    copy.start()

            for copy in row_loads(r, slot):
                copy.wait()

            @pl.when(r >= 2)
            def _():
                spill(r - 2, slot).wait()

            at = pl.ds(pl.multiple_of(r * 128, 128), 128)
            value = hbuf[slot]
            scale = rms(value)
            normed = value * scale
            grad = fin_rows(0, pl.multiple_of(r * 128, 128), 128)
            vec[0, 1:2] += jnp.sum(grad * normed, axis=0, keepdims=True)
            scaled = grad * wide(n2_ref[...])
            inner = jnp.mean(scaled * normed, axis=-1, keepdims=True)
            dh = wide(cbuf[slot]) * factor_ref[at] + scale * (scaled - normed * inner)
            dbuf[slot] = dh
            wide_a[at] = low(dh)
            spill(r, slot).start()

        spill(n_chunks - 2, n_chunks % 2).wait()
        spill(n_chunks - 1, (n_chunks - 1) % 2).wait()

        after("p4a")
        ones = jnp.ones((8, 128), jnp.bfloat16)
        for n in range(2):
            for copy in tile_loads(n):
                copy.wait()
            dy = dot_rows(wide_a[...], wob[n])
            sig, o = sbuf[n], obuf[n]
            do = low(dy * sig)
            acts[base + 2 + n, 0] = low(dy * o * sig * (1.0 - sig))
            wide_b[:, n * TILE : (n + 1) * TILE] = do
            both = wide(do) * o
            for g in range(2):
                part = both[:, g * 128 : (g + 1) * 128]
                top = low(part)
                rest = low(part - wide(top))
                delta[n, g] = dot_rows(ones, top) + dot_rows(ones, rest)

        spread(3, wide_a)
        after("p4b")
        for device in (core_dev, x_dev):
            pl.semaphore_signal(credit, inc=1, device_id=device, device_id_type=MESH)

    pl.run_scoped(
        fourth_phase,
        pltpu.VMEM((2, 128, width), jnp.float32),
        pltpu.VMEM((2, 128, width), jnp.bfloat16),
        pltpu.VMEM((2, 128, width), jnp.float32),
        pltpu.VMEM((2, TILE, width), jnp.bfloat16),
        pltpu.VMEM((2, tokens, TILE), jnp.float32),
        pltpu.VMEM((2, tokens, TILE), jnp.float32),
        pltpu.SemaphoreType.DMA((2, 2)),
        pltpu.SemaphoreType.DMA((2,)),
        pltpu.SemaphoreType.DMA((2, 3)),
    )

    def attention_back(keep, ysend, lsend, dq_ref, dkv_ref):
        def ky_copy(s):
            return remote(ysend.at[lax.rem(s, 2)], yrecv.at[s], ky_s.at[s], ky_r.at[s], y_dev)

        def kl_copy(s):
            return remote(lsend.at[s], lrecv.at[s], kl_s.at[s], kl_r.at[s], lo_dev)

        def km_copy(s):
            return remote(lsend.at[s, pl.ds(0, 2)], mrecv.at[s], km_s.at[s], km_r.at[s], mid_dev)

        def kh_copy(s):
            return remote(lsend.at[s, 2], hrecv.at[s], kh_s.at[s], kh_r.at[s], lo_dev)

        def ky_step(s):
            ky_copy(s).wait_recv()
            for m in range(4):
                keep[s, m] += wide(yrecv[s, m])

            @pl.when(at_end)
            def _():
                for k in range(3):
                    lsend[s, k] = low(keep[s, k + 1])
                kl_copy(s).start()

        def kl_step(s):
            @pl.when(inside)
            def _():
                kl_copy(s).wait_recv()
                keep[s, 0] += wide(lrecv[s, 0])
                lsend[s, 0] = low(keep[s, 2] + wide(lrecv[s, 2]))
                lsend[s, 1] = low(keep[s, 3] + wide(lrecv[s, 1]))
                km_copy(s).start()

        def km_step(s):
            @pl.when(inside)
            def _():
                km_copy(s).wait_recv()
                keep[s, 0] += wide(mrecv[s, 1])
                lsend[s, 2] = low(keep[s, 1] + wide(mrecv[s, 0]))
                kh_copy(s).start()

        actions["ky"] = ky_step
        actions["kl"] = kl_step
        actions["km"] = km_step
        keys_total = bias.shape[0]

        def fifth_phase(qbuf, kvbuf, q_sem, sems):
            def kv_load(s, slot):
                return pltpu.make_async_copy(kv_hbm.at[s], kvbuf.at[slot], sems.at[slot])

            q_load = pltpu.make_async_copy(q_hbm, qbuf, q_sem)
            q_load.start()
            kv_load(0, 0).start()
            q_load.wait()

            @pl.loop(0, seqs)
            def _(s):
                slot = lax.rem(s, 2)

                @pl.when(s < seqs - 1)
                def _():
                    kv_load(s + 1, 1 - slot).start()

                kv_load(s, slot).wait()
                at = pl.ds(pl.multiple_of(s * rows, 128), rows)
                @pl.when(s >= 2)
                def _():
                    ky_copy(s - 2).wait_send()

                for n in range(2):
                    lanes = [slice((2 * n + g) * 128, (2 * n + g + 1) * 128) for g in range(2)]
                    key = kvbuf[slot, :, n * 128 : (n + 1) * 128]
                    value = kvbuf[slot, :, 256 + n * 128 : 256 + (n + 1) * 128]
                    q = jnp.concatenate([qbuf[at, lane] for lane in lanes], axis=0)
                    do = jnp.concatenate([wide_b[at, lane] for lane in lanes], axis=0)
                    drow = jnp.concatenate([delta[n, g, 0:1, at] for g in range(2)], axis=1)
                    scores = dot_rows(key, q)
                    probs = jnp.exp(scores - lse_ref[s, n] + bias[...])
                    grad_probs = dot_rows(value, do)
                    ds = low(probs * (grad_probs - drow))
                    for start, grad in ((0, dot_plain(ds, q)), (256, dot_plain(low(probs), do))):
                        into = slice(start + n * 128, start + (n + 1) * 128)
                        for m in range(4):
                            keep[s, m, :, into] = grad[2 * m * rows : (2 * m + 1) * rows]
                            ysend[slot, m, :, into] = low(grad[(2 * m + 1) * rows : (2 * m + 2) * rows])
                    dq = dot_first(key, ds).T
                    for g in range(2):
                        dq_ref[at, lanes[g]] = dq[g * rows : (g + 1) * rows]

                ky_copy(s).start()
                after_step("p5", s, seqs)

        pl.run_scoped(
            fifth_phase,
            pltpu.VMEM(q_hbm.shape, jnp.bfloat16),
            pltpu.VMEM((2, keys_total, 512), jnp.bfloat16),
            pltpu.SemaphoreType.DMA,
            pltpu.SemaphoreType.DMA((2,)),
        )

        lt_copy(3).start()
        lt_copy(2).start()
        after("sl3")

        def query_phase(rbuf, sem):
            load = pltpu.make_async_copy(qraw_hbm, rbuf, sem)
            load.start()
            load.wait()
            factor = 128.0**-0.5
            for hd in range(4):
                lane = slice(hd * 128, (hd + 1) * 128)
                raw = rbuf[:, lane]
                scale = rms(raw)
                normed = raw * scale
                grad = dq_ref[:, lane]
                gvec[0, 0:1, 0:128] = (
                    jnp.sum(grad * normed * factor, axis=0, keepdims=True)
                    + (gvec[0, 0:1, 0:128] if hd else 0.0)
                )
                scaled = grad * (wide(qg_ref[...]) * factor)
                out = scale * (scaled - normed * jnp.mean(scaled * normed, axis=-1, keepdims=True))
                acts[base + 4 + hd // 2, 0, :, (hd % 2) * 128 : (hd % 2 + 1) * 128] = low(out)

        gvec[0] = jnp.zeros_like(gvec[0])
        pl.run_scoped(query_phase, pltpu.VMEM(qraw_hbm.shape, jnp.float32), pltpu.SemaphoreType.DMA)

        after("qp")
        reduce_end(1)

        def out_phase(hbuf, obuf, sems, o_sems):
            def load(r, slot):
                return pltpu.make_async_copy(h_hbm.at[pl.ds(r * 128, 128)], hbuf.at[slot], sems.at[slot])

            def store(r, slot):
                return pltpu.make_async_copy(obuf.at[slot], block_out.at[pl.ds(r * 128, 128)], o_sems.at[slot])

            load(0, 0).start()

            @pl.loop(0, n_chunks)
            def _(r):
                slot = lax.rem(r, 2)

                @pl.when(r < n_chunks - 1)
                def _():
                    load(r + 1, 1 - slot).start()

                load(r, slot).wait()

                @pl.when(r >= 2)
                def _():
                    store(r - 2, slot).wait()

                obuf[slot] = low(hbuf[slot] + fin_rows(1, pl.multiple_of(r * 128, 128), 128))
                store(r, slot).start()

            store(n_chunks - 2, n_chunks % 2).wait()
            store(n_chunks - 1, (n_chunks - 1) % 2).wait()

        pl.run_scoped(
            out_phase,
            pltpu.VMEM((2, 128, width), jnp.float32),
            pltpu.VMEM((2, 128, width), jnp.bfloat16),
            pltpu.SemaphoreType.DMA((2,)),
            pltpu.SemaphoreType.DMA((2,)),
        )

        after("op")

        @pl.loop(0, seqs)
        def _(s):
            at = pl.ds(pl.multiple_of(s * rows, 128), rows)

            @pl.when(inside)
            def _():
                dkv_ref[at] = keep[s, 0]

            @pl.when(at_end)
            def _():
                kh_copy(s).wait_recv()
                dkv_ref[at] = keep[s, 0] + wide(hrecv[s])

        def key_phase(rbuf, sem):
            load = pltpu.make_async_copy(kraw_hbm, rbuf, sem)
            load.start()
            load.wait()
            for hd in range(2):
                lane = slice(hd * 128, (hd + 1) * 128)
                raw = rbuf[:, lane]
                scale = rms(raw)
                normed = raw * scale
                grad = dkv_ref[:, lane]
                gvec[0, 0:1, 128:256] = (
                    jnp.sum(grad * normed, axis=0, keepdims=True)
                    + (gvec[0, 0:1, 128:256] if hd else 0.0)
                )
                scaled = grad * wide(kg_ref[...])
                out = scale * (scaled - normed * jnp.mean(scaled * normed, axis=-1, keepdims=True))
                acts[base + 6, 0, :, lane] = low(out)
            acts[base + 7, 0] = low(dkv_ref[:, 256:512])

        pl.run_scoped(key_phase, pltpu.VMEM(kraw_hbm.shape, jnp.float32), pltpu.SemaphoreType.DMA)
        after("kp")

        @pl.loop(seqs - 2, seqs)
        def _(s):
            ky_copy(s).wait_send()

        @pl.loop(0, seqs)
        def _(s):
            @pl.when(at_end)
            def _():
                kl_copy(s).wait_send()

            @pl.when(inside)
            def _():
                km_copy(s).wait_send()
                kh_copy(s).wait_send()

    pl.run_scoped(
        attention_back,
        pltpu.VMEM((seqs, 4, rows, 512), jnp.float32),
        pltpu.VMEM((2, 4, rows, 512), jnp.bfloat16),
        pltpu.VMEM((seqs, 3, rows, 512), jnp.bfloat16),
        pltpu.VMEM((tokens, 512), jnp.float32),
        pltpu.VMEM((tokens, 512), jnp.float32),
    )

    def sixth_phase(wb, sems):
        pieces = ((wga_hbm, base + 2, 2), (wq_hbm, base + 4, 2), (wk_hbm, base + 6, 1), (wv_hbm, base + 7, 1))

        def loads(n, slot):
            at = pl.ds(pl.multiple_of(n * TILE, TILE), TILE)
            out, start = [], 0
            for p, (ref, _, count) in enumerate(pieces):
                out.append(
                    pltpu.make_async_copy(
                        ref.at[at], wb.at[slot, :, pl.ds(start, count * TILE)], sems.at[slot, p]
                    )
                )
                start += count * TILE
            return out

        def compute(slot):
            total, start = None, 0
            for _, first, count in pieces:
                for n in range(count):
                    part = dot_rows(acts[first + n, 0], wb[slot, :, pl.ds(start, TILE)])
                    total = part if total is None else total + part
                    start += TILE
            return total

        pl.semaphore_wait(credit, 2)
        reduce_start(2, loads, compute, "p7")

    pl.run_scoped(
        sixth_phase,
        pltpu.VMEM((2, TILE, 6 * TILE), jnp.bfloat16),
        pltpu.SemaphoreType.DMA((2, 4)),
    )

    for step in range(5):
        device = (y_dev, lo_dev, hi_dev, core_dev, x_dev)[step]
        copy = remote(gvec.at[step], gvec_got.at[step], gv_s.at[step], gv_r.at[step], device)
        copy.start()
        copy.wait()
        gvec[step + 1] = gvec[step] + gvec_got[step]
    piece = qg_out.shape[1]
    turn = lax.rem(128 - seq * piece, 128)
    for out, at in ((qg_out, 0), (kg_out, 128)):
        out[...] = pltpu.roll(gvec[5, :, at : at + 128], turn, 1)[0:1, 0:piece]

    reduce_end(2)

    def last_phase(xbuf, dbuf, obuf, sems, o_sems):
        def loads(r, slot):
            at = pl.ds(r * 128, 128)
            return (
                pltpu.make_async_copy(x_hbm.at[at], xbuf.at[slot], sems.at[slot, 0]),
                pltpu.make_async_copy(dh_hbm.at[at], dbuf.at[slot], sems.at[slot, 1]),
            )

        def store(r, slot):
            return pltpu.make_async_copy(obuf.at[slot], x_out.at[pl.ds(r * 128, 128)], o_sems.at[slot])

        for copy in loads(0, 0):
            copy.start()

        @pl.loop(0, n_chunks)
        def _(r):
            slot = lax.rem(r, 2)

            @pl.when(r < n_chunks - 1)
            def _():
                for copy in loads(r + 1, 1 - slot):
                    copy.start()

            for copy in loads(r, slot):
                copy.wait()

            @pl.when(r >= 2)
            def _():
                store(r - 2, slot).wait()

            value = wide(xbuf[slot])
            scale = rms(value)
            normed = value * scale
            grad = fin_rows(2, pl.multiple_of(r * 128, 128), 128)
            vec[0, 0:1] += jnp.sum(grad * normed, axis=0, keepdims=True)
            scaled = grad * wide(n1_ref[...])
            inner = jnp.mean(scaled * normed, axis=-1, keepdims=True)
            obuf[slot] = low(dbuf[slot] + scale * (scaled - normed * inner))
            store(r, slot).start()

        store(n_chunks - 2, n_chunks % 2).wait()
        store(n_chunks - 1, (n_chunks - 1) % 2).wait()

    pl.run_scoped(
        last_phase,
        pltpu.VMEM((2, 128, width), jnp.bfloat16),
        pltpu.VMEM((2, 128, width), jnp.float32),
        pltpu.VMEM((2, 128, width), jnp.bfloat16),
        pltpu.SemaphoreType.DMA((2, 2)),
        pltpu.SemaphoreType.DMA((2,)),
    )

    after("lp")
    for step in range(3):
        device = (y_dev, lo_dev, hi_dev)[step]
        copy = remote(vec.at[step], vec_got.at[step], nv_s.at[step], nv_r.at[step], device)
        copy.start()
        copy.wait()
        vec[step + 1] = vec[step] + vec_got[step]
    own = pl.ds(pl.multiple_of(seq * TILE, TILE), TILE)
    n1_out[...] = vec[3, 0:1, own]
    n2_out[...] = vec[3, 1:2, own]

    after("vec")

    @pl.loop(0, item_count)
    def _(i):
        act_copy(i).wait_send()

    for i in range(item_count - 4, item_count):

        @pl.when(at_end)
        def _():
            z1_copy(i).wait_send()

        @pl.when(inside)
        def _():
            z2_copy(i).wait_send()
            z3_copy(i).wait_send()

    for i in range(item_count - 2, item_count):
        out_wait(i)

    for l in (0, 2, 3):
        lt_copy(l).wait_send()
        lt_core(l, head).wait_send()
        lt_x(l, head).wait_send()
        lt_far(l, x_head).wait_send()


def back_call(hbm, vmem, smem, sizes):
    tokens, width, seqs, rows, keys_total, hidden = sizes
    count = 3 * (hidden // TILE) + 8
    bf, f32 = jnp.bfloat16, jnp.float32
    dma = pltpu.SemaphoreType.DMA
    scratch = [
        pltpu.VMEM((count, 2, tokens, TILE), bf),
        pltpu.VMEM((4, 2, 4, TILE, tokens), bf),
        pltpu.VMEM((4, TILE, tokens), bf),
        pltpu.VMEM((4, tokens, TILE), bf),
        pltpu.VMEM((2, 4, tokens, TILE), bf),
        pltpu.VMEM((2, 4, tokens, TILE), bf),
        pltpu.VMEM((2, 8, tokens, TILE), bf),
        pltpu.VMEM((seqs, 4, rows, 512), bf),
        pltpu.VMEM((seqs, 3, rows, 512), bf),
        pltpu.VMEM((seqs, 2, rows, 512), bf),
        pltpu.VMEM((seqs, rows, 512), bf),
        pltpu.VMEM((4, 3, TILE, TILE), bf),
        pltpu.VMEM((4, TILE, TILE), bf),
        pltpu.VMEM((2, TILE, TILE), f32),
        pltpu.VMEM((tokens, width), bf),
        pltpu.VMEM((tokens, width), bf),
        pltpu.VMEM((2, 2, 8, tokens), f32),
        pltpu.VMEM((4, 8, width), f32),
        pltpu.VMEM((3, 8, width), f32),
        pltpu.VMEM((6, 8, 256), f32),
        pltpu.VMEM((5, 8, 256), f32),
        pltpu.VMEM((keys_total, 2 * rows), f32),
        pltpu.VMEM((tokens, 1), f32),
        *(dma((count,)) for _ in range(8)),
        *(dma((4,)) for _ in range(8)),
        *(dma((3, 4)) for _ in range(6)),
        *(dma((seqs,)) for _ in range(8)),
        dma((3,)), dma((3,)), dma((5,)), dma((5,)),
        dma((4,)), dma((2,)), dma((8,)), pltpu.SemaphoreType.REGULAR,
    ]
    any_spec = pl.BlockSpec(memory_space=pl.ANY)
    vmem_spec = pl.BlockSpec(memory_space=pltpu.VMEM)
    smem_spec = pl.BlockSpec(memory_space=pltpu.SMEM)
    return pl.pallas_call(
        back_kernel,
        out_shape=[
            jax.ShapeDtypeStruct((tokens, width), bf),
            jax.ShapeDtypeStruct((tokens, width), bf),
            jax.ShapeDtypeStruct((hidden, TILE), f32),
            jax.ShapeDtypeStruct((TILE, hidden), f32),
            jax.ShapeDtypeStruct((TILE, hidden), f32),
            jax.ShapeDtypeStruct((512, TILE), f32),
            jax.ShapeDtypeStruct((TILE, 512), f32),
            jax.ShapeDtypeStruct((TILE, 512), f32),
            jax.ShapeDtypeStruct((TILE, TILE), f32),
            jax.ShapeDtypeStruct((TILE, TILE), f32),
            jax.ShapeDtypeStruct((1, width // 8), f32),
            jax.ShapeDtypeStruct((1, width // 8), f32),
            jax.ShapeDtypeStruct((1, 16), f32),
            jax.ShapeDtypeStruct((1, 16), f32),
            jax.ShapeDtypeStruct((tokens, width), f32),
            jax.ShapeDtypeStruct((count, 3, TILE, TILE), bf),
            jax.ShapeDtypeStruct((count, 2, TILE, TILE), bf),
            jax.ShapeDtypeStruct((count, TILE, TILE), bf),
        ],
        in_specs=[any_spec] * len(hbm) + [vmem_spec] * len(vmem) + [smem_spec] * len(smem),
        out_specs=[any_spec] * 10 + [vmem_spec] * 4 + [any_spec] * 4,
        scratch_shapes=scratch,
        compiler_params=pltpu.CompilerParams(
            collective_id=1, has_side_effects=True, vmem_limit_bytes=61 << 20
        ),
    )(*hbm, *vmem, *smem)


def hand_over_kernel(count, *refs):
    src, dst, held, sems = refs[:count], refs[count : 2 * count], refs[2 * count : -1], refs[-1]
    into = [pltpu.make_async_copy(src[i], held[i], sems.at[0, i]) for i in range(count)]
    out = [pltpu.make_async_copy(held[i], dst[i], sems.at[1, i]) for i in range(count)]
    for copy in into:
        copy.start()
    for i in range(count):
        into[i].wait()
        out[i].start()
    for copy in out:
        copy.wait()


def hand_over(arrays):
    any_spec = pl.BlockSpec(memory_space=pl.ANY)
    count = len(arrays)
    return pl.pallas_call(
        functools.partial(hand_over_kernel, count),
        out_shape=[jax.ShapeDtypeStruct(a.shape, a.dtype) for a in arrays],
        in_specs=[any_spec] * count,
        out_specs=[any_spec] * count,
        scratch_shapes=[
            *(pltpu.VMEM(a.shape, a.dtype) for a in arrays),
            pltpu.SemaphoreType.DMA((2, count)),
        ],
        compiler_params=pltpu.CompilerParams(vmem_limit_bytes=61 << 20),
    )(*arrays)


def forward_kernel(
    x_hbm, wq_hbm, wk_hbm, wv_hbm, wga_hbm, wo_hbm, cot_hbm, wd_hbm,
    ids_ref, n1_ref, qg_ref, kg_ref, order_ref, counts_ref, weights_ref,
    h_out, xt_out, q_out, kv_out, o_out, sig_out, y_out, qraw_out, kraw_out, ltd_out, dm_out, lse_ref,
    xv, xn, wqv, wkv, wvv, wgav, wov, kv, qv, qraw, kraw, sig, ov, yv, xtv, hv,
    dout, ltd, odd, wdv, dmv, bias, factor_ref,
    csend, crecv, fin, xrecv,
    x_sem, w_sem, out_sem, h_sem, kz_s, kz_r, kf_s, ky_s, ky_r, l_sem, d_sem, m_sem, c1_s, c1_r, x_s, x_r, c2_s, c2_r,
):
    seq, head = lax.axis_index("seq"), lax.axis_index("head")
    z, y = lax.div(seq, 2), lax.rem(seq, 2)
    c = lax.rem(head, 2)
    y_dev = {"seq": z * 2 + 1 - y}
    lo_dev, mid_dev = {"seq": other_z(z, 1) * 2 + y}, {"seq": (3 - z) * 2 + y}
    at_end, inside = lax.rem(z, 3) == 0, lax.rem(z, 3) != 0
    core_dev = {"head": head + 1 - 2 * c}
    x_dev = {"head": head + 2 - 4 * lax.div(head, 2)}
    seqs, slots, rows = kv.shape[0], kv.shape[1], kv.shape[2]
    tokens, width = x_hbm.shape
    half = width // 2
    epsilon_k = 1e-06

    def rms(value):
        return lax.rsqrt(jnp.mean(value * value, axis=-1, keepdims=True) + epsilon_k)

    def rows_at(s):
        return pl.ds(pl.multiple_of(s * rows, 128), rows)

    def x_load(s):
        return pltpu.make_async_copy(x_hbm.at[rows_at(s)], xv.at[rows_at(s)], x_sem.at[s])

    weight_loads = [
        pltpu.make_async_copy(src, dst, w_sem.at[i])
        for i, (src, dst) in enumerate(
            ((wk_hbm, wkv), (wv_hbm, wvv), (wq_hbm, wqv), (wga_hbm, wgav), (wo_hbm, wov))
        )
    ]
    for s in range(seqs):
        x_load(s).start()
    for load in weight_loads:
        load.start()
    for s in range(seqs):
        pltpu.make_async_copy(cot_hbm.at[rows_at(s)], dout.at[rows_at(s)], d_sem.at[s]).start()

    barrier = pltpu.get_barrier_semaphore()
    for device in (y_dev, lo_dev, core_dev, x_dev):
        pl.semaphore_signal(barrier, inc=1, device_id=device, device_id_type=MESH)

    @pl.when(inside)
    def _():
        pl.semaphore_signal(barrier, inc=1, device_id=mid_dev, device_id_type=MESH)
        pl.semaphore_wait(barrier, 5)

    @pl.when(at_end)
    def _():
        pl.semaphore_wait(barrier, 4)

    def remote(src, dst, send, recv, device):
        return pltpu.make_async_remote_copy(
            src_ref=src, dst_ref=dst, send_sem=send, recv_sem=recv, device_id=device, device_id_type=MESH
        )

    def own_out(s):
        return remote(kv.at[s, 0], kv.at[s, 2], kz_s.at[s, 1], kz_r.at[s, 1], lo_dev)

    def own_over(s):
        return remote(kv.at[s, 0], kv.at[s, 6], kz_s.at[s, 3], kz_r.at[s, 3], mid_dev)

    def end_over(s):
        return remote(kv.at[s, 2], kv.at[s, 4], kz_s.at[s, 2], kz_r.at[s, 2], mid_dev)

    def mid_out(s):
        return remote(kv.at[s, 6], kv.at[s, 4], kf_s.at[s, 0], kz_r.at[s, 2], lo_dev)

    def far_out(s):
        return remote(kv.at[s, 4], kv.at[s, 6], kf_s.at[s, 1], kz_r.at[s, 3], lo_dev)

    def y_copy(s, t):
        return remote(kv.at[s, 2 * t], kv.at[s, 2 * t + 1], ky_s.at[s, t], ky_r.at[s, t], y_dev)

    def core_copy(s):
        return remote(csend.at[s], crecv.at[s], c1_s.at[s], c1_r.at[s], core_dev)

    def x_copy(s):
        return remote(fin.at[s, c], xrecv.at[s], x_s.at[s], x_r.at[s], x_dev)

    def fin_copy(s):
        return remote(fin.at[s, c], fin.at[s, c], c2_s.at[s], c2_r.at[s], core_dev)

    def fin_copy_in(s):
        piece = fin.at[s, 1 - c]
        return remote(piece, piece, c2_s.at[s], c2_r.at[s], core_dev)

    weight_loads[0].wait()
    weight_loads[1].wait()

    @pl.loop(0, seqs)
    def _(s):
        x_load(s).wait()
        at = rows_at(s)
        value = wide(xv[at])
        xn[at] = low(value * rms(value) * wide(n1_ref[...]))
        raw = dot_plain(xn[at], wkv[...])
        kraw[at] = raw
        for n in range(2):
            lane = slice(n * 128, (n + 1) * 128)
            part = raw[:, lane]
            kv[s, 0, :, lane] = low(part * rms(part) * wide(kg_ref[...]))
        kv[s, 0, :, 256:512] = low(dot_plain(xn[at], wvv[...]))
        y_copy(s, 0).start()
        own_out(s).start()

        @pl.when(inside)
        def _():
            own_over(s).start()

    outs = []

    def leave(src, dst):
        copy = pltpu.make_async_copy(src, dst, out_sem.at[len(outs)])
        copy.start()
        outs.append(copy)

    leave(kraw, kraw_out)

    def forward_keys(s):
        own_out(s).wait_recv()

        @pl.when(inside)
        def _():
            end_over(s).start()
            y_copy(s, 1).start()
            own_over(s).wait_recv()
            mid_out(s).start()
            y_copy(s, 3).start()
            end_over(s).wait_recv()
            far_out(s).start()
            y_copy(s, 2).start()

        @pl.when(at_end)
        def _():
            y_copy(s, 1).start()
            mid_out(s).wait_recv()
            y_copy(s, 2).start()
            far_out(s).wait_recv()
            y_copy(s, 3).start()

    hidden_tiles = wd_hbm.shape[0] // TILE

    def cot_load(s):
        return pltpu.make_async_copy(cot_hbm.at[rows_at(s)], dout.at[rows_at(s)], d_sem.at[s])

    def wd_load(j):
        at = pl.ds(pl.multiple_of(j * TILE, TILE), TILE)
        return pltpu.make_async_copy(wd_hbm.at[at], wdv.at[lax.rem(j, 2)], l_sem.at[lax.rem(j, 2)])

    def dm_store(j):
        return pltpu.make_async_copy(dmv.at[lax.rem(j, 2)], dm_out.at[j], m_sem.at[lax.rem(j, 2)])

    def spread_copy():
        return remote(odd, ltd.at[1, pl.ds(2 * c, 2)], l_sem.at[2], l_sem.at[3], y_dev)

    def relay_copy(part):
        piece = ltd.at[1, pl.ds(2 * part, 2)]
        return remote(piece, piece, l_sem.at[4], l_sem.at[5], core_dev)

    def dm_tile(j):
        @pl.when(j < hidden_tiles - 1)
        def _():
            wd_load(j + 1).start()

        wd_load(j).wait()

        @pl.when(j >= 2)
        def _():
            dm_store(j - 2).wait()

        dmv[lax.rem(j, 2)] = dot_rows(dout[...], wdv[lax.rem(j, 2)])
        dm_store(j).start()

    fill_bias(order_ref, bias, rows, z, y, seq)
    fill_factor(ids_ref, counts_ref, weights_ref, factor_ref, float(tokens * 8))

    weight_loads[2].wait()
    weight_loads[3].wait()
    scale_q = 128.0**-0.5

    @pl.loop(0, seqs)
    def _(s):
        at = rows_at(s)
        raw = dot_plain(xn[at], wqv[...])
        qraw[at] = raw
        for n in range(4):
            lane = slice(n * 128, (n + 1) * 128)
            part = raw[:, lane]
            qv[at, lane] = low(part * rms(part) * (wide(qg_ref[...]) * scale_q))
        sig[at] = jax.nn.sigmoid(dot_plain(xn[at], wgav[...]))

    leave(qraw, qraw_out)
    leave(qv, q_out)
    leave(sig, sig_out)
    forward_keys(0)

    @pl.loop(0, width // TILE)
    def _(n):
        at = pl.ds(pl.multiple_of(n * TILE, TILE), TILE)
        xtv[n] = xn[:, at].T

    leave(xtv, xt_out)
    wd_load(0).start()

    @pl.loop(0, seqs)
    def _(s):
        cot_load(s).wait()
        at = rows_at(s)
        dout[at] = low(wide(dout[at]) * factor_ref[at])

    @pl.loop(0, 4)
    def _(t):
        at = pl.multiple_of((other_z(z, t) * 2 + y) * TILE, TILE)
        ltd[0, t] = dout[:, pl.ds(at, TILE)].T

    @pl.loop(0, 2)
    def _(k):
        at = pl.multiple_of((other_z(z, 2 * c + k) * 2 + 1 - y) * TILE, TILE)
        odd[k] = dout[:, pl.ds(at, TILE)].T

    weight_loads[4].wait()

    def finish(s):
        x_copy(s).wait()
        fin[s, c] = low(wide(fin[s, c]) + wide(xrecv[s]))
        fin_copy(s).start()

    def h_store(s, slot):
        return pltpu.make_async_copy(hv.at[slot], h_out.at[rows_at(s)], h_sem.at[slot])

    def finish_rows(s):
        slot = lax.rem(s, 2)
        fin_copy_in(s).wait_recv()

        @pl.when(s >= 2)
        def _():
            h_store(s - 2, slot).wait()

        hv[slot, :, 0:half] = wide(xv[rows_at(s), 0:half]) + wide(fin[s, 0])
        hv[slot, :, half:width] = wide(xv[rows_at(s), half:width]) + wide(fin[s, 1])
        h_store(s, slot).start()

    @pl.loop(0, seqs)
    def _(s):
        @pl.when(s < seqs - 1)
        def _():
            forward_keys(s + 1)

            @pl.when(s == seqs - 2)
            def _():
                spread_copy().start()

            dm_tile(2 * s)
            dm_tile(2 * s + 1)

        for t in range(4):
            y_copy(s, t).wait_recv()
        at = rows_at(s)
        for n in range(2):
            lanes = [slice((2 * n + g) * 128, (2 * n + g + 1) * 128) for g in range(2)]
            key = kv[s, :, :, n * 128 : (n + 1) * 128].reshape(slots * rows, 128)
            value = kv[s, :, :, 256 + n * 128 : 256 + (n + 1) * 128].reshape(slots * rows, 128)
            q = jnp.concatenate([qv[at, lane] for lane in lanes], axis=0)
            scores = dot_rows(key, q) + bias[...]
            top = jnp.max(scores, axis=0, keepdims=True)
            probs = jnp.exp(scores - top)
            total = jnp.sum(probs, axis=0, keepdims=True)
            out = (dot_first(value, low(probs)) / total).T
            lse_ref[s, n] = top + jnp.log(total)
            for g in range(2):
                ov[at, lanes[g]] = out[g * rows : (g + 1) * rows]
        gated = low(ov[at] * sig[at])
        yv[at] = gated
        away = pl.ds(pl.multiple_of((1 - c) * half, 128), half)
        mine = pl.ds(pl.multiple_of(c * half, 128), half)
        csend[s] = low(dot_plain(gated, wov[:, away]))
        core_copy(s).start()
        part = dot_plain(gated, wov[:, mine])
        core_copy(s).wait_recv()
        fin[s, c] = low(part + wide(crecv[s]))
        x_copy(s).start()

        @pl.when(s >= 1)
        def _():
            finish(s - 1)

        @pl.when(s >= 2)
        def _():
            finish_rows(s - 2)

    leave(kv, kv_out)
    leave(ov, o_out)
    leave(yv, y_out)
    finish_rows(seqs - 2)
    spread_copy().wait_recv()
    relay_copy(c).start()
    finish(seqs - 1)
    finish_rows(seqs - 1)
    h_store(seqs - 2, seqs % 2).wait()
    h_store(seqs - 1, (seqs - 1) % 2).wait()
    relay_copy(1 - c).wait_recv()
    leave(ltd, ltd_out)
    spread_copy().wait_send()
    relay_copy(c).wait_send()
    dm_store(hidden_tiles - 2).wait()
    dm_store(hidden_tiles - 1).wait()
    for copy in outs:
        copy.wait()

    @pl.loop(0, seqs)
    def _(s):
        own_out(s).wait_send()

        @pl.when(inside)
        def _():
            for copy in (own_over, end_over, mid_out, far_out):
                copy(s).wait_send()

        for t in range(4):
            y_copy(s, t).wait_send()
        core_copy(s).wait_send()
        fin_copy(s).wait_send()


def forward_call(hbm, vmem, smem, sizes):
    tokens, width, seqs, rows, slots, hidden = sizes
    bf, f32 = jnp.bfloat16, jnp.float32
    dma = pltpu.SemaphoreType.DMA
    half = width // 2
    kv_shape = (seqs, slots, rows, 512)
    scratch = [
        pltpu.VMEM((tokens, width), bf),
        pltpu.VMEM((tokens, width), bf),
        pltpu.VMEM((width, 512), bf),
        pltpu.VMEM((width, 256), bf),
        pltpu.VMEM((width, 256), bf),
        pltpu.VMEM((width, 512), bf),
        pltpu.VMEM((512, width), bf),
        pltpu.VMEM(kv_shape, bf),
        pltpu.VMEM((tokens, 512), bf),
        pltpu.VMEM((tokens, 512), f32),
        pltpu.VMEM((tokens, 256), f32),
        pltpu.VMEM((tokens, 512), f32),
        pltpu.VMEM((tokens, 512), f32),
        pltpu.VMEM((tokens, 512), bf),
        pltpu.VMEM((width // TILE, TILE, tokens), bf),
        pltpu.VMEM((2, rows, width), f32),
        pltpu.VMEM((tokens, width), bf),
        pltpu.VMEM((2, 4, TILE, tokens), bf),
        pltpu.VMEM((2, TILE, tokens), bf),
        pltpu.VMEM((2, TILE, width), bf),
        pltpu.VMEM((2, tokens, TILE), f32),
        pltpu.VMEM((slots * rows, 2 * rows), f32),
        pltpu.VMEM((tokens, 1), f32),
        pltpu.VMEM((seqs, rows, half), bf),
        pltpu.VMEM((seqs, rows, half), bf),
        pltpu.VMEM((seqs, 2, rows, half), bf),
        pltpu.VMEM((seqs, rows, half), bf),
        dma((seqs,)), dma((5,)), dma((9,)), dma((2,)),
        *(dma((seqs, 4)) for _ in range(5)),
        dma((6,)), dma((seqs,)), dma((2,)),
        *(dma((seqs,)) for _ in range(6)),
    ]
    any_spec = pl.BlockSpec(memory_space=pl.ANY)
    vmem_spec = pl.BlockSpec(memory_space=pltpu.VMEM)
    smem_spec = pl.BlockSpec(memory_space=pltpu.SMEM)
    return pl.pallas_call(
        forward_kernel,
        out_shape=[
            jax.ShapeDtypeStruct((tokens, width), f32),
            jax.ShapeDtypeStruct((width // TILE, TILE, tokens), bf),
            jax.ShapeDtypeStruct((tokens, 512), bf),
            jax.ShapeDtypeStruct(kv_shape, bf),
            jax.ShapeDtypeStruct((tokens, 512), f32),
            jax.ShapeDtypeStruct((tokens, 512), f32),
            jax.ShapeDtypeStruct((tokens, 512), bf),
            jax.ShapeDtypeStruct((tokens, 512), f32),
            jax.ShapeDtypeStruct((tokens, 256), f32),
            jax.ShapeDtypeStruct((2, 4, TILE, tokens), bf),
            jax.ShapeDtypeStruct((hidden // TILE, tokens, TILE), f32),
            jax.ShapeDtypeStruct((seqs, 2, 1, 2 * rows), f32),
        ],
        in_specs=[any_spec] * len(hbm) + [vmem_spec] * len(vmem) + [smem_spec] * len(smem),
        out_specs=[any_spec] * 11 + [vmem_spec],
        scratch_shapes=scratch,
        compiler_params=pltpu.CompilerParams(
            collective_id=2, has_side_effects=True, vmem_limit_bytes=60 << 20
        ),
    )(*hbm, *vmem, *smem)


def on_device(
    x_in,
    cot,
    domain_ids,
    domain_counts,
    domain_weights,
    block_order,
    norm1,
    w_query,
    w_key,
    w_value,
    w_gate_attn,
    w_out,
    query_gain,
    key_gain,
    norm2,
    w_gate,
    w_up,
    w_down,
):
    sequences, local_rows, width = x_in.shape
    row_total = sequences * local_rows
    devices = lax.axis_size("seq")
    x_rows = x_in.reshape(row_total, width)
    scalars = (block_order, domain_counts, domain_weights)
    h, xt, query, kv, attn, sig, gated, query_raw, key_raw, ltd, dm, lse = forward_call(
        (x_rows, w_query, w_key, w_value, w_gate_attn, w_out, cot.reshape(row_total, width), w_down),
        (domain_ids, norm1[None, :], query_gain[None, :], key_gain[None, :]),
        scalars,
        (row_total, width, sequences, local_rows, devices, w_down.shape[0]),
    )
    out, x_grad, down, gate, up, wout, wga, wquery, wkey, wvalue, *small = back_call(
        (
            h,
            cot.reshape(row_total, width),
            x_rows,
            xt,
            ltd,
            dm,
            query,
            kv.reshape(sequences, devices * local_rows, -1),
            attn,
            sig,
            gated,
            query_raw,
            key_raw,
            w_gate,
            w_up,
            w_down,
            w_out,
            w_query,
            w_key,
            w_value,
            w_gate_attn,
        ),
        (
            domain_ids,
            lse,
            norm1[None, :],
            norm2[None, :],
            query_gain[None, :],
            key_gain[None, :],
        ),
        scalars,
        (row_total, width, sequences, local_rows, local_rows * devices, w_down.shape[0]),
    )

    out, x_grad, down, gate, up, wout, wga, wquery, wkey, wvalue, *small = hand_over(
        (out, x_grad, down, gate, up, wout, wga, wquery, wkey, wvalue, *small[:4])
    )
    return (
        out.reshape(x_in.shape),
        x_grad.reshape(x_in.shape),
        small[0].reshape(-1),
        wquery,
        wkey,
        wvalue,
        wga,
        wout,
        small[2].reshape(-1),
        small[3].reshape(-1),
        small[1].reshape(-1),
        gate,
        up,
        down,
    )


def on_device_plain(
    x_in,
    cot,
    domain_ids,
    domain_counts,
    domain_weights,
    block_order,
    norm1,
    w_query,
    w_key,
    w_value,
    w_gate_attn,
    w_out,
    query_gain,
    key_gain,
    norm2,
    w_gate,
    w_up,
    w_down,
):
    sequences, local_rows, model_width = x_in.shape
    row_total = sequences * local_rows
    head_dim = query_gain.shape[0]
    kv_local = w_key.shape[1] // head_dim
    q_local = w_query.shape[1] // head_dim
    group_size = q_local // kv_local
    block_rows = local_rows // 2
    seq_devices = lax.axis_size("seq")
    first_row = lax.axis_index("seq") * local_rows
    query_pos = positions(block_order, first_row, local_rows, block_rows)
    query_factor = head_dim ** (-0.5)
    q_gain = query_gain.astype(jnp.float32)
    k_gain = key_gain.astype(jnp.float32)
    gain_one = norm1.astype(jnp.float32)
    gain_two = norm2.astype(jnp.float32)
    x_float = x_in.reshape(row_total, model_width).astype(jnp.float32)
    scale_one = norm_scale(x_float)
    normed_one = x_float * scale_one
    x_normed = (normed_one * gain_one).astype(jnp.bfloat16)
    query_raw = product(x_normed, w_query).reshape(row_total, q_local, head_dim)
    key_raw = product(x_normed, w_key).reshape(row_total, kv_local, head_dim)
    value_rows = product(x_normed, w_value).astype(jnp.bfloat16)
    gate_pre = product(x_normed, w_gate_attn)
    query_scale = norm_scale(query_raw)
    query_normed = query_raw * query_scale
    key_scale = norm_scale(key_raw)
    key_normed = key_raw * key_scale
    query = (query_normed * q_gain * query_factor).astype(jnp.bfloat16)
    key_rows = (key_normed * k_gain).astype(jnp.bfloat16)
    project_query_heads = query.reshape(
        sequences, local_rows, kv_local, group_size, head_dim
    ).transpose(0, 2, 3, 1, 4)
    (
        query_scale,
        query_normed,
        key_scale,
        key_normed,
        query_heads,
        key_rows,
        value_rows,
        gate_pre,
    ) = (
        query_scale,
        query_normed,
        key_scale,
        key_normed,
        project_query_heads,
        key_rows,
        value_rows,
        gate_pre,
    )
    key_seq = key_rows.reshape(sequences, local_rows, kv_local * head_dim)
    value_seq = value_rows.reshape(sequences, local_rows, kv_local * head_dim)
    stat_shape = (sequences, kv_local, group_size, local_rows)
    running_max = jnp.full(stat_shape, -1e30, jnp.float32)
    key_piece = lax.all_gather(key_seq, "seq", axis=1, tiled=True)
    value_piece = lax.all_gather(value_seq, "seq", axis=1, tiled=True)
    row_count = key_piece.shape[1]
    key_block = key_piece.reshape(sequences, row_count, kv_local, head_dim)
    value_block = value_piece.reshape(sequences, row_count, kv_local, head_dim)
    key_pos = positions(block_order, jnp.int32(0), row_count, block_rows)
    allowed = key_pos[None, :] <= query_pos[:, None]
    scores = jnp.einsum(
        "skgqd,spkd->skgqp", query_heads, key_block, preferred_element_type=jnp.float32
    )
    scores = jnp.where(allowed, scores, -1e30)
    new_max = jnp.maximum(running_max, jnp.max(scores, axis=-1))
    weights = jnp.where(allowed, jnp.exp(scores - new_max[..., None]), 0.0)
    running_sum = jnp.sum(weights, axis=-1)
    weighted = jnp.einsum(
        "skgqp,spkd->skgqd",
        weights.astype(jnp.bfloat16),
        value_block,
        preferred_element_type=jnp.float32,
    )
    running_max, running_sum, weighted = (new_max, running_sum, weighted)
    log_total = running_max + jnp.log(running_sum)
    attn_heads = weighted / running_sum[..., None]
    attn_flat = attn_heads.transpose(0, 3, 1, 2, 4).reshape(row_total, q_local * head_dim)
    gate_sig = jax.nn.sigmoid(gate_pre)
    gated = (attn_flat * gate_sig).astype(jnp.bfloat16)
    attn_sum = lax.psum(product(gated, w_out).astype(jnp.bfloat16), "head").astype(jnp.float32)
    residual = x_float + attn_sum
    scale_two = norm_scale(residual)
    normed_two = residual * scale_two
    h_normed = (normed_two * gain_two).astype(jnp.bfloat16)
    gate_proj = product(h_normed, w_gate)
    up_proj = product(h_normed, w_up)
    gate_logit = jax.nn.sigmoid(gate_proj)
    gate_act = gate_proj * gate_logit
    mixed = (gate_act * up_proj).astype(jnp.bfloat16)
    mlp_sum = lax.psum(product(mixed, w_down).astype(jnp.bfloat16), "head").astype(jnp.float32)
    block_out = (
        (residual + mlp_sum).astype(jnp.bfloat16).reshape(sequences, local_rows, model_width)
    )
    domain_total = domain_weights.shape[0]
    domain_index = jnp.arange(domain_total, dtype=jnp.int32)
    factor = (
        domain_weights
        * (row_total * seq_devices)
        / (domain_total * domain_counts.astype(jnp.float32))
    )
    picked = domain_ids.reshape(row_total)[:, None] == domain_index[None, :]
    row_scale = jnp.sum(jnp.where(picked, factor[None, :], 0.0), axis=1)
    grad_out = cot.reshape(row_total, model_width).astype(jnp.float32) * row_scale[:, None]
    grad_low = grad_out.astype(jnp.bfloat16)
    grad_down = outer_sum(mixed, grad_low)
    grad_mixed = back_product(grad_low, w_down)
    grad_gate = (grad_mixed * up_proj * gate_logit * (1.0 + gate_proj * (1.0 - gate_logit))).astype(
        jnp.bfloat16
    )
    grad_up = (grad_mixed * gate_act).astype(jnp.bfloat16)
    grad_mlp_gate = outer_sum(h_normed, grad_gate)
    grad_mlp_up = outer_sum(h_normed, grad_up)
    grad_hnorm = lax.psum(
        (back_product(grad_gate, w_gate) + back_product(grad_up, w_up)).astype(jnp.bfloat16), "head"
    ).astype(jnp.float32)
    grad_norm_two = jnp.sum(grad_hnorm * normed_two, axis=0)
    grad_resid = grad_out + norm_back(grad_hnorm, normed_two, scale_two, gain_two)
    grad_attn = grad_resid.astype(jnp.bfloat16)
    grad_wout = outer_sum(gated, grad_attn)
    grad_gated = back_product(grad_attn, w_out)
    grad_heads_flat = (grad_gated * gate_sig).astype(jnp.bfloat16)
    grad_gatepre = (grad_gated * attn_flat * gate_sig * (1.0 - gate_sig)).astype(jnp.bfloat16)
    grad_wgate_attn = outer_sum(x_normed, grad_gatepre)
    grad_heads = grad_heads_flat.reshape(
        sequences, local_rows, kv_local, group_size, head_dim
    ).transpose(0, 2, 3, 1, 4)
    row_delta = jnp.sum(grad_heads.astype(jnp.float32) * attn_heads, axis=-1)
    key_piece = lax.all_gather(key_seq, "seq", axis=1, tiled=True)
    value_piece = lax.all_gather(value_seq, "seq", axis=1, tiled=True)
    row_count = key_piece.shape[1]
    key_block = key_piece.reshape(sequences, row_count, kv_local, head_dim)
    value_block = value_piece.reshape(sequences, row_count, kv_local, head_dim)
    key_pos = positions(block_order, jnp.int32(0), row_count, block_rows)
    allowed = key_pos[None, :] <= query_pos[:, None]
    scores = jnp.einsum(
        "skgqd,spkd->skgqp", query_heads, key_block, preferred_element_type=jnp.float32
    )
    probs = jnp.where(
        allowed, jnp.exp(jnp.where(allowed, scores, -1e30) - log_total[..., None]), 0.0
    )
    grad_probs = jnp.einsum(
        "skgqd,spkd->skgqp", grad_heads, value_block, preferred_element_type=jnp.float32
    )
    grad_scores = (probs * (grad_probs - row_delta[..., None])).astype(jnp.bfloat16)
    grad_query = jnp.einsum(
        "skgqp,spkd->skgqd", grad_scores, key_block, preferred_element_type=jnp.float32
    )
    key_term = jnp.einsum(
        "skgqp,skgqd->spkd", grad_scores, query_heads, preferred_element_type=jnp.float32
    ).reshape(sequences, row_count, kv_local * head_dim)
    value_term = jnp.einsum(
        "skgqp,skgqd->spkd",
        probs.astype(jnp.bfloat16),
        grad_heads,
        preferred_element_type=jnp.float32,
    ).reshape(sequences, row_count, kv_local * head_dim)
    grad_keys = key_term
    grad_values = value_term
    grad_query, grad_keys, grad_values = (grad_query, grad_keys, grad_values)
    grad_key_own, grad_value_own = (
        lax.psum_scatter(
            grad_keys.astype(jnp.bfloat16), "seq", scatter_dimension=1, tiled=True
        ).astype(jnp.float32),
        lax.psum_scatter(
            grad_values.astype(jnp.bfloat16), "seq", scatter_dimension=1, tiled=True
        ).astype(jnp.float32),
    )
    grad_query_rows = grad_query.transpose(0, 3, 1, 2, 4).reshape(row_total, q_local, head_dim)
    grad_qgain_part = jnp.sum(grad_query_rows * query_normed * query_factor, axis=(0, 1))
    grad_query_raw = (
        norm_back(grad_query_rows, query_normed, query_scale, q_gain * query_factor)
        .astype(jnp.bfloat16)
        .reshape(row_total, q_local * head_dim)
    )
    grad_key_rows = grad_key_own.reshape(row_total, kv_local, head_dim)
    grad_kgain_part = jnp.sum(grad_key_rows * key_normed, axis=(0, 1))
    grad_key_raw = (
        norm_back(grad_key_rows, key_normed, key_scale, k_gain)
        .astype(jnp.bfloat16)
        .reshape(row_total, kv_local * head_dim)
    )
    grad_value_low = grad_value_own.reshape(row_total, kv_local * head_dim).astype(jnp.bfloat16)
    grad_xnorm_part = (
        back_product(grad_query_raw, w_query)
        + back_product(grad_key_raw, w_key)
        + back_product(grad_value_low, w_value)
        + back_product(grad_gatepre, w_gate_attn)
    )
    grad_xnorm, grad_qgain, grad_kgain = (
        lax.psum(grad_xnorm_part.astype(jnp.bfloat16), "head").astype(jnp.float32),
        lax.psum(grad_qgain_part.astype(jnp.bfloat16), "head").astype(jnp.float32),
        lax.psum(grad_kgain_part.astype(jnp.bfloat16), "head").astype(jnp.float32),
    )
    grad_norm_one = jnp.sum(grad_xnorm * normed_one, axis=0)
    x_grad = (
        (grad_resid + norm_back(grad_xnorm, normed_one, scale_one, gain_one))
        .astype(jnp.bfloat16)
        .reshape(sequences, local_rows, model_width)
    )
    grad_wquery = outer_sum(x_normed, grad_query_raw)
    grad_wkey = outer_sum(x_normed, grad_key_raw)
    grad_wvalue = outer_sum(x_normed, grad_value_low)
    all_totals = (
        lax.psum_scatter(
            grad_norm_one.astype(jnp.bfloat16), "seq", scatter_dimension=0, tiled=True
        ).astype(jnp.float32),
        lax.psum_scatter(
            grad_wquery.astype(jnp.bfloat16), "seq", scatter_dimension=0, tiled=True
        ).astype(jnp.float32),
        lax.psum_scatter(
            grad_wkey.astype(jnp.bfloat16), "seq", scatter_dimension=0, tiled=True
        ).astype(jnp.float32),
        lax.psum_scatter(
            grad_wvalue.astype(jnp.bfloat16), "seq", scatter_dimension=0, tiled=True
        ).astype(jnp.float32),
        lax.psum_scatter(
            grad_wgate_attn.astype(jnp.bfloat16), "seq", scatter_dimension=0, tiled=True
        ).astype(jnp.float32),
        lax.psum_scatter(
            grad_wout.astype(jnp.bfloat16), "seq", scatter_dimension=1, tiled=True
        ).astype(jnp.float32),
        lax.psum_scatter(
            grad_qgain.astype(jnp.bfloat16), "seq", scatter_dimension=0, tiled=True
        ).astype(jnp.float32),
        lax.psum_scatter(
            grad_kgain.astype(jnp.bfloat16), "seq", scatter_dimension=0, tiled=True
        ).astype(jnp.float32),
        lax.psum_scatter(
            grad_mlp_gate.astype(jnp.bfloat16), "seq", scatter_dimension=0, tiled=True
        ).astype(jnp.float32),
        lax.psum_scatter(
            grad_mlp_up.astype(jnp.bfloat16), "seq", scatter_dimension=0, tiled=True
        ).astype(jnp.float32),
        lax.psum_scatter(
            grad_down.astype(jnp.bfloat16), "seq", scatter_dimension=1, tiled=True
        ).astype(jnp.float32),
        lax.psum_scatter(
            grad_norm_two.astype(jnp.bfloat16), "seq", scatter_dimension=0, tiled=True
        ).astype(jnp.float32),
    )
    return (
        block_out,
        x_grad,
        all_totals[0],
        all_totals[1],
        all_totals[2],
        all_totals[3],
        all_totals[4],
        all_totals[5],
        all_totals[6],
        all_totals[7],
        all_totals[11],
        all_totals[8],
        all_totals[9],
        all_totals[10],
    )


def solution(mesh):
    fits = mesh.shape["seq"] == 8 and mesh.shape["head"] == 4
    return jax.shard_map(
        on_device if fits else on_device_plain,
        mesh=mesh,
        in_specs=(
            P(None, "seq", None),
            P(None, "seq", None),
            P(None, "seq"),
            P(),
            P(),
            P(),
            P(),
            P(None, "head"),
            P(None, "head"),
            P(None, "head"),
            P(None, "head"),
            P("head", None),
            P(),
            P(),
            P(),
            P(None, "head"),
            P(None, "head"),
            P("head", None),
        ),
        out_specs=(
            P(None, "seq", None),
            P(None, "seq", None),
            P("seq"),
            P("seq", "head"),
            P("seq", "head"),
            P("seq", "head"),
            P("seq", "head"),
            P("head", "seq"),
            P("seq"),
            P("seq"),
            P("seq"),
            P("seq", "head"),
            P("seq", "head"),
            P("head", "seq"),
        ),
        check_vma=False,
    )
```
